32 devices in a mesh: wide: 4 (over y, core), blk: 8 (over z, x).
Axes of the slice: x: 2, y: 2, z: 4, core: 2. Of those that a mesh axis runs over, the one named last changes fastest.
Arguments:
- text_blocks: bfloat16 [8, 1024, 768], P('wide', 'blk'), may hold values from -6 to 6
- image_blocks: bfloat16 [8, 1024, 768], P('wide', 'blk'), may hold values from -6 to 6
- cotangent: bfloat16 [8, 1024, 768], P('wide', 'blk'), may hold values from -6 to 6
- text_mask: int32 [8, 1024], P('wide', 'blk'), may hold values 0 or 1
- page_regions: int32 [8, 8], P('wide', 'blk'), may hold values from 5 to 100
- doc_pages: int32 [8], P('wide'), may hold values from 1 to 8, as said below
- self_project: bfloat16 [768, 2304], replicated, may hold values from -0.21875 to 0.21875
- self_output: bfloat16 [768, 768], replicated, may hold values from -1.25 to 1.25
- cross_query: bfloat16 [768, 768], replicated, may hold values from -0.21875 to 0.21875
- cross_pairs: bfloat16 [768, 1536], replicated, may hold values from -0.21875 to 0.21875
- cross_output: bfloat16 [768, 768], replicated, may hold values from -1.25 to 1.25
- gate_weight: bfloat16 [768, 12], replicated, may hold values from -0.21875 to 0.21875
- expand_weight: bfloat16 [768, 3072], replicated, may hold values from -0.21875 to 0.21875
- expand_bias: float32 [3072], replicated, may hold values from -3 to 3
- reduce_weight: bfloat16 [3072, 768], replicated, may hold values from -0.109375 to 0.109375
- reduce_bias: float32 [768], replicated, may hold values from -3 to 3
- norm_gain: float32 [4, 768], replicated, may hold values from 0.5 to 1.5
- norm_bias: float32 [4, 768], replicated, may hold values from -2 to 2
Outputs:
- joined_blocks: bfloat16 [8, 1024, 768], P('wide', 'blk')
- text_grad: bfloat16 [8, 1024, 768], P('wide', 'blk')
- image_grad: bfloat16 [8, 1024, 768], P('wide', 'blk')
- grad_self_project: float32 [768, 2304], P('wide', 'blk')
- grad_self_output: float32 [768, 768], P('wide', 'blk')
- grad_cross_query: float32 [768, 768], P('wide', 'blk')
- grad_cross_pairs: float32 [768, 1536], P('wide', 'blk')
- grad_cross_output: float32 [768, 768], P('wide', 'blk')
- grad_expand_weight: float32 [768, 3072], P('wide', 'blk')
- grad_reduce_weight: float32 [3072, 768], P('wide', 'blk')
- grad_gate_weight: float32 [768, 12], replicated
- grad_expand_bias: float32 [3072], replicated
- grad_reduce_bias: float32 [768], replicated
- grad_norm_gain: float32 [4, 768], replicated
- grad_norm_bias: float32 [4, 768], replicated
The draws below stay inside these ranges and needn't reach their ends.
Inputs may be any that keep to these rules, and one draw needn't show every extreme that they name: `doc_pages`: of the 2 documents of each index of wide, one uses all pages.
All inputs are finite; a program needn't handle non-finite values. No bound on the sum of `text_mask` on one device may be relied on, other than what follows from the above.
Results may differ from the reference program's by a relative error of at most 0.024.
Values may be sent and summed in bfloat16 or wider, within the bound.
A program may use at most 320 MiB of HBM per device.

```python
import jax
import jax.numpy as jnp
from jax import lax

D = 768
H = 12
HD = 64
FF = 3072
PAGE = 128
DOCS = 2
L = 1024
ROWS = 8
N_WIDE = 4
N_BLK = 8


def draw_doc_pages(key, part):
    key = jax.random.fold_in(key, 11)
    first_key, second_key = jax.random.split(key)
    page_counts = jax.random.randint(first_key, (ROWS,), 1, N_BLK + 1)
    chosen = jax.random.randint(second_key, (N_WIDE,), 0, DOCS)
    row_index = jnp.arange(ROWS, dtype=jnp.int32)
    is_full = row_index % DOCS == chosen[row_index // DOCS]
    return jnp.where(is_full, N_BLK, page_counts).astype(jnp.int32)


def plant(entries, stream_key, low, top_value):
    index_at = [jax.random.randint(jax.random.fold_in(stream_key, axis), (), 0, length) for axis, length in enumerate(entries.shape)]
    widest = entries.shape.index(max(entries.shape))
    beside = index_at[:widest] + [(index_at[widest] + 1) % entries.shape[widest]] + index_at[widest + 1:]
    return entries.at[tuple(index_at)].set(low).at[tuple(beside)].set(top_value)


def shard_levels(stream_key, dims, cuts, low, high):
    def one(position, parts):
        steps = jax.random.uniform(jax.random.fold_in(jax.random.fold_in(stream_key, 6), position), (parts,), jnp.float32, low / len(cuts), high / len(cuts))
        return jnp.repeat(jnp.exp(steps), dims[position] // parts).reshape((-1,) + (1,) * (len(dims) - position - 1))

    loudness = one(*cuts[0])
    for cut in cuts[1:]:
        loudness = loudness * one(*cut)
    return loudness


def bell_draw(key, dims, deviation, reach, cuts=(), kind=jnp.bfloat16):
    level = shard_levels(key, dims, cuts, -0.22, 0.18) if cuts else 1.0
    result = jax.random.normal(key, dims, jnp.float32) * deviation * level
    return jnp.minimum(jnp.maximum(result, -reach), reach).astype(kind)


def setup_inputs(seed: int = 0) -> dict:
    streams_of = jax.random.split(jax.random.key(seed), 19)
    text_blocks = bell_draw(streams_of[0], (ROWS, L, D), 1.0, 6.0, ((0, 4), (1, 8)))
    image_blocks = bell_draw(streams_of[1], (ROWS, L, D), 1.0, 6.0, ((0, 4), (1, 8)))
    cotangent = bell_draw(streams_of[2], (ROWS, L, D), 1.0, 6.0, ((0, 4), (1, 8)))
    text_mask = plant((jax.random.randint(streams_of[3], (ROWS, L), 0, 4) < 3).astype(jnp.int32), jax.random.fold_in(streams_of[3], 1), 0, 1)
    page_regions = plant(jax.random.randint(streams_of[4], (ROWS, N_BLK), 1 + PAGE // 32, PAGE * 25 // 32 + 1), jax.random.fold_in(streams_of[4], 1), 1 + PAGE // 32, (PAGE * 25 // 32 + 1) - 1).astype(jnp.int32)
    doc_pages = draw_doc_pages(jax.random.fold_in(streams_of[18], 71), 0)
    self_project = bell_draw(streams_of[6], (D, 3 * D), D ** -0.5, 0.21875)
    self_output = bell_draw(streams_of[7], (D, D), (D // 32) ** -0.5, 1.25)
    cross_query = bell_draw(streams_of[8], (D, D), D ** -0.5, 0.21875)
    cross_pairs = bell_draw(streams_of[9], (D, 2 * D), D ** -0.5, 0.21875)
    cross_output = bell_draw(streams_of[10], (D, D), (D // 32) ** -0.5, 1.25)
    gate_weight = bell_draw(streams_of[11], (D, H), D ** -0.5, 0.21875)
    expand_weight = bell_draw(streams_of[12], (D, FF), D ** -0.5, 0.21875)
    expand_bias = bell_draw(streams_of[13], (FF,), 0.5, 3.0, (), jnp.float32)
    reduce_weight = bell_draw(streams_of[14], (FF, D), FF ** -0.5, 0.109375)
    reduce_bias = bell_draw(streams_of[15], (D,), 0.5, 3.0, (), jnp.float32)
    norm_gain = jnp.clip(1.0 + 0.1 * jax.random.normal(streams_of[16], (4, D), jnp.float32), 0.5, 1.5)
    norm_bias = bell_draw(streams_of[17], (4, D), 0.3, 2.0, (), jnp.float32)
    return {"text_blocks": text_blocks, "image_blocks": image_blocks, "cotangent": cotangent, "text_mask": text_mask, "page_regions": page_regions, "doc_pages": doc_pages, "self_project": self_project, "self_output": self_output, "cross_query": cross_query, "cross_pairs": cross_pairs, "cross_output": cross_output, "gate_weight": gate_weight, "expand_weight": expand_weight, "expand_bias": expand_bias, "reduce_weight": reduce_weight, "reduce_bias": reduce_bias, "norm_gain": norm_gain, "norm_bias": norm_bias}


NEGATIVE = -1e+30

@jax.custom_vjp
def low(v):
    return lax.optimization_barrier(v.astype(jnp.bfloat16)).astype(jnp.float32)

@jax.custom_vjp
def low_back(v):
    return v

def low_keep(v):
    return (low(v), None)

def low_pass(kept, grad):
    return (grad,)

def back_keep(v):
    return (v, None)

def back_low(kept, grad):
    return (low(grad),)
low.defvjp(low_keep, low_pass)
low_back.defvjp(back_keep, back_low)

def layer_norm(values, gains, biases):
    average = lax.optimization_barrier(jnp.mean(values, axis=-1, keepdims=True))
    centred = values - average
    variance = lax.optimization_barrier(jnp.mean(centred * centred, axis=-1, keepdims=True))
    return centred * lax.rsqrt(variance + 1e-05) * gains + biases

def matmul(left, right):
    return jnp.dot(left, right, precision=lax.Precision.HIGHEST, preferred_element_type=jnp.float32)

def attend(queries, keys_in, values_in, open_keys):
    length = queries.shape[0]
    query_heads = queries.reshape(length, H, HD)
    key_heads = keys_in.reshape(length, H, HD)
    value_heads = values_in.reshape(length, H, HD)
    scores = jnp.einsum('qhd,khd->hqk', query_heads, key_heads, precision=lax.Precision.HIGHEST) * HD ** (-0.5)
    scores = low_back(scores)
    scores = jnp.where(open_keys[None, None, :] > 0, scores, NEGATIVE)
    probabilities = jax.nn.softmax(scores, axis=-1)
    mixed = jnp.einsum('hqk,khd->qhd', low(probabilities), value_heads, precision=lax.Precision.HIGHEST)
    return mixed.reshape(length, D)

def doc_forward(text_doc, image_doc, text_open, image_open, params):
    self_project, self_output, cross_query, cross_pairs, cross_output, gate_weight, expand_weight, expand_bias, reduce_weight, reduce_bias, norm_gain, norm_bias = params
    length = text_doc.shape[0]
    normed_text = low(layer_norm(text_doc, norm_gain[0], norm_bias[0]))
    triples = low(low_back(matmul(normed_text, self_project)))
    self_result = low(low_back(attend(triples[:, :D], triples[:, D:2 * D], triples[:, 2 * D:], text_open)))
    hidden = text_doc + low_back(matmul(self_result, self_output))
    cross_normed = low(layer_norm(hidden, norm_gain[1], norm_bias[1]))
    gate = jax.nn.sigmoid(matmul(cross_normed, gate_weight))
    image_normed = low(layer_norm(image_doc, norm_gain[2], norm_bias[2]))
    image_pairs = low(low_back(matmul(image_normed, cross_pairs)))
    cross_queries = low(low_back(matmul(cross_normed, cross_query)))
    cross_raw = low_back(attend(cross_queries, image_pairs[:, :D], image_pairs[:, D:], image_open))
    gated_rows = low(low_back((cross_raw.reshape(length, H, HD) * gate[:, :, None]).reshape(length, D)))
    mixed_rows = hidden + low_back(matmul(gated_rows, cross_output))
    final_normed = low(layer_norm(mixed_rows, norm_gain[3], norm_bias[3]))
    inner_rows = low_back(matmul(final_normed, expand_weight) + expand_bias)
    active_rows = low(low_back(jax.nn.gelu(inner_rows, approximate=True)))
    return mixed_rows + matmul(active_rows, reduce_weight) + reduce_bias

def key_masks(text_mask, page_regions, doc_pages):
    slot_index = jnp.arange(L, dtype=jnp.int32)
    page_index = slot_index // PAGE
    within = slot_index % PAGE
    living = page_index[None, :] < doc_pages[:, None]
    text_keys = living & ((text_mask > 0) | (within[None, :] == 0))
    regions = jnp.take(page_regions, page_index, axis=1)
    image_keys = living & (within[None, :] < regions)
    return (text_keys.astype(jnp.float32), image_keys.astype(jnp.float32))

def reference(text_blocks, image_blocks, cotangent, text_mask, page_regions, doc_pages, self_project, self_output, cross_query, cross_pairs, cross_output, gate_weight, expand_weight, expand_bias, reduce_weight, reduce_bias, norm_gain, norm_bias):
    params = tuple((weight.astype(jnp.float32) for weight in (self_project, self_output, cross_query, cross_pairs, cross_output, gate_weight, expand_weight, expand_bias, reduce_weight, reduce_bias, norm_gain, norm_bias)))
    text_keys, image_keys = key_masks(text_mask, page_regions, doc_pages)

    def one_doc(totals, doc_items):
        text_doc, image_doc, cot_doc, text_open, image_open = doc_items

        def forward(text_in, image_in, weights):
            return doc_forward(text_in, image_in, text_open, image_open, weights)
        output, pull_back = jax.vjp(forward, text_doc.astype(jnp.float32), image_doc.astype(jnp.float32), params)
        text_part, image_part, param_grads = pull_back(cot_doc.astype(jnp.float32))
        totals = jax.tree.map(jnp.add, totals, param_grads)
        return (totals, (output.astype(jnp.bfloat16), text_part.astype(jnp.bfloat16), image_part.astype(jnp.bfloat16)))
    zero_grads = jax.tree.map(jnp.zeros_like, params)
    totals, (joined_blocks, text_grads, image_grads) = lax.scan(one_doc, zero_grads, (text_blocks, image_blocks, cotangent, text_keys, image_keys))
    return (joined_blocks, text_grads, image_grads, totals[0], totals[1], totals[2], totals[3], totals[4], totals[6], totals[8], totals[5], totals[7], totals[9], totals[10], totals[11])
```

```python
import functools

import jax
import jax.numpy as jnp
from jax import lax
from jax.experimental import pallas as pl
from jax.experimental.pallas import tpu as pltpu
from jax.sharding import PartitionSpec as P

D = 768
H = 12
HD = 64
FF = 3072
PAGE = 128
DOCS = 2
ROWS = DOCS * PAGE
QUAD = 256
QUADS = D // QUAD
PAIR = 128
EPSILON = 1e-05
NEGATIVE = -1e30
HIGHEST = lax.Precision.HIGHEST
AXES = ("wide", "blk")
BF16 = jnp.bfloat16
F32 = jnp.float32
VMEM_LIMIT = 60 * 1024 * 1024


def product(left, right):
    return jnp.dot(left, right, preferred_element_type=F32)


def against(left, right, precision=None):
    return lax.dot_general(
        left, right, (((1,), (1,)), ((), ())), preferred_element_type=F32, precision=precision
    )


def transposed(left, right, precision=None):
    return lax.dot_general(
        left, right, (((0,), (0,)), ((), ())), preferred_element_type=F32, precision=precision
    )


def standardize(values):
    centred = values - jnp.mean(values, axis=-1, keepdims=True)
    inverse = lax.rsqrt(jnp.mean(centred * centred, axis=-1, keepdims=True) + EPSILON)
    return centred * inverse, inverse


def norm_back(upstream, scaled, inverse, gains):
    weighted = upstream * gains
    return inverse * (
        weighted
        - jnp.mean(weighted, axis=-1, keepdims=True)
        - scaled * jnp.mean(weighted * scaled, axis=-1, keepdims=True)
    )


def column_sum(values):
    return jnp.sum(values, axis=0, keepdims=True)


def normalize_pages(pages, gain, shift, normed):
    for index, page in enumerate(pages):
        scaled, _ = standardize(page[...].astype(F32))
        normed[index * PAGE : (index + 1) * PAGE, :] = (scaled * gain + shift).astype(BF16)


def lane_index(rows):
    return lax.broadcasted_iota(jnp.int32, (rows, PAIR), 1)


def side_masks(rows):
    lanes = lane_index(rows)
    return [(lanes < HD).astype(BF16), (lanes >= HD).astype(BF16)]


def attend_forward(q_ref, k_ref, v_ref, closed_ref, out_ref, lse_ref):
    lanes = lane_index(ROWS)
    masks = side_masks(ROWS)
    first_lane = (lanes == 0).astype(BF16)
    stats = jnp.zeros((ROWS, PAIR), F32)
    for pair in range(QUAD // PAIR):
        cols = slice(pair * PAIR, (pair + 1) * PAIR)
        keys = jnp.concatenate([k_ref[:, cols], closed_ref[...]], axis=1)
        values = v_ref[:, cols]
        queries = q_ref[:, cols]
        results = []
        for side in range(2):
            query = jnp.concatenate([queries * masks[side], first_lane], axis=1)
            scores = against(query, keys)
            top = jnp.max(scores, axis=1, keepdims=True)
            weights = jnp.exp(scores - top)
            total = jnp.sum(weights, axis=1, keepdims=True)
            results.append(product(weights.astype(BF16), values) / total)
            stats = jnp.where(lanes == pair * 2 + side, top + jnp.log(total), stats)
        out_ref[:, cols] = jnp.where(lanes < HD, results[0], results[1])
    lse_ref[...] = jnp.transpose(stats)[:8, :]


def attend_backward(q_ref, k_ref, v_ref, do_ref, lse_ref, delta_ref, closed_ref, dq_ref, dkv_ref):
    lanes = lane_index(ROWS)
    masks = side_masks(ROWS)
    first_lane = (lanes == 0).astype(BF16)
    for pair in range(QUAD // PAIR):
        cols = slice(pair * PAIR, (pair + 1) * PAIR)
        key_part = k_ref[:, cols]
        keys = jnp.concatenate([key_part, closed_ref[...]], axis=1)
        values = v_ref[:, cols]
        dq_parts = []
        dk = None
        dv = None
        for side in range(2):
            row = pair * 2 + side
            query = q_ref[:, cols] * masks[side]
            grad_out = do_ref[:, cols] * masks[side]
            scores = against(keys, jnp.concatenate([query, first_lane], axis=1))
            weights = jnp.exp(scores - lse_ref[row : row + 1, :])
            grad_weights = against(values, grad_out)
            grad_scores = (weights * (grad_weights - delta_ref[row : row + 1, :])).astype(BF16)
            dv_part = product(weights.astype(BF16), grad_out)
            dk_part = product(grad_scores, query)
            dv = dv_part if dv is None else dv + dv_part
            dk = dk_part if dk is None else dk + dk_part
            dq_parts.append(transposed(grad_scores, key_part))
        dq_ref[:, cols] = (jnp.where(lanes < HD, dq_parts[0], dq_parts[1]) * HD ** (-0.5)).astype(
            BF16
        )
        dkv_ref[:, cols] = dk.astype(BF16)
        dkv_ref[:, QUAD + pair * PAIR : QUAD + (pair + 1) * PAIR] = dv.astype(BF16)


def head_sums(values):
    sums = []
    lanes = lane_index(values.shape[0])
    for pair in range(H // 2):
        part = values[:, pair * PAIR : (pair + 1) * PAIR]
        sums.append(jnp.sum(jnp.where(lanes < HD, part, 0.0), axis=1, keepdims=True))
        sums.append(jnp.sum(jnp.where(lanes >= HD, part, 0.0), axis=1, keepdims=True))
    return sums


def head_rows(sums):
    lanes = lane_index(ROWS)
    stats = jnp.zeros((ROWS, PAIR), F32)
    for head, value in enumerate(sums):
        stats = jnp.where(lanes == (head // 4) * 8 + head % 4, value, stats)
    return jnp.transpose(stats)[: 8 * QUADS, :]


def spread_heads(gates):
    lanes = lane_index(gates.shape[0])
    parts = []
    for pair in range(H // 2):
        parts.append(
            jnp.where(lanes < HD, gates[:, 2 * pair : 2 * pair + 1], gates[:, 2 * pair + 1 : 2 * pair + 2])
        )
    return jnp.concatenate(parts, axis=1)


def store_tiles(out_ref, rows, value):
    cuts = out_ref.shape[0]
    lanes = out_ref.shape[2]
    for cut in range(cuts):
        out_ref[cut, rows, :] = value[:, cut * lanes : (cut + 1) * lanes].astype(BF16)


def self_forward_kernel(count, *refs):
    pages = refs[:count]
    gain, shift, closed, wq, wk, wv, out, lse, q_out, k_out, v_out, normed = refs[count:]

    @pl.when(pl.program_id(0) == 0)
    def _():
        normalize_pages(pages, gain[0:1, :], shift[0:1, :], normed)

    q_out[...] = (product(normed[0:ROWS, :], wq[...]).astype(BF16) * HD ** (-0.5)).astype(BF16)
    k_out[...] = product(normed[...], wk[...]).astype(BF16)
    v_out[...] = product(normed[...], wv[...]).astype(BF16)
    attend_forward(q_out, k_out, v_out, closed, out, lse)


def cross_forward_kernel(count, *refs):
    texts = refs[:DOCS]
    pages = refs[DOCS : DOCS + count]
    (
        self_out, w_self, w_gate, gain, shift, closed, wq, wk, wv,
        hidden, gate, out, lse, q_out, k_out, v_out, normed, cross,
    ) = refs[DOCS + count :]

    @pl.when(pl.program_id(0) == 0)
    def _():
        normalize_pages(pages, gain[2:3, :], shift[2:3, :], normed)
        branch = product(self_out[...].astype(BF16), w_self[...])
        for index, text in enumerate(texts):
            rows = slice(index * PAGE, (index + 1) * PAGE)
            hidden[rows, :] = text[...].astype(F32) + branch[rows, :]
        scaled, _ = standardize(hidden[...])
        cross[...] = (scaled * gain[1:2, :] + shift[1:2, :]).astype(BF16)
        gate[...] = jax.nn.sigmoid(product(cross[...], w_gate[...]))

    q_out[...] = (product(cross[...], wq[...]).astype(BF16) * HD ** (-0.5)).astype(BF16)
    k_out[...] = product(normed[...], wk[...]).astype(BF16)
    v_out[...] = product(normed[...], wv[...]).astype(BF16)
    attend_forward(q_out, k_out, v_out, closed, out, lse)


def forward_back_kernel(
    steps, hidden, raw, gate, cot0, cot1, w_out, gain, shift, w_expand, b_expand, w_reduce, b_reduce,
    joined, d_expand, d_reduce, d_out, grad_mixed, grad_raw, delta, grad_logit, d_bias, small,
    gated, mixed, final, upstream, joined_sum, back_sum,
):
    step = pl.program_id(0)

    @pl.when(step == 0)
    def _():
        upstream[0:PAGE, :] = cot0[...]
        upstream[PAGE:ROWS, :] = cot1[...]
        gated[...] = (spread_heads(gate[...]) * raw[...]).astype(BF16)
        rows = hidden[...] + product(gated[...], w_out[...])
        mixed[...] = rows
        scaled, _ = standardize(rows)
        final[...] = (scaled * gain[3:4, :] + shift[3:4, :]).astype(BF16)
        joined_sum[...] = rows + b_reduce[...]
        back_sum[...] = jnp.zeros_like(back_sum)

    inner = product(final[...], w_expand[...]) + b_expand[...]
    squared = inner * inner
    root = (2.0 / jnp.pi) ** 0.5
    curve = jnp.tanh(root * inner * (1.0 + 0.044715 * squared))
    half = 0.5 * (1.0 + curve)
    active = (inner * half).astype(BF16)
    slope = half + 0.5 * inner * (1.0 - curve * curve) * (root * (1.0 + 3.0 * 0.044715 * squared))
    joined_sum[...] += product(active, w_reduce[...])
    grad_active = against(upstream[...], w_reduce[...]).astype(BF16)
    grad_inner = (grad_active.astype(F32) * slope).astype(BF16)
    d_bias[...] = column_sum(grad_inner.astype(F32))
    back_sum[...] += against(grad_inner, w_expand[...])
    store_tiles(d_expand, slice(None), transposed(grad_inner, final[...]))
    store_tiles(d_reduce, slice(None), transposed(upstream[...], active))

    @pl.when(step == steps - 1)
    def _():
        joined[...] = joined_sum[...].astype(BF16)
        scaled, inverse = standardize(mixed[...])
        back = back_sum[...]
        cotangent = upstream[...].astype(F32)
        grad = cotangent + norm_back(back, scaled, inverse, gain[3:4, :])
        grad_mixed[...] = grad
        branch = grad.astype(BF16)
        store_tiles(d_out, slice(None), transposed(branch, gated[...]))
        grad_gated = against(branch, w_out[...]).astype(BF16).astype(F32)
        gates = gate[...]
        lanes = lane_index(ROWS)
        logit = jnp.zeros((ROWS, PAIR), F32)
        for head, value in enumerate(head_sums(grad_gated * raw[...])):
            logit = jnp.where(lanes == head, value, logit)
        grad_logit[...] = logit * gates * (1.0 - gates)
        rounded = (spread_heads(gates) * grad_gated).astype(BF16)
        grad_raw[...] = rounded
        delta[...] = head_rows(head_sums(rounded.astype(F32) * raw[...]))
        small[...] = jnp.concatenate(
            [
                column_sum(cotangent),
                column_sum(back * scaled),
                column_sum(back),
                jnp.zeros((5, D), F32),
            ],
            axis=0,
        )


def spread_back(normed, dkv, wk, wv, dx, dw_k, dw_v, k_rows, v_rows):
    store_tiles(dw_k, k_rows, transposed(dkv[:, :QUAD], normed[...]))
    store_tiles(dw_v, v_rows, transposed(dkv[:, QUAD:], normed[...]))
    weights = jnp.concatenate([wk[...], wv[...]], axis=1)

    def chunk(index, carry):
        rows = pl.ds(pl.multiple_of(index * ROWS, ROWS), ROWS)
        dx[rows, :] += against(dkv[rows, :], weights)
        return carry

    lax.fori_loop(0, dx.shape[0] // ROWS, chunk, 0)


def finish_pages(pages, dx, keep, send):
    gain_sum = jnp.zeros((1, D), F32)
    shift_sum = jnp.zeros((1, D), F32)
    half = len(pages) // 2
    for index, page in enumerate(pages):
        scaled, _ = standardize(page[...].astype(F32))
        part = dx[index * PAGE : (index + 1) * PAGE, :]
        gain_sum += column_sum(part * scaled)
        shift_sum += column_sum(part)
        target = keep if index < half else send
        place = index % half
        target[place * PAGE : (place + 1) * PAGE, :] = part.astype(BF16)
    return gain_sum, shift_sum


def cross_back_kernel(count, *refs):
    pages = refs[:count]
    (
        gain, shift, closed, q_in, k_in, v_in, do_in, lse, delta, wk, wv,
        w_query, w_gate, w_self, hidden, self_out, grad_mixed, grad_logit,
        keep, send, dw_pairs, dw_query, dw_self, dw_gate, grad_hidden, self_do, self_delta, small,
        normed, dkv, dx, dq,
    ) = refs[count:]
    step = pl.program_id(0)

    @pl.when(step == 0)
    def _():
        normalize_pages(pages, gain[2:3, :], shift[2:3, :], normed)
        dx[...] = jnp.zeros_like(dx)

    cols = pl.ds(pl.multiple_of(step * QUAD, QUAD), QUAD)
    attend_backward(
        q_in, k_in, v_in, do_in, lse, delta, closed, dq.at[:, cols], dkv
    )
    spread_back(
        normed, dkv, wk, wv, dx, dw_pairs, dw_pairs,
        cols, pl.ds(pl.multiple_of(D + step * QUAD, QUAD), QUAD),
    )

    @pl.when(step == QUADS - 1)
    def _():
        image_gain, image_shift = finish_pages(pages, dx, keep, send)
        scaled, inverse = standardize(hidden[...])
        cross = (scaled * gain[1:2, :] + shift[1:2, :]).astype(BF16)
        grad_query = dq[...]
        store_tiles(dw_query, slice(None), transposed(grad_query, cross))
        dw_gate[...] = transposed(grad_logit[...], cross.astype(F32), HIGHEST)[:16, :]
        upstream = against(grad_query, w_query[...]) + against(
            grad_logit[...], w_gate[...].astype(F32), HIGHEST
        )
        grad = grad_mixed[...] + norm_back(upstream, scaled, inverse, gain[1:2, :])
        grad_hidden[...] = grad
        branch = grad.astype(BF16)
        store_tiles(dw_self, slice(None), transposed(branch, self_out[...].astype(BF16)))
        grad_result = against(branch, w_self[...]).astype(BF16)
        self_do[...] = grad_result
        self_delta[...] = head_rows(head_sums(grad_result.astype(F32) * self_out[...]))
        small[...] = jnp.concatenate(
            [
                column_sum(upstream * scaled),
                column_sum(upstream),
                image_gain,
                image_shift,
                jnp.zeros((4, D), F32),
            ],
            axis=0,
        )


def self_back_kernel(count, *refs):
    pages = refs[:count]
    (
        gain, shift, closed, q_in, k_in, v_in, do_in, lse, delta, wq, wk, wv,
        keep, send, dw_project, small,
        normed, dkv, dx, dq,
    ) = refs[count:]
    step = pl.program_id(0)

    @pl.when(step == 0)
    def _():
        normalize_pages(pages, gain[0:1, :], shift[0:1, :], normed)
        dx[...] = jnp.zeros_like(dx)

    attend_backward(q_in, k_in, v_in, do_in, lse, delta, closed, dq, dkv)
    spread_back(
        normed, dkv, wk, wv, dx, dw_project, dw_project,
        pl.ds(pl.multiple_of(D + step * QUAD, QUAD), QUAD),
        pl.ds(pl.multiple_of(2 * D + step * QUAD, QUAD), QUAD),
    )
    store_tiles(
        dw_project,
        pl.ds(pl.multiple_of(step * QUAD, QUAD), QUAD),
        transposed(dq[...], normed[0:ROWS, :]),
    )
    dx[0:ROWS, :] += against(dq[...], wq[...])

    @pl.when(step == QUADS - 1)
    def _():
        gain_sum, shift_sum = finish_pages(pages, dx, keep, send)
        small[...] = jnp.concatenate([gain_sum, shift_sum, jnp.zeros((6, D), F32)], axis=0)


def norm_back_kernel(index, added, *refs):
    pages = refs[:DOCS]
    gain, mine, other = refs[DOCS : DOCS + 3]
    rest = refs[DOCS + 3 :]
    for place, page in enumerate(pages):
        rows = slice(place * PAGE, (place + 1) * PAGE)
        scaled, inverse = standardize(page[...].astype(F32))
        upstream = mine[rows, :].astype(F32) + other[rows, :].astype(F32)
        grad = norm_back(upstream, scaled, inverse, gain[index : index + 1, :])
        if added:
            grad = grad + rest[0][rows, :]
        rest[-1][place] = grad.astype(BF16)


def whole(shape):
    return pl.BlockSpec(shape, lambda step: (0,) * len(shape))


def columns(rows, offset=0):
    return pl.BlockSpec((rows, QUAD), lambda step: (0, offset + step))


def stat_rows():
    return pl.BlockSpec((8, ROWS), lambda step: (step, 0))


def shaped(shape, kind):
    return jax.ShapeDtypeStruct(shape, kind)


def call(kernel, name, steps, ins, outs, scratch, flops, byte_count):
    in_specs, operands = zip(*ins)
    out_specs, out_shapes = zip(*outs)
    return pl.pallas_call(
        kernel,
        grid=(steps,),
        in_specs=list(in_specs),
        out_specs=list(out_specs),
        out_shape=list(out_shapes),
        scratch_shapes=scratch,
        name=name,
        compiler_params=pltpu.CompilerParams(vmem_limit_bytes=VMEM_LIMIT),
        cost_estimate=pl.CostEstimate(flops=flops, bytes_accessed=byte_count, transcendentals=0),
    )(*operands)


def page_inputs(pages):
    return [(whole((PAGE, D)), page) for page in pages]


def self_forward(pages, gain, shift, closed, project):
    keys = len(pages) * PAGE
    return call(
        functools.partial(self_forward_kernel, len(pages)),
        "self_forward",
        QUADS,
        page_inputs(pages)
        + [
            (whole(gain.shape), gain),
            (whole(shift.shape), shift),
            (whole(closed.shape), closed),
            (columns(D), project),
            (columns(D, QUADS), project),
            (columns(D, 2 * QUADS), project),
        ],
        [
            (columns(ROWS), shaped((ROWS, D), F32)),
            (stat_rows(), shaped((8 * QUADS, ROWS), F32)),
            (columns(ROWS), shaped((ROWS, D), BF16)),
            (columns(keys), shaped((keys, D), BF16)),
            (columns(keys), shaped((keys, D), BF16)),
        ],
        [pltpu.VMEM((keys, D), BF16)],
        6 * 10**9,
        12 * 10**6,
    )


def cross_forward(texts, pages, self_out, w_self, w_gate, gain, shift, closed, w_query, w_pairs):
    keys = len(pages) * PAGE
    return call(
        functools.partial(cross_forward_kernel, len(pages)),
        "cross_forward",
        QUADS,
        page_inputs(texts)
        + page_inputs(pages)
        + [
            (whole(self_out.shape), self_out),
            (whole(w_self.shape), w_self),
            (whole(w_gate.shape), w_gate),
            (whole(gain.shape), gain),
            (whole(shift.shape), shift),
            (whole(closed.shape), closed),
            (columns(D), w_query),
            (columns(D), w_pairs),
            (columns(D, QUADS), w_pairs),
        ],
        [
            (whole((ROWS, D)), shaped((ROWS, D), F32)),
            (whole((ROWS, PAIR)), shaped((ROWS, PAIR), F32)),
            (columns(ROWS), shaped((ROWS, D), F32)),
            (stat_rows(), shaped((8 * QUADS, ROWS), F32)),
            (columns(ROWS), shaped((ROWS, D), BF16)),
            (columns(keys), shaped((keys, D), BF16)),
            (columns(keys), shaped((keys, D), BF16)),
        ],
        [pltpu.VMEM((keys, D), BF16), pltpu.VMEM((ROWS, D), BF16)],
        7 * 10**9,
        14 * 10**6,
    )


def forward_back(
    hidden, raw, gate, cots, w_out, gain, shift, w_expand, b_expand, w_reduce, b_reduce, cuts, far_cuts
):
    steps = FF // D
    far = FF // far_cuts
    if far >= D:
        far_spec = pl.BlockSpec((1, D, D), lambda step: (step * D // far, 0, (step * D % far) // D))
    else:
        far_spec = pl.BlockSpec((D // far, D, far), lambda step: (step, 0, 0))
    return call(
        functools.partial(forward_back_kernel, steps),
        "forward_back",
        steps,
        [
            (whole((ROWS, D)), hidden),
            (whole((ROWS, D)), raw),
            (whole((ROWS, PAIR)), gate),
        ]
        + page_inputs(cots)
        + [
            (whole((D, D)), w_out),
            (whole(gain.shape), gain),
            (whole(shift.shape), shift),
            (pl.BlockSpec((D, D), lambda step: (0, step)), w_expand),
            (pl.BlockSpec((1, D), lambda step: (0, step)), b_expand),
            (pl.BlockSpec((D, D), lambda step: (step, 0)), w_reduce),
            (whole((1, D)), b_reduce),
        ],
        [
            (whole((ROWS, D)), shaped((ROWS, D), BF16)),
            (
                pl.BlockSpec((cuts, D, D // cuts), lambda step: (0, step, 0)),
                shaped((cuts, FF, D // cuts), BF16),
            ),
            (far_spec, shaped((far_cuts, D, far), BF16)),
            (whole((cuts, D, D // cuts)), shaped((cuts, D, D // cuts), BF16)),
            (whole((ROWS, D)), shaped((ROWS, D), F32)),
            (whole((ROWS, D)), shaped((ROWS, D), BF16)),
            (whole((8 * QUADS, ROWS)), shaped((8 * QUADS, ROWS), F32)),
            (whole((ROWS, PAIR)), shaped((ROWS, PAIR), F32)),
            (pl.BlockSpec((1, D), lambda step: (0, step)), shaped((1, FF), F32)),
            (whole((8, D)), shaped((8, D), F32)),
        ],
        [
            pltpu.VMEM((ROWS, D), BF16),
            pltpu.VMEM((ROWS, D), F32),
            pltpu.VMEM((ROWS, D), BF16),
            pltpu.VMEM((ROWS, D), BF16),
            pltpu.VMEM((ROWS, D), F32),
            pltpu.VMEM((ROWS, D), F32),
        ],
        8 * 10**9,
        25 * 10**6,
    )


def back_scratch(keys, dq_columns):
    return [
        pltpu.VMEM((keys, D), BF16),
        pltpu.VMEM((keys, 2 * QUAD), BF16),
        pltpu.VMEM((keys, D), F32),
        pltpu.VMEM((ROWS, dq_columns), BF16),
    ]


def cross_back(
    pages, gain, shift, closed, q, k, v, grad_out, lse, delta, w_pairs,
    w_query, w_gate, w_self, hidden, self_out, grad_mixed, grad_logit, cuts,
):
    keys = len(pages) * PAGE
    half = keys // 2
    return call(
        functools.partial(cross_back_kernel, len(pages)),
        "cross_back",
        QUADS,
        page_inputs(pages)
        + [
            (whole(gain.shape), gain),
            (whole(shift.shape), shift),
            (whole(closed.shape), closed),
            (columns(ROWS), q),
            (columns(keys), k),
            (columns(keys), v),
            (columns(ROWS), grad_out),
            (stat_rows(), lse),
            (stat_rows(), delta),
            (columns(D), w_pairs),
            (columns(D, QUADS), w_pairs),
            (whole((D, D)), w_query),
            (whole((D, PAIR)), w_gate),
            (whole((D, D)), w_self),
            (whole((ROWS, D)), hidden),
            (whole((ROWS, D)), self_out),
            (whole((ROWS, D)), grad_mixed),
            (whole((ROWS, PAIR)), grad_logit),
        ],
        [
            (whole((half, D)), shaped((half, D), BF16)),
            (whole((half, D)), shaped((half, D), BF16)),
            (whole((cuts, 2 * D, D // cuts)), shaped((cuts, 2 * D, D // cuts), BF16)),
            (whole((cuts, D, D // cuts)), shaped((cuts, D, D // cuts), BF16)),
            (whole((cuts, D, D // cuts)), shaped((cuts, D, D // cuts), BF16)),
            (whole((16, D)), shaped((16, D), F32)),
            (whole((ROWS, D)), shaped((ROWS, D), F32)),
            (whole((ROWS, D)), shaped((ROWS, D), BF16)),
            (whole((8 * QUADS, ROWS)), shaped((8 * QUADS, ROWS), F32)),
            (whole((8, D)), shaped((8, D), F32)),
        ],
        back_scratch(keys, D),
        12 * 10**9,
        20 * 10**6,
    )


def self_back(pages, gain, shift, closed, q, k, v, grad_out, lse, delta, project, cuts):
    keys = len(pages) * PAGE
    half = keys // 2
    return call(
        functools.partial(self_back_kernel, len(pages)),
        "self_back",
        QUADS,
        page_inputs(pages)
        + [
            (whole(gain.shape), gain),
            (whole(shift.shape), shift),
            (whole(closed.shape), closed),
            (columns(ROWS), q),
            (columns(keys), k),
            (columns(keys), v),
            (columns(ROWS), grad_out),
            (stat_rows(), lse),
            (stat_rows(), delta),
            (columns(D), project),
            (columns(D, QUADS), project),
            (columns(D, 2 * QUADS), project),
        ],
        [
            (whole((half, D)), shaped((half, D), BF16)),
            (whole((half, D)), shaped((half, D), BF16)),
            (whole((cuts, 3 * D, D // cuts)), shaped((cuts, 3 * D, D // cuts), BF16)),
            (whole((8, D)), shaped((8, D), F32)),
        ],
        back_scratch(keys, QUAD),
        11 * 10**9,
        17 * 10**6,
    )


def final_norm(index, pages, gain, mine, other, added):
    ins = page_inputs(pages) + [
        (whole(gain.shape), gain),
        (whole((ROWS, D)), mine),
        (whole((ROWS, D)), other),
    ]
    if added is not None:
        ins.append((whole((ROWS, D)), added))
    (result,) = call(
        functools.partial(norm_back_kernel, index, added is not None),
        "final_norm",
        1,
        ins,
        [(whole((DOCS, PAGE, D)), shaped((DOCS, PAGE, D), BF16))],
        [],
        10**7,
        3 * 10**6,
    )
    return result


class Layout:
    def __init__(self):
        self.wide = lax.axis_size("wide")
        self.blk = lax.axis_size("blk")
        self.part = self.blk // 4
        self.w = lax.axis_index("wide")
        self.b = lax.axis_index("blk")
        self.turn = lax.rem(self.b // self.part, 2)
        self.bits = {}
        for bit in range(self.wide.bit_length() - 1):
            self.bits["w", bit] = (self.w >> bit) & 1
        for bit in range(self.blk.bit_length() - 1):
            self.bits["b", bit] = (self.b >> bit) & 1

    def exchange(self, value, move):
        pairs = []
        for w in range(self.wide):
            for b in range(self.blk):
                to_w, to_b = move(w, b)
                pairs.append((w * self.blk + b, to_w * self.blk + to_b))
        return lax.ppermute(value, AXES, pairs)

    def flip(self, value, name):
        axis, bit = name
        if axis == "w":
            return self.exchange(value, lambda w, b: (w ^ (1 << bit), b))
        return self.exchange(value, lambda w, b: (w, b ^ (1 << bit)))

    def swap(self, value, turn):
        def move(w, b):
            quarter, rest = divmod(b, self.part)
            return (w - w % 2 + quarter // 2, (2 * (w % 2) + ((quarter % 2) ^ turn)) * self.part + rest)

        return self.exchange(value, move)

    def to_group(self, value):
        return [
            self.swap(
                lax.dynamic_index_in_dim(value, self.turn ^ turn, 0, keepdims=False), turn
            )
            for turn in range(DOCS)
        ]

    def from_group(self, pages):
        first, second = (self.swap(page, turn) for turn, page in enumerate(pages))
        flag = self.turn == 0
        return jnp.stack([jnp.where(flag, first, second), jnp.where(flag, second, first)])

    def group_bits(self):
        return [("b", bit) for bit in range(self.part.bit_length() - 1)] + [("w", 0)]

    def gather(self, page):
        pages = [page]
        for name in self.group_bits():
            pages = pages + [self.flip(item, name) for item in pages]
        return pages

    def group_sum(self, keep, send):
        names = self.group_bits()
        for name in reversed(names):
            got = self.flip(send, name)
            if name == names[0]:
                return keep, got
            half = keep.shape[0] // 2
            keep, send = (keep[:half] + got[:half]), (keep[half:] + got[half:])

    def reduce_scatter(self, grads, order):
        wide_names = [("w", bit) for bit in range(self.wide.bit_length() - 2, 0, -1)]
        blk_names = [("b", bit) for bit in range(self.blk.bit_length() - 2, -1, -1)]
        names = wide_names + blk_names + [("w", 0)]
        parts = [
            grad.reshape((2,) * len(names) + (grad.shape[1] // (2 * self.blk), grad.shape[2]))
            for grad in grads
        ]
        for name in order:
            axis = names.index(name)
            names.remove(name)
            bit = self.bits[name]

            def pick(index):
                picked = [
                    lax.dynamic_index_in_dim(part, index, axis, keepdims=False) for part in parts
                ]
                return picked[0] if len(picked) == 1 else jnp.concatenate(picked, axis=-2)

            parts = [pick(bit) + self.flip(pick(1 - bit), name)]
        return parts[0]

    def finish(self, piece):
        rows, lanes = piece.shape
        halves = jnp.stack([piece[:, : lanes // 2], piece[:, lanes // 2 :]])
        bit = self.bits["w", 0]
        mine = lax.dynamic_index_in_dim(halves, bit, 0, keepdims=False)
        other = self.flip(lax.dynamic_index_in_dim(halves, 1 - bit, 0, keepdims=False), ("w", 0))
        flag = bit == 0
        return jnp.stack([jnp.where(flag, mine, other), jnp.where(flag, other, mine)])

    def tiles(self, piece, counts):
        both = self.finish(piece)
        results = []
        start = 0
        for count in counts:
            part = both[:, start : start + count, :]
            start += count
            results.append(jnp.transpose(part.reshape(-1, part.shape[-1])).astype(F32))
        return results

    def all_sum(self, value):
        for name in self.bits:
            value = value + self.flip(value, name)
        return value


def cut_lanes(grad, cuts):
    if grad.shape[0] == cuts:
        return grad
    _, rows, lanes = grad.shape
    return jnp.transpose(grad.reshape(rows, cuts, lanes // cuts), (1, 0, 2))


def body(
    text_blocks,
    image_blocks,
    cotangent,
    text_mask,
    page_regions,
    doc_pages,
    self_project,
    self_output,
    cross_query,
    cross_pairs,
    cross_output,
    gate_weight,
    expand_weight,
    expand_bias,
    reduce_weight,
    reduce_bias,
    norm_gain,
    norm_bias,
):
    lay = Layout()
    blk_count = lay.blk
    wide_half = lay.wide // 2
    cuts = wide_half if (D // wide_half) % PAIR == 0 else 1
    far_cuts = wide_half if (FF // wide_half) % PAIR == 0 else 1

    offsets = jnp.arange(PAGE, dtype=jnp.int32)
    living = (lay.b < doc_pages)[:, None]
    text_open = living & ((text_mask > 0) | (offsets[None, :] == 0))
    image_open = living & (offsets[None, :] < page_regions)
    closed_here = jnp.where(
        jnp.concatenate([text_open, image_open], axis=1), 0.0, NEGATIVE
    ).astype(BF16)

    text_own = lay.to_group(text_blocks)
    text_sets = [lay.gather(page) for page in text_own]
    text_pages = [page for pair in zip(*text_sets) for page in pair]

    masks = jnp.stack(lay.to_group(closed_here))
    for name in lay.group_bits():
        masks = jnp.concatenate([masks, lay.flip(masks, name)], axis=0)
    keys = masks.shape[0] * PAGE
    first_lane = jnp.arange(PAIR)[None, :] == 0

    def closed_column(part):
        return jnp.where(first_lane, part.reshape(keys, 1), 0.0).astype(BF16)

    text_closed = closed_column(masks[:, :PAGE])
    image_closed = closed_column(masks[:, PAGE:])

    image_own = lay.to_group(image_blocks)
    image_sets = [lay.gather(page) for page in image_own]
    image_pages = [page for pair in zip(*image_sets) for page in pair]
    cots = lay.to_group(cotangent)

    gate_wide = jnp.pad(gate_weight, ((0, 0), (0, PAIR - H)))

    self_out, self_lse, self_q, self_k, self_v = self_forward(
        text_pages, norm_gain, norm_bias, text_closed, self_project
    )
    hidden, gate, raw, cross_lse, cross_q, cross_k, cross_v = cross_forward(
        text_own, image_pages, self_out, self_output, gate_wide, norm_gain, norm_bias,
        image_closed, cross_query, cross_pairs,
    )
    (
        joined, d_expand, d_reduce, d_cross_output, grad_mixed, grad_raw, cross_delta, grad_logit,
        d_expand_bias, small_last,
    ) = forward_back(
        hidden, raw, gate, cots, cross_output, norm_gain, norm_bias, expand_weight,
        expand_bias.reshape(1, FF), reduce_weight, reduce_bias.reshape(1, D), cuts, far_cuts,
    )
    wide_bits = [("w", bit) for bit in range(1, lay.wide.bit_length() - 1)]
    low_blk = [("b", 0)]
    high_blk = [("b", bit) for bit in range(1, blk_count.bit_length() - 1)]
    core = [("w", 0)]
    expand_piece = lay.reduce_scatter([cut_lanes(d_expand, wide_half)], core + wide_bits + high_blk + low_blk)
    reduce_piece = lay.reduce_scatter([cut_lanes(d_reduce, wide_half)], core + low_blk + high_blk + wide_bits)
    joined_blocks = lay.from_group([joined[:PAGE], joined[PAGE:]])

    (
        image_keep, image_send, d_pairs, d_query, d_self_output, d_gate, grad_hidden, self_do,
        self_delta, small_cross,
    ) = cross_back(
        image_pages, norm_gain, norm_bias, image_closed, cross_q, cross_k, cross_v, grad_raw,
        cross_lse, cross_delta, cross_pairs, cross_query, gate_wide, self_output, hidden, self_out,
        grad_mixed, grad_logit, cuts,
    )
    cross_piece = lay.reduce_scatter(
        [cut_lanes(item, wide_half) for item in (d_pairs, d_query, d_cross_output, d_self_output)],
        core + wide_bits + low_blk + high_blk,
    )
    image_mine, image_other = lay.group_sum(image_keep, image_send)
    image_back = final_norm(2, image_own, norm_gain, image_mine, image_other, None)
    image_grad = lay.from_group([image_back[0], image_back[1]])
    small_first = lay.all_sum(
        jnp.concatenate([d_gate, d_expand_bias.reshape(-1, D), small_last[:4], small_cross[:4]], axis=0)
    )

    text_keep, text_send, d_project, small_self = self_back(
        text_pages, norm_gain, norm_bias, text_closed, self_q, self_k, self_v, self_do,
        self_lse, self_delta, self_project, cuts,
    )
    text_mine, text_other = lay.group_sum(text_keep, text_send)
    text_back = final_norm(0, text_own, norm_gain, text_mine, text_other, grad_hidden)
    text_grad = lay.from_group([text_back[0], text_back[1]])
    project_piece = lay.reduce_scatter(
        [cut_lanes(d_project, wide_half)], core + low_blk + wide_bits + high_blk
    )
    small_second = lay.all_sum(small_self)

    share = 2 * blk_count
    (grad_expand_weight,) = lay.tiles(expand_piece, [FF // share])
    (grad_reduce_weight,) = lay.tiles(reduce_piece, [D // share])
    grad_cross_pairs, grad_cross_query, grad_cross_output, grad_self_output = lay.tiles(
        cross_piece, [2 * D // share, D // share, D // share, D // share]
    )
    (grad_self_project,) = lay.tiles(project_piece, [3 * D // share])
    grad_gate_weight = jnp.transpose(small_first[:H])
    at_bias = 16
    at_last = at_bias + FF // D
    at_cross = at_last + 4
    return (
        joined_blocks,
        text_grad,
        image_grad,
        grad_self_project,
        grad_self_output,
        grad_cross_query,
        grad_cross_pairs,
        grad_cross_output,
        grad_expand_weight,
        grad_reduce_weight,
        grad_gate_weight,
        small_first[at_bias:at_last].reshape(FF),
        small_first[at_last],
        jnp.stack(
            [
                small_second[0],
                small_first[at_cross],
                small_first[at_cross + 2],
                small_first[at_last + 1],
            ]
        ),
        jnp.stack(
            [
                small_second[1],
                small_first[at_cross + 1],
                small_first[at_cross + 3],
                small_first[at_last + 2],
            ]
        ),
    )


def solution(mesh):
    rows = P("wide", "blk", None)
    return jax.shard_map(
        body,
        mesh=mesh,
        in_specs=(rows,) * 3 + (P("wide", "blk"),) * 2 + (P("wide"),) + (P(),) * 12,
        out_specs=(rows,) * 3 + (P("wide", "blk"),) * 7 + (P(),) * 5,
        check_vma=False,
    )
```

```python
import functools

import jax
import jax.numpy as jnp
from jax import lax
from jax.experimental import pallas as pl
from jax.experimental.pallas import tpu as pltpu
from jax.sharding import PartitionSpec as P

D = 768
H = 12
HD = 64
FF = 3072
PAGE = 128
DOCS = 2
ROWS = DOCS * PAGE
QUAD = 256
QUADS = D // QUAD
PAIR = 128
EPSILON = 1e-05
NEGATIVE = -1e30
HIGHEST = lax.Precision.HIGHEST
AXES = ("wide", "blk")
BF16 = jnp.bfloat16
F32 = jnp.float32
VMEM_LIMIT = 60 * 1024 * 1024


def product(left, right):
    return jnp.dot(left, right, preferred_element_type=F32)


def against(left, right, precision=None):
    return lax.dot_general(
        left, right, (((1,), (1,)), ((), ())), preferred_element_type=F32, precision=precision
    )


def transposed(left, right, precision=None):
    return lax.dot_general(
        left, right, (((0,), (0,)), ((), ())), preferred_element_type=F32, precision=precision
    )


def standardize(values):
    centred = values - jnp.mean(values, axis=-1, keepdims=True)
    inverse = lax.rsqrt(jnp.mean(centred * centred, axis=-1, keepdims=True) + EPSILON)
    return centred * inverse, inverse


def norm_back(upstream, scaled, inverse, gains):
    weighted = upstream * gains
    return inverse * (
        weighted
        - jnp.mean(weighted, axis=-1, keepdims=True)
        - scaled * jnp.mean(weighted * scaled, axis=-1, keepdims=True)
    )


def column_sum(values):
    return jnp.sum(values, axis=0, keepdims=True)


def normalize_pages(pages, gain, shift, normed):
    for index, page in enumerate(pages):
        scaled, _ = standardize(page[...].astype(F32))
        normed[index * PAGE : (index + 1) * PAGE, :] = (scaled * gain + shift).astype(BF16)


def lane_index(rows):
    return lax.broadcasted_iota(jnp.int32, (rows, PAIR), 1)


def side_masks(rows):
    lanes = lane_index(rows)
    return [(lanes < HD).astype(BF16), (lanes >= HD).astype(BF16)]


def attend_forward(q_ref, k_ref, v_ref, closed_ref, out_ref, lse_ref):
    lanes = lane_index(ROWS)
    masks = side_masks(ROWS)
    first_lane = (lanes == 0).astype(BF16)
    stats = jnp.zeros((ROWS, PAIR), F32)
    for pair in range(QUAD // PAIR):
        cols = slice(pair * PAIR, (pair + 1) * PAIR)
        keys = jnp.concatenate([k_ref[:, cols], closed_ref[...]], axis=1)
        values = v_ref[:, cols]
        queries = q_ref[:, cols]
        results = []
        for side in range(2):
            query = jnp.concatenate([queries * masks[side], first_lane], axis=1)
            scores = against(query, keys)
            top = jnp.max(scores, axis=1, keepdims=True)
            weights = jnp.exp(scores - top)
            total = jnp.sum(weights, axis=1, keepdims=True)
            results.append(product(weights.astype(BF16), values) / total)
            stats = jnp.where(lanes == pair * 2 + side, top + jnp.log(total), stats)
        out_ref[:, cols] = jnp.where(lanes < HD, results[0], results[1])
    lse_ref[...] = jnp.transpose(stats)[:8, :]


def attend_backward(q_ref, k_ref, v_ref, do_ref, lse_ref, delta_ref, closed_ref, dq_ref, dkv_ref):
    lanes = lane_index(ROWS)
    masks = side_masks(ROWS)
    first_lane = (lanes == 0).astype(BF16)
    for pair in range(QUAD // PAIR):
        cols = slice(pair * PAIR, (pair + 1) * PAIR)
        key_part = k_ref[:, cols]
        keys = jnp.concatenate([key_part, closed_ref[...]], axis=1)
        values = v_ref[:, cols]
        dq_parts = []
        dk = None
        dv = None
        for side in range(2):
            row = pair * 2 + side
            query = q_ref[:, cols] * masks[side]
            grad_out = do_ref[:, cols] * masks[side]
            scores = against(keys, jnp.concatenate([query, first_lane], axis=1))
            weights = jnp.exp(scores - lse_ref[row : row + 1, :])
            grad_weights = against(values, grad_out)
            grad_scores = (weights * (grad_weights - delta_ref[row : row + 1, :])).astype(BF16)
            dv_part = product(weights.astype(BF16), grad_out)
            dk_part = product(grad_scores, query)
            dv = dv_part if dv is None else dv + dv_part
            dk = dk_part if dk is None else dk + dk_part
            dq_parts.append(transposed(grad_scores, key_part))
        dq_ref[:, cols] = (jnp.where(lanes < HD, dq_parts[0], dq_parts[1]) * HD ** (-0.5)).astype(
            BF16
        )
        dkv_ref[:, cols] = dk.astype(BF16)
        dkv_ref[:, QUAD + pair * PAIR : QUAD + (pair + 1) * PAIR] = dv.astype(BF16)


def head_sums(values):
    sums = []
    lanes = lane_index(values.shape[0])
    for pair in range(H // 2):
        part = values[:, pair * PAIR : (pair + 1) * PAIR]
        sums.append(jnp.sum(jnp.where(lanes < HD, part, 0.0), axis=1, keepdims=True))
        sums.append(jnp.sum(jnp.where(lanes >= HD, part, 0.0), axis=1, keepdims=True))
    return sums


def head_rows(sums):
    lanes = lane_index(ROWS)
    stats = jnp.zeros((ROWS, PAIR), F32)
    for head, value in enumerate(sums):
        stats = jnp.where(lanes == (head // 4) * 8 + head % 4, value, stats)
    return jnp.transpose(stats)[: 8 * QUADS, :]


def spread_heads(gates):
    lanes = lane_index(gates.shape[0])
    parts = []
    for pair in range(H // 2):
        parts.append(
            jnp.where(lanes < HD, gates[:, 2 * pair : 2 * pair + 1], gates[:, 2 * pair + 1 : 2 * pair + 2])
        )
    return jnp.concatenate(parts, axis=1)


def store_tiles(out_ref, rows, value):
    cuts = out_ref.shape[0]
    lanes = out_ref.shape[2]
    for cut in range(cuts):
        out_ref[cut, rows, :] = value[:, cut * lanes : (cut + 1) * lanes].astype(BF16)


def self_forward_kernel(count, *refs):
    pages = refs[:count]
    gain, shift, closed, wq, wk, wv, out, lse, q_out, k_out, v_out, normed = refs[count:]

    @pl.when(pl.program_id(0) == 0)
    def _():
        normalize_pages(pages, gain[0:1, :], shift[0:1, :], normed)

    q_out[...] = (product(normed[0:ROWS, :], wq[...]).astype(BF16) * HD ** (-0.5)).astype(BF16)
    k_out[...] = product(normed[...], wk[...]).astype(BF16)
    v_out[...] = product(normed[...], wv[...]).astype(BF16)
    attend_forward(q_out, k_out, v_out, closed, out, lse)


def cross_forward_kernel(count, *refs):
    texts = refs[:DOCS]
    pages = refs[DOCS : DOCS + count]
    (
        self_out, w_self, w_gate, gain, shift, closed, wq, wk, wv,
        hidden, gate, out, lse, q_out, k_out, v_out, normed, cross,
    ) = refs[DOCS + count :]

    @pl.when(pl.program_id(0) == 0)
    def _():
        normalize_pages(pages, gain[2:3, :], shift[2:3, :], normed)
        branch = product(self_out[...].astype(BF16), w_self[...])
        for index, text in enumerate(texts):
            rows = slice(index * PAGE, (index + 1) * PAGE)
            hidden[rows, :] = text[...].astype(F32) + branch[rows, :]
        scaled, _ = standardize(hidden[...])
        cross[...] = (scaled * gain[1:2, :] + shift[1:2, :]).astype(BF16)
        gate[...] = jax.nn.sigmoid(product(cross[...], w_gate[...]))

    q_out[...] = (product(cross[...], wq[...]).astype(BF16) * HD ** (-0.5)).astype(BF16)
    k_out[...] = product(normed[...], wk[...]).astype(BF16)
    v_out[...] = product(normed[...], wv[...]).astype(BF16)
    attend_forward(q_out, k_out, v_out, closed, out, lse)


def forward_back_kernel(
    steps, hidden, raw, gate, cot0, cot1, w_out, gain, shift, w_expand, b_expand, w_reduce, b_reduce,
    joined, d_expand, d_reduce, d_out, grad_mixed, grad_raw, delta, grad_logit, d_bias, small,
    gated, mixed, final, upstream, joined_sum, back_sum,
):
    step = pl.program_id(0)

    @pl.when(step == 0)
    def _():
        upstream[0:PAGE, :] = cot0[...]
        upstream[PAGE:ROWS, :] = cot1[...]
        gated[...] = (spread_heads(gate[...]) * raw[...]).astype(BF16)
        rows = hidden[...] + product(gated[...], w_out[...])
        mixed[...] = rows
        scaled, _ = standardize(rows)
        final[...] = (scaled * gain[3:4, :] + shift[3:4, :]).astype(BF16)
        joined_sum[...] = rows + b_reduce[...]
        back_sum[...] = jnp.zeros_like(back_sum)

    inner = product(final[...], w_expand[...]) + b_expand[...]
    squared = inner * inner
    root = (2.0 / jnp.pi) ** 0.5
    curve = jnp.tanh(root * inner * (1.0 + 0.044715 * squared))
    half = 0.5 * (1.0 + curve)
    active = (inner * half).astype(BF16)
    slope = half + 0.5 * inner * (1.0 - curve * curve) * (root * (1.0 + 3.0 * 0.044715 * squared))
    joined_sum[...] += product(active, w_reduce[...])
    grad_active = against(upstream[...], w_reduce[...]).astype(BF16)
    grad_inner = (grad_active.astype(F32) * slope).astype(BF16)
    d_bias[...] = column_sum(grad_inner.astype(F32))
    back_sum[...] += against(grad_inner, w_expand[...])
    store_tiles(d_expand, slice(None), transposed(grad_inner, final[...]))
    store_tiles(d_reduce, slice(None), transposed(upstream[...], active))

    @pl.when(step == steps - 1)
    def _():
        joined[...] = joined_sum[...].astype(BF16)
        scaled, inverse = standardize(mixed[...])
        back = back_sum[...]
        cotangent = upstream[...].astype(F32)
        grad = cotangent + norm_back(back, scaled, inverse, gain[3:4, :])
        grad_mixed[...] = grad
        branch = grad.astype(BF16)
        store_tiles(d_out, slice(None), transposed(branch, gated[...]))
        grad_gated = against(branch, w_out[...]).astype(BF16).astype(F32)
        gates = gate[...]
        lanes = lane_index(ROWS)
        logit = jnp.zeros((ROWS, PAIR), F32)
        for head, value in enumerate(head_sums(grad_gated * raw[...])):
            logit = jnp.where(lanes == head, value, logit)
        grad_logit[...] = logit * gates * (1.0 - gates)
        rounded = (spread_heads(gates) * grad_gated).astype(BF16)
        grad_raw[...] = rounded
        delta[...] = head_rows(head_sums(rounded.astype(F32) * raw[...]))
        small[...] = jnp.concatenate(
            [
                column_sum(cotangent),
                column_sum(back * scaled),
                column_sum(back),
                jnp.zeros((5, D), F32),
            ],
            axis=0,
        )


def spread_back(normed, dkv, wk, wv, dx, dw_k, dw_v, k_rows, v_rows):
    store_tiles(dw_k, k_rows, transposed(dkv[:, :QUAD], normed[...]))
    store_tiles(dw_v, v_rows, transposed(dkv[:, QUAD:], normed[...]))
    weights = jnp.concatenate([wk[...], wv[...]], axis=1)

    def chunk(index, carry):
        rows = pl.ds(pl.multiple_of(index * ROWS, ROWS), ROWS)
        dx[rows, :] += against(dkv[rows, :], weights)
        return carry

    lax.fori_loop(0, dx.shape[0] // ROWS, chunk, 0)


def finish_pages(pages, dx, keep, send):
    gain_sum = jnp.zeros((1, D), F32)
    shift_sum = jnp.zeros((1, D), F32)
    half = len(pages) // 2
    for index, page in enumerate(pages):
        scaled, _ = standardize(page[...].astype(F32))
        part = dx[index * PAGE : (index + 1) * PAGE, :]
        gain_sum += column_sum(part * scaled)
        shift_sum += column_sum(part)
        target = keep if index < half else send
        place = index % half
        target[place * PAGE : (place + 1) * PAGE, :] = part.astype(BF16)
    return gain_sum, shift_sum


def cross_back_kernel(count, *refs):
    pages = refs[:count]
    (
        gain, shift, closed, q_in, k_in, v_in, do_in, lse, delta, wk, wv,
        w_query, w_gate, w_self, hidden, self_out, grad_mixed, grad_logit,
        keep, send, dw_pairs, dw_query, dw_self, dw_gate, grad_hidden, self_do, self_delta, small,
        normed, dkv, dx, dq,
    ) = refs[count:]
    step = pl.program_id(0)

    @pl.when(step == 0)
    def _():
        normalize_pages(pages, gain[2:3, :], shift[2:3, :], normed)
        dx[...] = jnp.zeros_like(dx)

    cols = pl.ds(pl.multiple_of(step * QUAD, QUAD), QUAD)
    attend_backward(
        q_in, k_in, v_in, do_in, lse, delta, closed, dq.at[:, cols], dkv
    )
    spread_back(
        normed, dkv, wk, wv, dx, dw_pairs, dw_pairs,
        cols, pl.ds(pl.multiple_of(D + step * QUAD, QUAD), QUAD),
    )

    @pl.when(step == QUADS - 1)
    def _():
        image_gain, image_shift = finish_pages(pages, dx, keep, send)
        scaled, inverse = standardize(hidden[...])
        cross = (scaled * gain[1:2, :] + shift[1:2, :]).astype(BF16)
        grad_query = dq[...]
        store_tiles(dw_query, slice(None), transposed(grad_query, cross))
        dw_gate[...] = transposed(grad_logit[...], cross.astype(F32), HIGHEST)[:16, :]
        upstream = against(grad_query, w_query[...]) + against(
            grad_logit[...], w_gate[...].astype(F32), HIGHEST
        )
        grad = grad_mixed[...] + norm_back(upstream, scaled, inverse, gain[1:2, :])
        grad_hidden[...] = grad
        branch = grad.astype(BF16)
        store_tiles(dw_self, slice(None), transposed(branch, self_out[...].astype(BF16)))
        grad_result = against(branch, w_self[...]).astype(BF16)
        self_do[...] = grad_result
        self_delta[...] = head_rows(head_sums(grad_result.astype(F32) * self_out[...]))
        small[...] = jnp.concatenate(
            [
                column_sum(upstream * scaled),
                column_sum(upstream),
                image_gain,
                image_shift,
                jnp.zeros((4, D), F32),
            ],
            axis=0,
        )


def self_back_kernel(count, *refs):
    pages = refs[:count]
    (
        gain, shift, closed, q_in, k_in, v_in, do_in, lse, delta, wq, wk, wv,
        keep, send, dw_project, small,
        normed, dkv, dx, dq,
    ) = refs[count:]
    step = pl.program_id(0)

    @pl.when(step == 0)
    def _():
        normalize_pages(pages, gain[0:1, :], shift[0:1, :], normed)
        dx[...] = jnp.zeros_like(dx)

    attend_backward(q_in, k_in, v_in, do_in, lse, delta, closed, dq, dkv)
    spread_back(
        normed, dkv, wk, wv, dx, dw_project, dw_project,
        pl.ds(pl.multiple_of(D + step * QUAD, QUAD), QUAD),
        pl.ds(pl.multiple_of(2 * D + step * QUAD, QUAD), QUAD),
    )
    store_tiles(
        dw_project,
        pl.ds(pl.multiple_of(step * QUAD, QUAD), QUAD),
        transposed(dq[...], normed[0:ROWS, :]),
    )
    dx[0:ROWS, :] += against(dq[...], wq[...])

    @pl.when(step == QUADS - 1)
    def _():
        gain_sum, shift_sum = finish_pages(pages, dx, keep, send)
        small[...] = jnp.concatenate([gain_sum, shift_sum, jnp.zeros((6, D), F32)], axis=0)


class Places:
    def __init__(self, wide, blk):
        self.wide = wide
        self.blk = blk
        self.part = blk // 4
        self.w = lax.axis_index("wide")
        self.b = lax.axis_index("blk")
        self.quarter = self.b // self.part
        self.turn = self.quarter % 2

    def bit(self, name):
        axis, bit = name
        return ((self.w if axis == "w" else self.b) // (1 << bit)) % 2

    def flip(self, name):
        axis, bit = name
        step = (1 << bit) * (1 - 2 * self.bit(name))
        return (self.w + step, self.b) if axis == "w" else (self.w, self.b + step)

    def swap(self, turn):
        core = self.w % 2
        turned = self.turn if turn == 0 else 1 - self.turn
        return (
            self.w - core + self.quarter // 2,
            (2 * core + turned) * self.part + self.b % self.part,
        )

    def swap_stays(self):
        return self.w % 2 == self.quarter // 2


def bit_names(wide, blk):
    return [("w", bit) for bit in range(wide.bit_length() - 1)] + [
        ("b", bit) for bit in range(blk.bit_length() - 1)
    ]


def group_bits(blk):
    return [("b", bit) for bit in range((blk // 4).bit_length() - 1)] + [("w", 0)]


def tile_bits(wide, blk):
    return (
        [("w", bit) for bit in range(wide.bit_length() - 2, 0, -1)]
        + [("b", bit) for bit in range(blk.bit_length() - 2, -1, -1)]
        + [("w", 0)]
    )


def remote(source, target, send, receive, device):
    return pltpu.make_async_remote_copy(
        src_ref=source,
        dst_ref=target,
        send_sem=send,
        recv_sem=receive,
        device_id=device,
        device_id_type=pl.DeviceIdType.MESH,
    )


def greet(places, names, swaps):
    barrier = pltpu.get_barrier_semaphore()
    for name in names:
        pl.semaphore_signal(
            barrier, inc=1, device_id=places.flip(name), device_id_type=pl.DeviceIdType.MESH
        )
    count = len(names)
    if swaps:
        pl.semaphore_signal(
            barrier, inc=1, device_id=places.swap(1), device_id_type=pl.DeviceIdType.MESH
        )

        @pl.when(jnp.logical_not(places.swap_stays()))
        def _():
            pl.semaphore_signal(
                barrier, inc=1, device_id=places.swap(0), device_id_type=pl.DeviceIdType.MESH
            )

        count = count + 2 - places.swap_stays().astype(jnp.int32)
    pl.semaphore_wait(barrier, count)


class Scatter:
    def __init__(self, places, names, order, grad, own, got, ends, sends, receives, local):
        self.places = places
        self.grad = grad
        self.own = own
        self.got = got
        self.ends = ends
        self.sends = sends
        self.receives = receives
        self.local = local
        self.order = order
        self.axes = []
        left = list(names)
        for name in order:
            self.axes.append(left.index(name))
            left.remove(name)
        self.stages = len(order)

    def cut(self, ref, stage, index):
        axis = self.axes[stage]
        return ref.at[(slice(None),) * axis + (index,)]

    def copy(self, stage):
        place = self.places
        if stage == self.stages:
            source, target, name = self.ends.at[0], self.ends.at[1], ("w", 0)
        else:
            name = self.order[stage]
            source = self.grad if stage == 0 else self.got[stage - 1]
            source = self.cut(source, stage, 1 - place.bit(name))
            target = self.got[stage]
        return remote(
            source, target, self.sends.at[stage], self.receives.at[stage], place.flip(name)
        )

    def fetch(self):
        kept = self.cut(self.grad, 0, self.places.bit(self.order[0]))
        return pltpu.make_async_copy(kept, self.own, self.local)

    def start(self):
        self.copy(0).start()
        self.fetch().start()

    def add(self, stage):
        self.copy(stage).wait_recv()
        target = self.got[stage]
        if stage == 0:
            self.fetch().wait()
            source = self.own
        else:
            source = self.cut(self.got[stage - 1], stage, self.places.bit(self.order[stage]))
        lead = len(target.shape) - 2
        if lead == 0:
            target[...] = target[...] + source[...]
        else:

            def block(index, carry):
                at = tuple((index // (1 << (lead - 1 - axis))) % 2 for axis in range(lead))
                target[at] = target[at] + source[at]
                return carry

            lax.fori_loop(0, 1 << lead, block, 0)
        if stage + 1 == self.stages:
            lanes = target.shape[-1] // 2
            piece = target[...]
            second = self.places.bit(("w", 0)) == 1
            self.ends[0] = jnp.where(second, piece[:, :lanes], piece[:, lanes:])
        self.copy(stage + 1).start()

    def end(self, out):
        self.copy(self.stages).wait_recv()
        lanes = out.shape[-1]
        piece = self.got[-1][...]
        other = self.ends[1]
        second = self.places.bit(("w", 0)) == 1
        mine = jnp.where(second, piece[:, lanes:], piece[:, :lanes])
        out[0] = jnp.where(second, other, mine)
        out[1] = jnp.where(second, mine, other)
        for stage in range(self.stages + 1):
            self.copy(stage).wait_send()


class Rows:
    def __init__(self, places, names, keep, send, sums, got, home, landed, sends, receives):
        self.places = places
        self.names = list(reversed(names))
        self.keep = keep
        self.send = send
        self.sums = sums
        self.got = got
        self.home = home
        self.landed = landed
        self.sends = sends
        self.receives = receives

    def copy(self, stage):
        source = self.send if stage == 0 else self.sums
        rows = self.got[stage].shape[0]
        if stage > 0:
            source = source.at[pl.ds(rows, rows)]
        return remote(
            source, self.got[stage], self.sends.at[stage], self.receives.at[stage],
            self.places.flip(self.names[stage]),
        )

    def start(self):
        self.copy(0).start()

    def add(self, stage):
        self.copy(stage).wait_recv()
        if stage > 0:
            self.copy(stage).wait_send()
        source = self.keep if stage == 0 else self.sums
        rows = self.got[stage].shape[0]

        def block(index, carry):
            at = pl.ds(pl.multiple_of(index * PAGE, PAGE), PAGE)
            self.sums[at, :] = source[at, :] + self.got[stage][at, :]
            return carry

        lax.fori_loop(0, rows // PAGE, block, 0)
        if stage + 1 < len(self.names):
            self.copy(stage + 1).start()

    def norm(self, pages, gain, added):
        for turn, page in enumerate(pages):
            rows = slice(turn * PAGE, (turn + 1) * PAGE)
            scaled, inverse = standardize(page[...].astype(F32))
            grad = norm_back(self.sums[rows, :].astype(F32), scaled, inverse, gain)
            if added is not None:
                grad = grad + added[rows, :]
            self.home[turn] = grad.astype(BF16)
            self.go(turn, True)

    def back(self, turn):
        stage = len(self.names) + turn
        return remote(
            self.home.at[turn], self.landed.at[self.places.turn], self.sends.at[stage],
            self.receives.at[stage], self.places.swap(turn),
        )

    def go(self, turn, begin):
        def carry():
            copy = self.back(turn)
            copy.start() if begin else copy.wait()

        if turn > 0:
            carry()
            return
        stays = self.places.swap_stays()
        pl.when(jnp.logical_not(stays))(carry)
        if begin:

            @pl.when(stays)
            def _():
                self.landed[self.places.turn] = self.home[turn]

    def end(self, out):
        for turn in range(DOCS):
            self.go(turn, False)
        self.copy(0).wait_send()
        out[...] = self.landed[...]


class Total:
    def __init__(self, places, names, mine, got, sends, receives):
        self.places = places
        self.names = names
        self.mine = mine
        self.got = got
        self.sends = sends
        self.receives = receives

    def copy(self, stage):
        return remote(
            self.mine.at[stage], self.got.at[stage], self.sends.at[stage], self.receives.at[stage],
            self.places.flip(self.names[stage]),
        )

    def start(self):
        self.copy(0).start()

    def add(self, stage, out):
        self.copy(stage).wait()
        value = self.mine[stage] + self.got[stage]
        if stage + 1 < len(self.names):
            self.mine[stage + 1] = value
            self.copy(stage + 1).start()
        else:
            out[...] = value


def exchange_kernel(wide, blk, orders, *refs):
    count = len(orders)
    grads, refs = refs[:count], refs[count:]
    (
        text_keep, text_send, image_keep, image_send, text0, text1, image0, image1,
        grad_hidden, gain, small,
    ), refs = refs[:11], refs[11:]
    (text_out, image_out, small_out), refs = refs[:3], refs[3:]
    outs, refs = refs[:count], refs[count:]
    places = Places(wide, blk)
    names = bit_names(wide, blk)
    stages = len(names)
    groups = group_bits(blk)
    scatters = []
    for index, order in enumerate(orders):
        own, got, ends, sends, receives, local = (
            refs[0], refs[1 : 1 + stages], refs[1 + stages], refs[2 + stages], refs[3 + stages],
            refs[4 + stages],
        )
        refs = refs[5 + stages :]
        scatters.append(
            Scatter(
                places, tile_bits(wide, blk), order, grads[index], own, got, ends, sends,
                receives, local,
            )
        )
    streams = []
    for keep, send in ((text_keep, text_send), (image_keep, image_send)):
        sums, got, home, landed, sends, receives = (
            refs[0], refs[1 : 1 + len(groups)], refs[1 + len(groups)], refs[2 + len(groups)],
            refs[3 + len(groups)], refs[4 + len(groups)],
        )
        refs = refs[5 + len(groups) :]
        streams.append(
            Rows(places, groups, keep, send, sums, got, home, landed, sends, receives)
        )
    text, image = streams
    total = Total(places, names, *refs)

    greet(places, names, True)
    total.mine[0] = small[...]
    text.start()
    image.start()
    total.start()
    for scatter in scatters:
        scatter.start()
    for stage in range(len(groups)):
        text.add(stage)
        image.add(stage)
        if stage == 0:
            scatters[0].add(0)
            scatters[1].add(0)
    total.add(0, small_out)
    text.norm((text0, text1), gain[0:1, :], grad_hidden)
    image.norm((image0, image1), gain[2:3, :], None)
    for scatter in scatters[2:]:
        scatter.add(0)
    for stage in range(1, stages):
        total.add(stage, small_out)
        for scatter in scatters:
            scatter.add(stage)
    for scatter, out in zip(scatters, outs):
        scatter.end(out)
    text.end(text_out)
    image.end(image_out)


def whole(shape):
    return pl.BlockSpec(shape, lambda step: (0,) * len(shape))


def columns(rows, offset=0):
    return pl.BlockSpec((rows, QUAD), lambda step: (0, offset + step))


def stat_rows():
    return pl.BlockSpec((8, ROWS), lambda step: (step, 0))


def shaped(shape, kind):
    return jax.ShapeDtypeStruct(shape, kind)


def call(kernel, name, steps, ins, outs, scratch, flops, byte_count):
    in_specs, operands = zip(*ins)
    out_specs, out_shapes = zip(*outs)
    return pl.pallas_call(
        kernel,
        grid=(steps,),
        in_specs=list(in_specs),
        out_specs=list(out_specs),
        out_shape=list(out_shapes),
        scratch_shapes=scratch,
        name=name,
        compiler_params=pltpu.CompilerParams(vmem_limit_bytes=VMEM_LIMIT),
        cost_estimate=pl.CostEstimate(flops=flops, bytes_accessed=byte_count, transcendentals=0),
    )(*operands)


def page_inputs(pages):
    return [(whole((PAGE, D)), page) for page in pages]


def self_forward(pages, gain, shift, closed, project):
    keys = len(pages) * PAGE
    return call(
        functools.partial(self_forward_kernel, len(pages)),
        "self_forward",
        QUADS,
        page_inputs(pages)
        + [
            (whole(gain.shape), gain),
            (whole(shift.shape), shift),
            (whole(closed.shape), closed),
            (columns(D), project),
            (columns(D, QUADS), project),
            (columns(D, 2 * QUADS), project),
        ],
        [
            (columns(ROWS), shaped((ROWS, D), F32)),
            (stat_rows(), shaped((8 * QUADS, ROWS), F32)),
            (columns(ROWS), shaped((ROWS, D), BF16)),
            (columns(keys), shaped((keys, D), BF16)),
            (columns(keys), shaped((keys, D), BF16)),
        ],
        [pltpu.VMEM((keys, D), BF16)],
        6 * 10**9,
        12 * 10**6,
    )


def cross_forward(texts, pages, self_out, w_self, w_gate, gain, shift, closed, w_query, w_pairs):
    keys = len(pages) * PAGE
    return call(
        functools.partial(cross_forward_kernel, len(pages)),
        "cross_forward",
        QUADS,
        page_inputs(texts)
        + page_inputs(pages)
        + [
            (whole(self_out.shape), self_out),
            (whole(w_self.shape), w_self),
            (whole(w_gate.shape), w_gate),
            (whole(gain.shape), gain),
            (whole(shift.shape), shift),
            (whole(closed.shape), closed),
            (columns(D), w_query),
            (columns(D), w_pairs),
            (columns(D, QUADS), w_pairs),
        ],
        [
            (whole((ROWS, D)), shaped((ROWS, D), F32)),
            (whole((ROWS, PAIR)), shaped((ROWS, PAIR), F32)),
            (columns(ROWS), shaped((ROWS, D), F32)),
            (stat_rows(), shaped((8 * QUADS, ROWS), F32)),
            (columns(ROWS), shaped((ROWS, D), BF16)),
            (columns(keys), shaped((keys, D), BF16)),
            (columns(keys), shaped((keys, D), BF16)),
        ],
        [pltpu.VMEM((keys, D), BF16), pltpu.VMEM((ROWS, D), BF16)],
        7 * 10**9,
        14 * 10**6,
    )


def forward_back(
    hidden, raw, gate, cots, w_out, gain, shift, w_expand, b_expand, w_reduce, b_reduce, cuts, far_cuts
):
    steps = FF // D
    far = FF // far_cuts
    if far >= D:
        far_spec = pl.BlockSpec((1, D, D), lambda step: (step * D // far, 0, (step * D % far) // D))
    else:
        far_spec = pl.BlockSpec((D // far, D, far), lambda step: (step, 0, 0))
    return call(
        functools.partial(forward_back_kernel, steps),
        "forward_back",
        steps,
        [
            (whole((ROWS, D)), hidden),
            (whole((ROWS, D)), raw),
            (whole((ROWS, PAIR)), gate),
        ]
        + page_inputs(cots)
        + [
            (whole((D, D)), w_out),
            (whole(gain.shape), gain),
            (whole(shift.shape), shift),
            (pl.BlockSpec((D, D), lambda step: (0, step)), w_expand),
            (pl.BlockSpec((1, D), lambda step: (0, step)), b_expand),
            (pl.BlockSpec((D, D), lambda step: (step, 0)), w_reduce),
            (whole((1, D)), b_reduce),
        ],
        [
            (whole((ROWS, D)), shaped((ROWS, D), BF16)),
            (
                pl.BlockSpec((cuts, D, D // cuts), lambda step: (0, step, 0)),
                shaped((cuts, FF, D // cuts), BF16),
            ),
            (far_spec, shaped((far_cuts, D, far), BF16)),
            (whole((cuts, D, D // cuts)), shaped((cuts, D, D // cuts), BF16)),
            (whole((ROWS, D)), shaped((ROWS, D), F32)),
            (whole((ROWS, D)), shaped((ROWS, D), BF16)),
            (whole((8 * QUADS, ROWS)), shaped((8 * QUADS, ROWS), F32)),
            (whole((ROWS, PAIR)), shaped((ROWS, PAIR), F32)),
            (pl.BlockSpec((1, D), lambda step: (0, step)), shaped((1, FF), F32)),
            (whole((8, D)), shaped((8, D), F32)),
        ],
        [
            pltpu.VMEM((ROWS, D), BF16),
            pltpu.VMEM((ROWS, D), F32),
            pltpu.VMEM((ROWS, D), BF16),
            pltpu.VMEM((ROWS, D), BF16),
            pltpu.VMEM((ROWS, D), F32),
            pltpu.VMEM((ROWS, D), F32),
        ],
        8 * 10**9,
        25 * 10**6,
    )


def back_scratch(keys, dq_columns):
    return [
        pltpu.VMEM((keys, D), BF16),
        pltpu.VMEM((keys, 2 * QUAD), BF16),
        pltpu.VMEM((keys, D), F32),
        pltpu.VMEM((ROWS, dq_columns), BF16),
    ]


def cross_back(
    pages, gain, shift, closed, q, k, v, grad_out, lse, delta, w_pairs,
    w_query, w_gate, w_self, hidden, self_out, grad_mixed, grad_logit, cuts,
):
    keys = len(pages) * PAGE
    half = keys // 2
    return call(
        functools.partial(cross_back_kernel, len(pages)),
        "cross_back",
        QUADS,
        page_inputs(pages)
        + [
            (whole(gain.shape), gain),
            (whole(shift.shape), shift),
            (whole(closed.shape), closed),
            (columns(ROWS), q),
            (columns(keys), k),
            (columns(keys), v),
            (columns(ROWS), grad_out),
            (stat_rows(), lse),
            (stat_rows(), delta),
            (columns(D), w_pairs),
            (columns(D, QUADS), w_pairs),
            (whole((D, D)), w_query),
            (whole((D, PAIR)), w_gate),
            (whole((D, D)), w_self),
            (whole((ROWS, D)), hidden),
            (whole((ROWS, D)), self_out),
            (whole((ROWS, D)), grad_mixed),
            (whole((ROWS, PAIR)), grad_logit),
        ],
        [
            (whole((half, D)), shaped((half, D), BF16)),
            (whole((half, D)), shaped((half, D), BF16)),
            (whole((cuts, 2 * D, D // cuts)), shaped((cuts, 2 * D, D // cuts), BF16)),
            (whole((cuts, D, D // cuts)), shaped((cuts, D, D // cuts), BF16)),
            (whole((cuts, D, D // cuts)), shaped((cuts, D, D // cuts), BF16)),
            (whole((16, D)), shaped((16, D), F32)),
            (whole((ROWS, D)), shaped((ROWS, D), F32)),
            (whole((ROWS, D)), shaped((ROWS, D), BF16)),
            (whole((8 * QUADS, ROWS)), shaped((8 * QUADS, ROWS), F32)),
            (whole((8, D)), shaped((8, D), F32)),
        ],
        back_scratch(keys, D),
        12 * 10**9,
        20 * 10**6,
    )


def self_back(pages, gain, shift, closed, q, k, v, grad_out, lse, delta, project, cuts):
    keys = len(pages) * PAGE
    half = keys // 2
    return call(
        functools.partial(self_back_kernel, len(pages)),
        "self_back",
        QUADS,
        page_inputs(pages)
        + [
            (whole(gain.shape), gain),
            (whole(shift.shape), shift),
            (whole(closed.shape), closed),
            (columns(ROWS), q),
            (columns(keys), k),
            (columns(keys), v),
            (columns(ROWS), grad_out),
            (stat_rows(), lse),
            (stat_rows(), delta),
            (columns(D), project),
            (columns(D, QUADS), project),
            (columns(D, 2 * QUADS), project),
        ],
        [
            (whole((half, D)), shaped((half, D), BF16)),
            (whole((half, D)), shaped((half, D), BF16)),
            (whole((cuts, 3 * D, D // cuts)), shaped((cuts, 3 * D, D // cuts), BF16)),
            (whole((8, D)), shaped((8, D), F32)),
        ],
        back_scratch(keys, QUAD),
        11 * 10**9,
        17 * 10**6,
    )


def exchange(wide, blk, orders, grads, keeps, texts, images, grad_hidden, gain, small):
    names = bit_names(wide, blk)
    stages = len(names)
    groups = group_bits(blk)
    vmem = pl.BlockSpec(memory_space=pltpu.VMEM)
    scratch = []
    results = []
    for grad in grads:
        *lead, rows, lanes = grad.shape
        scratch.append(pltpu.VMEM((*lead[1:], rows, lanes), BF16))
        for stage in range(stages):
            scratch.append(pltpu.VMEM((*lead[stage + 1 :], rows, lanes), BF16))
        scratch.append(pltpu.VMEM((2, rows, lanes // 2), BF16))
        scratch += [pltpu.SemaphoreType.DMA((stages + 1,))] * 2 + [pltpu.SemaphoreType.DMA]
        results.append(shaped((2, rows, lanes // 2), BF16))
    for keep, _ in keeps:
        rows = keep.shape[0]
        scratch.append(pltpu.VMEM((rows, D), BF16))
        for stage in range(len(groups)):
            scratch.append(pltpu.VMEM((rows >> stage, D), BF16))
        scratch += [pltpu.VMEM((DOCS, PAGE, D), BF16)] * 2
        scratch += [pltpu.SemaphoreType.DMA((len(groups) + DOCS,))] * 2
    scratch += [pltpu.VMEM((stages, *small.shape), F32)] * 2
    scratch += [pltpu.SemaphoreType.DMA((stages,))] * 2
    stream = shaped((DOCS, PAGE, D), BF16)
    operands = [*grads, *keeps[0], *keeps[1], *texts, *images, grad_hidden, gain, small]
    return pl.pallas_call(
        functools.partial(exchange_kernel, wide, blk, orders),
        in_specs=[pl.BlockSpec(memory_space=pl.ANY)] * len(grads)
        + [vmem] * (len(operands) - len(grads)),
        out_specs=[vmem] * (3 + len(grads)),
        out_shape=[stream, stream, shaped(small.shape, F32), *results],
        scratch_shapes=scratch,
        name="exchange",
        compiler_params=pltpu.CompilerParams(
            vmem_limit_bytes=VMEM_LIMIT, collective_id=0, has_side_effects=True
        ),
        cost_estimate=pl.CostEstimate(flops=10**7, bytes_accessed=4 * 10**8, transcendentals=0),
    )(*operands)


class Layout:
    def __init__(self):
        self.wide = lax.axis_size("wide")
        self.blk = lax.axis_size("blk")
        self.part = self.blk // 4
        self.w = lax.axis_index("wide")
        self.b = lax.axis_index("blk")
        self.turn = lax.rem(self.b // self.part, 2)
        self.bits = {}
        for bit in range(self.wide.bit_length() - 1):
            self.bits["w", bit] = (self.w >> bit) & 1
        for bit in range(self.blk.bit_length() - 1):
            self.bits["b", bit] = (self.b >> bit) & 1

    def exchange(self, value, move):
        pairs = []
        for w in range(self.wide):
            for b in range(self.blk):
                to_w, to_b = move(w, b)
                pairs.append((w * self.blk + b, to_w * self.blk + to_b))
        return lax.ppermute(value, AXES, pairs)

    def flip(self, value, name):
        axis, bit = name
        if axis == "w":
            return self.exchange(value, lambda w, b: (w ^ (1 << bit), b))
        return self.exchange(value, lambda w, b: (w, b ^ (1 << bit)))

    def swap(self, value, turn):
        def move(w, b):
            quarter, rest = divmod(b, self.part)
            return (w - w % 2 + quarter // 2, (2 * (w % 2) + ((quarter % 2) ^ turn)) * self.part + rest)

        return self.exchange(value, move)

    def to_group(self, value):
        return [
            self.swap(
                lax.dynamic_index_in_dim(value, self.turn ^ turn, 0, keepdims=False), turn
            )
            for turn in range(DOCS)
        ]

    def from_group(self, pages):
        first, second = (self.swap(page, turn) for turn, page in enumerate(pages))
        flag = self.turn == 0
        return jnp.stack([jnp.where(flag, first, second), jnp.where(flag, second, first)])

    def group_bits(self):
        return [("b", bit) for bit in range(self.part.bit_length() - 1)] + [("w", 0)]

    def gather(self, page):
        pages = [page]
        for name in self.group_bits():
            pages = pages + [self.flip(item, name) for item in pages]
        return pages


def tiled(grad, wide, blk):
    cuts = wide // 2
    if grad.shape[0] != cuts:
        _, rows, lanes = grad.shape
        grad = jnp.transpose(grad.reshape(rows, cuts, lanes // cuts), (1, 0, 2))
    names = tile_bits(wide, blk)
    return grad.reshape((2,) * len(names) + (grad.shape[1] // (2 * blk), grad.shape[2]))


def body(
    text_blocks,
    image_blocks,
    cotangent,
    text_mask,
    page_regions,
    doc_pages,
    self_project,
    self_output,
    cross_query,
    cross_pairs,
    cross_output,
    gate_weight,
    expand_weight,
    expand_bias,
    reduce_weight,
    reduce_bias,
    norm_gain,
    norm_bias,
):
    lay = Layout()
    blk_count = lay.blk
    wide_half = lay.wide // 2
    cuts = wide_half if (D // wide_half) % PAIR == 0 else 1
    far_cuts = wide_half if (FF // wide_half) % PAIR == 0 else 1

    offsets = jnp.arange(PAGE, dtype=jnp.int32)
    living = (lay.b < doc_pages)[:, None]
    text_open = living & ((text_mask > 0) | (offsets[None, :] == 0))
    image_open = living & (offsets[None, :] < page_regions)
    closed_here = jnp.where(
        jnp.concatenate([text_open, image_open], axis=1), 0.0, NEGATIVE
    ).astype(BF16)

    text_own = lay.to_group(text_blocks)
    text_sets = [lay.gather(page) for page in text_own]
    text_pages = [page for pair in zip(*text_sets) for page in pair]

    masks = jnp.stack(lay.to_group(closed_here))
    for name in lay.group_bits():
        masks = jnp.concatenate([masks, lay.flip(masks, name)], axis=0)
    keys = masks.shape[0] * PAGE
    first_lane = jnp.arange(PAIR)[None, :] == 0

    def closed_column(part):
        return jnp.where(first_lane, part.reshape(keys, 1), 0.0).astype(BF16)

    text_closed = closed_column(masks[:, :PAGE])
    image_closed = closed_column(masks[:, PAGE:])

    image_own = lay.to_group(image_blocks)
    image_sets = [lay.gather(page) for page in image_own]
    image_pages = [page for pair in zip(*image_sets) for page in pair]
    cots = lay.to_group(cotangent)

    gate_wide = jnp.pad(gate_weight, ((0, 0), (0, PAIR - H)))

    self_out, self_lse, self_q, self_k, self_v = self_forward(
        text_pages, norm_gain, norm_bias, text_closed, self_project
    )
    hidden, gate, raw, cross_lse, cross_q, cross_k, cross_v = cross_forward(
        text_own, image_pages, self_out, self_output, gate_wide, norm_gain, norm_bias,
        image_closed, cross_query, cross_pairs,
    )
    (
        joined, d_expand, d_reduce, d_cross_output, grad_mixed, grad_raw, cross_delta, grad_logit,
        d_expand_bias, small_last,
    ) = forward_back(
        hidden, raw, gate, cots, cross_output, norm_gain, norm_bias, expand_weight,
        expand_bias.reshape(1, FF), reduce_weight, reduce_bias.reshape(1, D), cuts, far_cuts,
    )
    joined_blocks = lay.from_group([joined[:PAGE], joined[PAGE:]])

    (
        image_keep, image_send, d_pairs, d_query, d_self_output, d_gate, grad_hidden, self_do,
        self_delta, small_cross,
    ) = cross_back(
        image_pages, norm_gain, norm_bias, image_closed, cross_q, cross_k, cross_v, grad_raw,
        cross_lse, cross_delta, cross_pairs, cross_query, gate_wide, self_output, hidden, self_out,
        grad_mixed, grad_logit, cuts,
    )
    text_keep, text_send, d_project, small_self = self_back(
        text_pages, norm_gain, norm_bias, text_closed, self_q, self_k, self_v, self_do,
        self_lse, self_delta, self_project, cuts,
    )
    core = [("w", 0)]
    wide_bits = [("w", bit) for bit in range(1, lay.wide.bit_length() - 1)]
    low_blk = [("b", 0)]
    high_blk = [("b", bit) for bit in range(1, blk_count.bit_length() - 1)]
    plan = [
        (d_expand, core + wide_bits + high_blk + low_blk),
        (d_reduce, core + low_blk + high_blk + wide_bits),
        (d_project, core + wide_bits + low_blk + high_blk),
        (d_pairs, core + low_blk + wide_bits + high_blk),
        (d_query, core + low_blk + high_blk + wide_bits),
        (d_cross_output, core + wide_bits + high_blk + low_blk),
        (d_self_output, core + low_blk + wide_bits + high_blk),
    ]
    small = jnp.concatenate(
        [d_gate, d_expand_bias.reshape(-1, D), small_last[:4], small_cross[:4], small_self[:4]],
        axis=0,
    )
    text_grad, image_grad, sums, *pieces = exchange(
        lay.wide,
        lay.blk,
        [order for _, order in plan],
        [tiled(grad, lay.wide, lay.blk) for grad, _ in plan],
        ((text_keep, text_send), (image_keep, image_send)),
        text_own,
        image_own,
        grad_hidden,
        norm_gain,
        small,
    )
    (
        grad_expand_weight, grad_reduce_weight, grad_self_project, grad_cross_pairs,
        grad_cross_query, grad_cross_output, grad_self_output,
    ) = [
        jnp.transpose(piece.reshape(-1, piece.shape[-1])).astype(F32) for piece in pieces
    ]
    at_bias = 16
    at_last = at_bias + FF // D
    at_cross = at_last + 4
    at_self = at_cross + 4
    return (
        joined_blocks,
        text_grad,
        image_grad,
        grad_self_project,
        grad_self_output,
        grad_cross_query,
        grad_cross_pairs,
        grad_cross_output,
        grad_expand_weight,
        grad_reduce_weight,
        jnp.transpose(sums[:H]),
        sums[at_bias:at_last].reshape(FF),
        sums[at_last],
        jnp.stack([sums[at_self], sums[at_cross], sums[at_cross + 2], sums[at_last + 1]]),
        jnp.stack([sums[at_self + 1], sums[at_cross + 1], sums[at_cross + 3], sums[at_last + 2]]),
    )


def solution(mesh):
    rows = P("wide", "blk", None)
    return jax.shard_map(
        body,
        mesh=mesh,
        in_specs=(rows,) * 3 + (P("wide", "blk"),) * 2 + (P("wide"),) + (P(),) * 12,
        out_specs=(rows,) * 3 + (P("wide", "blk"),) * 7 + (P(),) * 5,
        check_vma=False,
    )
```

```python
import functools
from typing import NamedTuple

import jax
import jax.numpy as jnp
from jax import lax
from jax.experimental import pallas as pl
from jax.experimental.pallas import tpu as pltpu
from jax.sharding import PartitionSpec as P

D = 768
H = 12
HD = 64
FF = 3072
PAGE = 128
DOCS = 2
ROWS = DOCS * PAGE
QUAD = 256
QUADS = D // QUAD
PAIR = 128
IMAGE = 112
EXTRA = 16
EPSILON = 1e-05
NEGATIVE = -1e30
HIGHEST = lax.Precision.HIGHEST
BF16 = jnp.bfloat16
F32 = jnp.float32
VMEM_LIMIT = 60 * 1024 * 1024


def product(left, right):
    return jnp.dot(left, right, preferred_element_type=F32)


def against(left, right, precision=None):
    return lax.dot_general(
        left, right, (((1,), (1,)), ((), ())), preferred_element_type=F32, precision=precision
    )


def transposed(left, right, precision=None):
    return lax.dot_general(
        left, right, (((0,), (0,)), ((), ())), preferred_element_type=F32, precision=precision
    )


def standardize(values):
    centred = values - jnp.mean(values, axis=-1, keepdims=True)
    inverse = lax.rsqrt(jnp.mean(centred * centred, axis=-1, keepdims=True) + EPSILON)
    return centred * inverse, inverse


def norm_back(upstream, scaled, inverse, gains):
    weighted = upstream * gains
    return inverse * (
        weighted
        - jnp.mean(weighted, axis=-1, keepdims=True)
        - scaled * jnp.mean(weighted * scaled, axis=-1, keepdims=True)
    )


def column_sum(values):
    return jnp.sum(values, axis=0, keepdims=True)


def normalize_page(page, index, gain, shift, normed):
    rows = page.shape[0]
    scaled, _ = standardize(page[...].astype(F32))
    normed[index * rows : (index + 1) * rows, :] = (scaled * gain + shift).astype(BF16)


def normalize_pages(pages, gain, shift, normed):
    for index in range(pages.shape[0]):
        normalize_page(pages.at[index], index, gain, shift, normed)


def lane_index(rows):
    return lax.broadcasted_iota(jnp.int32, (rows, PAIR), 1)


def side_masks(rows):
    lanes = lane_index(rows)
    return [(lanes < HD).astype(BF16), (lanes >= HD).astype(BF16)]


def attend_forward(q_ref, k_ref, v_ref, closed_ref, out_ref, lse_ref):
    lanes = lane_index(ROWS)
    masks = side_masks(ROWS)
    first_lane = (lanes == 0).astype(BF16)
    stats = jnp.zeros((ROWS, PAIR), F32)
    for pair in range(QUAD // PAIR):
        cols = slice(pair * PAIR, (pair + 1) * PAIR)
        keys = jnp.concatenate([k_ref[:, cols], closed_ref[...]], axis=1)
        values = v_ref[:, cols]
        queries = q_ref[:, cols]
        results = []
        for side in range(2):
            query = jnp.concatenate([queries * masks[side], first_lane], axis=1)
            scores = against(query, keys)
            top = jnp.max(scores, axis=1, keepdims=True)
            weights = jnp.exp(scores - top)
            total = jnp.sum(weights, axis=1, keepdims=True)
            results.append(product(weights.astype(BF16), values) / total)
            stats = jnp.where(lanes == pair * 2 + side, top + jnp.log(total), stats)
        out_ref[:, cols] = jnp.where(lanes < HD, results[0], results[1])
    lse_ref[...] = jnp.transpose(stats)[:8, :]


def attend_backward(q_ref, k_ref, v_ref, do_ref, lse_ref, delta_ref, closed_ref, dq_ref, dkv_ref, hook):
    lanes = lane_index(ROWS)
    masks = side_masks(ROWS)
    first_lane = (lanes == 0).astype(BF16)
    for pair in range(QUAD // PAIR):
        cols = slice(pair * PAIR, (pair + 1) * PAIR)
        key_part = k_ref[:, cols]
        keys = jnp.concatenate([key_part, closed_ref[...]], axis=1)
        values = v_ref[:, cols]
        dq_parts = []
        dk = None
        dv = None
        for side in range(2):
            row = pair * 2 + side
            query = q_ref[:, cols] * masks[side]
            grad_out = do_ref[:, cols] * masks[side]
            scores = against(keys, jnp.concatenate([query, first_lane], axis=1))
            weights = jnp.exp(scores - lse_ref[row : row + 1, :])
            grad_weights = against(values, grad_out)
            grad_scores = (weights * (grad_weights - delta_ref[row : row + 1, :])).astype(BF16)
            dv_part = product(weights.astype(BF16), grad_out)
            dk_part = product(grad_scores, query)
            dv = dv_part if dv is None else dv + dv_part
            dk = dk_part if dk is None else dk + dk_part
            dq_parts.append(transposed(grad_scores, key_part))
        dq_ref[:, cols] = (jnp.where(lanes < HD, dq_parts[0], dq_parts[1]) * HD ** (-0.5)).astype(
            BF16
        )
        dkv_ref[:, cols] = dk.astype(BF16)
        dkv_ref[:, QUAD + pair * PAIR : QUAD + (pair + 1) * PAIR] = dv.astype(BF16)
        if pair == 0:
            hook()


def head_sums(values):
    sums = []
    lanes = lane_index(values.shape[0])
    for pair in range(H // 2):
        part = values[:, pair * PAIR : (pair + 1) * PAIR]
        sums.append(jnp.sum(jnp.where(lanes < HD, part, 0.0), axis=1, keepdims=True))
        sums.append(jnp.sum(jnp.where(lanes >= HD, part, 0.0), axis=1, keepdims=True))
    return sums


def head_rows(sums):
    lanes = lane_index(ROWS)
    stats = jnp.zeros((ROWS, PAIR), F32)
    for head, value in enumerate(sums):
        stats = jnp.where(lanes == (head // 4) * 8 + head % 4, value, stats)
    return jnp.transpose(stats)[: 8 * QUADS, :]


def spread_heads(gates):
    lanes = lane_index(gates.shape[0])
    parts = []
    for pair in range(H // 2):
        parts.append(
            jnp.where(lanes < HD, gates[:, 2 * pair : 2 * pair + 1], gates[:, 2 * pair + 1 : 2 * pair + 2])
        )
    return jnp.concatenate(parts, axis=1)


def store_tiles(out_ref, rows, value):
    cuts = out_ref.shape[0]
    lanes = out_ref.shape[2]
    for cut in range(cuts):
        out_ref[cut, rows, :] = value[:, cut * lanes : (cut + 1) * lanes].astype(BF16)


class Gather:
    def __init__(self, places, names, packed, landed, waits):
        self.places = places
        self.names = names
        self.packed = packed
        self.landed = landed
        self.sends, self.receives = waits

    @staticmethod
    def waits(names):
        count = DOCS << len(names)
        return [pltpu.SemaphoreType.DMA((count,))] * 2

    def swap(self, turn):
        doc = self.places.turn if turn == 0 else 1 - self.places.turn
        return remote(
            self.packed.at[doc], self.landed.at[turn], self.sends.at[turn], self.receives.at[turn],
            self.places.swap(turn),
        )

    def start(self):
        stays = self.places.swap_stays()
        pl.when(jnp.logical_not(stays))(lambda: self.swap(0).start())
        self.swap(1).start()

        @pl.when(stays)
        def _():
            self.landed[0] = self.packed[self.places.turn]

    def copy(self, block, turn):
        stage = block.bit_length() - 1
        source = (block - (1 << stage)) * DOCS + turn
        at = block * DOCS + turn
        return remote(
            self.landed.at[source], self.landed.at[at], self.sends.at[at], self.receives.at[at],
            self.places.flip(self.names[stage]),
        )

    def arrive(self, block, turn):
        if block > 0:
            self.copy(block, turn).wait_recv()
        elif turn > 0:
            self.swap(turn).wait_recv()
        else:
            stays = self.places.swap_stays()
            pl.when(jnp.logical_not(stays))(lambda: self.swap(0).wait_recv())
        for stage in range(block.bit_length(), len(self.names)):
            self.copy(block + (1 << stage), turn).start()

    def end(self):
        stays = self.places.swap_stays()
        pl.when(jnp.logical_not(stays))(lambda: self.swap(0).wait_send())
        self.swap(1).wait_send()
        for block in range(1, 1 << len(self.names)):
            for turn in range(DOCS):
                self.copy(block, turn).wait_send()


def closed_rows(is_open):
    row = jnp.where(is_open, 0.0, NEGATIVE)
    wide = jnp.concatenate([row, jnp.zeros((1, D - PAGE), F32)], axis=1)
    return jnp.broadcast_to(wide, (EXTRA, D)).astype(BF16)


def closed_column(rows):
    row = rows[0:1, 0:PAGE].astype(F32)
    turned = jnp.transpose(jnp.broadcast_to(row, (PAGE, PAGE)))
    return jnp.where(lane_index(PAGE) == 0, turned, 0.0).astype(BF16)


def self_forward_kernel(
    wide, blk,
    regions, doc_pages, text_in, image_in, cot_in, mask, gain, shift, wq, wk, wv,
    out, lse, q_out, k_out, v_out, text_out, image_out, cot_out, text_closed, image_closed,
    normed, text_packed, image_packed, text_landed, image_landed, cot_landed,
    text_sends, text_receives, image_sends, image_receives, cot_sends, cot_receives, local,
):
    step = pl.program_id(0)
    places = Places(wide, blk)
    groups = group_bits(blk)
    blocks = 1 << len(groups)
    text = Gather(places, groups, text_packed, text_landed, (text_sends, text_receives))
    image = Gather(places, groups, image_packed, image_landed, (image_sends, image_receives))
    cot = Gather(places, [], cot_in, cot_landed, (cot_sends, cot_receives))
    outward = [
        pltpu.make_async_copy(text_landed.at[:, pl.ds(0, PAGE)], text_out, local.at[0]),
        pltpu.make_async_copy(image_landed.at[:, pl.ds(0, IMAGE)], image_out, local.at[1]),
        pltpu.make_async_copy(cot_landed, cot_out, local.at[2]),
    ]

    @pl.when(step == 0)
    def _():
        offsets = lax.broadcasted_iota(jnp.int32, (1, PAGE), 1)
        for doc in range(DOCS):
            text_packed[doc, 0:PAGE, :] = text_in[doc]
            living = places.b < doc_pages[doc]
            is_open = ((mask[doc : doc + 1, :] > 0) | (offsets == 0)) & living
            text_packed[doc, PAGE : PAGE + EXTRA, :] = closed_rows(is_open)
        greet(places, groups, True)
        text.start()
        for doc in range(DOCS):
            image_packed[doc, 0:IMAGE, :] = image_in[doc, 0:IMAGE, :]
            living = places.b < doc_pages[doc]
            is_open = (offsets < regions[doc, 0]) & living
            image_packed[doc, IMAGE : IMAGE + EXTRA, :] = closed_rows(is_open)
        text.arrive(0, 0)
        text.arrive(0, 1)
        image.start()

        def take(block, turn):
            index = block * DOCS + turn
            page = text_landed.at[index, pl.ds(0, PAGE)]
            normalize_page(page, index, gain[0:1, :], shift[0:1, :], normed)
            text_closed[index * PAGE : (index + 1) * PAGE, :] = closed_column(
                text_landed[index, PAGE : PAGE + EXTRA, :]
            )

        for turn in range(DOCS):
            take(0, turn)
        for block in range(1, blocks):
            for turn in range(DOCS):
                text.arrive(block, turn)
            if block == 1:
                image.arrive(0, 0)
                image.arrive(0, 1)
                cot.start()
            for turn in range(DOCS):
                take(block, turn)

    @pl.when(step == 1)
    def _():
        outward[0].start()
        for block in range(1, blocks // 2):
            for turn in range(DOCS):
                image.arrive(block, turn)

    q_out[...] = (product(normed[0:ROWS, :], wq[...]).astype(BF16) * HD ** (-0.5)).astype(BF16)
    k_out[...] = product(normed[...], wk[...]).astype(BF16)
    v_out[...] = product(normed[...], wv[...]).astype(BF16)
    attend_forward(q_out, k_out, v_out, text_closed, out, lse)

    @pl.when(step == QUADS - 1)
    def _():
        for turn in range(DOCS):
            cot.arrive(0, turn)
        outward[2].start()
        for block in range(max(1, blocks // 2), blocks):
            for turn in range(DOCS):
                image.arrive(block, turn)
        outward[1].start()
        for index in range(blocks * DOCS):
            column = closed_column(image_landed[index, IMAGE : IMAGE + EXTRA, :])
            image_closed[index * IMAGE : (index + 1) * IMAGE, :] = column[0:IMAGE, :]
        for stream in (text, image, cot):
            stream.end()
        for copy in outward:
            copy.wait()


def cross_forward_kernel(
    text, pages, self_out, w_self, w_gate, gain, shift, closed, wq, wk, wv,
    hidden, gate, out, lse, q_out, k_out, v_out,
    normed, cross, gates,
):
    @pl.when(pl.program_id(0) == 0)
    def _():
        normalize_pages(pages, gain[2:3, :], shift[2:3, :], normed)
        branch = product(self_out[...].astype(BF16), w_self[...])
        for index in range(DOCS):
            rows = slice(index * PAGE, (index + 1) * PAGE)
            hidden[rows, :] = text[index].astype(F32) + branch[rows, :]
        scaled, _ = standardize(hidden[...])
        cross[...] = (scaled * gain[1:2, :] + shift[1:2, :]).astype(BF16)
        gates[...] = jnp.zeros_like(gates)
        gates[0:H, :] = w_gate[...]
        gate[...] = jax.nn.sigmoid(against(cross[...], gates[...]))

    q_out[...] = (product(cross[...], wq[...]).astype(BF16) * HD ** (-0.5)).astype(BF16)
    k_out[...] = product(normed[...], wk[...]).astype(BF16)
    v_out[...] = product(normed[...], wv[...]).astype(BF16)
    attend_forward(q_out, k_out, v_out, closed, out, lse)


def expand_part(wide, blk, step):
    few = (slice(None),) * (wide.bit_length() - 2)
    rest = (slice(None),) * (blk.bit_length() - 3)
    return few + (step // 2, step % 2) + rest, (slice(None), slice(None))


def reduce_part(wide, blk, step):
    cuts = wide.bit_length() - 2
    rest = (slice(None),) * (blk.bit_length() - 1)
    if cuts >= 2:
        lead = (step // 2, step % 2) + (slice(None),) * (cuts - 2) + rest
        return lead, (slice(None), slice(None))
    lanes = pl.ds(pl.multiple_of((step % 2) * D, D), D)
    return (step // 2,) + rest, (slice(None), lanes)


def put_expand(out, value, step, wide, blk):
    cuts, bits = wide.bit_length() - 2, blk.bit_length() - 1
    rows, lanes = out.shape[-2:]
    for cut in range(1 << cuts):
        for part in range(D // rows):
            at = bits_of(cut, cuts) + (step // 2, step % 2) + bits_of(part, bits - 1)
            out[at] = value[part * rows : (part + 1) * rows, cut * lanes : (cut + 1) * lanes]


def put_reduce(out, value, step, wide, blk):
    cuts, bits = wide.bit_length() - 2, blk.bit_length() - 1
    rows, lanes = out.shape[-2:]
    for part in range(D // rows):
        place = bits_of(part, bits + 1)
        piece = value[part * rows : (part + 1) * rows, :]
        if cuts >= 2:
            for cut in range(D // lanes):
                at = (step // 2, step % 2) + bits_of(cut, cuts - 2) + place
                out[at] = piece[:, cut * lanes : (cut + 1) * lanes]
        else:
            out[(step // 2,) + place + (slice(None), pl.ds(pl.multiple_of((step % 2) * D, D), D))] = piece


def forward_back_kernel(
    steps, wide, blk,
    hidden, raw, gate, cots, w_out, gain, shift, w_expand, b_expand, w_reduce, b_reduce,
    joined, expand_out, reduce_out, d_out, grad_mixed, grad_raw, delta, grad_logit, small,
    gated, mixed, final, upstream, joined_sum, back_sum,
    expand_all, reduce_all, expand_got, reduce_got, sends, receives, local,
):
    step = pl.program_id(0)
    places = Places(wide, blk)
    core = ("w", 0)

    def copies(at):
        found = []
        for index, (part, grad, got) in enumerate(
            ((expand_part, expand_all, expand_got), (reduce_part, reduce_all, reduce_got))
        ):
            lead, tail = part(wide, blk, at)
            found.append(
                remote(
                    grad.at[lead + (1 - places.bit(core),) + tail],
                    got.at[lead + tail],
                    sends.at[index, at],
                    receives.at[index, at],
                    places.flip(core),
                )
            )
        return found

    @pl.when(step == 0)
    def _():
        greet(places, [core], False)
        upstream[0:PAGE, :] = cots[0]
        upstream[PAGE:ROWS, :] = cots[1]
        small[...] = jnp.zeros_like(small)
        gated[...] = (spread_heads(gate[...]) * raw[...]).astype(BF16)
        rows = hidden[...] + product(gated[...], w_out[...])
        mixed[...] = rows
        scaled, _ = standardize(rows)
        final[...] = (scaled * gain[3:4, :] + shift[3:4, :]).astype(BF16)
        joined_sum[...] = rows + b_reduce[...]
        back_sum[...] = jnp.zeros_like(back_sum)

    inner = product(final[...], w_expand[...]) + b_expand[...]
    squared = inner * inner
    root = (2.0 / jnp.pi) ** 0.5
    curve = jnp.tanh(root * inner * (1.0 + 0.044715 * squared))
    half = 0.5 * (1.0 + curve)
    active = (inner * half).astype(BF16)
    slope = half + 0.5 * inner * (1.0 - curve * curve) * (root * (1.0 + 3.0 * 0.044715 * squared))
    joined_sum[...] += product(active, w_reduce[...])
    grad_active = against(upstream[...], w_reduce[...]).astype(BF16)
    grad_inner = (grad_active.astype(F32) * slope).astype(BF16)
    small[pl.ds(8 + step, 1), :] = column_sum(grad_inner.astype(F32))
    back_sum[...] += against(grad_inner, w_expand[...])
    put_expand(expand_all, transposed(grad_inner, final[...]).astype(BF16), step, wide, blk)
    put_reduce(reduce_all, transposed(upstream[...], active).astype(BF16), step, wide, blk)
    for copy in copies(step):
        copy.start()

    @pl.when(step == steps - 1)
    def _():
        total = joined_sum[...].astype(BF16)
        joined[0] = total[:PAGE]
        joined[1] = total[PAGE:]
        scaled, inverse = standardize(mixed[...])
        back = back_sum[...]
        cotangent = upstream[...].astype(F32)
        grad = cotangent + norm_back(back, scaled, inverse, gain[3:4, :])
        grad_mixed[...] = grad
        branch = grad.astype(BF16)
        store_tiles(d_out, slice(None), transposed(branch, gated[...]))
        grad_gated = against(branch, w_out[...]).astype(BF16).astype(F32)
        gates = gate[...]
        lanes = lane_index(ROWS)
        logit = jnp.zeros((ROWS, PAIR), F32)
        for head, value in enumerate(head_sums(grad_gated * raw[...])):
            logit = jnp.where(lanes == head, value, logit)
        grad_logit[...] = logit * gates * (1.0 - gates)
        rounded = (spread_heads(gates) * grad_gated).astype(BF16)
        grad_raw[...] = rounded
        delta[...] = head_rows(head_sums(rounded.astype(F32) * raw[...]))
        small[0:1, :] = column_sum(cotangent)
        small[1:2, :] = column_sum(back * scaled)
        small[2:3, :] = column_sum(back)
        for at in range(steps):
            for copy in copies(at):
                copy.wait_recv()
        moves = []
        for index, (grad, got, out) in enumerate(
            ((expand_all, expand_got, expand_out), (reduce_all, reduce_got, reduce_out))
        ):
            lead = len(got.shape) - 2
            add_blocks(got, grad.at[(slice(None),) * lead + (places.bit(core),)])
            moves.append(pltpu.make_async_copy(got, out, local.at[index]))
            moves[-1].start()
        for at in range(steps):
            for copy in copies(at):
                copy.wait_send()
        for move in moves:
            move.wait()


def spread_back(normed, dkv, wk, wv, dx, dw_k, dw_v, k_rows, v_rows):
    store_tiles(dw_k, k_rows, transposed(dkv[:, :QUAD], normed[...]))
    store_tiles(dw_v, v_rows, transposed(dkv[:, QUAD:], normed[...]))
    weights = jnp.concatenate([wk[...], wv[...]], axis=1)

    size = dx.shape[0] // 4

    def chunk(index, carry):
        rows = pl.ds(pl.multiple_of(index * size, 16), size)
        dx[rows, :] += against(dkv[rows, :], weights)
        return carry

    lax.fori_loop(0, 4, chunk, 0)


def finish_pages(pages, dx, keep, send):
    gain_sum = jnp.zeros((1, D), F32)
    shift_sum = jnp.zeros((1, D), F32)
    count, size, _ = pages.shape
    half = count // 2
    for index in range(count):
        scaled, _ = standardize(pages[index].astype(F32))
        part = dx[index * size : (index + 1) * size, :]
        gain_sum += column_sum(part * scaled)
        shift_sum += column_sum(part)
        target = keep if index < half else send
        place = index % half
        target[place * size : (place + 1) * size, :] = part.astype(BF16)
    return gain_sum, shift_sum


END = 99


def moves_of(plan, jobs):
    done = [-1] * len(jobs)
    moves = {}
    for point in sorted(plan):
        moves[point] = []
        for index in plan[point]:
            moves[point].append((index, done[index]))
            done[index] += 1
    moves[END] = [
        (index, stage)
        for stage in range(-1, max(len(job.order) for job in jobs))
        for index, job in enumerate(jobs)
        if done[index] <= stage < len(job.order)
    ]
    return moves


def run_moves(moves, point, scatters, outs):
    for index, stage in moves.get(point, ()):
        scatter = scatters[index]
        if stage < 0:
            scatter.start()
        else:
            scatter.add(stage)
        if stage + 1 == scatter.stages and not scatter.job.ends:
            scatter.store(outs[index]).start()


def finish_moves(moves, scatters, outs):
    run_moves(moves, END, scatters, outs)
    for scatter, out in zip(scatters, outs):
        scatter.end(out)


def cross_back_kernel(wide, blk, jobs, plan, *refs):
    refs = iter(refs)
    (
        pages, gain, shift, closed, q_in, k_in, v_in, do_in, lse, delta, wk, wv,
        w_query, w_gate, w_self, hidden, self_out, grad_mixed, grad_logit, joined,
    ) = (next(refs) for _ in range(20))
    sources = [next(refs) for _ in jobs]
    (
        keep, send, dw_pairs, dw_query, dw_self, dw_gate, grad_hidden, self_do, self_delta, small,
        joined_out,
    ) = (next(refs) for _ in range(11))
    outs = [next(refs) for _ in jobs]
    normed, dkv, dx, dq, gates = (next(refs) for _ in range(5))
    step = pl.program_id(0)
    moves = moves_of(plan, jobs)
    places = Places(wide, blk)
    scatters = [Scatter(places, job, source, refs) for job, source in zip(jobs, sources)]
    home = Home(places, refs)

    def pump(point):
        run_moves(moves, point, scatters, outs)

    @pl.when(step == 0)
    def _():
        greet(places, bit_names(wide, blk), True)
        pump(0)
        for turn in range(DOCS):
            home.put(turn, joined[turn])
        normalize_pages(pages, gain[2:3, :], shift[2:3, :], normed)
        dx[...] = jnp.zeros_like(dx)

    def middle():
        for at in range(QUADS):
            pl.when(step == at)(functools.partial(pump, 2 * at + 1))

    cols = pl.ds(pl.multiple_of(step * QUAD, QUAD), QUAD)
    attend_backward(
        q_in, k_in, v_in, do_in, lse, delta, closed, dq.at[:, cols], dkv, middle
    )
    spread_back(
        normed, dkv, wk, wv, dx, dw_pairs, dw_pairs,
        cols, pl.ds(pl.multiple_of(D + step * QUAD, QUAD), QUAD),
    )
    for at in range(QUADS):
        pl.when(step == at)(functools.partial(pump, 2 * at + 2))

    @pl.when(step == QUADS - 1)
    def _():
        image_gain, image_shift = finish_pages(pages, dx, keep, send)
        scaled, inverse = standardize(hidden[...])
        cross = (scaled * gain[1:2, :] + shift[1:2, :]).astype(BF16)
        grad_query = dq[...]
        store_tiles(dw_query, slice(None), transposed(grad_query, cross))
        dw_gate[...] = transposed(grad_logit[...], cross.astype(F32), HIGHEST)[:16, :]
        gates[...] = jnp.zeros_like(gates)
        gates[0:H, :] = w_gate[...]
        upstream = against(grad_query, w_query[...]) + jnp.dot(
            grad_logit[...], gates[...].astype(F32), precision=HIGHEST
        )
        grad = grad_mixed[...] + norm_back(upstream, scaled, inverse, gain[1:2, :])
        grad_hidden[...] = grad
        branch = grad.astype(BF16)
        store_tiles(dw_self, slice(None), transposed(branch, self_out[...].astype(BF16)))
        grad_result = against(branch, w_self[...]).astype(BF16)
        self_do[...] = grad_result
        self_delta[...] = head_rows(head_sums(grad_result.astype(F32) * self_out[...]))
        small[...] = jnp.concatenate(
            [
                column_sum(upstream * scaled),
                column_sum(upstream),
                image_gain,
                image_shift,
                jnp.zeros((4, D), F32),
            ],
            axis=0,
        )
        home.end(joined_out)
        finish_moves(moves, scatters, outs)


def self_back_kernel(wide, blk, jobs, plan, *refs):
    refs = iter(refs)
    (
        pages, gain, shift, closed, q_in, k_in, v_in, do_in, lse, delta, wq, wk, wv,
        image_keep, image_send, image_own,
    ) = (next(refs) for _ in range(16))
    sources = [next(refs) for _ in jobs]
    keep, send, dw_project, small, image_out = (next(refs) for _ in range(5))
    outs = [next(refs) for _ in jobs]
    normed, dkv, dx, dq = (next(refs) for _ in range(4))
    step = pl.program_id(0)
    moves = moves_of(plan, jobs)
    places = Places(wide, blk)
    groups = group_bits(blk)
    scatters = [Scatter(places, job, source, refs) for job, source in zip(jobs, sources)]
    image = Rows(places, groups, image_keep, image_send, refs)

    def pump(point):
        if point == 1:
            image.add(0)
        if point == 4:
            for stage in range(1, len(groups)):
                image.add(stage)
            image.norm(image_own, gain[2:3, :], None)
        run_moves(moves, point, scatters, outs)

    @pl.when(step == 0)
    def _():
        greet(places, bit_names(wide, blk), True)
        image.start()
        pump(0)
        normalize_pages(pages, gain[0:1, :], shift[0:1, :], normed)
        dx[...] = jnp.zeros_like(dx)

    def middle():
        for at in range(QUADS):
            pl.when(step == at)(functools.partial(pump, 2 * at + 1))

    attend_backward(q_in, k_in, v_in, do_in, lse, delta, closed, dq, dkv, middle)
    spread_back(
        normed, dkv, wk, wv, dx, dw_project, dw_project,
        pl.ds(pl.multiple_of(D + step * QUAD, QUAD), QUAD),
        pl.ds(pl.multiple_of(2 * D + step * QUAD, QUAD), QUAD),
    )
    store_tiles(
        dw_project,
        pl.ds(pl.multiple_of(step * QUAD, QUAD), QUAD),
        transposed(dq[...], normed[0:ROWS, :]),
    )
    dx[0:ROWS, :] += against(dq[...], wq[...])
    for at in range(QUADS - 1):
        pl.when(step == at)(functools.partial(pump, 2 * at + 2))

    @pl.when(step == QUADS - 1)
    def _():
        gain_sum, shift_sum = finish_pages(pages, dx, keep, send)
        small[...] = jnp.concatenate([gain_sum, shift_sum, jnp.zeros((6, D), F32)], axis=0)
        finish_moves(moves, scatters, outs)
        image.end(image_out)


class Places:
    def __init__(self, wide, blk):
        self.wide = wide
        self.blk = blk
        self.part = blk // 4
        self.w = lax.axis_index("wide")
        self.b = lax.axis_index("blk")
        self.quarter = self.b // self.part
        self.turn = self.quarter % 2

    def bit(self, name):
        axis, bit = name
        return ((self.w if axis == "w" else self.b) // (1 << bit)) % 2

    def flip(self, name):
        axis, bit = name
        step = (1 << bit) * (1 - 2 * self.bit(name))
        return (self.w + step, self.b) if axis == "w" else (self.w, self.b + step)

    def swap(self, turn):
        core = self.w % 2
        turned = self.turn if turn == 0 else 1 - self.turn
        return (
            self.w - core + self.quarter // 2,
            (2 * core + turned) * self.part + self.b % self.part,
        )

    def swap_stays(self):
        return self.w % 2 == self.quarter // 2


def bit_names(wide, blk):
    return [("w", bit) for bit in range(wide.bit_length() - 1)] + [
        ("b", bit) for bit in range(blk.bit_length() - 1)
    ]


def group_bits(blk):
    return [("b", bit) for bit in range((blk // 4).bit_length() - 1)] + [("w", 0)]


def tile_bits(wide, blk):
    return (
        [("w", bit) for bit in range(wide.bit_length() - 2, 0, -1)]
        + [("b", bit) for bit in range(blk.bit_length() - 2, -1, -1)]
        + [("w", 0)]
    )


def remote(source, target, send, receive, device):
    return pltpu.make_async_remote_copy(
        src_ref=source,
        dst_ref=target,
        send_sem=send,
        recv_sem=receive,
        device_id=device,
        device_id_type=pl.DeviceIdType.MESH,
    )


def greet(places, names, swaps):
    barrier = pltpu.get_barrier_semaphore()
    for name in names:
        pl.semaphore_signal(
            barrier, inc=1, device_id=places.flip(name), device_id_type=pl.DeviceIdType.MESH
        )
    count = len(names)
    if swaps:
        pl.semaphore_signal(
            barrier, inc=1, device_id=places.swap(1), device_id_type=pl.DeviceIdType.MESH
        )

        @pl.when(jnp.logical_not(places.swap_stays()))
        def _():
            pl.semaphore_signal(
                barrier, inc=1, device_id=places.swap(0), device_id_type=pl.DeviceIdType.MESH
            )

        count = count + 2 - places.swap_stays().astype(jnp.int32)
    pl.semaphore_wait(barrier, count)


class Job(NamedTuple):
    left: tuple
    order: tuple
    start: int
    rows: int
    lanes: int
    ends: bool

    def after(self):
        return tuple(name for name in self.left if name not in self.order)

    def scratch(self):
        count = len(self.left)
        kinds = []
        if self.order:
            kinds.append(pltpu.VMEM((2,) * (count - 1) + (self.rows, self.lanes), BF16))
        for stage in range(len(self.order)):
            kinds.append(pltpu.VMEM((2,) * (count - 1 - stage) + (self.rows, self.lanes), BF16))
        if self.ends:
            kinds.append(pltpu.VMEM((2, self.rows, self.lanes // 2), BF16))
        waits = len(self.order) + int(self.ends)
        return kinds + [pltpu.SemaphoreType.DMA((waits,))] * 2 + [pltpu.SemaphoreType.DMA]

    def result(self):
        if self.ends:
            return shaped((2, self.rows, self.lanes // 2), BF16)
        return shaped((2,) * len(self.after()) + (self.rows, self.lanes), BF16)


def bits_of(index, count):
    return tuple((index // (1 << (count - 1 - place))) % 2 for place in range(count))


def add_blocks(target, source):
    lead = len(target.shape) - 2
    if lead == 0:
        target[...] = target[...] + source[...]
        return

    def block(index, carry):
        at = bits_of(index, lead)
        target[at] = target[at] + source[at]
        return carry

    lax.fori_loop(0, 1 << lead, block, 0)


class Scatter:
    def __init__(self, places, job, source, scratch):
        self.places = places
        self.job = job
        self.source = source
        self.own = next(scratch) if job.order else None
        self.got = [next(scratch) for _ in job.order] or [source]
        self.ends = next(scratch) if job.ends else None
        self.sends, self.receives, self.local = next(scratch), next(scratch), next(scratch)
        self.stages = len(job.order)
        self.axes = []
        left = list(job.left)
        for name in job.order:
            self.axes.append(left.index(name))
            left.remove(name)

    def cut(self, ref, stage, index):
        axis = self.axes[stage]
        at = (slice(None),) * axis + (index,)
        if ref.shape[-2] != self.job.rows:
            at += (slice(None),) * (len(ref.shape) - 3 - axis)
            at += (pl.ds(self.job.start, self.job.rows), slice(None))
        return ref.at[at]

    def copy(self, stage):
        if stage == self.stages:
            source, target, name = self.ends.at[0], self.ends.at[1], ("w", 0)
        else:
            name = self.job.order[stage]
            source = self.source if stage == 0 else self.got[stage - 1]
            source = self.cut(source, stage, 1 - self.places.bit(name))
            target = self.got[stage]
        return remote(
            source, target, self.sends.at[stage], self.receives.at[stage], self.places.flip(name)
        )

    def fetch(self):
        kept = self.cut(self.source, 0, self.places.bit(self.job.order[0]))
        return pltpu.make_async_copy(kept, self.own, self.local)

    def start(self):
        if self.stages == 0:
            self.halve()
        self.copy(0).start()
        if self.stages > 0:
            self.fetch().start()

    def halve(self):
        lanes = self.job.lanes // 2
        piece = self.got[-1][...]
        second = self.places.bit(("w", 0)) == 1
        self.ends[0] = jnp.where(second, piece[:, :lanes], piece[:, lanes:])

    def add(self, stage):
        self.copy(stage).wait_recv()
        if stage == 0:
            self.fetch().wait()
            source = self.own
        else:
            bit = self.places.bit(self.job.order[stage])
            source = self.cut(self.got[stage - 1], stage, bit)
        add_blocks(self.got[stage], source)
        if stage + 1 < self.stages:
            self.copy(stage + 1).start()
        elif self.job.ends:
            self.halve()
            self.copy(stage + 1).start()

    def store(self, out):
        return pltpu.make_async_copy(self.got[-1], out, self.local)

    def end(self, out):
        if self.job.ends:
            self.copy(self.stages).wait_recv()
            lanes = self.job.lanes // 2
            piece = self.got[-1][...]
            other = self.ends[1]
            second = self.places.bit(("w", 0)) == 1
            mine = jnp.where(second, piece[:, lanes:], piece[:, :lanes])
            out[0] = jnp.where(second, other, mine)
            out[1] = jnp.where(second, mine, other)
        else:
            self.store(out).wait()
        for stage in range(self.stages + int(self.job.ends)):
            self.copy(stage).wait_send()


class Home:
    def __init__(self, places, scratch):
        self.places = places
        self.home, self.landed, self.sends, self.receives = (next(scratch) for _ in range(4))

    @staticmethod
    def scratch():
        return [pltpu.VMEM((DOCS, PAGE, D), BF16)] * 2 + [pltpu.SemaphoreType.DMA((DOCS,))] * 2

    def copy(self, turn):
        return remote(
            self.home.at[turn], self.landed.at[self.places.turn], self.sends.at[turn],
            self.receives.at[turn], self.places.swap(turn),
        )

    def go(self, turn, begin):
        def carry():
            if begin:
                self.copy(turn).start()
            else:
                self.copy(turn).wait()

        if turn > 0:
            carry()
            return
        stays = self.places.swap_stays()
        pl.when(jnp.logical_not(stays))(carry)
        if begin:

            @pl.when(stays)
            def _():
                self.landed[self.places.turn] = self.home[turn]

    def put(self, turn, page):
        self.home[turn] = page
        self.go(turn, True)

    def end(self, out):
        for turn in range(DOCS):
            self.go(turn, False)
        out[...] = self.landed[...]


class Rows:
    def __init__(self, places, names, keep, send, scratch):
        self.places = places
        self.size = keep.shape[0] // (DOCS << (len(names) - 1))
        self.names = list(reversed(names))
        self.keep = keep
        self.send = send
        self.sums = next(scratch)
        self.got = [next(scratch) for _ in names]
        self.sends, self.receives = next(scratch), next(scratch)
        self.back = Home(places, scratch)

    @staticmethod
    def scratch(names, rows):
        kinds = [pltpu.VMEM((rows, D), BF16)]
        kinds += [pltpu.VMEM((rows >> stage, D), BF16) for stage in range(len(names))]
        return kinds + [pltpu.SemaphoreType.DMA((len(names),))] * 2 + Home.scratch()

    def copy(self, stage):
        source = self.send if stage == 0 else self.sums
        rows = self.got[stage].shape[0]
        if stage > 0:
            source = source.at[pl.ds(rows, rows)]
        return remote(
            source, self.got[stage], self.sends.at[stage], self.receives.at[stage],
            self.places.flip(self.names[stage]),
        )

    def start(self):
        self.copy(0).start()

    def add(self, stage):
        self.copy(stage).wait_recv()
        if stage > 0:
            self.copy(stage).wait_send()
        source = self.keep if stage == 0 else self.sums
        rows = self.got[stage].shape[0]

        def block(index, carry):
            at = pl.ds(pl.multiple_of(index * self.size, 16), self.size)
            self.sums[at, :] = source[at, :] + self.got[stage][at, :]
            return carry

        lax.fori_loop(0, rows // self.size, block, 0)
        if stage + 1 < len(self.names):
            self.copy(stage + 1).start()

    def norm(self, pages, gain, added):
        for turn in range(DOCS):
            rows = slice(turn * self.size, (turn + 1) * self.size)
            scaled, inverse = standardize(pages[turn].astype(F32))
            grad = norm_back(self.sums[rows, :].astype(F32), scaled, inverse, gain)
            if added is not None:
                grad = grad + added[rows, :]
            if self.size < PAGE:
                rest = jnp.zeros((PAGE - self.size, D), F32)
                grad = jnp.concatenate([grad, rest], axis=0)
            self.back.put(turn, grad.astype(BF16))

    def end(self, out):
        self.back.end(out)
        self.copy(0).wait_send()


class Total:
    def __init__(self, places, names, scratch):
        self.places = places
        self.names = names
        self.mine, self.got, self.sends, self.receives = (next(scratch) for _ in range(4))

    @staticmethod
    def scratch(names, rows):
        count = len(names)
        return [pltpu.VMEM((count, rows, D), F32)] * 2 + [pltpu.SemaphoreType.DMA((count,))] * 2

    def copy(self, stage):
        return remote(
            self.mine.at[stage], self.got.at[stage], self.sends.at[stage], self.receives.at[stage],
            self.places.flip(self.names[stage]),
        )

    def start(self, value):
        self.mine[0] = value
        self.copy(0).start()

    def add(self, stage, out):
        self.copy(stage).wait()
        value = self.mine[stage] + self.got[stage]
        if stage + 1 < len(self.names):
            self.mine[stage + 1] = value
            self.copy(stage + 1).start()
        else:
            out[...] = value


def tail_kernel(wide, blk, jobs, plan, *refs):
    refs = iter(refs)
    sources = [next(refs) for _ in jobs]
    keep, send, texts, grad_hidden, gain = (next(refs) for _ in range(5))
    small = [next(refs) for _ in range(4)]
    text_out, small_out = next(refs), next(refs)
    outs = [next(refs) for _ in jobs]
    moves = moves_of(plan, jobs)
    places = Places(wide, blk)
    names = bit_names(wide, blk)
    groups = group_bits(blk)
    scatters = [Scatter(places, job, source, refs) for job, source in zip(jobs, sources)]
    text = Rows(places, groups, keep, send, refs)
    total = Total(places, names, refs)

    greet(places, names, True)
    text.start()
    run_moves(moves, 0, scatters, outs)
    total.start(jnp.concatenate([part[...] for part in small], axis=0))
    for stage in range(len(groups) - 1):
        text.add(stage)
    run_moves(moves, 1, scatters, outs)
    total.add(0, small_out)
    run_moves(moves, 2, scatters, outs)
    text.add(len(groups) - 1)
    text.norm(texts, gain[0:1, :], grad_hidden)
    total.add(1, small_out)
    run_moves(moves, 3, scatters, outs)
    for stage in range(2, len(names)):
        total.add(stage, small_out)
        run_moves(moves, 2 + stage, scatters, outs)
    text.end(text_out)
    finish_moves(moves, scatters, outs)


def finish_kernel(layout, *refs):
    refs = iter(refs)
    pieces = [[next(refs) for _ in range(count)] for count in layout]
    streams = [next(refs) for _ in range(3)]
    sums = next(refs)
    for index, parts in enumerate(pieces):
        out = next(refs)
        halves = [part[half] for half in range(2) for part in parts]
        value = jnp.concatenate(halves, axis=0).astype(F32)
        out[...] = value if index + 1 == len(pieces) else jnp.transpose(value)
    for stream in streams:
        out = next(refs)
        out[...] = stream[...]
    gate, bias, last, gains, shifts = (next(refs) for _ in range(5))
    gate[...] = sums[0:H, :]
    for index in range(FF // D):
        bias[pl.ds(index * D, D)] = sums[24 + index, :]
    last[...] = sums[16, :]
    for out, at in ((gains, 0), (shifts, 1)):
        for index, row in enumerate((40 + at, 32 + at, 34 + at, 17 + at)):
            out[index : index + 1, :] = sums[row : row + 1, :]


def whole(shape):
    return pl.BlockSpec(shape, lambda step: (0,) * len(shape))


def columns(rows, offset=0):
    return pl.BlockSpec((rows, QUAD), lambda step: (0, offset + step))


def stat_rows():
    return pl.BlockSpec((8, ROWS), lambda step: (step, 0))


def shaped(shape, kind):
    return jax.ShapeDtypeStruct(shape, kind)


ANY = pl.BlockSpec(memory_space=pl.ANY)


def call(kernel, name, steps, ins, outs, scratch, flops, byte_count, collective=None):
    in_specs, operands = zip(*ins)
    out_specs, out_shapes = zip(*outs)
    return pl.pallas_call(
        kernel,
        grid=(steps,),
        in_specs=list(in_specs),
        out_specs=list(out_specs),
        out_shape=list(out_shapes),
        scratch_shapes=scratch,
        name=name,
        compiler_params=pltpu.CompilerParams(
            vmem_limit_bytes=VMEM_LIMIT,
            collective_id=collective,
            has_side_effects=collective is not None,
        ),
        cost_estimate=pl.CostEstimate(flops=flops, bytes_accessed=byte_count, transcendentals=0),
    )(*operands)


def own_pages(pages):
    return (whole((DOCS, *pages.shape[1:])), pages)


SMEM = pl.BlockSpec(memory_space=pltpu.SMEM)


def self_forward(texts, images, cots, mask, regions, doc_pages, gain, shift, project, wide, blk):
    groups = group_bits(blk)
    count = DOCS << len(groups)
    keys = count * PAGE
    return call(
        functools.partial(self_forward_kernel, wide, blk),
        "self_forward",
        QUADS,
        [
            (SMEM, regions),
            (SMEM, doc_pages),
            (whole(texts.shape), texts),
            (whole(images.shape), images),
            (whole(cots.shape), cots),
            (whole(mask.shape), mask),
            (whole(gain.shape), gain),
            (whole(shift.shape), shift),
            (columns(D), project),
            (columns(D, QUADS), project),
            (columns(D, 2 * QUADS), project),
        ],
        [
            (columns(ROWS), shaped((ROWS, D), F32)),
            (stat_rows(), shaped((8 * QUADS, ROWS), F32)),
            (columns(ROWS), shaped((ROWS, D), BF16)),
            (columns(keys), shaped((keys, D), BF16)),
            (columns(keys), shaped((keys, D), BF16)),
            (ANY, shaped((count, PAGE, D), BF16)),
            (ANY, shaped((count, IMAGE, D), BF16)),
            (ANY, shaped((DOCS, PAGE, D), BF16)),
            (whole((keys, PAIR)), shaped((keys, PAIR), BF16)),
            (whole((count * IMAGE, PAIR)), shaped((count * IMAGE, PAIR), BF16)),
        ],
        [
            pltpu.VMEM((keys, D), BF16),
            pltpu.VMEM((DOCS, PAGE + EXTRA, D), BF16),
            pltpu.VMEM((DOCS, IMAGE + EXTRA, D), BF16),
            pltpu.VMEM((count, PAGE + EXTRA, D), BF16),
            pltpu.VMEM((count, IMAGE + EXTRA, D), BF16),
            pltpu.VMEM((DOCS, PAGE, D), BF16),
        ]
        + Gather.waits(groups) * 2
        + Gather.waits([])
        + [pltpu.SemaphoreType.DMA((3,))],
        6 * 10**9,
        12 * 10**6,
        0,
    )


def cross_forward(texts, pages, self_out, w_self, w_gate, gain, shift, closed, w_query, w_pairs):
    keys = closed.shape[0]
    return call(
        cross_forward_kernel,
        "cross_forward",
        QUADS,
        [
            own_pages(texts),
            (whole(pages.shape), pages),
            (whole(self_out.shape), self_out),
            (whole(w_self.shape), w_self),
            (whole(w_gate.shape), w_gate),
            (whole(gain.shape), gain),
            (whole(shift.shape), shift),
            (whole(closed.shape), closed),
            (columns(D), w_query),
            (columns(D), w_pairs),
            (columns(D, QUADS), w_pairs),
        ],
        [
            (whole((ROWS, D)), shaped((ROWS, D), F32)),
            (whole((ROWS, PAIR)), shaped((ROWS, PAIR), F32)),
            (columns(ROWS), shaped((ROWS, D), F32)),
            (stat_rows(), shaped((8 * QUADS, ROWS), F32)),
            (columns(ROWS), shaped((ROWS, D), BF16)),
            (columns(keys), shaped((keys, D), BF16)),
            (columns(keys), shaped((keys, D), BF16)),
        ],
        [
            pltpu.VMEM((keys, D), BF16),
            pltpu.VMEM((ROWS, D), BF16),
            pltpu.VMEM((PAIR, D), BF16),
        ],
        7 * 10**9,
        14 * 10**6,
    )


def forward_back(
    hidden, raw, gate, cots, w_out, gain, shift, w_expand, b_expand, w_reduce, b_reduce, wide, blk
):
    steps = FF // D
    cuts = tile_cuts(wide)
    names = tile_bits(wide, blk)
    expand = (FF // (2 * blk), D // (wide // 2))
    reduce = (D // (2 * blk), FF // (wide // 2))
    full, part = (2,) * len(names), (2,) * (len(names) - 1)
    return call(
        functools.partial(forward_back_kernel, steps, wide, blk),
        "forward_back",
        steps,
        [
            (whole((ROWS, D)), hidden),
            (whole((ROWS, D)), raw),
            (whole((ROWS, PAIR)), gate),
            (whole((DOCS, PAGE, D)), cots),
            (whole((D, D)), w_out),
            (whole(gain.shape), gain),
            (whole(shift.shape), shift),
            (pl.BlockSpec((D, D), lambda step: (0, step)), w_expand),
            (pl.BlockSpec((1, D), lambda step: (0, step)), b_expand),
            (pl.BlockSpec((D, D), lambda step: (step, 0)), w_reduce),
            (whole((1, D)), b_reduce),
        ],
        [
            (whole((DOCS, PAGE, D)), shaped((DOCS, PAGE, D), BF16)),
            (ANY, shaped(part + expand, BF16)),
            (ANY, shaped(part + reduce, BF16)),
            (whole((cuts, D, D // cuts)), shaped((cuts, D, D // cuts), BF16)),
            (whole((ROWS, D)), shaped((ROWS, D), F32)),
            (whole((ROWS, D)), shaped((ROWS, D), BF16)),
            (whole((8 * QUADS, ROWS)), shaped((8 * QUADS, ROWS), F32)),
            (whole((ROWS, PAIR)), shaped((ROWS, PAIR), F32)),
            (whole((16, D)), shaped((16, D), F32)),
        ],
        [
            pltpu.VMEM((ROWS, D), BF16),
            pltpu.VMEM((ROWS, D), F32),
            pltpu.VMEM((ROWS, D), BF16),
            pltpu.VMEM((ROWS, D), BF16),
            pltpu.VMEM((ROWS, D), F32),
            pltpu.VMEM((ROWS, D), F32),
            pltpu.VMEM(full + expand, BF16),
            pltpu.VMEM(full + reduce, BF16),
            pltpu.VMEM(part + expand, BF16),
            pltpu.VMEM(part + reduce, BF16),
            pltpu.SemaphoreType.DMA((2, steps)),
            pltpu.SemaphoreType.DMA((2, steps)),
            pltpu.SemaphoreType.DMA((2,)),
        ],
        8 * 10**9,
        25 * 10**6,
        1,
    )


def back_scratch(keys, dq_columns):
    return [
        pltpu.VMEM((keys, D), BF16),
        pltpu.VMEM((keys, 2 * QUAD), BF16),
        pltpu.VMEM((keys, D), F32),
        pltpu.VMEM((ROWS, dq_columns), BF16),
    ]


def cross_back(
    pages, gain, shift, closed, q, k, v, grad_out, lse, delta, w_pairs,
    w_query, w_gate, w_self, hidden, self_out, grad_mixed, grad_logit, joined, jobs, sources,
    plan, wide, blk,
):
    keys = closed.shape[0]
    half = keys // 2
    cuts = tile_cuts(wide)
    return call(
        functools.partial(cross_back_kernel, wide, blk, jobs, plan),
        "cross_back",
        QUADS,
        [
            (whole(pages.shape), pages),
            (whole(gain.shape), gain),
            (whole(shift.shape), shift),
            (whole(closed.shape), closed),
            (columns(ROWS), q),
            (columns(keys), k),
            (columns(keys), v),
            (columns(ROWS), grad_out),
            (stat_rows(), lse),
            (stat_rows(), delta),
            (columns(D), w_pairs),
            (columns(D, QUADS), w_pairs),
            (whole((D, D)), w_query),
            (whole(w_gate.shape), w_gate),
            (whole((D, D)), w_self),
            (whole((ROWS, D)), hidden),
            (whole((ROWS, D)), self_out),
            (whole((ROWS, D)), grad_mixed),
            (whole((ROWS, PAIR)), grad_logit),
            (whole((DOCS, PAGE, D)), joined),
        ]
        + [(ANY, source) for source in sources],
        [
            (whole((half, D)), shaped((half, D), BF16)),
            (whole((half, D)), shaped((half, D), BF16)),
            (whole((cuts, 2 * D, D // cuts)), shaped((cuts, 2 * D, D // cuts), BF16)),
            (whole((cuts, D, D // cuts)), shaped((cuts, D, D // cuts), BF16)),
            (whole((cuts, D, D // cuts)), shaped((cuts, D, D // cuts), BF16)),
            (whole((16, D)), shaped((16, D), F32)),
            (whole((ROWS, D)), shaped((ROWS, D), F32)),
            (whole((ROWS, D)), shaped((ROWS, D), BF16)),
            (whole((8 * QUADS, ROWS)), shaped((8 * QUADS, ROWS), F32)),
            (whole((8, D)), shaped((8, D), F32)),
            (whole((DOCS, PAGE, D)), shaped((DOCS, PAGE, D), BF16)),
        ]
        + [(ANY, job.result()) for job in jobs],
        back_scratch(keys, D) + [pltpu.VMEM((PAIR, D), BF16)] + [kind for job in jobs for kind in job.scratch()] + Home.scratch(),
        12 * 10**9,
        20 * 10**6,
        2,
    )


def self_back(
    pages, gain, shift, closed, q, k, v, grad_out, lse, delta, project, image_sums, images,
    jobs, sources, plan, wide, blk,
):
    keys = closed.shape[0]
    half = keys // 2
    cuts = tile_cuts(wide)
    image_half = image_sums[0].shape[0]
    return call(
        functools.partial(self_back_kernel, wide, blk, jobs, plan),
        "self_back",
        QUADS,
        [
            (whole(pages.shape), pages),
            (whole(gain.shape), gain),
            (whole(shift.shape), shift),
            (whole(closed.shape), closed),
            (columns(ROWS), q),
            (columns(keys), k),
            (columns(keys), v),
            (columns(ROWS), grad_out),
            (stat_rows(), lse),
            (stat_rows(), delta),
            (columns(D), project),
            (columns(D, QUADS), project),
            (columns(D, 2 * QUADS), project),
        ]
        + [(whole((image_half, D)), part) for part in image_sums]
        + [own_pages(images)]
        + [(ANY, source) for source in sources],
        [
            (whole((half, D)), shaped((half, D), BF16)),
            (whole((half, D)), shaped((half, D), BF16)),
            (whole((cuts, 3 * D, D // cuts)), shaped((cuts, 3 * D, D // cuts), BF16)),
            (whole((8, D)), shaped((8, D), F32)),
            (whole((DOCS, PAGE, D)), shaped((DOCS, PAGE, D), BF16)),
        ]
        + [(ANY, job.result()) for job in jobs],
        back_scratch(keys, QUAD)
        + [kind for job in jobs for kind in job.scratch()]
        + Rows.scratch(group_bits(blk), image_half),
        11 * 10**9,
        17 * 10**6,
        3,
    )


def tail(wide, blk, jobs, plan, sources, sums, texts, grad_hidden, gain, small):
    names = bit_names(wide, blk)
    vmem = pl.BlockSpec(memory_space=pltpu.VMEM)
    rows = sum(part.shape[0] for part in small)
    operands = [*sources, *sums, texts, grad_hidden, gain, *small]
    own = len(jobs) + len(sums)
    in_specs = [ANY if job.order else vmem for job in jobs] + [vmem] * (len(operands) - len(jobs))
    in_specs[own] = own_pages(texts)[0]
    return pl.pallas_call(
        functools.partial(tail_kernel, wide, blk, jobs, plan),
        grid=(1,),
        in_specs=in_specs,
        out_specs=[vmem] * (2 + len(jobs)),
        out_shape=[
            shaped((DOCS, PAGE, D), BF16),
            shaped((rows, D), F32),
            *(job.result() for job in jobs),
        ],
        scratch_shapes=[kind for job in jobs for kind in job.scratch()]
        + Rows.scratch(group_bits(blk), sums[0].shape[0])
        + Total.scratch(names, rows),
        name="tail",
        compiler_params=pltpu.CompilerParams(
            vmem_limit_bytes=VMEM_LIMIT, collective_id=4, has_side_effects=True
        ),
        cost_estimate=pl.CostEstimate(flops=10**7, bytes_accessed=10**8, transcendentals=0),
    )(*operands)


def finish(pieces, streams, sums):
    vmem = pl.BlockSpec(memory_space=pltpu.VMEM)
    operands = [part for parts in pieces for part in parts] + [*streams, sums]
    results = []
    for index, parts in enumerate(pieces):
        shape = (parts[0].shape[2], sum(2 * part.shape[1] for part in parts))
        results.append(shaped(shape[::-1] if index + 1 == len(pieces) else shape, F32))
    results += [shaped(stream.shape, BF16) for stream in streams]
    results += [shaped((H, D), F32), shaped((FF,), F32), shaped((D,), F32)]
    results += [shaped((4, D), F32)] * 2
    return pl.pallas_call(
        functools.partial(finish_kernel, tuple(len(parts) for parts in pieces)),
        in_specs=[vmem] * len(operands),
        out_specs=[vmem] * len(results),
        out_shape=results,
        name="finish",
        compiler_params=pltpu.CompilerParams(vmem_limit_bytes=VMEM_LIMIT),
        cost_estimate=pl.CostEstimate(flops=10**6, bytes_accessed=5 * 10**6, transcendentals=0),
    )(*operands)


def tile_cuts(wide):
    cuts = wide // 2
    return cuts if (D // cuts) % PAIR == 0 else 1


def tiled(grad, wide, blk):
    cuts = wide // 2
    if grad.shape[0] != cuts:
        _, rows, lanes = grad.shape
        grad = jnp.transpose(grad.reshape(rows, cuts, lanes // cuts), (1, 0, 2))
    names = tile_bits(wide, blk)
    return grad.reshape((2,) * len(names) + (grad.shape[1] // (2 * blk), grad.shape[2]))


def body(
    text_blocks,
    image_blocks,
    cotangent,
    text_mask,
    page_regions,
    doc_pages,
    self_project,
    self_output,
    cross_query,
    cross_pairs,
    cross_output,
    gate_weight,
    expand_weight,
    expand_bias,
    reduce_weight,
    reduce_bias,
    norm_gain,
    norm_bias,
):
    wide = lax.axis_size("wide")
    blk = lax.axis_size("blk")
    names = tuple(tile_bits(wide, blk))
    core = ("w", 0)
    first = (("w", 1),)
    others = tuple(("w", bit) for bit in range(2, wide.bit_length() - 1))
    low = (("b", 0),)
    high = tuple(("b", bit) for bit in range(1, blk.bit_length() - 1))
    share = 2 * blk
    lanes = 2 * D // wide
    far = 2 * FF // wide
    gate_rows = jnp.transpose(gate_weight)

    (
        self_out, self_lse, self_q, self_k, self_v, text_pages, image_pages, cots, text_closed,
        image_closed,
    ) = self_forward(
        text_blocks, image_blocks, cotangent, text_mask, page_regions, doc_pages, norm_gain,
        norm_bias, self_project, wide, blk,
    )
    hidden, gate, raw, cross_lse, cross_q, cross_k, cross_v = cross_forward(
        text_pages, image_pages, self_out, self_output, gate_rows, norm_gain, norm_bias,
        image_closed, cross_query, cross_pairs,
    )
    (
        joined, expand_sum, reduce_sum, d_cross_output, grad_mixed, grad_raw, cross_delta,
        grad_logit, small_last,
    ) = forward_back(
        hidden, raw, gate, cots, cross_output, norm_gain, norm_bias, expand_weight,
        expand_bias.reshape(1, FF), reduce_weight, reduce_bias.reshape(1, D), wide, blk,
    )

    def jobs_of(rows, split, size, left, orders):
        if rows % 16 or not 0 < split < rows:
            return [Job(left, orders[-1], 0, rows, size, False)]
        return [
            Job(left, orders[0], 0, split, size, False),
            Job(left, orders[1], split, rows - split, size, False),
        ]

    expand_rows, reduce_rows = FF // share, D // share
    expand_jobs = jobs_of(
        expand_rows, expand_rows // 32 * 16, lanes, names[:-1], (first + high, first)
    )
    reduce_jobs = jobs_of(reduce_rows, 16, far, names[:-1], (low + high, low))
    jobs = tuple(expand_jobs + reduce_jobs)
    sources = [expand_sum] * len(expand_jobs) + [reduce_sum] * len(reduce_jobs)
    plan = {0: (0, 2), 1: (3,), 2: (2, 1), 4: (0, 2)} if len(jobs) == 4 else {0: range(len(jobs))}
    (
        image_keep, image_send, d_pairs, d_query, d_self_output, d_gate, grad_hidden, self_do,
        self_delta, small_cross, joined_home, *partial,
    ) = cross_back(
        image_pages, norm_gain, norm_bias, image_closed, cross_q, cross_k, cross_v, grad_raw,
        cross_lse, cross_delta, cross_pairs, cross_query, gate_rows, self_output, hidden, self_out,
        grad_mixed, grad_logit, joined, jobs, sources, plan, wide, blk,
    )

    def rest(job, order, ends):
        left = job.after()
        wanted = tuple(name for name in order if name in left)
        return Job(left, wanted, 0, job.rows, job.lanes, ends)

    count = len(jobs)
    jobs = tuple(
        [rest(job, high + low + first + others, False) for job in expand_jobs]
        + [rest(job, high + first + others + low, False) for job in reduce_jobs]
    )
    one = (0, D // share, lanes, False)
    cross_jobs = (
        Job(names, (core,) + low, 0, 2 * D // share, lanes, False),
        Job(names, (core,) + first, *one),
        Job(names, (core,) + first, *one),
        Job(names, (core,) + first, *one),
    )
    cross_grads = [
        tiled(grad, wide, blk) for grad in (d_pairs, d_query, d_cross_output, d_self_output)
    ]
    late = tuple(range(count, count + 4))
    plan = {0: late + tuple(range(count)), 2: late}
    if count == 4:
        plan = {
            0: late + (1, 0, 2), 1: (3,), 2: late + (1,), 3: (3, 0, 2), 4: (1,), 5: (3, 1),
        }
    text_keep, text_send, d_project, small_self, image_home, *partial = self_back(
        text_pages, norm_gain, norm_bias, text_closed, self_q, self_k, self_v, self_do,
        self_lse, self_delta, self_project, (image_keep, image_send), image_pages,
        jobs + cross_jobs, partial + cross_grads, plan, wide, blk,
    )

    project_rows = 3 * D // share
    project_jobs = [
        job._replace(ends=True)
        for job in jobs_of(
            project_rows,
            project_rows // 2 // 16 * 16 + 16,
            lanes,
            names,
            ((core,) + first + low + others + high, (core,) + low + first + others + high),
        )
    ]
    last_jobs = [rest(cross_jobs[0], first + high + others, True)] + [
        rest(job, high + low + others, True) for job in cross_jobs[1:]
    ]
    ended = [Job((), (), 0, job.rows, job.lanes, True) for job in jobs]
    most = len(project_jobs)
    both = tuple(range(most))
    crossed = tuple(range(most, most + 4))
    plan = {
        0: both + crossed + tuple(range(most + 4, most + 4 + count)),
        1: both,
        2: crossed,
        3: both + crossed,
        4: both + crossed,
        5: both,
        6: both,
    }
    text_home, sums, *pieces = tail(
        wide, blk, (*project_jobs, *last_jobs, *ended), plan,
        [tiled(d_project, wide, blk)] * most + partial[count:] + partial[:count],
        (text_keep, text_send), text_pages, grad_hidden, norm_gain,
        (d_gate, small_last, small_cross, small_self),
    )
    project_pieces = pieces[:most]
    cross_pieces = pieces[most : most + 4]
    expand_pieces = pieces[most + 4 : most + 4 + len(expand_jobs)]
    reduce_pieces = pieces[most + 4 + len(expand_jobs) :]
    (
        grad_cross_pairs, grad_cross_query, grad_cross_output, grad_self_output,
        grad_expand_weight, grad_self_project, grad_reduce_weight,
        joined_blocks, text_grad, image_grad,
        grad_gate_weight, grad_expand_bias, grad_reduce_bias, gains, shifts,
    ) = finish(
        [[piece] for piece in cross_pieces] + [expand_pieces, project_pieces, reduce_pieces],
        [joined_home, text_home, image_home], sums,
    )
    return (
        joined_blocks,
        text_grad,
        image_grad,
        grad_self_project,
        grad_self_output,
        grad_cross_query,
        grad_cross_pairs,
        grad_cross_output,
        grad_expand_weight,
        jnp.transpose(grad_reduce_weight),
        jnp.transpose(grad_gate_weight),
        grad_expand_bias,
        grad_reduce_bias,
        gains,
        shifts,
    )


def solution(mesh):
    rows = P("wide", "blk", None)
    return jax.shard_map(
        body,
        mesh=mesh,
        in_specs=(rows,) * 3 + (P("wide", "blk"),) * 2 + (P("wide"),) + (P(),) * 12,
        out_specs=(rows,) * 3 + (P("wide", "blk"),) * 7 + (P(),) * 5,
        check_vma=False,
    )
```

```python
import functools
from typing import NamedTuple

import jax
import jax.numpy as jnp
from jax import lax
from jax.experimental import pallas as pl
from jax.experimental.pallas import tpu as pltpu
from jax.sharding import PartitionSpec as P

D = 768
H = 12
HD = 64
FF = 3072
PAGE = 128
DOCS = 2
ROWS = DOCS * PAGE
QUAD = 256
QUADS = D // QUAD
PAIR = 128
IMAGE = 112
EXTRA = 16
SUMS = 24
LONGEST = 1024
EPSILON = 1e-05
NEGATIVE = -1e30
HIGHEST = lax.Precision.HIGHEST
BF16 = jnp.bfloat16
F32 = jnp.float32
VMEM_LIMIT = 62 * 1024 * 1024


def product(left, right):
    return jnp.dot(left, right, preferred_element_type=F32)


def against(left, right, precision=None):
    return lax.dot_general(
        left, right, (((1,), (1,)), ((), ())), preferred_element_type=F32, precision=precision
    )


def transposed(left, right, precision=None):
    return lax.dot_general(
        left, right, (((0,), (0,)), ((), ())), preferred_element_type=F32, precision=precision
    )


def standardize(values):
    centred = values - jnp.mean(values, axis=-1, keepdims=True)
    inverse = lax.rsqrt(jnp.mean(centred * centred, axis=-1, keepdims=True) + EPSILON)
    return centred * inverse, inverse


def norm_back(upstream, scaled, inverse, gains):
    weighted = upstream * gains
    return inverse * (
        weighted
        - jnp.mean(weighted, axis=-1, keepdims=True)
        - scaled * jnp.mean(weighted * scaled, axis=-1, keepdims=True)
    )


def column_sum(values):
    return jnp.sum(values, axis=0, keepdims=True)


def normalize_page(page, index, gain, shift, normed):
    rows = page.shape[0]
    scaled, _ = standardize(page[...].astype(F32))
    normed[index * rows : (index + 1) * rows, :] = (scaled * gain + shift).astype(BF16)


def normalize_pages(pages, gain, shift, normed):
    for index in range(pages.shape[0]):
        normalize_page(pages.at[index], index, gain, shift, normed)


def lane_index(rows):
    return lax.broadcasted_iota(jnp.int32, (rows, PAIR), 1)


def side_masks(rows):
    lanes = lane_index(rows)
    return [(lanes < HD).astype(BF16), (lanes >= HD).astype(BF16)]


def attend_forward(q_ref, k_ref, v_ref, closed_ref, out_ref, lse_ref):
    lanes = lane_index(ROWS)
    masks = side_masks(ROWS)
    first_lane = (lanes == 0).astype(BF16)
    stats = jnp.zeros((ROWS, PAIR), F32)
    for pair in range(QUAD // PAIR):
        cols = slice(pair * PAIR, (pair + 1) * PAIR)
        keys = jnp.concatenate([k_ref[:, cols], closed_ref[...]], axis=1)
        values = v_ref[:, cols]
        queries = q_ref[:, cols]
        results = []
        for side in range(2):
            query = jnp.concatenate([queries * masks[side], first_lane], axis=1)
            scores = against(query, keys)
            top = jnp.max(scores, axis=1, keepdims=True)
            weights = jnp.exp(scores - top)
            total = jnp.sum(weights, axis=1, keepdims=True)
            results.append(product(weights.astype(BF16), values) / total)
            stats = jnp.where(lanes == pair * 2 + side, top + jnp.log(total), stats)
        out_ref[:, cols] = jnp.where(lanes < HD, results[0], results[1])
    lse_ref[...] = jnp.transpose(stats)[:8, :]


def attend_backward(q_ref, k_ref, v_ref, do_ref, lse_ref, delta_ref, closed_ref, dq_ref, dkv_ref, hook):
    lanes = lane_index(ROWS)
    masks = side_masks(ROWS)
    first_lane = (lanes == 0).astype(BF16)
    for pair in range(QUAD // PAIR):
        cols = slice(pair * PAIR, (pair + 1) * PAIR)
        key_part = k_ref[:, cols]
        keys = jnp.concatenate([key_part, closed_ref[...]], axis=1)
        values = v_ref[:, cols]
        dq_parts = []
        dk = None
        dv = None
        for side in range(2):
            row = pair * 2 + side
            query = q_ref[:, cols] * masks[side]
            grad_out = do_ref[:, cols] * masks[side]
            scores = against(keys, jnp.concatenate([query, first_lane], axis=1))
            weights = jnp.exp(scores - lse_ref[row : row + 1, :])
            grad_weights = against(values, grad_out)
            grad_scores = (weights * (grad_weights - delta_ref[row : row + 1, :])).astype(BF16)
            dv_part = product(weights.astype(BF16), grad_out)
            dk_part = product(grad_scores, query)
            dv = dv_part if dv is None else dv + dv_part
            dk = dk_part if dk is None else dk + dk_part
            dq_parts.append(transposed(grad_scores, key_part))
        dq_ref[:, cols] = (jnp.where(lanes < HD, dq_parts[0], dq_parts[1]) * HD ** (-0.5)).astype(
            BF16
        )
        dkv_ref[:, cols] = dk.astype(BF16)
        dkv_ref[:, QUAD + pair * PAIR : QUAD + (pair + 1) * PAIR] = dv.astype(BF16)
        if pair == 0:
            hook()


def head_sums(values):
    sums = []
    lanes = lane_index(values.shape[0])
    for pair in range(H // 2):
        part = values[:, pair * PAIR : (pair + 1) * PAIR]
        sums.append(jnp.sum(jnp.where(lanes < HD, part, 0.0), axis=1, keepdims=True))
        sums.append(jnp.sum(jnp.where(lanes >= HD, part, 0.0), axis=1, keepdims=True))
    return sums


def head_rows(sums):
    lanes = lane_index(ROWS)
    stats = jnp.zeros((ROWS, PAIR), F32)
    for head, value in enumerate(sums):
        stats = jnp.where(lanes == (head // 4) * 8 + head % 4, value, stats)
    return jnp.transpose(stats)[: 8 * QUADS, :]


def spread_heads(gates):
    lanes = lane_index(gates.shape[0])
    parts = []
    for pair in range(H // 2):
        parts.append(
            jnp.where(lanes < HD, gates[:, 2 * pair : 2 * pair + 1], gates[:, 2 * pair + 1 : 2 * pair + 2])
        )
    return jnp.concatenate(parts, axis=1)


def put_rows(out, start, value):
    rows, lanes = out.shape[-2:]
    cuts = (value.shape[1] // lanes).bit_length() - 1
    lead = len(out.shape) - 2
    low = start
    while low < start + value.shape[0]:
        tile = low // rows
        high = min(start + value.shape[0], (tile + 1) * rows)
        for cut in range(1 << cuts):
            piece = value[low - start : high - start, cut * lanes : (cut + 1) * lanes]
            at = bits_of(cut, cuts) + bits_of(tile, lead - cuts)
            out[at + (slice(low - tile * rows, high - tile * rows), slice(None))] = piece
        low = high


class Gather:
    def __init__(self, places, names, packed, landed, waits):
        self.places = places
        self.names = names
        self.packed = packed
        self.landed = landed
        self.sends, self.receives = waits

    @staticmethod
    def waits(names):
        count = DOCS << len(names)
        return [pltpu.SemaphoreType.DMA((count,))] * 2

    def swap(self, turn):
        doc = self.places.turn if turn == 0 else 1 - self.places.turn
        return remote(
            self.packed.at[doc], self.landed.at[turn], self.sends.at[turn], self.receives.at[turn],
            self.places.swap(turn),
        )

    def start(self):
        stays = self.places.swap_stays()
        pl.when(jnp.logical_not(stays))(lambda: self.swap(0).start())
        self.swap(1).start()

        @pl.when(stays)
        def _():
            self.landed[0] = self.packed[self.places.turn]

    def copy(self, block, turn):
        stage = block.bit_length() - 1
        source = (block - (1 << stage)) * DOCS + turn
        at = block * DOCS + turn
        return remote(
            self.landed.at[source], self.landed.at[at], self.sends.at[at], self.receives.at[at],
            self.places.flip(self.names[stage]),
        )

    def arrive(self, block, turn):
        if block > 0:
            self.copy(block, turn).wait_recv()
        elif turn > 0:
            self.swap(turn).wait_recv()
        else:
            stays = self.places.swap_stays()
            pl.when(jnp.logical_not(stays))(lambda: self.swap(0).wait_recv())
        for stage in range(block.bit_length(), len(self.names)):
            self.copy(block + (1 << stage), turn).start()

    def end(self):
        stays = self.places.swap_stays()
        pl.when(jnp.logical_not(stays))(lambda: self.swap(0).wait_send())
        self.swap(1).wait_send()
        for block in range(1, 1 << len(self.names)):
            for turn in range(DOCS):
                self.copy(block, turn).wait_send()


def closed_rows(is_open):
    row = jnp.where(is_open, 0.0, NEGATIVE)
    wide = jnp.concatenate([row, jnp.zeros((1, D - PAGE), F32)], axis=1)
    return jnp.broadcast_to(wide, (EXTRA, D)).astype(BF16)


def closed_column(rows):
    row = rows[0:1, 0:PAGE].astype(F32)
    turned = jnp.transpose(jnp.broadcast_to(row, (PAGE, PAGE)))
    return jnp.where(lane_index(PAGE) == 0, turned, 0.0).astype(BF16)


def self_forward_kernel(
    wide, blk,
    regions, doc_pages, text_in, image_in, cot_in, mask, gain, shift, wq, wk, wv,
    out, lse, q_out, k_out, v_out, text_out, image_out, cot_out, text_closed, image_closed,
    normed, text_packed, image_packed, text_landed, image_landed, cot_landed,
    text_sends, text_receives, image_sends, image_receives, cot_sends, cot_receives, local,
):
    step = pl.program_id(0)
    places = Places(wide, blk)
    groups = group_bits(blk)
    blocks = 1 << len(groups)
    text = Gather(places, groups, text_packed, text_landed, (text_sends, text_receives))
    image = Gather(places, groups, image_packed, image_landed, (image_sends, image_receives))
    cot = Gather(places, [], cot_in, cot_landed, (cot_sends, cot_receives))
    outward = [
        pltpu.make_async_copy(text_landed.at[:, pl.ds(0, PAGE)], text_out, local.at[0]),
        pltpu.make_async_copy(image_landed.at[:, pl.ds(0, IMAGE)], image_out, local.at[1]),
        pltpu.make_async_copy(cot_landed, cot_out, local.at[2]),
    ]

    @pl.when(step == 0)
    def _():
        offsets = lax.broadcasted_iota(jnp.int32, (1, PAGE), 1)
        for doc in range(DOCS):
            text_packed[doc, 0:PAGE, :] = text_in[doc]
            living = places.b < doc_pages[doc]
            is_open = ((mask[doc : doc + 1, :] > 0) | (offsets == 0)) & living
            text_packed[doc, PAGE : PAGE + EXTRA, :] = closed_rows(is_open)
        greet(places, groups, True)
        text.start()
        for doc in range(DOCS):
            image_packed[doc, 0:IMAGE, :] = image_in[doc, 0:IMAGE, :]
            living = places.b < doc_pages[doc]
            is_open = (offsets < regions[doc, 0]) & living
            image_packed[doc, IMAGE : IMAGE + EXTRA, :] = closed_rows(is_open)
        text.arrive(0, 0)
        text.arrive(0, 1)
        image.start()

        def take(block, turn):
            index = block * DOCS + turn
            page = text_landed.at[index, pl.ds(0, PAGE)]
            normalize_page(page, index, gain[0:1, :], shift[0:1, :], normed)
            text_closed[index * PAGE : (index + 1) * PAGE, :] = closed_column(
                text_landed[index, PAGE : PAGE + EXTRA, :]
            )

        for turn in range(DOCS):
            take(0, turn)
        for block in range(1, blocks):
            for turn in range(DOCS):
                text.arrive(block, turn)
            if block == 1:
                image.arrive(0, 0)
                image.arrive(0, 1)
                cot.start()
            for turn in range(DOCS):
                take(block, turn)

    @pl.when(step == 1)
    def _():
        outward[0].start()
        for block in range(1, blocks // 2):
            for turn in range(DOCS):
                image.arrive(block, turn)

    q_out[...] = (product(normed[0:ROWS, :], wq[...]).astype(BF16) * HD ** (-0.5)).astype(BF16)
    k_out[...] = product(normed[...], wk[...]).astype(BF16)
    v_out[...] = product(normed[...], wv[...]).astype(BF16)
    attend_forward(q_out, k_out, v_out, text_closed, out, lse)

    @pl.when(step == QUADS - 1)
    def _():
        for turn in range(DOCS):
            cot.arrive(0, turn)
        outward[2].start()
        for block in range(max(1, blocks // 2), blocks):
            for turn in range(DOCS):
                image.arrive(block, turn)
        outward[1].start()
        for index in range(blocks * DOCS):
            column = closed_column(image_landed[index, IMAGE : IMAGE + EXTRA, :])
            image_closed[index * IMAGE : (index + 1) * IMAGE, :] = column[0:IMAGE, :]
        for stream in (text, image, cot):
            stream.end()
        for copy in outward:
            copy.wait()


def cross_forward_kernel(
    text, pages, self_out, w_self, w_gate, gain, shift, closed, wq, wk, wv,
    hidden, gate, out, lse, q_out, k_out, v_out,
    normed, cross, gates,
):
    @pl.when(pl.program_id(0) == 0)
    def _():
        normalize_pages(pages, gain[2:3, :], shift[2:3, :], normed)
        branch = product(self_out[...].astype(BF16), w_self[...])
        for index in range(DOCS):
            rows = slice(index * PAGE, (index + 1) * PAGE)
            hidden[rows, :] = text[index].astype(F32) + branch[rows, :]
        scaled, _ = standardize(hidden[...])
        cross[...] = (scaled * gain[1:2, :] + shift[1:2, :]).astype(BF16)
        gates[...] = jnp.zeros_like(gates)
        gates[0:H, :] = w_gate[...]
        gate[...] = jax.nn.sigmoid(against(cross[...], gates[...]))

    q_out[...] = (product(cross[...], wq[...]).astype(BF16) * HD ** (-0.5)).astype(BF16)
    k_out[...] = product(normed[...], wk[...]).astype(BF16)
    v_out[...] = product(normed[...], wv[...]).astype(BF16)
    attend_forward(q_out, k_out, v_out, closed, out, lse)


def expand_part(wide, blk, step):
    few = (slice(None),) * (wide.bit_length() - 2)
    rest = (slice(None),) * (blk.bit_length() - 3)
    return few + (step // 2, step % 2) + rest, (slice(None), slice(None))


def reduce_part(wide, blk, step):
    cuts = wide.bit_length() - 2
    rest = (slice(None),) * (blk.bit_length() - 1)
    if cuts >= 2:
        lead = (step // 2, step % 2) + (slice(None),) * (cuts - 2) + rest
        return lead, (slice(None), slice(None))
    lanes = pl.ds(pl.multiple_of((step % 2) * D, D), D)
    return (step // 2,) + rest, (slice(None), lanes)


def put_expand(out, value, step, wide, blk):
    cuts, bits = wide.bit_length() - 2, blk.bit_length() - 1
    rows, lanes = out.shape[-2:]
    for cut in range(1 << cuts):
        for part in range(D // rows):
            at = bits_of(cut, cuts) + (step // 2, step % 2) + bits_of(part, bits - 1)
            out[at] = value[part * rows : (part + 1) * rows, cut * lanes : (cut + 1) * lanes]


def put_reduce(out, value, step, wide, blk):
    cuts, bits = wide.bit_length() - 2, blk.bit_length() - 1
    rows, lanes = out.shape[-2:]
    for part in range(D // rows):
        place = bits_of(part, bits + 1)
        piece = value[part * rows : (part + 1) * rows, :]
        if cuts >= 2:
            for cut in range(D // lanes):
                at = (step // 2, step % 2) + bits_of(cut, cuts - 2) + place
                out[at] = piece[:, cut * lanes : (cut + 1) * lanes]
        else:
            out[(step // 2,) + place + (slice(None), pl.ds(pl.multiple_of((step % 2) * D, D), D))] = piece


def forward_back_kernel(
    steps, wide, blk,
    hidden, raw, gate, cots, w_out, gain, shift, w_expand, b_expand, w_reduce, b_reduce,
    joined, early_expand, late_expand, early_reduce, late_reduce, d_out, grad_mixed, grad_raw,
    delta, grad_logit, small,
    gated, mixed, final, upstream, joined_sum, back_sum,
    expand_all, reduce_all, expand_got, reduce_got, expand_next, reduce_next,
    sends, receives, next_sends, next_receives, local,
):
    step = pl.program_id(0)
    places = Places(wide, blk)
    core, along, across = ("w", 0), ("w", 1), ("b", 0)
    cuts = wide.bit_length() - 2
    kinds = (
        (expand_part, expand_all, expand_got, expand_next, along),
        (reduce_part, reduce_all, reduce_got, reduce_next, across),
    )

    def copies(at):
        found = []
        for index, (part, grad, got, _, _) in enumerate(kinds):
            lead, tail = part(wide, blk, at)
            found.append(
                remote(
                    grad.at[lead + (1 - places.bit(core),) + tail],
                    got.at[lead + tail],
                    sends.at[index, at],
                    receives.at[index, at],
                    places.flip(core),
                )
            )
        return found

    def add(at):
        for (part, grad, got, _, _), copy in zip(kinds, copies(at)):
            copy.wait_recv()
            lead, tail = part(wide, blk, at)
            add_blocks(got.at[lead + tail], grad.at[lead + (places.bit(core),) + tail])

    def pieces(at):
        (lead, tail), (far_lead, far_tail) = (
            expand_part(wide, blk, at), reduce_part(wide, blk, at)
        )
        bit, far_bit = places.bit(along), places.bit(across)
        head, rest = lead[: cuts - 1], lead[cuts:]
        yield (
            expand_got.at[head + (bit,) + rest + tail],
            expand_got.at[head + (1 - bit,) + rest + tail],
            expand_next.at[head + rest[1:] + tail],
        )
        yield (
            reduce_got.at[far_lead[:-1] + (far_bit,) + far_tail],
            reduce_got.at[far_lead[:-1] + (1 - far_bit,) + far_tail],
            reduce_next.at[far_lead[1:-1] + far_tail],
        )

    def onward(at):
        return [
            remote(
                send, land, next_sends.at[index, at], next_receives.at[index, at],
                places.flip(kinds[index][4]),
            )
            for index, (_, send, land) in enumerate(pieces(at))
        ]

    @pl.when(step == 0)
    def _():
        greet(places, [core, along, across], False)
        upstream[0:PAGE, :] = cots[0]
        upstream[PAGE:ROWS, :] = cots[1]
        small[...] = jnp.zeros_like(small)
        gated[...] = (spread_heads(gate[...]) * raw[...]).astype(BF16)
        rows = hidden[...] + product(gated[...], w_out[...])
        mixed[...] = rows
        scaled, _ = standardize(rows)
        final[...] = (scaled * gain[3:4, :] + shift[3:4, :]).astype(BF16)
        joined_sum[...] = rows + b_reduce[...]
        back_sum[...] = jnp.zeros_like(back_sum)

    inner = product(final[...], w_expand[...]) + b_expand[...]
    squared = inner * inner
    root = (2.0 / jnp.pi) ** 0.5
    curve = jnp.tanh(root * inner * (1.0 + 0.044715 * squared))
    half = 0.5 * (1.0 + curve)
    active = (inner * half).astype(BF16)
    slope = half + 0.5 * inner * (1.0 - curve * curve) * (root * (1.0 + 3.0 * 0.044715 * squared))
    joined_sum[...] += product(active, w_reduce[...])
    grad_active = against(upstream[...], w_reduce[...]).astype(BF16)
    grad_inner = (grad_active.astype(F32) * slope).astype(BF16)
    small[pl.ds(4 + step, 1), :] = column_sum(grad_inner.astype(F32))
    back_sum[...] += against(grad_inner, w_expand[...])
    put_expand(expand_all, transposed(grad_inner, final[...]).astype(BF16), step, wide, blk)
    put_reduce(reduce_all, transposed(upstream[...], active).astype(BF16), step, wide, blk)
    for copy in copies(step):
        copy.start()
    for at in range(steps - 1):

        @pl.when(step == at + 1)
        def _():
            add(at)
            if at < steps // 2:
                for copy in onward(at):
                    copy.start()

    @pl.when(step == steps - 1)
    def _():
        total = joined_sum[...].astype(BF16)
        joined[0] = total[:PAGE]
        joined[1] = total[PAGE:]
        scaled, inverse = standardize(mixed[...])
        back = back_sum[...]
        cotangent = upstream[...].astype(F32)
        grad = cotangent + norm_back(back, scaled, inverse, gain[3:4, :])
        grad_mixed[...] = grad
        branch = grad.astype(BF16)
        put_rows(d_out, 0, transposed(branch, gated[...]).astype(BF16))
        grad_gated = against(branch, w_out[...]).astype(BF16).astype(F32)
        gates = gate[...]
        lanes = lane_index(ROWS)
        logit = jnp.zeros((ROWS, PAIR), F32)
        for head, value in enumerate(head_sums(grad_gated * raw[...])):
            logit = jnp.where(lanes == head, value, logit)
        grad_logit[...] = logit * gates * (1.0 - gates)
        rounded = (spread_heads(gates) * grad_gated).astype(BF16)
        grad_raw[...] = rounded
        delta[...] = head_rows(head_sums(rounded.astype(F32) * raw[...]))
        small[0:1, :] = column_sum(cotangent)
        small[1:2, :] = column_sum(back * scaled)
        small[2:3, :] = column_sum(back)
        add(steps - 1)
        half = (slice(None),) * cuts
        moves = [
            pltpu.make_async_copy(expand_got.at[half + (1,)], late_expand, local.at[0]),
            pltpu.make_async_copy(reduce_got.at[1], late_reduce, local.at[1]),
        ]
        for move in moves:
            move.start()
        for at in range(steps // 2):
            for copy, (kept, _, land) in zip(onward(at), pieces(at)):
                copy.wait()
                add_blocks(land, kept)
        moves += [
            pltpu.make_async_copy(expand_next, early_expand, local.at[2]),
            pltpu.make_async_copy(reduce_next, early_reduce, local.at[3]),
        ]
        for move in moves[2:]:
            move.start()
        for at in range(steps):
            for copy in copies(at):
                copy.wait_send()
        for move in moves:
            move.wait()


def spread_back(dkv, wk, wv, dx):
    weights = jnp.concatenate([wk[...], wv[...]], axis=1)

    size = dx.shape[0] // 4

    def chunk(index, carry):
        rows = pl.ds(pl.multiple_of(index * size, 16), size)
        dx[rows, :] += against(dkv[rows, :], weights)
        return carry

    lax.fori_loop(0, 4, chunk, 0)


def finish_pages(pages, dx, keep, send):
    gain_sum = jnp.zeros((1, D), F32)
    shift_sum = jnp.zeros((1, D), F32)
    count, size, _ = pages.shape
    half = count // 2
    for index in range(count):
        scaled, _ = standardize(pages[index].astype(F32))
        part = dx[index * size : (index + 1) * size, :]
        gain_sum += column_sum(part * scaled)
        shift_sum += column_sum(part)
        target = keep if index < half else send
        place = index % half
        target[place * size : (place + 1) * size, :] = part.astype(BF16)
    return gain_sum, shift_sum


END = 99


def moves_of(plan, jobs):
    done = [-1] * len(jobs)
    moves = {}
    for point in sorted(plan):
        moves[point] = []
        for index in plan[point]:
            moves[point].append((index, done[index]))
            done[index] += 1
    moves[END] = [
        (index, stage)
        for stage in range(-1, max(len(job.order) for job in jobs))
        for index, job in enumerate(jobs)
        if done[index] <= stage < len(job.order)
    ]
    return moves


def run_moves(moves, point, scatters):
    for index, stage in moves.get(point, ()):
        if stage < 0:
            scatters[index].start()
        else:
            scatters[index].add(stage)


def back_kernel(wide, blk, jobs, plan, *refs):
    refs = iter(refs)
    (
        images, image_own, texts, gain, shift, cross_closed, self_closed,
        q_cross, k_cross, v_cross, do_cross, lse_cross, delta_cross, wk_cross, wv_cross,
        q_self, k_self, v_self, lse_self, wq_self, wk_self, wv_self,
        w_query, w_gate, w_self, hidden, self_out, grad_mixed, grad_logit, joined, last_small,
    ) = (next(refs) for _ in range(31))
    early_expand, late_expand, early_reduce, late_reduce, d_cross_output = (
        next(refs) for _ in range(5)
    )
    joined_out, text_out, image_out, sums_out, last_out = (next(refs) for _ in range(5))
    outs = [next(refs) if job.ends else None for job in jobs]
    normed, dkv, dx, dq, gates, grad_hidden, self_do, self_delta = (next(refs) for _ in range(8))
    pages, keep, send, row_sums, sums_in, local = (next(refs) for _ in range(6))
    d_pairs, d_query, d_self_output, d_project, expand_both, reduce_both = (
        next(refs) for _ in range(6)
    )
    sources = [
        early_expand, late_expand, early_reduce, late_reduce, expand_both, reduce_both,
        d_pairs, d_query, d_cross_output, d_self_output,
    ] + [d_project] * (len(jobs) - 10)
    lands = [expand_both.at[0], expand_both.at[1], reduce_both.at[0], reduce_both.at[1]]
    lands += [None] * (len(jobs) - 4)
    step = pl.program_id(0)
    places = Places(wide, blk)
    names = bit_names(wide, blk)
    groups = group_bits(blk)
    scatters = [
        Scatter(places, job, source, refs, last)
        for job, source, last in zip(jobs, sources, lands)
    ]
    moves = moves_of(plan, jobs)
    home = Home(places, refs)
    image_rows = pl.ds(0, k_cross.shape[0] // 2)
    image = Rows(
        places, groups, keep.at[image_rows], send.at[image_rows], row_sums.at[image_rows], refs
    )
    text = Rows(places, groups, keep, send, row_sums, refs)
    image_pages = pages.at[:, pl.ds(0, IMAGE)]
    fetches = [
        pltpu.make_async_copy(images, image_pages, local.at[0]),
        pltpu.make_async_copy(texts, pages, local.at[1]),
        pltpu.make_async_copy(grad_mixed, grad_hidden, local.at[2]),
        pltpu.make_async_copy(w_self, normed.at[pl.ds(0, D)], local.at[3]),
    ]
    sums = Total(places, names, refs)
    last_sums = Total(places, names, refs)

    def pump(point):
        if 7 <= point <= 11:
            sums.add(point - 7, sums_out)
        if point == 7:
            image.add(0)
        if point == 10:
            for stage in range(1, len(groups)):
                image.add(stage)
            image.norm(image_own, gain[2:3, :], None)
        run_moves(moves, point, scatters)

    def pumps(points):
        for point in points:
            pl.when(step == (point - 1) // 2)(functools.partial(pump, point))

    @pl.when(step == 0)
    def _():
        fetches[0].start()
        fetches[2].start()
        greet(places, names, True)
        pump(0)
        for turn in range(DOCS):
            home.put(turn, joined[turn])

    @pl.when(step < QUADS)
    def _():
        keys = k_cross.shape[0]
        rows = pl.ds(0, keys)
        my_normed, my_dkv, my_dx = normed.at[rows], dkv.at[rows], dx.at[rows]

        @pl.when(step == 0)
        def _():
            fetches[0].wait()
            normalize_pages(image_pages, gain[2:3, :], shift[2:3, :], my_normed)
            my_dx[...] = jnp.zeros(my_dx.shape, F32)

        cols = pl.ds(pl.multiple_of(step * QUAD, QUAD), QUAD)
        attend_backward(
            q_cross, k_cross, v_cross, do_cross, lse_cross, delta_cross, cross_closed,
            dq.at[:, cols], my_dkv, lambda: pumps((1, 3, 5)),
        )
        spread_back(my_dkv, wk_cross, wv_cross, my_dx)
        for part in range(2):
            value = transposed(my_dkv[:, part * QUAD : (part + 1) * QUAD], my_normed[...])
            value = value.astype(BF16)
            for at in range(QUADS):

                @pl.when(step == at)
                def _():
                    put_rows(d_pairs, part * D + at * QUAD, value)

        pumps((2, 4))

        @pl.when(step == QUADS - 1)
        def _():
            image_gain, image_shift = finish_pages(
                image_pages, my_dx, image.keep, image.send
            )
            fetches[1].start()
            fetches[3].start()
            image.start()
            scaled, inverse = standardize(hidden[...])
            cross = (scaled * gain[1:2, :] + shift[1:2, :]).astype(BF16)
            grad_query = dq[...]
            put_rows(d_query, 0, transposed(grad_query, cross).astype(BF16))
            d_gate = transposed(grad_logit[...], cross.astype(F32), HIGHEST)[:H, :]
            gates[...] = jnp.zeros_like(gates)
            gates[0:H, :] = w_gate[...]
            upstream = against(grad_query, w_query[...]) + jnp.dot(
                grad_logit[...], gates[...].astype(F32), precision=HIGHEST
            )
            fetches[2].wait()
            grad = grad_hidden[...] + norm_back(upstream, scaled, inverse, gain[1:2, :])
            grad_hidden[...] = grad
            branch = grad.astype(BF16)
            put_rows(
                d_self_output, 0, transposed(branch, self_out[...].astype(BF16)).astype(BF16)
            )
            fetches[3].wait()
            grad_result = against(branch, normed[0:D, :]).astype(BF16)
            self_do[...] = grad_result
            self_delta[...] = head_rows(head_sums(grad_result.astype(F32) * self_out[...]))
            sums_in[0:H, :] = d_gate
            sums_in[H : H + 8, :] = last_small[...]
            sums_in[H + 8 : SUMS, :] = jnp.concatenate(
                [column_sum(upstream * scaled), column_sum(upstream), image_gain, image_shift],
                axis=0,
            )
            sums.start(sums_in[...])
            home.end(joined_out)
            pump(6)
            fetches[1].wait()
            normalize_pages(pages, gain[0:1, :], shift[0:1, :], normed)
            dx[...] = jnp.zeros(dx.shape, F32)

    @pl.when(step >= QUADS)
    def _():
        quad = step - QUADS
        cols = pl.ds(pl.multiple_of(quad * QUAD, QUAD), QUAD)
        my_dq = dq.at[:, cols]
        attend_backward(
            q_self, k_self, v_self, self_do.at[:, cols], lse_self,
            self_delta.at[pl.ds(pl.multiple_of(quad * 8, 8), 8)], self_closed,
            my_dq, dkv, lambda: pumps((7, 9, 11)),
        )
        spread_back(dkv, wk_self, wv_self, dx)
        dx[0:ROWS, :] += against(my_dq[...], wq_self[...])
        for part in range(3):
            if part == 0:
                value = transposed(my_dq[...], normed[0:ROWS, :])
            else:
                value = transposed(dkv[:, (part - 1) * QUAD : part * QUAD], normed[...])
            value = value.astype(BF16)
            for at in range(QUADS):

                @pl.when(quad == at)
                def _():
                    put_rows(d_project, part * D + at * QUAD, value)

        pumps((8, 10))

        @pl.when(quad == QUADS - 1)
        def _():
            gain_sum, shift_sum = finish_pages(pages, dx, keep, send)
            text.start()
            run_moves(moves, 12, scatters)
            last_sums.start(jnp.concatenate([gain_sum, shift_sum, jnp.zeros((6, D), F32)], axis=0))
            for stage in range(5, len(names)):
                sums.add(stage, sums_out)
            run_moves(moves, 13, scatters)
            for stage in range(len(groups) - 1):
                text.add(stage)
            run_moves(moves, 14, scatters)
            last_sums.add(0, last_out)
            run_moves(moves, 15, scatters)
            text.add(len(groups) - 1)
            text.norm(pages, gain[0:1, :], grad_hidden)
            for stage in range(1, len(names)):
                last_sums.add(stage, last_out)
                run_moves(moves, 15 + stage, scatters)
            image.end(image_out)
            text.end(text_out)
            run_moves(moves, END, scatters)
            for scatter, out in zip(scatters, outs):
                scatter.end(out)


class Places:
    def __init__(self, wide, blk):
        self.wide = wide
        self.blk = blk
        self.part = blk // 4
        self.w = lax.axis_index("wide")
        self.b = lax.axis_index("blk")
        self.quarter = self.b // self.part
        self.turn = self.quarter % 2

    def bit(self, name):
        axis, bit = name
        return ((self.w if axis == "w" else self.b) // (1 << bit)) % 2

    def flip(self, name):
        axis, bit = name
        step = (1 << bit) * (1 - 2 * self.bit(name))
        return (self.w + step, self.b) if axis == "w" else (self.w, self.b + step)

    def swap(self, turn):
        core = self.w % 2
        turned = self.turn if turn == 0 else 1 - self.turn
        return (
            self.w - core + self.quarter // 2,
            (2 * core + turned) * self.part + self.b % self.part,
        )

    def swap_stays(self):
        return self.w % 2 == self.quarter // 2


def bit_names(wide, blk):
    return [("w", bit) for bit in range(wide.bit_length() - 1)] + [
        ("b", bit) for bit in range(blk.bit_length() - 1)
    ]


def group_bits(blk):
    return [("b", bit) for bit in range((blk // 4).bit_length() - 1)] + [("w", 0)]


def tile_bits(wide, blk):
    return (
        [("w", bit) for bit in range(wide.bit_length() - 2, 0, -1)]
        + [("b", bit) for bit in range(blk.bit_length() - 2, -1, -1)]
        + [("w", 0)]
    )


def remote(source, target, send, receive, device):
    return pltpu.make_async_remote_copy(
        src_ref=source,
        dst_ref=target,
        send_sem=send,
        recv_sem=receive,
        device_id=device,
        device_id_type=pl.DeviceIdType.MESH,
    )


def greet(places, names, swaps):
    barrier = pltpu.get_barrier_semaphore()
    for name in names:
        pl.semaphore_signal(
            barrier, inc=1, device_id=places.flip(name), device_id_type=pl.DeviceIdType.MESH
        )
    count = len(names)
    if swaps:
        pl.semaphore_signal(
            barrier, inc=1, device_id=places.swap(1), device_id_type=pl.DeviceIdType.MESH
        )

        @pl.when(jnp.logical_not(places.swap_stays()))
        def _():
            pl.semaphore_signal(
                barrier, inc=1, device_id=places.swap(0), device_id_type=pl.DeviceIdType.MESH
            )

        count = count + 2 - places.swap_stays().astype(jnp.int32)
    pl.semaphore_wait(barrier, count)


class Job(NamedTuple):
    left: tuple
    order: tuple
    start: int
    rows: int
    lanes: int
    ends: bool
    near: bool = False
    inner: bool = False

    def after(self):
        return tuple(name for name in self.left if name not in self.order)

    def scratch(self):
        count = len(self.left)
        kinds = []
        if not self.near:
            kinds.append(pltpu.VMEM((2,) * (count - 1) + (self.rows, self.lanes), BF16))
        for stage in range(len(self.order) - int(self.inner)):
            kinds.append(pltpu.VMEM((2,) * (count - 1 - stage) + (self.rows, self.lanes), BF16))
        if self.ends:
            kinds.append(pltpu.VMEM((2, self.rows, self.lanes // 2), BF16))
        waits = len(self.order) + int(self.ends)
        return kinds + [pltpu.SemaphoreType.DMA((waits,))] * 2 + [pltpu.SemaphoreType.DMA]

    def result(self):
        return shaped((2, self.rows, self.lanes // 2), BF16)


def bits_of(index, count):
    return tuple((index // (1 << (count - 1 - place))) % 2 for place in range(count))


def add_blocks(target, source):
    lead = len(target.shape) - 2
    if lead == 0:
        target[...] = target[...] + source[...]
        return

    def block(index, carry):
        at = bits_of(index, lead)
        target[at] = target[at] + source[at]
        return carry

    lax.fori_loop(0, 1 << lead, block, 0)


class Scatter:
    def __init__(self, places, job, source, scratch, last=None):
        self.places = places
        self.job = job
        self.source = source
        self.own = None if job.near else next(scratch)
        self.got = [next(scratch) for _ in range(len(job.order) - int(job.inner))]
        if job.inner:
            self.got.append(last)
        self.ends = next(scratch) if job.ends else None
        self.sends, self.receives, self.local = next(scratch), next(scratch), next(scratch)
        self.stages = len(job.order)
        self.axes = []
        left = list(job.left)
        for name in job.order:
            self.axes.append(left.index(name))
            left.remove(name)

    def cut(self, ref, stage, index):
        axis = self.axes[stage]
        at = (slice(None),) * axis + (index,)
        if ref.shape[-2] != self.job.rows:
            at += (slice(None),) * (len(ref.shape) - 3 - axis)
            at += (pl.ds(self.job.start, self.job.rows), slice(None))
        return ref.at[at]

    def copy(self, stage):
        if stage == self.stages:
            source, target, name = self.ends.at[0], self.ends.at[1], ("w", 0)
        else:
            name = self.job.order[stage]
            source = self.source if stage == 0 else self.got[stage - 1]
            source = self.cut(source, stage, 1 - self.places.bit(name))
            target = self.got[stage]
        return remote(
            source, target, self.sends.at[stage], self.receives.at[stage], self.places.flip(name)
        )

    def fetch(self):
        kept = self.cut(self.source, 0, self.places.bit(self.job.order[0]))
        return pltpu.make_async_copy(kept, self.own, self.local)

    def start(self):
        self.copy(0).start()
        if not self.job.near:
            self.fetch().start()

    def halve(self):
        lanes = self.job.lanes // 2
        piece = self.got[-1][...]
        second = self.places.bit(("w", 0)) == 1
        self.ends[0] = jnp.where(second, piece[:, :lanes], piece[:, lanes:])

    def add(self, stage):
        self.copy(stage).wait_recv()
        if stage == 0 and not self.job.near:
            self.fetch().wait()
            source = self.own
        else:
            bit = self.places.bit(self.job.order[stage])
            source = self.cut(self.source if stage == 0 else self.got[stage - 1], stage, bit)
        add_blocks(self.got[stage], source)
        if stage + 1 < self.stages:
            self.copy(stage + 1).start()
        elif self.job.ends:
            self.halve()
            self.copy(stage + 1).start()

    def end(self, out):
        for stage in range(self.stages + int(self.job.ends)):
            self.copy(stage).wait_send()
        if not self.job.ends:
            return
        self.copy(self.stages).wait_recv()
        lanes = self.job.lanes // 2
        piece = self.got[-1][...]
        other = self.ends[1]
        second = self.places.bit(("w", 0)) == 1
        mine = jnp.where(second, piece[:, lanes:], piece[:, :lanes])
        out[0] = jnp.where(second, other, mine)
        out[1] = jnp.where(second, mine, other)


class Home:
    def __init__(self, places, scratch):
        self.places = places
        self.home, self.landed, self.sends, self.receives, self.local = (
            next(scratch) for _ in range(5)
        )

    @staticmethod
    def scratch():
        waits = [pltpu.SemaphoreType.DMA((DOCS,))] * 2 + [pltpu.SemaphoreType.DMA]
        return [pltpu.VMEM((DOCS, PAGE, D), BF16)] * 2 + waits

    def copy(self, turn):
        return remote(
            self.home.at[turn], self.landed.at[self.places.turn], self.sends.at[turn],
            self.receives.at[turn], self.places.swap(turn),
        )

    def go(self, turn, begin):
        def carry():
            if begin:
                self.copy(turn).start()
            else:
                self.copy(turn).wait()

        if turn > 0:
            carry()
            return
        stays = self.places.swap_stays()
        pl.when(jnp.logical_not(stays))(carry)
        if begin:

            @pl.when(stays)
            def _():
                self.landed[self.places.turn] = self.home[turn]

    def put(self, turn, page):
        self.home[turn] = page
        self.go(turn, True)

    def end(self, out):
        for turn in range(DOCS):
            self.go(turn, False)
        copy = pltpu.make_async_copy(self.landed, out, self.local)
        copy.start()
        copy.wait()


class Rows:
    def __init__(self, places, names, keep, send, sums, scratch):
        self.places = places
        self.size = keep.shape[0] // (DOCS << (len(names) - 1))
        self.names = list(reversed(names))
        self.keep = keep
        self.send = send
        self.sums = sums
        self.got = [next(scratch) for _ in names]
        self.sends, self.receives = next(scratch), next(scratch)
        self.back = Home(places, scratch)

    @staticmethod
    def scratch(names, rows):
        kinds = [pltpu.VMEM((rows >> stage, D), BF16) for stage in range(len(names))]
        return kinds + [pltpu.SemaphoreType.DMA((len(names),))] * 2 + Home.scratch()

    def copy(self, stage):
        source = self.send if stage == 0 else self.sums
        rows = self.got[stage].shape[0]
        if stage > 0:
            source = source.at[pl.ds(rows, rows)]
        return remote(
            source, self.got[stage], self.sends.at[stage], self.receives.at[stage],
            self.places.flip(self.names[stage]),
        )

    def start(self):
        self.copy(0).start()

    def add(self, stage):
        self.copy(stage).wait()
        source = self.keep if stage == 0 else self.sums
        rows = self.got[stage].shape[0]

        def block(index, carry):
            at = pl.ds(pl.multiple_of(index * self.size, 16), self.size)
            self.sums[at, :] = source[at, :] + self.got[stage][at, :]
            return carry

        lax.fori_loop(0, rows // self.size, block, 0)
        if stage + 1 < len(self.names):
            self.copy(stage + 1).start()

    def norm(self, pages, gain, added):
        for turn in range(DOCS):
            rows = slice(turn * self.size, (turn + 1) * self.size)
            scaled, inverse = standardize(pages[turn].astype(F32))
            grad = norm_back(self.sums[rows, :].astype(F32), scaled, inverse, gain)
            if added is not None:
                grad = grad + added[rows, :]
            if self.size < PAGE:
                rest = jnp.zeros((PAGE - self.size, D), F32)
                grad = jnp.concatenate([grad, rest], axis=0)
            self.back.put(turn, grad.astype(BF16))

    def end(self, out):
        self.back.end(out)


class Total:
    def __init__(self, places, names, scratch):
        self.places = places
        self.names = names
        self.mine, self.got, self.sends, self.receives = (next(scratch) for _ in range(4))

    @staticmethod
    def scratch(names, rows):
        count = len(names)
        return [pltpu.VMEM((count, rows, D), F32)] * 2 + [pltpu.SemaphoreType.DMA((count,))] * 2

    def copy(self, stage):
        return remote(
            self.mine.at[stage], self.got.at[stage], self.sends.at[stage], self.receives.at[stage],
            self.places.flip(self.names[stage]),
        )

    def start(self, value):
        self.mine[0] = value
        self.copy(0).start()

    def add(self, stage, out):
        self.copy(stage).wait()
        value = self.mine[stage] + self.got[stage]
        if stage + 1 < len(self.names):
            self.mine[stage + 1] = value
            self.copy(stage + 1).start()
        else:
            out[...] = value


def finish_kernel(layout, *refs):
    refs = iter(refs)
    pieces = [[next(refs) for _ in range(count)] for count in layout]
    streams = [next(refs) for _ in range(3)]
    sums, last_sums = next(refs), next(refs)
    for index, parts in enumerate(pieces):
        out = next(refs)
        halves = [part[half] for half in range(2) for part in parts]
        value = jnp.concatenate(halves, axis=0).astype(F32)
        out[...] = value if index + 1 == len(pieces) else jnp.transpose(value)
    for stream in streams:
        out = next(refs)
        out[...] = stream[...]
    gate, bias, last, gains, shifts = (next(refs) for _ in range(5))
    gate[...] = sums[0:H, :]
    for index in range(FF // D):
        bias[pl.ds(index * D, D)] = sums[H + 4 + index, :]
    last[...] = sums[H, :]
    for out, at in ((gains, 0), (shifts, 1)):
        out[0:1, :] = last_sums[at : at + 1, :]
        for index, row in enumerate((H + 8 + at, H + 10 + at, H + 1 + at)):
            out[index + 1 : index + 2, :] = sums[row : row + 1, :]


def whole(shape):
    return pl.BlockSpec(shape, lambda step: (0,) * len(shape))


def columns(rows, offset=0):
    return pl.BlockSpec((rows, QUAD), lambda step: (0, offset + step))


def stat_rows():
    return pl.BlockSpec((8, ROWS), lambda step: (step, 0))


def shaped(shape, kind):
    return jax.ShapeDtypeStruct(shape, kind)


ANY = pl.BlockSpec(memory_space=pl.ANY)


def call(kernel, name, steps, ins, outs, scratch, flops, byte_count, collective=None):
    in_specs, operands = zip(*ins)
    out_specs, out_shapes = zip(*outs)
    return pl.pallas_call(
        kernel,
        grid=(steps,),
        in_specs=list(in_specs),
        out_specs=list(out_specs),
        out_shape=list(out_shapes),
        scratch_shapes=scratch,
        name=name,
        compiler_params=pltpu.CompilerParams(
            vmem_limit_bytes=VMEM_LIMIT,
            collective_id=collective,
            has_side_effects=collective is not None,
        ),
        cost_estimate=pl.CostEstimate(flops=flops, bytes_accessed=byte_count, transcendentals=0),
    )(*operands)


def own_pages(pages):
    return (whole((DOCS, *pages.shape[1:])), pages)


SMEM = pl.BlockSpec(memory_space=pltpu.SMEM)


def self_forward(texts, images, cots, mask, regions, doc_pages, gain, shift, project, wide, blk):
    groups = group_bits(blk)
    count = DOCS << len(groups)
    keys = count * PAGE
    return call(
        functools.partial(self_forward_kernel, wide, blk),
        "self_forward",
        QUADS,
        [
            (SMEM, regions),
            (SMEM, doc_pages),
            (whole(texts.shape), texts),
            (whole(images.shape), images),
            (whole(cots.shape), cots),
            (whole(mask.shape), mask),
            (whole(gain.shape), gain),
            (whole(shift.shape), shift),
            (columns(D), project),
            (columns(D, QUADS), project),
            (columns(D, 2 * QUADS), project),
        ],
        [
            (columns(ROWS), shaped((ROWS, D), F32)),
            (stat_rows(), shaped((8 * QUADS, ROWS), F32)),
            (columns(ROWS), shaped((ROWS, D), BF16)),
            (columns(keys), shaped((keys, D), BF16)),
            (columns(keys), shaped((keys, D), BF16)),
            (ANY, shaped((count, PAGE, D), BF16)),
            (ANY, shaped((count, IMAGE, D), BF16)),
            (ANY, shaped((DOCS, PAGE, D), BF16)),
            (whole((keys, PAIR)), shaped((keys, PAIR), BF16)),
            (whole((count * IMAGE, PAIR)), shaped((count * IMAGE, PAIR), BF16)),
        ],
        [
            pltpu.VMEM((keys, D), BF16),
            pltpu.VMEM((DOCS, PAGE + EXTRA, D), BF16),
            pltpu.VMEM((DOCS, IMAGE + EXTRA, D), BF16),
            pltpu.VMEM((count, PAGE + EXTRA, D), BF16),
            pltpu.VMEM((count, IMAGE + EXTRA, D), BF16),
            pltpu.VMEM((DOCS, PAGE, D), BF16),
        ]
        + Gather.waits(groups) * 2
        + Gather.waits([])
        + [pltpu.SemaphoreType.DMA((3,))],
        6 * 10**9,
        12 * 10**6,
        0,
    )


def cross_forward(texts, pages, self_out, w_self, w_gate, gain, shift, closed, w_query, w_pairs):
    keys = closed.shape[0]
    return call(
        cross_forward_kernel,
        "cross_forward",
        QUADS,
        [
            own_pages(texts),
            (whole(pages.shape), pages),
            (whole(self_out.shape), self_out),
            (whole(w_self.shape), w_self),
            (whole(w_gate.shape), w_gate),
            (whole(gain.shape), gain),
            (whole(shift.shape), shift),
            (whole(closed.shape), closed),
            (columns(D), w_query),
            (columns(D), w_pairs),
            (columns(D, QUADS), w_pairs),
        ],
        [
            (whole((ROWS, D)), shaped((ROWS, D), F32)),
            (whole((ROWS, PAIR)), shaped((ROWS, PAIR), F32)),
            (columns(ROWS), shaped((ROWS, D), F32)),
            (stat_rows(), shaped((8 * QUADS, ROWS), F32)),
            (columns(ROWS), shaped((ROWS, D), BF16)),
            (columns(keys), shaped((keys, D), BF16)),
            (columns(keys), shaped((keys, D), BF16)),
        ],
        [
            pltpu.VMEM((keys, D), BF16),
            pltpu.VMEM((ROWS, D), BF16),
            pltpu.VMEM((PAIR, D), BF16),
        ],
        7 * 10**9,
        14 * 10**6,
    )


def forward_back(
    hidden, raw, gate, cots, w_out, gain, shift, w_expand, b_expand, w_reduce, b_reduce, wide, blk
):
    steps = FF // D
    names = tile_bits(wide, blk)
    small = (D // (2 * blk), D // (wide // 2))
    expand = (FF // (2 * blk), D // (wide // 2))
    reduce = (D // (2 * blk), FF // (wide // 2))
    full, part, half, less = ((2,) * (len(names) - gone) for gone in range(4))
    return call(
        functools.partial(forward_back_kernel, steps, wide, blk),
        "forward_back",
        steps,
        [
            (whole((ROWS, D)), hidden),
            (whole((ROWS, D)), raw),
            (whole((ROWS, PAIR)), gate),
            (whole((DOCS, PAGE, D)), cots),
            (whole((D, D)), w_out),
            (whole(gain.shape), gain),
            (whole(shift.shape), shift),
            (pl.BlockSpec((D, D), lambda step: (0, step)), w_expand),
            (pl.BlockSpec((1, D), lambda step: (0, step)), b_expand),
            (pl.BlockSpec((D, D), lambda step: (step, 0)), w_reduce),
            (whole((1, D)), b_reduce),
        ],
        [
            (whole((DOCS, PAGE, D)), shaped((DOCS, PAGE, D), BF16)),
            (ANY, shaped(less + expand, BF16)),
            (ANY, shaped(half + expand, BF16)),
            (ANY, shaped(less + reduce, BF16)),
            (ANY, shaped(half + reduce, BF16)),
            (whole(full + small), shaped(full + small, BF16)),
            (whole((ROWS, D)), shaped((ROWS, D), F32)),
            (whole((ROWS, D)), shaped((ROWS, D), BF16)),
            (whole((8 * QUADS, ROWS)), shaped((8 * QUADS, ROWS), F32)),
            (whole((ROWS, PAIR)), shaped((ROWS, PAIR), F32)),
            (whole((8, D)), shaped((8, D), F32)),
        ],
        [
            pltpu.VMEM((ROWS, D), BF16),
            pltpu.VMEM((ROWS, D), F32),
            pltpu.VMEM((ROWS, D), BF16),
            pltpu.VMEM((ROWS, D), BF16),
            pltpu.VMEM((ROWS, D), F32),
            pltpu.VMEM((ROWS, D), F32),
            pltpu.VMEM(full + expand, BF16),
            pltpu.VMEM(full + reduce, BF16),
            pltpu.VMEM(part + expand, BF16),
            pltpu.VMEM(part + reduce, BF16),
            pltpu.VMEM(less + expand, BF16),
            pltpu.VMEM(less + reduce, BF16),
            pltpu.SemaphoreType.DMA((2, steps)),
            pltpu.SemaphoreType.DMA((2, steps)),
            pltpu.SemaphoreType.DMA((2, steps // 2)),
            pltpu.SemaphoreType.DMA((2, steps // 2)),
            pltpu.SemaphoreType.DMA((4,)),
        ],
        8 * 10**9,
        25 * 10**6,
        1,
    )


def back(
    cross, own, images, texts, gain, shift, closed, w_pairs, project, w_query, w_gate, w_self,
    hidden, self_out, grad_mixed, grad_logit, joined, last_small, far_sources, jobs, plan, wide, blk,
):
    q_cross, k_cross, v_cross, do_cross, lse_cross, delta_cross = cross
    q_self, k_self, v_self, lse_self = own
    cross_keys, self_keys = k_cross.shape[0], k_self.shape[0]
    names = bit_names(wide, blk)
    groups = group_bits(blk)
    tile = (2,) * len(tile_bits(wide, blk))
    lanes = 2 * D // wide
    stream = shaped((DOCS, PAGE, D), BF16)

    def fixed(array):
        count = len(array.shape)
        spec = pl.BlockSpec(
            array.shape, lambda step: (0,) * count, pipeline_mode=pl.Buffered(buffer_count=1)
        )
        return (spec, array)

    def early(array, rows, offset=0):
        last = QUADS - 1
        return (
            pl.BlockSpec(
                (rows, QUAD), lambda step: (0, offset + step - step // QUADS * (step - last))
            ),
            array,
        )

    def late(array, rows, offset=0):
        return (
            pl.BlockSpec((rows, QUAD), lambda step: (0, offset + step // QUADS * (step - QUADS))),
            array,
        )

    def early_rows(array):
        last = QUADS - 1
        return (
            pl.BlockSpec((8, ROWS), lambda step: (step - step // QUADS * (step - last), 0)), array
        )

    def late_rows(array):
        return (pl.BlockSpec((8, ROWS), lambda step: (step // QUADS * (step - QUADS), 0)), array)

    def tiles(columns_here):
        return pltpu.VMEM(tile + (columns_here // (2 * blk), lanes), BF16)

    def both(job):
        return pltpu.VMEM((2,) * (1 + len(job.after())) + (job.rows, job.lanes), BF16)

    image_rows, text_rows = cross_keys // 2, self_keys // 2
    return call(
        functools.partial(back_kernel, wide, blk, jobs, plan),
        "back",
        2 * QUADS,
        [
            (ANY, images),
            own_pages(images),
            (ANY, texts),
            fixed(gain),
            fixed(shift),
            fixed(closed[0]),
            fixed(closed[1]),
            early(q_cross, ROWS),
            early(k_cross, cross_keys),
            early(v_cross, cross_keys),
            early(do_cross, ROWS),
            early_rows(lse_cross),
            early_rows(delta_cross),
            early(w_pairs, D),
            early(w_pairs, D, QUADS),
            late(q_self, ROWS),
            late(k_self, self_keys),
            late(v_self, self_keys),
            late_rows(lse_self),
            late(project, D),
            late(project, D, QUADS),
            late(project, D, 2 * QUADS),
            fixed(w_query),
            fixed(w_gate),
            (ANY, w_self),
            fixed(hidden),
            fixed(self_out),
            (ANY, grad_mixed),
            fixed(grad_logit),
            fixed(joined),
            fixed(last_small),
        ]
        + [(ANY, source) for source in far_sources],
        [(ANY, stream)] * 3
        + [(whole((SUMS, D)), shaped((SUMS, D), F32)), (whole((8, D)), shaped((8, D), F32))]
        + [(whole(job.result().shape), job.result()) for job in jobs if job.ends],
        [
            pltpu.VMEM((self_keys, D), BF16),
            pltpu.VMEM((self_keys, 2 * QUAD), BF16),
            pltpu.VMEM((self_keys, D), F32),
            pltpu.VMEM((ROWS, D), BF16),
            pltpu.VMEM((PAIR, D), BF16),
            pltpu.VMEM((ROWS, D), F32),
            pltpu.VMEM((ROWS, D), BF16),
            pltpu.VMEM((8 * QUADS, ROWS), F32),
            pltpu.VMEM(texts.shape, BF16),
            pltpu.VMEM((text_rows, D), BF16),
            pltpu.VMEM((text_rows, D), BF16),
            pltpu.VMEM((text_rows, D), BF16),
            pltpu.VMEM((SUMS, D), F32),
            pltpu.SemaphoreType.DMA((4,)),
            tiles(2 * D),
            tiles(D),
            tiles(D),
            tiles(3 * D),
            both(jobs[0]),
            both(jobs[2]),
        ]
        + [kind for job in jobs for kind in job.scratch()]
        + Home.scratch()
        + Rows.scratch(groups, image_rows)
        + Rows.scratch(groups, text_rows)
        + Total.scratch(names, SUMS)
        + Total.scratch(names, 8),
        23 * 10**9,
        30 * 10**6,
        2,
    )


def finish(pieces, streams, sums, last_sums):
    vmem = pl.BlockSpec(memory_space=pltpu.VMEM)
    operands = [part for parts in pieces for part in parts] + [*streams, sums, last_sums]
    results = []
    for index, parts in enumerate(pieces):
        shape = (parts[0].shape[2], sum(2 * part.shape[1] for part in parts))
        results.append(shaped(shape[::-1] if index + 1 == len(pieces) else shape, F32))
    results += [shaped(stream.shape, BF16) for stream in streams]
    results += [shaped((H, D), F32), shaped((FF,), F32), shaped((D,), F32)]
    results += [shaped((4, D), F32)] * 2
    return pl.pallas_call(
        functools.partial(finish_kernel, tuple(len(parts) for parts in pieces)),
        in_specs=[vmem] * len(operands),
        out_specs=[vmem] * len(results),
        out_shape=results,
        name="finish",
        compiler_params=pltpu.CompilerParams(vmem_limit_bytes=VMEM_LIMIT),
        cost_estimate=pl.CostEstimate(flops=10**6, bytes_accessed=5 * 10**6, transcendentals=0),
    )(*operands)


def body(
    text_blocks,
    image_blocks,
    cotangent,
    text_mask,
    page_regions,
    doc_pages,
    self_project,
    self_output,
    cross_query,
    cross_pairs,
    cross_output,
    gate_weight,
    expand_weight,
    expand_bias,
    reduce_weight,
    reduce_bias,
    norm_gain,
    norm_bias,
):
    wide = lax.axis_size("wide")
    blk = lax.axis_size("blk")
    names = tuple(tile_bits(wide, blk))
    core = ("w", 0)
    first = (("w", 1),)
    others = tuple(("w", bit) for bit in range(2, wide.bit_length() - 1))
    low = (("b", 0),)
    high = tuple(("b", bit) for bit in range(1, blk.bit_length() - 1))
    share = 2 * blk
    lanes = 2 * D // wide
    far = 2 * FF // wide
    gate_rows = jnp.transpose(gate_weight)

    (
        self_out, self_lse, self_q, self_k, self_v, text_pages, image_pages, cots, text_closed,
        image_closed,
    ) = self_forward(
        text_blocks, image_blocks, cotangent, text_mask, page_regions, doc_pages, norm_gain,
        norm_bias, self_project, wide, blk,
    )
    hidden, gate, raw, cross_lse, cross_q, cross_k, cross_v = cross_forward(
        text_pages, image_pages, self_out, self_output, gate_rows, norm_gain, norm_bias,
        image_closed, cross_query, cross_pairs,
    )
    (
        joined, *partial, d_cross_output, grad_mixed, grad_raw, cross_delta,
        grad_logit, small_last,
    ) = forward_back(
        hidden, raw, gate, cots, cross_output, norm_gain, norm_bias, expand_weight,
        expand_bias.reshape(1, FF), reduce_weight, reduce_bias.reshape(1, D), wide, blk,
    )

    blk_names = names[wide.bit_length() - 2 : -1]
    top, top_wide = blk_names[:1], names[:1]
    below = tuple(name for name in high if name not in top)
    expand_shape = (0, FF // share, lanes, False)
    reduce_shape = (0, D // share, far, False)
    jobs = (
        Job(others[::-1] + blk_names[1:], below, *expand_shape),
        Job(others[::-1] + first + blk_names[1:], first + below, *expand_shape),
        Job(names[1 : wide.bit_length() - 2] + blk_names[:-1], below, *reduce_shape),
        Job(names[1 : wide.bit_length() - 2] + blk_names, low + below, *reduce_shape),
    )
    ends = {"ends": True, "near": True}
    parts = tuple(job._replace(inner=True) for job in jobs)
    middle_names = names[1 : wide.bit_length() - 2]
    one = (0, D // share, lanes, True)
    rows = 3 * D // share
    split = rows // 2 // 16 * 16 + 16 if rows % 16 == 0 else 0
    ahead = (core,) + first + low + others + high
    behind = (core,) + low + first + others + high
    cross_order = (core,) + first + high + low + others
    jobs = parts + (
        Job(top + jobs[0].after(), low + top + others, *expand_shape)._replace(**ends),
        Job(top_wide + jobs[2].after(), top_wide + top + middle_names, *reduce_shape)._replace(**ends),
        Job(names, (core,) + low + first + high + others, 0, 2 * D // share, lanes, True, True),
        Job(names, cross_order, *one, True),
        Job(names, cross_order, *one, False),
        Job(names, cross_order, *one, True),
    )
    if split:
        jobs += (Job(names, ahead, 0, split, lanes, True, True),)
    jobs += (Job(names, behind, split, rows - split, lanes, True, True),)
    project = tuple(range(10, len(jobs)))
    plan = {
        0: (1, 3, 0, 2),
        4: (1, 3, 0, 2),
        6: (6, 7, 8, 9),
        7: (7, 8, 9),
        8: (1, 3),
        9: (4, 6, 5),
        12: project,
        13: (7, 8, 9),
        14: project,
        15: (4, 5, 6),
        16: (7, 8, 9) + project,
        17: (4, 5, 6) + project,
        18: (7, 8, 9, 6) + project,
    }
    joined_home, text_home, image_home, sums, last_sums, *pieces = back(
        (cross_q, cross_k, cross_v, grad_raw, cross_lse, cross_delta),
        (self_q, self_k, self_v, self_lse),
        image_pages, text_pages, norm_gain, norm_bias, (image_closed, text_closed), cross_pairs,
        self_project, cross_query, gate_rows, self_output, hidden, self_out, grad_mixed,
        grad_logit, joined, small_last, (*partial, d_cross_output), jobs, plan, wide, blk,
    )
    expand_piece, reduce_piece, *cross_pieces = pieces[:6]
    project_pieces = pieces[6:]
    (
        grad_cross_pairs, grad_cross_query, grad_cross_output, grad_self_output,
        grad_expand_weight, grad_self_project, grad_reduce_weight,
        joined_blocks, text_grad, image_grad,
        grad_gate_weight, grad_expand_bias, grad_reduce_bias, gains, shifts,
    ) = finish(
        [[piece] for piece in cross_pieces] + [[expand_piece], project_pieces, [reduce_piece]],
        [joined_home, text_home, image_home], sums, last_sums,
    )
    return (
        joined_blocks,
        text_grad,
        image_grad,
        grad_self_project,
        grad_self_output,
        grad_cross_query,
        grad_cross_pairs,
        grad_cross_output,
        grad_expand_weight,
        jnp.transpose(grad_reduce_weight),
        jnp.transpose(grad_gate_weight),
        grad_expand_bias,
        grad_reduce_bias,
        gains,
        shifts,
    )


def normalize(values, gains, biases):
    scaled, inverse = standardize(values)
    return (scaled * gains + biases, scaled, inverse)


def normalize_back(upstream, scaled, inverse, gains):
    result = norm_back(upstream, scaled, inverse, gains)
    return (result, jnp.sum(upstream * scaled, axis=0), jnp.sum(upstream, axis=0))


def gelu_tanh(values):
    return jax.nn.gelu(values, approximate=True)


def forward_doc(queries, carried, key_pairs, allowed, scaling):
    running_max, summed, accumulated = carried
    key_count = key_pairs.shape[0]
    keys_part = key_pairs[:, :D].reshape(key_count, H, HD)
    values_part = key_pairs[:, D:].reshape(key_count, H, HD)
    open_keys = (allowed > 0)[None, None, :]
    scores = (
        jnp.einsum("qhd,khd->hqk", queries, keys_part, preferred_element_type=F32) * scaling
    )
    scores = jnp.where(open_keys, scores, NEGATIVE)
    new_max = jnp.maximum(running_max, jnp.max(scores, axis=-1))
    fading = jnp.exp(running_max - new_max)
    weights = jnp.where(open_keys, jnp.exp(scores - new_max[..., None]), 0.0)
    summed = summed * fading + jnp.sum(weights, axis=-1)
    accumulated = accumulated * fading[..., None] + jnp.einsum(
        "hqk,khd->hqd",
        weights.astype(BF16),
        values_part,
        preferred_element_type=F32,
    )
    return (new_max, summed, accumulated)


def forward_fold(queries, scaling, carried, pieces):
    key_pairs, allowed = pieces

    def forward_per_doc(doc_items):
        doc_queries, doc_max, doc_sum, doc_acc, doc_pairs, doc_allowed = doc_items
        doc_carry = (doc_max, doc_sum, doc_acc)
        result = forward_doc(doc_queries, doc_carry, doc_pairs, doc_allowed, scaling)
        return result

    return lax.map(
        forward_per_doc, (queries, carried[0], carried[1], carried[2], key_pairs, allowed)
    )


def backward_doc(queries, grad_out, log_sum, row_delta, key_pairs, allowed, scaling):
    key_count = key_pairs.shape[0]
    keys_part = key_pairs[:, :D].reshape(key_count, H, HD)
    values_part = key_pairs[:, D:].reshape(key_count, H, HD)
    open_keys = (allowed > 0)[None, None, :]
    scores = (
        jnp.einsum("qhd,khd->hqk", queries, keys_part, preferred_element_type=F32) * scaling
    )
    probabilities = jnp.where(open_keys, jnp.exp(scores - log_sum[..., None]), 0.0)
    grad_probs = jnp.einsum(
        "qhd,khd->hqk", grad_out, values_part, preferred_element_type=F32
    )
    grad_scores = (probabilities * (grad_probs - row_delta[..., None])).astype(BF16)
    query_grad = (
        jnp.einsum("hqk,khd->qhd", grad_scores, keys_part, preferred_element_type=F32)
        * scaling
    )
    key_grad = (
        jnp.einsum("hqk,qhd->khd", grad_scores, queries, preferred_element_type=F32)
        * scaling
    )
    value_grad = jnp.einsum(
        "hqk,qhd->khd",
        probabilities.astype(BF16),
        grad_out,
        preferred_element_type=F32,
    )
    return (
        query_grad,
        jnp.concatenate(
            [key_grad.reshape(key_count, D), value_grad.reshape(key_count, D)], axis=-1
        ),
    )


def backward_fold(queries, grad_out, log_sum, row_delta, scaling, pieces):
    key_pairs, allowed = pieces

    def backward_per_doc(doc_items):
        doc_queries, doc_grad, doc_log, doc_delta, doc_pairs, doc_allowed = doc_items
        result = backward_doc(
            doc_queries, doc_grad, doc_log, doc_delta, doc_pairs, doc_allowed, scaling
        )
        return result

    query_parts, pair_parts = lax.map(
        backward_per_doc, (queries, grad_out, log_sum, row_delta, key_pairs, allowed)
    )
    return (query_parts, pair_parts)


def start_state():
    return (
        jnp.full((DOCS, H, PAGE), NEGATIVE, F32),
        jnp.zeros((DOCS, H, PAGE), F32),
        jnp.zeros((DOCS, H, PAGE, HD), F32),
    )


def finish_state(state):
    running_max, summed, accumulated = state
    result = jnp.transpose(accumulated / summed[..., None], (0, 2, 1, 3))
    return (result, running_max + jnp.log(summed))


def tile_order(grad, wide_count, blk_count):
    rows, cols = grad.shape
    tiled = grad.reshape(wide_count, rows // wide_count, blk_count, cols // blk_count)
    return jnp.transpose(tiled, (0, 2, 1, 3)).reshape(
        wide_count * blk_count * (rows // wide_count), cols // blk_count
    )


def plain_body(
    text_blocks,
    image_blocks,
    cotangent,
    text_mask,
    page_regions,
    doc_pages,
    self_project,
    self_output,
    cross_query,
    cross_pairs,
    cross_output,
    gate_weight,
    expand_weight,
    expand_bias,
    reduce_weight,
    reduce_bias,
    norm_gain,
    norm_bias,
):
    scaling = HD ** (-0.5)
    block_shape = text_blocks.shape
    offsets = jnp.arange(PAGE, dtype=jnp.int32)
    living = (lax.axis_index("blk") < doc_pages)[:, None]
    text_open = (living & ((text_mask > 0) | (offsets[None, :] == 0))).astype(BF16)
    image_open = (living & (offsets[None, :] < page_regions)).astype(BF16)
    text_rows = text_blocks.reshape(-1, D).astype(F32)
    image_rows = image_blocks.reshape(-1, D).astype(F32)
    normed_text, scaled_first, inverse_first = normalize(text_rows, norm_gain[0], norm_bias[0])
    normed_low = normed_text.astype(BF16)
    triples = product(normed_low, self_project).astype(BF16)
    self_queries = triples[:, :D].reshape(DOCS, PAGE, H, HD)
    self_pairs = triples[:, D:].reshape(DOCS, PAGE, 2 * D)
    self_state = forward_fold(
        self_queries,
        scaling,
        start_state(),
        (
            lax.all_gather(self_pairs, "blk", axis=1, tiled=True),
            lax.all_gather(text_open, "blk", axis=1, tiled=True),
        ),
    )
    self_result, self_logsum = finish_state(self_state)
    self_low = self_result.reshape(-1, D).astype(BF16)
    hidden = text_rows + product(self_low, self_output)
    cross_normed, scaled_cross, inverse_cross = normalize(hidden, norm_gain[1], norm_bias[1])
    cross_low = cross_normed.astype(BF16)
    gate_values = jax.nn.sigmoid(product(cross_low, gate_weight))
    image_normed, scaled_image, inverse_image = normalize(image_rows, norm_gain[2], norm_bias[2])
    image_low = image_normed.astype(BF16)
    image_pairs = product(image_low, cross_pairs).astype(BF16).reshape(DOCS, PAGE, 2 * D)
    cross_queries = product(cross_low, cross_query).astype(BF16).reshape(DOCS, PAGE, H, HD)
    cross_state = forward_fold(
        cross_queries,
        scaling,
        start_state(),
        (
            lax.all_gather(image_pairs, "blk", axis=1, tiled=True),
            lax.all_gather(image_open, "blk", axis=1, tiled=True),
        ),
    )
    cross_result, cross_logsum = finish_state(cross_state)
    gate_heads = gate_values.reshape(DOCS, PAGE, H, 1)
    gated_low = (cross_result * gate_heads).reshape(-1, D).astype(BF16)
    mixed_rows = hidden + product(gated_low, cross_output)
    final_normed, scaled_final, inverse_final = normalize(mixed_rows, norm_gain[3], norm_bias[3])
    final_low = final_normed.astype(BF16)
    inner_rows = product(final_low, expand_weight) + expand_bias
    active_low = gelu_tanh(inner_rows).astype(BF16)
    joined_blocks = (
        (mixed_rows + product(active_low, reduce_weight) + reduce_bias)
        .reshape(block_shape)
        .astype(BF16)
    )
    upstream = cotangent.reshape(-1, D)
    upstream_float = upstream.astype(F32)
    grad_reduce_bias = jnp.sum(upstream_float, axis=0)
    grad_reduce_weight = transposed(active_low, upstream)
    grad_active = against(upstream, reduce_weight).astype(BF16)
    gelu_value, gelu_pull = jax.vjp(gelu_tanh, inner_rows)
    grad_inner = gelu_pull(grad_active.astype(F32))[0].astype(BF16)
    grad_expand_bias = jnp.sum(grad_inner.astype(F32), axis=0)
    grad_expand_weight = transposed(final_low, grad_inner)
    back_final, gain_final, shift_final = normalize_back(
        against(grad_inner, expand_weight), scaled_final, inverse_final, norm_gain[3]
    )
    grad_mixed = upstream_float + back_final
    grad_branch = grad_mixed.astype(BF16)
    grad_cross_output = transposed(gated_low, grad_branch)
    grad_gated = against(grad_branch, cross_output).astype(BF16)
    grad_gated_heads = grad_gated.astype(F32).reshape(DOCS, PAGE, H, HD)
    grad_gate = jnp.sum(grad_gated_heads * cross_result, axis=-1).reshape(-1, H)
    grad_logit = grad_gate * gate_values * (1.0 - gate_values)
    grad_gate_weight = lax.dot_general(
        cross_low.astype(F32), grad_logit, (((0,), (0,)), ((), ())), precision=HIGHEST
    )
    grad_raw = (grad_gated_heads * gate_heads).astype(BF16)
    cross_delta = jnp.transpose(
        jnp.sum(grad_raw.astype(F32) * cross_result, axis=-1), (0, 2, 1)
    )
    cross_carry = backward_fold(
        cross_queries,
        grad_raw,
        cross_logsum,
        cross_delta,
        scaling,
        (
            lax.all_gather(image_pairs, "blk", axis=1, tiled=True),
            lax.all_gather(image_open, "blk", axis=1, tiled=True),
        ),
    )
    cross_home = lax.psum_scatter(
        cross_carry[1].astype(BF16), "blk", scatter_dimension=1, tiled=True
    ).astype(F32)
    cross_query_sum = cross_carry[0]
    cross_query_low = cross_query_sum.reshape(-1, D).astype(BF16)
    cross_pair_low = cross_home.reshape(-1, 2 * D).astype(BF16)
    grad_cross_query = transposed(cross_low, cross_query_low)
    grad_cross_pairs = transposed(image_low, cross_pair_low)
    back_image, gain_image, shift_image = normalize_back(
        against(cross_pair_low, cross_pairs), scaled_image, inverse_image, norm_gain[2]
    )
    image_grad = back_image.reshape(block_shape).astype(BF16)
    grad_cross_in = against(cross_query_low, cross_query) + lax.dot_general(
        grad_logit, gate_weight.astype(F32), (((1,), (1,)), ((), ())), precision=HIGHEST
    )
    back_cross, gain_cross, shift_cross = normalize_back(
        grad_cross_in, scaled_cross, inverse_cross, norm_gain[1]
    )
    grad_hidden = grad_mixed + back_cross
    grad_self_branch = grad_hidden.astype(BF16)
    grad_self_output = transposed(self_low, grad_self_branch)
    grad_self_result = (
        against(grad_self_branch, self_output).astype(BF16).reshape(DOCS, PAGE, H, HD)
    )
    self_delta = jnp.transpose(
        jnp.sum(grad_self_result.astype(F32) * self_result, axis=-1), (0, 2, 1)
    )
    self_carry = backward_fold(
        self_queries,
        grad_self_result,
        self_logsum,
        self_delta,
        scaling,
        (
            lax.all_gather(self_pairs, "blk", axis=1, tiled=True),
            lax.all_gather(text_open, "blk", axis=1, tiled=True),
        ),
    )
    self_home = lax.psum_scatter(
        self_carry[1].astype(BF16), "blk", scatter_dimension=1, tiled=True
    ).astype(F32)
    self_query_sum = self_carry[0]
    grad_triples = jnp.concatenate(
        [self_query_sum.reshape(-1, D), self_home.reshape(-1, 2 * D)], axis=-1
    ).astype(BF16)
    grad_self_project = transposed(normed_low, grad_triples)
    back_first, gain_first, shift_first = normalize_back(
        against(grad_triples, self_project), scaled_first, inverse_first, norm_gain[0]
    )
    text_grad = (grad_hidden + back_first).reshape(block_shape).astype(BF16)
    wide_count = lax.axis_size("wide")
    blk_count = lax.axis_size("blk")
    large_grads = (
        grad_self_project,
        grad_self_output,
        grad_cross_query,
        grad_cross_pairs,
        grad_cross_output,
        grad_expand_weight,
        grad_reduce_weight,
    )
    ordered = tuple((tile_order(grad, wide_count, blk_count) for grad in large_grads))
    summed_grads = lax.psum_scatter(ordered, ("wide", "blk"), scatter_dimension=0, tiled=True)
    small_sums = lax.psum(
        (
            grad_gate_weight,
            grad_expand_bias,
            grad_reduce_bias,
            jnp.stack([gain_first, gain_cross, gain_image, gain_final]),
            jnp.stack([shift_first, shift_cross, shift_image, shift_final]),
        ),
        ("wide", "blk"),
    )
    return (
        joined_blocks,
        text_grad,
        image_grad,
        summed_grads[0],
        summed_grads[1],
        summed_grads[2],
        summed_grads[3],
        summed_grads[4],
        summed_grads[5],
        summed_grads[6],
        small_sums[0],
        small_sums[1],
        small_sums[2],
        small_sums[3],
        small_sums[4],
    )


def solution(mesh):
    rows = P("wide", "blk", None)
    longest = mesh.shape["blk"] * PAGE
    return jax.shard_map(
        body if longest <= LONGEST else plain_body,
        mesh=mesh,
        in_specs=(rows,) * 3 + (P("wide", "blk"),) * 2 + (P("wide"),) + (P(),) * 12,
        out_specs=(rows,) * 3 + (P("wide", "blk"),) * 7 + (P(),) * 5,
        check_vma=False,
    )
```

```python
import functools
from typing import NamedTuple

import jax
import jax.numpy as jnp
from jax import lax
from jax.experimental import pallas as pl
from jax.experimental.pallas import tpu as pltpu
from jax.sharding import PartitionSpec as P

D = 768
H = 12
HD = 64
FF = 3072
PAGE = 128
DOCS = 2
ROWS = DOCS * PAGE
QUAD = 256
QUADS = D // QUAD
PAIR = 128
IMAGE = 112
EXTRA = 16
SUMS = 24
PLANNED = (4, 8)
EPSILON = 1e-05
NEGATIVE = -1e30
HIGHEST = lax.Precision.HIGHEST
BF16 = jnp.bfloat16
F32 = jnp.float32
VMEM_LIMIT = 62 * 1024 * 1024


def product(left, right):
    return jnp.dot(left, right, preferred_element_type=F32)


def against(left, right, precision=None):
    return lax.dot_general(
        left, right, (((1,), (1,)), ((), ())), preferred_element_type=F32, precision=precision
    )


def transposed(left, right, precision=None):
    return lax.dot_general(
        left, right, (((0,), (0,)), ((), ())), preferred_element_type=F32, precision=precision
    )


def standardize(values):
    centred = values - jnp.mean(values, axis=-1, keepdims=True)
    inverse = lax.rsqrt(jnp.mean(centred * centred, axis=-1, keepdims=True) + EPSILON)
    return centred * inverse, inverse


def norm_back(upstream, scaled, inverse, gains):
    weighted = upstream * gains
    return inverse * (
        weighted
        - jnp.mean(weighted, axis=-1, keepdims=True)
        - scaled * jnp.mean(weighted * scaled, axis=-1, keepdims=True)
    )


def column_sum(values):
    return jnp.sum(values, axis=0, keepdims=True)


def normalize_page(page, index, gain, shift, normed):
    rows = page.shape[0]
    scaled, _ = standardize(page[...].astype(F32))
    normed[index * rows : (index + 1) * rows, :] = (scaled * gain + shift).astype(BF16)


def normalize_pages(pages, gain, shift, normed):
    for index in range(pages.shape[0]):
        normalize_page(pages.at[index], index, gain, shift, normed)


def lane_index(rows):
    return lax.broadcasted_iota(jnp.int32, (rows, PAIR), 1)


def side_masks(rows):
    lanes = lane_index(rows)
    return [(lanes < HD).astype(BF16), (lanes >= HD).astype(BF16)]


def attend_forward(q_ref, k_ref, v_ref, closed_ref, out_ref, lse_ref):
    lanes = lane_index(ROWS)
    masks = side_masks(ROWS)
    first_lane = (lanes == 0).astype(BF16)
    stats = jnp.zeros((ROWS, PAIR), F32)
    for pair in range(QUAD // PAIR):
        cols = slice(pair * PAIR, (pair + 1) * PAIR)
        keys = jnp.concatenate([k_ref[:, cols], closed_ref[...]], axis=1)
        values = v_ref[:, cols]
        queries = q_ref[:, cols]
        results = []
        for side in range(2):
            query = jnp.concatenate([queries * masks[side], first_lane], axis=1)
            scores = against(query, keys)
            top = jnp.max(scores, axis=1, keepdims=True)
            weights = jnp.exp(scores - top)
            total = jnp.sum(weights, axis=1, keepdims=True)
            results.append(product(weights.astype(BF16), values) / total)
            stats = jnp.where(lanes == pair * 2 + side, top + jnp.log(total), stats)
        out_ref[:, cols] = jnp.where(lanes < HD, results[0], results[1])
    lse_ref[...] = jnp.transpose(stats)[:8, :]


def attend_backward(q_ref, k_ref, v_ref, do_ref, lse_ref, delta_ref, closed_ref, dq_ref, dkv_ref, hook):
    lanes = lane_index(ROWS)
    masks = side_masks(ROWS)
    first_lane = (lanes == 0).astype(BF16)
    for pair in range(QUAD // PAIR):
        cols = slice(pair * PAIR, (pair + 1) * PAIR)
        key_part = k_ref[:, cols]
        keys = jnp.concatenate([key_part, closed_ref[...]], axis=1)
        values = v_ref[:, cols]
        dq_parts = []
        dk = None
        dv = None
        for side in range(2):
            row = pair * 2 + side
            query = q_ref[:, cols] * masks[side]
            grad_out = do_ref[:, cols] * masks[side]
            scores = against(keys, jnp.concatenate([query, first_lane], axis=1))
            weights = jnp.exp(scores - lse_ref[row : row + 1, :])
            grad_weights = against(values, grad_out)
            grad_scores = (weights * (grad_weights - delta_ref[row : row + 1, :])).astype(BF16)
            dv_part = product(weights.astype(BF16), grad_out)
            dk_part = product(grad_scores, query)
            dv = dv_part if dv is None else dv + dv_part
            dk = dk_part if dk is None else dk + dk_part
            dq_parts.append(transposed(grad_scores, key_part))
        dq_ref[:, cols] = (jnp.where(lanes < HD, dq_parts[0], dq_parts[1]) * HD ** (-0.5)).astype(
            BF16
        )
        dkv_ref[:, cols] = dk.astype(BF16)
        dkv_ref[:, QUAD + pair * PAIR : QUAD + (pair + 1) * PAIR] = dv.astype(BF16)
        if pair == 0:
            hook()


def head_sums(values):
    sums = []
    lanes = lane_index(values.shape[0])
    for pair in range(H // 2):
        part = values[:, pair * PAIR : (pair + 1) * PAIR]
        sums.append(jnp.sum(jnp.where(lanes < HD, part, 0.0), axis=1, keepdims=True))
        sums.append(jnp.sum(jnp.where(lanes >= HD, part, 0.0), axis=1, keepdims=True))
    return sums


def head_rows(sums):
    lanes = lane_index(ROWS)
    stats = jnp.zeros((ROWS, PAIR), F32)
    for head, value in enumerate(sums):
        stats = jnp.where(lanes == (head // 4) * 8 + head % 4, value, stats)
    return jnp.transpose(stats)[: 8 * QUADS, :]


def spread_heads(gates):
    lanes = lane_index(gates.shape[0])
    parts = []
    for pair in range(H // 2):
        parts.append(
            jnp.where(lanes < HD, gates[:, 2 * pair : 2 * pair + 1], gates[:, 2 * pair + 1 : 2 * pair + 2])
        )
    return jnp.concatenate(parts, axis=1)


def put_rows(out, start, value):
    rows, lanes = out.shape[-2:]
    cuts = (value.shape[1] // lanes).bit_length() - 1
    lead = len(out.shape) - 2
    low = start
    while low < start + value.shape[0]:
        tile = low // rows
        high = min(start + value.shape[0], (tile + 1) * rows)
        for cut in range(1 << cuts):
            piece = value[low - start : high - start, cut * lanes : (cut + 1) * lanes]
            at = bits_of(cut, cuts) + bits_of(tile, lead - cuts)
            out[at + (slice(low - tile * rows, high - tile * rows), slice(None))] = piece
        low = high


class Gather:
    def __init__(self, places, names, packed, landed, waits):
        self.places = places
        self.names = names
        self.packed = packed
        self.landed = landed
        self.sends, self.receives = waits

    @staticmethod
    def waits(names):
        count = DOCS << len(names)
        return [pltpu.SemaphoreType.DMA((count,))] * 2

    def swap(self, turn):
        doc = self.places.turn if turn == 0 else 1 - self.places.turn
        return remote(
            self.packed.at[doc], self.landed.at[turn], self.sends.at[turn], self.receives.at[turn],
            self.places.swap(turn),
        )

    def start(self):
        stays = self.places.swap_stays()
        pl.when(jnp.logical_not(stays))(lambda: self.swap(0).start())
        self.swap(1).start()

        @pl.when(stays)
        def _():
            self.landed[0] = self.packed[self.places.turn]

    def copy(self, block, turn):
        stage = block.bit_length() - 1
        source = (block - (1 << stage)) * DOCS + turn
        at = block * DOCS + turn
        return remote(
            self.landed.at[source], self.landed.at[at], self.sends.at[at], self.receives.at[at],
            self.places.flip(self.names[stage]),
        )

    def arrive(self, block, turn):
        if block > 0:
            self.copy(block, turn).wait_recv()
        elif turn > 0:
            self.swap(turn).wait_recv()
        else:
            stays = self.places.swap_stays()
            pl.when(jnp.logical_not(stays))(lambda: self.swap(0).wait_recv())
        for stage in range(block.bit_length(), len(self.names)):
            self.copy(block + (1 << stage), turn).start()

    def end(self):
        stays = self.places.swap_stays()
        pl.when(jnp.logical_not(stays))(lambda: self.swap(0).wait_send())
        self.swap(1).wait_send()
        for block in range(1, 1 << len(self.names)):
            for turn in range(DOCS):
                self.copy(block, turn).wait_send()


def closed_rows(is_open):
    row = jnp.where(is_open, 0.0, NEGATIVE)
    wide = jnp.concatenate([row, jnp.zeros((1, D - PAGE), F32)], axis=1)
    return jnp.broadcast_to(wide, (EXTRA, D)).astype(BF16)


def closed_column(rows):
    row = rows[0:1, 0:PAGE].astype(F32)
    turned = jnp.transpose(jnp.broadcast_to(row, (PAGE, PAGE)))
    return jnp.where(lane_index(PAGE) == 0, turned, 0.0).astype(BF16)


def self_forward_kernel(
    wide, blk,
    regions, doc_pages, text_in, image_in, cot_in, mask, gain, shift, wq, wk, wv,
    out, lse, q_out, k_out, v_out, text_out, image_out, cot_out, text_closed, image_closed,
    normed, text_packed, image_packed, text_landed, image_landed, cot_landed,
    text_sends, text_receives, image_sends, image_receives, cot_sends, cot_receives, local,
):
    step = pl.program_id(0)
    places = Places(wide, blk)
    groups = group_bits(blk)
    blocks = 1 << len(groups)
    text = Gather(places, groups, text_packed, text_landed, (text_sends, text_receives))
    image = Gather(places, groups, image_packed, image_landed, (image_sends, image_receives))
    cot = Gather(places, [], cot_in, cot_landed, (cot_sends, cot_receives))
    outward = [
        pltpu.make_async_copy(text_landed.at[:, pl.ds(0, PAGE)], text_out, local.at[0]),
        pltpu.make_async_copy(image_landed.at[:, pl.ds(0, IMAGE)], image_out, local.at[1]),
        pltpu.make_async_copy(cot_landed, cot_out, local.at[2]),
    ]

    @pl.when(step == 0)
    def _():
        offsets = lax.broadcasted_iota(jnp.int32, (1, PAGE), 1)
        for doc in range(DOCS):
            text_packed[doc, 0:PAGE, :] = text_in[doc]
            living = places.b < doc_pages[doc]
            is_open = ((mask[doc : doc + 1, :] > 0) | (offsets == 0)) & living
            text_packed[doc, PAGE : PAGE + EXTRA, :] = closed_rows(is_open)
        greet(places, groups, True)
        text.start()
        for doc in range(DOCS):
            image_packed[doc, 0:IMAGE, :] = image_in[doc, 0:IMAGE, :]
            living = places.b < doc_pages[doc]
            is_open = (offsets < regions[0:1, doc : doc + 1]) & living
            image_packed[doc, IMAGE : IMAGE + EXTRA, :] = closed_rows(is_open)
        text.arrive(0, 0)
        text.arrive(0, 1)
        image.start()

        def take(block, turn):
            index = block * DOCS + turn
            page = text_landed.at[index, pl.ds(0, PAGE)]
            normalize_page(page, index, gain[0:1, :], shift[0:1, :], normed)
            text_closed[index * PAGE : (index + 1) * PAGE, :] = closed_column(
                text_landed[index, PAGE : PAGE + EXTRA, :]
            )

        for turn in range(DOCS):
            take(0, turn)
        for block in range(1, blocks):
            for turn in range(DOCS):
                text.arrive(block, turn)
            if block == 1:
                image.arrive(0, 0)
                image.arrive(0, 1)
                cot.start()
            for turn in range(DOCS):
                take(block, turn)

    @pl.when(step == 1)
    def _():
        outward[0].start()
        for block in range(1, blocks // 2):
            for turn in range(DOCS):
                image.arrive(block, turn)

    q_out[...] = (product(normed[0:ROWS, :], wq[...]).astype(BF16) * HD ** (-0.5)).astype(BF16)
    k_out[...] = product(normed[...], wk[...]).astype(BF16)
    v_out[...] = product(normed[...], wv[...]).astype(BF16)
    attend_forward(q_out, k_out, v_out, text_closed, out, lse)

    @pl.when(step == QUADS - 1)
    def _():
        for turn in range(DOCS):
            cot.arrive(0, turn)
        outward[2].start()
        for block in range(max(1, blocks // 2), blocks):
            for turn in range(DOCS):
                image.arrive(block, turn)
        outward[1].start()
        for index in range(blocks * DOCS):
            column = closed_column(image_landed[index, IMAGE : IMAGE + EXTRA, :])
            image_closed[index * IMAGE : (index + 1) * IMAGE, :] = column[0:IMAGE, :]
        for stream in (text, image, cot):
            stream.end()
        for copy in outward:
            copy.wait()


def cross_forward_kernel(
    text, pages, self_out, w_self, w_gate, gain, shift, closed, wq, wk, wv,
    hidden, gate, out, lse, q_out, k_out, v_out,
    normed, cross, gates,
):
    @pl.when(pl.program_id(0) == 0)
    def _():
        normalize_pages(pages, gain[2:3, :], shift[2:3, :], normed)
        branch = product(self_out[...].astype(BF16), w_self[...])
        for index in range(DOCS):
            rows = slice(index * PAGE, (index + 1) * PAGE)
            hidden[rows, :] = text[index].astype(F32) + branch[rows, :]
        scaled, _ = standardize(hidden[...])
        cross[...] = (scaled * gain[1:2, :] + shift[1:2, :]).astype(BF16)
        gates[...] = jnp.zeros_like(gates)
        gates[0:H, :] = w_gate[...]
        gate[...] = jax.nn.sigmoid(against(cross[...], gates[...]))

    q_out[...] = (product(cross[...], wq[...]).astype(BF16) * HD ** (-0.5)).astype(BF16)
    k_out[...] = product(normed[...], wk[...]).astype(BF16)
    v_out[...] = product(normed[...], wv[...]).astype(BF16)
    attend_forward(q_out, k_out, v_out, closed, out, lse)


def expand_part(wide, blk, step):
    few = (slice(None),) * (wide.bit_length() - 2)
    rest = (slice(None),) * (blk.bit_length() - 3)
    return few + (step // 2, step % 2) + rest, (slice(None), slice(None))


def reduce_part(wide, blk, step):
    cuts = wide.bit_length() - 2
    rest = (slice(None),) * (blk.bit_length() - 1)
    if cuts >= 2:
        lead = (step // 2, step % 2) + (slice(None),) * (cuts - 2) + rest
        return lead, (slice(None), slice(None))
    lanes = pl.ds(pl.multiple_of((step % 2) * D, D), D)
    return (step // 2,) + rest, (slice(None), lanes)


def put_expand(out, value, step, wide, blk):
    cuts, bits = wide.bit_length() - 2, blk.bit_length() - 1
    rows, lanes = out.shape[-2:]
    for cut in range(1 << cuts):
        for part in range(D // rows):
            at = bits_of(cut, cuts) + (step // 2, step % 2) + bits_of(part, bits - 1)
            out[at] = value[part * rows : (part + 1) * rows, cut * lanes : (cut + 1) * lanes]


def put_reduce(out, value, step, wide, blk):
    cuts, bits = wide.bit_length() - 2, blk.bit_length() - 1
    rows, lanes = out.shape[-2:]
    for part in range(D // rows):
        place = bits_of(part, bits + 1)
        piece = value[part * rows : (part + 1) * rows, :]
        if cuts >= 2:
            for cut in range(D // lanes):
                at = (step // 2, step % 2) + bits_of(cut, cuts - 2) + place
                out[at] = piece[:, cut * lanes : (cut + 1) * lanes]
        else:
            out[(step // 2,) + place + (slice(None), pl.ds(pl.multiple_of((step % 2) * D, D), D))] = piece


def forward_back_kernel(
    steps, wide, blk,
    hidden, raw, gate, cots, w_out, gain, shift, w_expand, b_expand, w_reduce, b_reduce,
    joined, early_expand, late_expand, early_reduce, late_reduce, d_out, grad_mixed, grad_raw,
    delta, grad_logit, small,
    gated, mixed, final, upstream, joined_sum, back_sum,
    expand_all, reduce_all, expand_got, reduce_got, expand_next, reduce_next,
    sends, receives, next_sends, next_receives, local,
):
    step = pl.program_id(0)
    places = Places(wide, blk)
    core, along, across = ("w", 0), ("w", 1), ("b", 0)
    cuts = wide.bit_length() - 2
    kinds = (
        (expand_part, expand_all, expand_got, expand_next, along),
        (reduce_part, reduce_all, reduce_got, reduce_next, across),
    )

    def copies(at):
        found = []
        for index, (part, grad, got, _, _) in enumerate(kinds):
            lead, tail = part(wide, blk, at)
            found.append(
                remote(
                    grad.at[lead + (1 - places.bit(core),) + tail],
                    got.at[lead + tail],
                    sends.at[index, at],
                    receives.at[index, at],
                    places.flip(core),
                )
            )
        return found

    def add(at):
        for (part, grad, got, _, _), copy in zip(kinds, copies(at)):
            copy.wait_recv()
            lead, tail = part(wide, blk, at)
            add_blocks(got.at[lead + tail], grad.at[lead + (places.bit(core),) + tail])

    def pieces(at):
        (lead, tail), (far_lead, far_tail) = (
            expand_part(wide, blk, at), reduce_part(wide, blk, at)
        )
        bit, far_bit = places.bit(along), places.bit(across)
        head, rest = lead[: cuts - 1], lead[cuts:]
        yield (
            expand_got.at[head + (bit,) + rest + tail],
            expand_got.at[head + (1 - bit,) + rest + tail],
            expand_next.at[head + rest[1:] + tail],
        )
        yield (
            reduce_got.at[far_lead[:-1] + (far_bit,) + far_tail],
            reduce_got.at[far_lead[:-1] + (1 - far_bit,) + far_tail],
            reduce_next.at[far_lead[1:-1] + far_tail],
        )

    def onward(at):
        return [
            remote(
                send, land, next_sends.at[index, at], next_receives.at[index, at],
                places.flip(kinds[index][4]),
            )
            for index, (_, send, land) in enumerate(pieces(at))
        ]

    @pl.when(step == 0)
    def _():
        greet(places, [core, along, across], False)
        upstream[0:PAGE, :] = cots[0]
        upstream[PAGE:ROWS, :] = cots[1]
        small[...] = jnp.zeros_like(small)
        gated[...] = (spread_heads(gate[...]) * raw[...]).astype(BF16)
        rows = hidden[...] + product(gated[...], w_out[...])
        mixed[...] = rows
        scaled, _ = standardize(rows)
        final[...] = (scaled * gain[3:4, :] + shift[3:4, :]).astype(BF16)
        joined_sum[...] = rows + b_reduce[...].reshape(1, D)
        back_sum[...] = jnp.zeros_like(back_sum)

    inner = product(final[...], w_expand[...]) + b_expand[...]
    squared = inner * inner
    root = (2.0 / jnp.pi) ** 0.5
    curve = jnp.tanh(root * inner * (1.0 + 0.044715 * squared))
    half = 0.5 * (1.0 + curve)
    active = (inner * half).astype(BF16)
    slope = half + 0.5 * inner * (1.0 - curve * curve) * (root * (1.0 + 3.0 * 0.044715 * squared))
    joined_sum[...] += product(active, w_reduce[...])
    grad_active = against(upstream[...], w_reduce[...]).astype(BF16)
    grad_inner = (grad_active.astype(F32) * slope).astype(BF16)
    small[pl.ds(4 + step, 1), :] = column_sum(grad_inner.astype(F32))
    back_sum[...] += against(grad_inner, w_expand[...])
    put_expand(expand_all, transposed(grad_inner, final[...]).astype(BF16), step, wide, blk)
    put_reduce(reduce_all, transposed(upstream[...], active).astype(BF16), step, wide, blk)
    for copy in copies(step):
        copy.start()
    for at in range(steps - 1):

        @pl.when(step == at + 1)
        def _():
            add(at)
            if at < steps // 2:
                for copy in onward(at):
                    copy.start()

    @pl.when(step == steps - 1)
    def _():
        total = joined_sum[...].astype(BF16)
        joined[0] = total[:PAGE]
        joined[1] = total[PAGE:]
        scaled, inverse = standardize(mixed[...])
        back = back_sum[...]
        cotangent = upstream[...].astype(F32)
        grad = cotangent + norm_back(back, scaled, inverse, gain[3:4, :])
        grad_mixed[...] = grad
        branch = grad.astype(BF16)
        put_rows(d_out, 0, transposed(branch, gated[...]).astype(BF16))
        grad_gated = against(branch, w_out[...]).astype(BF16).astype(F32)
        gates = gate[...]
        lanes = lane_index(ROWS)
        logit = jnp.zeros((ROWS, PAIR), F32)
        for head, value in enumerate(head_sums(grad_gated * raw[...])):
            logit = jnp.where(lanes == head, value, logit)
        grad_logit[...] = logit * gates * (1.0 - gates)
        rounded = (spread_heads(gates) * grad_gated).astype(BF16)
        grad_raw[...] = rounded
        delta[...] = head_rows(head_sums(rounded.astype(F32) * raw[...]))
        small[0:1, :] = column_sum(cotangent)
        small[1:2, :] = column_sum(back * scaled)
        small[2:3, :] = column_sum(back)
        add(steps - 1)
        half = (slice(None),) * cuts
        moves = [
            pltpu.make_async_copy(expand_got.at[half + (1,)], late_expand, local.at[0]),
            pltpu.make_async_copy(reduce_got.at[1], late_reduce, local.at[1]),
        ]
        for move in moves:
            move.start()
        for at in range(steps // 2):
            for copy, (kept, _, land) in zip(onward(at), pieces(at)):
                copy.wait()
                add_blocks(land, kept)
        moves += [
            pltpu.make_async_copy(expand_next, early_expand, local.at[2]),
            pltpu.make_async_copy(reduce_next, early_reduce, local.at[3]),
        ]
        for move in moves[2:]:
            move.start()
        for at in range(steps):
            for copy in copies(at):
                copy.wait_send()
        for move in moves:
            move.wait()


def spread_back(dkv, wk, wv, dx):
    weights = jnp.concatenate([wk[...], wv[...]], axis=1)

    size = dx.shape[0] // 4

    def chunk(index, carry):
        rows = pl.ds(pl.multiple_of(index * size, 16), size)
        dx[rows, :] += against(dkv[rows, :], weights)
        return carry

    lax.fori_loop(0, 4, chunk, 0)


def round_pages(dx, keep, send):
    half = dx.shape[0] // 2
    for target, start in ((send, half), (keep, 0)):
        size = half // 4
        for part in range(4):
            low = start + part * size
            target[part * size : (part + 1) * size, :] = dx[low : low + size, :].astype(BF16)


def page_sums(pages, dx):
    gain_sum = jnp.zeros((1, D), F32)
    shift_sum = jnp.zeros((1, D), F32)
    count, size, _ = pages.shape
    for index in range(count):
        scaled, _ = standardize(pages[index].astype(F32))
        part = dx[index * size : (index + 1) * size, :]
        gain_sum += column_sum(part * scaled)
        shift_sum += column_sum(part)
    return gain_sum, shift_sum


END = 99


def moves_of(plan, jobs):
    done = [-1] * len(jobs)
    moves = {}
    for point in sorted(plan):
        moves[point] = []
        for index in plan[point]:
            moves[point].append((index, done[index]))
            done[index] += 1
    moves[END] = [
        (index, stage)
        for stage in range(-1, max(len(job.order) for job in jobs))
        for index, job in enumerate(jobs)
        if done[index] <= stage < len(job.order)
    ]
    return moves


def run_moves(moves, point, scatters):
    for index, stage in moves.get(point, ()):
        if stage < 0:
            scatters[index].start()
        else:
            scatters[index].add(stage)


def back_kernel(wide, blk, jobs, plan, *refs):
    refs = iter(refs)
    (
        images, image_own, texts, gain, shift, cross_closed, self_closed,
        q_cross, k_cross, v_cross, do_cross, lse_cross, delta_cross, wk_cross, wv_cross,
        q_self, k_self, v_self, lse_self, wq_self, wk_self, wv_self,
        w_query, w_gate, w_self, hidden, self_out, grad_mixed, grad_logit, joined, last_small,
    ) = (next(refs) for _ in range(31))
    early_expand, late_expand, early_reduce, late_reduce, d_cross_output = (
        next(refs) for _ in range(5)
    )
    joined_out, text_out, image_out, sums_out, last_out = (next(refs) for _ in range(5))
    outs = [next(refs) if job.ends else None for job in jobs]
    normed, dkv, dx, dq, gates, grad_hidden, self_do, self_delta = (next(refs) for _ in range(8))
    pages, keep, send, row_sums, sums_in, local = (next(refs) for _ in range(6))
    d_pairs, d_query, d_self_output, d_project, expand_both, reduce_both = (
        next(refs) for _ in range(6)
    )
    sources = [
        early_expand, late_expand, early_reduce, late_reduce, expand_both, reduce_both,
        d_pairs, d_query, d_cross_output, d_self_output,
    ] + [d_project] * (len(jobs) - 10)
    lands = [expand_both.at[0], expand_both.at[1], reduce_both.at[0], reduce_both.at[1]]
    lands += [None] * (len(jobs) - 4)
    step = pl.program_id(0)
    places = Places(wide, blk)
    names = bit_names(wide, blk)
    groups = group_bits(blk)
    scatters = [
        Scatter(places, job, source, refs, last)
        for job, source, last in zip(jobs, sources, lands)
    ]
    moves = moves_of(plan, jobs)
    home = Home(places, refs)
    image_rows = pl.ds(0, k_cross.shape[0] // 2)
    image = Rows(
        places, groups, keep.at[image_rows], send.at[image_rows], row_sums.at[image_rows], refs
    )
    text = Rows(places, groups, keep, send, row_sums, refs)
    image_pages = pages.at[:, pl.ds(0, IMAGE)]
    fetches = [
        pltpu.make_async_copy(images, image_pages, local.at[0]),
        pltpu.make_async_copy(texts, pages, local.at[1]),
        pltpu.make_async_copy(grad_mixed, grad_hidden, local.at[2]),
        pltpu.make_async_copy(w_self, normed.at[pl.ds(0, D)], local.at[3]),
    ]
    sums = Total(places, refs)
    last_sums = Total(places, refs)

    def pump(point):
        if point in (7, 9, 11):
            sums.add((point - 7) // 2, sums_out)
        if point == 7:
            image.add(0)
        if point == 10:
            for stage in range(1, len(groups)):
                image.add(stage)
            image.norm(image_own, gain[2:3, :], None)
        run_moves(moves, point, scatters)

    def pumps(points):
        for point in points:
            pl.when(step == (point - 1) // 2)(functools.partial(pump, point))

    @pl.when(step == 0)
    def _():
        fetches[0].start()
        fetches[2].start()
        greet(places, names, True, ((("w", 1), ("b", 0)), (("b", 2), ("b", 1))))
        pump(0)
        for turn in range(DOCS):
            home.put(turn, joined[turn])

    @pl.when(step < QUADS)
    def _():
        keys = k_cross.shape[0]
        rows = pl.ds(0, keys)
        my_normed, my_dkv, my_dx = normed.at[rows], dkv.at[rows], dx.at[rows]

        @pl.when(step == 0)
        def _():
            fetches[0].wait()
            normalize_pages(image_pages, gain[2:3, :], shift[2:3, :], my_normed)
            my_dx[...] = jnp.zeros(my_dx.shape, F32)

        cols = pl.ds(pl.multiple_of(step * QUAD, QUAD), QUAD)
        attend_backward(
            q_cross, k_cross, v_cross, do_cross, lse_cross, delta_cross, cross_closed,
            dq.at[:, cols], my_dkv, lambda: pumps((1, 3, 5)),
        )
        spread_back(my_dkv, wk_cross, wv_cross, my_dx)
        for part in range(2):
            value = transposed(my_dkv[:, part * QUAD : (part + 1) * QUAD], my_normed[...])
            value = value.astype(BF16)
            for at in range(QUADS):

                @pl.when(step == at)
                def _():
                    put_rows(d_pairs, part * D + at * QUAD, value)

        pumps((2, 4))

        @pl.when(step == QUADS - 1)
        def _():
            round_pages(my_dx, image.keep, image.send)
            image.start()
            image_gain, image_shift = page_sums(image_pages, my_dx)
            fetches[1].start()
            fetches[3].start()
            scaled, inverse = standardize(hidden[...])
            cross = (scaled * gain[1:2, :] + shift[1:2, :]).astype(BF16)
            grad_query = dq[...]
            put_rows(d_query, 0, transposed(grad_query, cross).astype(BF16))
            d_gate = transposed(grad_logit[...], cross.astype(F32), HIGHEST)[:H, :]
            gates[...] = jnp.zeros_like(gates)
            gates[0:H, :] = w_gate[...]
            upstream = against(grad_query, w_query[...]) + jnp.dot(
                grad_logit[...], gates[...].astype(F32), precision=HIGHEST
            )
            fetches[2].wait()
            grad = grad_hidden[...] + norm_back(upstream, scaled, inverse, gain[1:2, :])
            grad_hidden[...] = grad
            branch = grad.astype(BF16)
            put_rows(
                d_self_output, 0, transposed(branch, self_out[...].astype(BF16)).astype(BF16)
            )
            fetches[3].wait()
            grad_result = against(branch, normed[0:D, :]).astype(BF16)
            self_do[...] = grad_result
            self_delta[...] = head_rows(head_sums(grad_result.astype(F32) * self_out[...]))
            sums_in[0:H, :] = d_gate
            sums_in[H : H + 8, :] = last_small[...]
            sums_in[H + 8 : SUMS, :] = jnp.concatenate(
                [column_sum(upstream * scaled), column_sum(upstream), image_gain, image_shift],
                axis=0,
            )
            sums.start(sums_in[...])
            home.end(joined_out)
            pump(6)
            fetches[1].wait()
            normalize_pages(pages, gain[0:1, :], shift[0:1, :], normed)
            dx[...] = jnp.zeros(dx.shape, F32)

    @pl.when(step >= QUADS)
    def _():
        quad = step - QUADS
        cols = pl.ds(pl.multiple_of(quad * QUAD, QUAD), QUAD)
        my_dq = dq.at[:, cols]
        attend_backward(
            q_self, k_self, v_self, self_do.at[:, cols], lse_self,
            self_delta.at[pl.ds(pl.multiple_of(quad * 8, 8), 8)], self_closed,
            my_dq, dkv, lambda: pumps((7, 9, 11)),
        )
        spread_back(dkv, wk_self, wv_self, dx)
        dx[0:ROWS, :] += against(my_dq[...], wq_self[...])

        @pl.when(quad == QUADS - 1)
        def _():
            round_pages(dx, keep, send)
            text.start()

        for part in range(3):
            if part == 0:
                value = transposed(my_dq[...], normed[0:ROWS, :])
            else:
                value = transposed(dkv[:, (part - 1) * QUAD : part * QUAD], normed[...])
            value = value.astype(BF16)
            for at in range(QUADS):

                @pl.when(quad == at)
                def _():
                    put_rows(d_project, part * D + at * QUAD, value)

        pumps((8, 10))

        @pl.when(quad == QUADS - 1)
        def _():
            run_moves(moves, 12, scatters)
            for stage in range(len(groups) - 1):
                text.add(stage)
            gain_sum, shift_sum = page_sums(pages, dx)
            last_sums.start(jnp.concatenate([gain_sum, shift_sum, jnp.zeros((6, D), F32)], axis=0))
            run_moves(moves, 13, scatters)
            text.add(len(groups) - 1)
            text.norm(pages, gain[0:1, :], grad_hidden)
            last_sums.add(0, last_out)
            run_moves(moves, 14, scatters)
            run_moves(moves, 15, scatters)
            last_sums.add(1, last_out)
            run_moves(moves, 16, scatters)
            last_sums.add(2, last_out)
            run_moves(moves, 17, scatters)
            image.end(image_out)
            text.end(text_out)
            run_moves(moves, END, scatters)
            for scatter, out in zip(scatters, outs):
                scatter.end(out)


class Places:
    def __init__(self, wide, blk):
        self.wide = wide
        self.blk = blk
        self.part = blk // 4
        self.w = lax.axis_index("wide")
        self.b = lax.axis_index("blk")
        self.quarter = self.b // self.part
        self.turn = self.quarter % 2

    def bit(self, name):
        axis, bit = name
        return ((self.w if axis == "w" else self.b) // (1 << bit)) % 2

    def flip(self, name):
        axis, bit = name
        step = (1 << bit) * (1 - 2 * self.bit(name))
        return (self.w + step, self.b) if axis == "w" else (self.w, self.b + step)

    def flips(self, names, which):
        w, b = self.w, self.b
        for name, taken in zip(names, (which // 2, which % 2)):
            if taken:
                there = self.flip(name)
                w, b = w + there[0] - self.w, b + there[1] - self.b
        return w, b

    def index(self, names):
        return 2 * self.bit(names[0]) + self.bit(names[1])

    def swap(self, turn):
        core = self.w % 2
        turned = self.turn if turn == 0 else 1 - self.turn
        return (
            self.w - core + self.quarter // 2,
            (2 * core + turned) * self.part + self.b % self.part,
        )

    def swap_stays(self):
        return self.w % 2 == self.quarter // 2


def bit_names(wide, blk):
    return [("w", bit) for bit in range(wide.bit_length() - 1)] + [
        ("b", bit) for bit in range(blk.bit_length() - 1)
    ]


def group_bits(blk):
    return [("b", bit) for bit in range((blk // 4).bit_length() - 1)] + [("w", 0)]


def tile_bits(wide, blk):
    return (
        [("w", bit) for bit in range(wide.bit_length() - 2, 0, -1)]
        + [("b", bit) for bit in range(blk.bit_length() - 2, -1, -1)]
        + [("w", 0)]
    )


def remote(source, target, send, receive, device):
    return pltpu.make_async_remote_copy(
        src_ref=source,
        dst_ref=target,
        send_sem=send,
        recv_sem=receive,
        device_id=device,
        device_id_type=pl.DeviceIdType.MESH,
    )


def greet(places, names, swaps, pairs=()):
    barrier = pltpu.get_barrier_semaphore()
    devices = [places.flip(name) for name in names] + [places.flips(pair, 3) for pair in pairs]
    for device in devices:
        pl.semaphore_signal(
            barrier, inc=1, device_id=device, device_id_type=pl.DeviceIdType.MESH
        )
    count = len(devices)
    if swaps:
        pl.semaphore_signal(
            barrier, inc=1, device_id=places.swap(1), device_id_type=pl.DeviceIdType.MESH
        )

        @pl.when(jnp.logical_not(places.swap_stays()))
        def _():
            pl.semaphore_signal(
                barrier, inc=1, device_id=places.swap(0), device_id_type=pl.DeviceIdType.MESH
            )

        count = count + 2 - places.swap_stays().astype(jnp.int32)
    pl.semaphore_wait(barrier, count)


class Job(NamedTuple):
    left: tuple
    order: tuple
    start: int
    rows: int
    lanes: int
    ends: bool
    near: bool = False
    inner: bool = False

    def after(self):
        return tuple(name for name in self.left if name not in self.order)

    def scratch(self):
        count = len(self.left)
        kinds = []
        if not self.near:
            kinds.append(pltpu.VMEM((2,) * (count - 1) + (self.rows, self.lanes), BF16))
        for stage in range(len(self.order) - int(self.inner)):
            kinds.append(pltpu.VMEM((2,) * (count - 1 - stage) + (self.rows, self.lanes), BF16))
        if self.ends:
            kinds.append(pltpu.VMEM((2, self.rows, self.lanes // 2), BF16))
        waits = len(self.order) + int(self.ends)
        return kinds + [pltpu.SemaphoreType.DMA((waits,))] * 2 + [pltpu.SemaphoreType.DMA]

    def result(self):
        return shaped((2, self.rows, self.lanes // 2), BF16)


def bits_of(index, count):
    return tuple((index // (1 << (count - 1 - place))) % 2 for place in range(count))


def add_blocks(target, source):
    lead = len(target.shape) - 2
    if lead == 0:
        target[...] = target[...] + source[...]
        return

    def block(index, carry):
        at = bits_of(index, lead)
        target[at] = target[at] + source[at]
        return carry

    lax.fori_loop(0, 1 << lead, block, 0)


class Scatter:
    def __init__(self, places, job, source, scratch, last=None):
        self.places = places
        self.job = job
        self.source = source
        self.own = None if job.near else next(scratch)
        self.got = [next(scratch) for _ in range(len(job.order) - int(job.inner))]
        if job.inner:
            self.got.append(last)
        self.ends = next(scratch) if job.ends else None
        self.sends, self.receives, self.local = next(scratch), next(scratch), next(scratch)
        self.stages = len(job.order)
        self.axes = []
        left = list(job.left)
        for name in job.order:
            self.axes.append(left.index(name))
            left.remove(name)

    def cut(self, ref, stage, index):
        axis = self.axes[stage]
        at = (slice(None),) * axis + (index,)
        if ref.shape[-2] != self.job.rows:
            at += (slice(None),) * (len(ref.shape) - 3 - axis)
            at += (pl.ds(self.job.start, self.job.rows), slice(None))
        return ref.at[at]

    def copy(self, stage):
        if stage == self.stages:
            source, target, name = self.ends.at[0], self.ends.at[1], ("w", 0)
        else:
            name = self.job.order[stage]
            source = self.source if stage == 0 else self.got[stage - 1]
            source = self.cut(source, stage, 1 - self.places.bit(name))
            target = self.got[stage]
        return remote(
            source, target, self.sends.at[stage], self.receives.at[stage], self.places.flip(name)
        )

    def fetch(self):
        kept = self.cut(self.source, 0, self.places.bit(self.job.order[0]))
        return pltpu.make_async_copy(kept, self.own, self.local)

    def start(self):
        self.copy(0).start()
        if not self.job.near:
            self.fetch().start()

    def halve(self):
        lanes = self.job.lanes // 2
        piece = self.got[-1][...]
        second = self.places.bit(("w", 0)) == 1
        self.ends[0] = jnp.where(second, piece[:, :lanes], piece[:, lanes:])

    def add(self, stage):
        self.copy(stage).wait_recv()
        if stage == 0 and not self.job.near:
            self.fetch().wait()
            source = self.own
        else:
            bit = self.places.bit(self.job.order[stage])
            source = self.cut(self.source if stage == 0 else self.got[stage - 1], stage, bit)
        add_blocks(self.got[stage], source)
        if stage + 1 < self.stages:
            self.copy(stage + 1).start()
        elif self.job.ends:
            self.halve()
            self.copy(stage + 1).start()

    def end(self, out):
        for stage in range(self.stages + int(self.job.ends)):
            self.copy(stage).wait_send()
        if not self.job.ends:
            return
        self.copy(self.stages).wait_recv()
        lanes = self.job.lanes // 2
        piece = self.got[-1][...]
        other = self.ends[1]
        second = self.places.bit(("w", 0)) == 1
        mine = jnp.where(second, piece[:, lanes:], piece[:, :lanes])
        out[0] = jnp.where(second, other, mine)
        out[1] = jnp.where(second, mine, other)


class Home:
    def __init__(self, places, scratch):
        self.places = places
        self.home, self.landed, self.sends, self.receives, self.local = (
            next(scratch) for _ in range(5)
        )

    @staticmethod
    def scratch():
        waits = [pltpu.SemaphoreType.DMA((DOCS,))] * 2 + [pltpu.SemaphoreType.DMA]
        return [pltpu.VMEM((DOCS, PAGE, D), BF16)] * 2 + waits

    def copy(self, turn):
        return remote(
            self.home.at[turn], self.landed.at[self.places.turn], self.sends.at[turn],
            self.receives.at[turn], self.places.swap(turn),
        )

    def go(self, turn, begin):
        def carry():
            if begin:
                self.copy(turn).start()
            else:
                self.copy(turn).wait()

        if turn > 0:
            carry()
            return
        stays = self.places.swap_stays()
        pl.when(jnp.logical_not(stays))(carry)
        if begin:

            @pl.when(stays)
            def _():
                self.landed[self.places.turn] = self.home[turn]

    def put(self, turn, page):
        self.home[turn] = page
        self.go(turn, True)

    def end(self, out):
        for turn in range(DOCS):
            self.go(turn, False)
        copy = pltpu.make_async_copy(self.landed, out, self.local)
        copy.start()
        copy.wait()


class Rows:
    def __init__(self, places, names, keep, send, sums, scratch):
        self.places = places
        self.size = keep.shape[0] // (DOCS << (len(names) - 1))
        self.names = list(reversed(names))
        self.keep = keep
        self.send = send
        self.sums = sums
        self.got = [next(scratch) for _ in names]
        self.sends, self.receives = next(scratch), next(scratch)
        self.back = Home(places, scratch)

    @staticmethod
    def scratch(names, rows):
        kinds = [pltpu.VMEM((rows >> stage, D), BF16) for stage in range(len(names))]
        return kinds + [pltpu.SemaphoreType.DMA((len(names),))] * 2 + Home.scratch()

    def copy(self, stage):
        source = self.send if stage == 0 else self.sums
        rows = self.got[stage].shape[0]
        if stage > 0:
            source = source.at[pl.ds(rows, rows)]
        return remote(
            source, self.got[stage], self.sends.at[stage], self.receives.at[stage],
            self.places.flip(self.names[stage]),
        )

    def start(self):
        self.copy(0).start()

    def add(self, stage):
        self.copy(stage).wait()
        source = self.keep if stage == 0 else self.sums
        rows = self.got[stage].shape[0]

        def block(index, carry):
            at = pl.ds(pl.multiple_of(index * self.size, 16), self.size)
            self.sums[at, :] = source[at, :] + self.got[stage][at, :]
            return carry

        lax.fori_loop(0, rows // self.size, block, 0)
        if stage + 1 < len(self.names):
            self.copy(stage + 1).start()

    def norm(self, pages, gain, added):
        for turn in range(DOCS):
            rows = slice(turn * self.size, (turn + 1) * self.size)
            scaled, inverse = standardize(pages[turn].astype(F32))
            grad = norm_back(self.sums[rows, :].astype(F32), scaled, inverse, gain)
            if added is not None:
                grad = grad + added[rows, :]
            if self.size < PAGE:
                rest = jnp.zeros((PAGE - self.size, D), F32)
                grad = jnp.concatenate([grad, rest], axis=0)
            self.back.put(turn, grad.astype(BF16))

    def end(self, out):
        self.back.end(out)


class Total:
    ROUNDS = 3

    def __init__(self, places, scratch):
        self.places = places
        self.chip, self.plane, self.line, self.sends, self.receives = (
            next(scratch) for _ in range(5)
        )

    @staticmethod
    def scratch(rows):
        return [
            pltpu.VMEM((2, rows, D), F32),
            pltpu.VMEM((4, rows, D), F32),
            pltpu.VMEM((4, rows, D), F32),
            pltpu.SemaphoreType.DMA((7,)),
            pltpu.SemaphoreType.DMA((7,)),
        ]

    def copies(self, stage):
        if stage == 0:
            return [
                remote(
                    self.chip.at[0], self.chip.at[1], self.sends.at[0], self.receives.at[0],
                    self.places.flip(("w", 0)),
                )
            ]
        names = (("w", 1), ("b", 0)) if stage == 1 else (("b", 2), ("b", 1))
        slots = self.plane if stage == 1 else self.line
        mine = slots.at[self.places.index(names)]
        found = []
        for which in range(1, 4):
            at = 3 * stage - 3 + which
            found.append(
                remote(
                    mine, mine, self.sends.at[at], self.receives.at[at],
                    self.places.flips(names, which),
                )
            )
        return found

    def start(self, value):
        self.chip[0] = value
        self.copies(0)[0].start()

    def add(self, stage, out):
        for copy in self.copies(stage):
            copy.wait()
        if stage == 0:
            value = self.chip[0] + self.chip[1]
            self.plane[self.places.index((("w", 1), ("b", 0)))] = value
        else:
            slots = self.plane if stage == 1 else self.line
            value = (slots[0] + slots[1]) + (slots[2] + slots[3])
            if stage == 1:
                self.line[self.places.index((("b", 2), ("b", 1)))] = value
        if stage + 1 < self.ROUNDS:
            for copy in self.copies(stage + 1):
                copy.start()
        else:
            out[...] = value


def finish_kernel(layout, *refs):
    refs = iter(refs)
    pieces = [[next(refs) for _ in range(count)] for count in layout]
    streams = [next(refs) for _ in range(3)]
    sums, last_sums = next(refs), next(refs)
    for index, parts in enumerate(pieces):
        out = next(refs)
        halves = [part[half] for half in range(2) for part in parts]
        value = jnp.concatenate(halves, axis=0).astype(F32)
        out[...] = value if index + 1 == len(pieces) else jnp.transpose(value)
    for stream in streams:
        out = next(refs)
        out[...] = stream[...]
    gate, bias, last, gains, shifts = (next(refs) for _ in range(5))
    gate[...] = sums[0:H, :]
    for index in range(FF // D):
        bias[pl.ds(index * D, D)] = sums[H + 4 + index, :]
    last[...] = sums[H, :]
    for out, at in ((gains, 0), (shifts, 1)):
        out[0:1, :] = last_sums[at : at + 1, :]
        for index, row in enumerate((H + 8 + at, H + 10 + at, H + 1 + at)):
            out[index + 1 : index + 2, :] = sums[row : row + 1, :]


def whole(shape):
    return pl.BlockSpec(shape, lambda step: (0,) * len(shape))


def columns(rows, offset=0):
    return pl.BlockSpec((rows, QUAD), lambda step: (0, offset + step))


def stat_rows():
    return pl.BlockSpec((8, ROWS), lambda step: (step, 0))


def shaped(shape, kind):
    return jax.ShapeDtypeStruct(shape, kind)


ANY = pl.BlockSpec(memory_space=pl.ANY)


def call(kernel, name, steps, ins, outs, scratch, flops, byte_count, collective=None):
    in_specs, operands = zip(*ins)
    out_specs, out_shapes = zip(*outs)
    return pl.pallas_call(
        kernel,
        grid=(steps,),
        in_specs=list(in_specs),
        out_specs=list(out_specs),
        out_shape=list(out_shapes),
        scratch_shapes=scratch,
        name=name,
        compiler_params=pltpu.CompilerParams(
            vmem_limit_bytes=VMEM_LIMIT,
            collective_id=collective,
            has_side_effects=collective is not None,
        ),
        cost_estimate=pl.CostEstimate(flops=flops, bytes_accessed=byte_count, transcendentals=0),
    )(*operands)


def own_pages(pages):
    return (whole((DOCS, *pages.shape[1:])), pages)


SMEM = pl.BlockSpec(memory_space=pltpu.SMEM)


def self_forward(texts, images, cots, mask, regions, doc_pages, gain, shift, project, wide, blk):
    groups = group_bits(blk)
    count = DOCS << len(groups)
    keys = count * PAGE
    return call(
        functools.partial(self_forward_kernel, wide, blk),
        "self_forward",
        QUADS,
        [
            (whole(regions.shape), regions),
            (SMEM, doc_pages),
            (whole(texts.shape), texts),
            (whole(images.shape), images),
            (whole(cots.shape), cots),
            (whole(mask.shape), mask),
            (whole(gain.shape), gain),
            (whole(shift.shape), shift),
            (columns(D), project),
            (columns(D, QUADS), project),
            (columns(D, 2 * QUADS), project),
        ],
        [
            (columns(ROWS), shaped((ROWS, D), F32)),
            (stat_rows(), shaped((8 * QUADS, ROWS), F32)),
            (columns(ROWS), shaped((ROWS, D), BF16)),
            (columns(keys), shaped((keys, D), BF16)),
            (columns(keys), shaped((keys, D), BF16)),
            (ANY, shaped((count, PAGE, D), BF16)),
            (ANY, shaped((count, IMAGE, D), BF16)),
            (ANY, shaped((DOCS, PAGE, D), BF16)),
            (whole((keys, PAIR)), shaped((keys, PAIR), BF16)),
            (whole((count * IMAGE, PAIR)), shaped((count * IMAGE, PAIR), BF16)),
        ],
        [
            pltpu.VMEM((keys, D), BF16),
            pltpu.VMEM((DOCS, PAGE + EXTRA, D), BF16),
            pltpu.VMEM((DOCS, IMAGE + EXTRA, D), BF16),
            pltpu.VMEM((count, PAGE + EXTRA, D), BF16),
            pltpu.VMEM((count, IMAGE + EXTRA, D), BF16),
            pltpu.VMEM((DOCS, PAGE, D), BF16),
        ]
        + Gather.waits(groups) * 2
        + Gather.waits([])
        + [pltpu.SemaphoreType.DMA((3,))],
        6 * 10**9,
        12 * 10**6,
        0,
    )


def cross_forward(texts, pages, self_out, w_self, w_gate, gain, shift, closed, w_query, w_pairs):
    keys = closed.shape[0]
    return call(
        cross_forward_kernel,
        "cross_forward",
        QUADS,
        [
            own_pages(texts),
            (whole(pages.shape), pages),
            (whole(self_out.shape), self_out),
            (whole(w_self.shape), w_self),
            (whole(w_gate.shape), w_gate),
            (whole(gain.shape), gain),
            (whole(shift.shape), shift),
            (whole(closed.shape), closed),
            (columns(D), w_query),
            (columns(D), w_pairs),
            (columns(D, QUADS), w_pairs),
        ],
        [
            (whole((ROWS, D)), shaped((ROWS, D), F32)),
            (whole((ROWS, PAIR)), shaped((ROWS, PAIR), F32)),
            (columns(ROWS), shaped((ROWS, D), F32)),
            (stat_rows(), shaped((8 * QUADS, ROWS), F32)),
            (columns(ROWS), shaped((ROWS, D), BF16)),
            (columns(keys), shaped((keys, D), BF16)),
            (columns(keys), shaped((keys, D), BF16)),
        ],
        [
            pltpu.VMEM((keys, D), BF16),
            pltpu.VMEM((ROWS, D), BF16),
            pltpu.VMEM((PAIR, D), BF16),
        ],
        7 * 10**9,
        14 * 10**6,
    )


def forward_back(
    hidden, raw, gate, cots, w_out, gain, shift, w_expand, b_expand, w_reduce, b_reduce, wide, blk
):
    steps = FF // D
    names = tile_bits(wide, blk)
    small = (D // (2 * blk), D // (wide // 2))
    expand = (FF // (2 * blk), D // (wide // 2))
    reduce = (D // (2 * blk), FF // (wide // 2))
    full, part, half, less = ((2,) * (len(names) - gone) for gone in range(4))
    return call(
        functools.partial(forward_back_kernel, steps, wide, blk),
        "forward_back",
        steps,
        [
            (whole((ROWS, D)), hidden),
            (whole((ROWS, D)), raw),
            (whole((ROWS, PAIR)), gate),
            (whole((DOCS, PAGE, D)), cots),
            (whole((D, D)), w_out),
            (whole(gain.shape), gain),
            (whole(shift.shape), shift),
            (pl.BlockSpec((D, D), lambda step: (0, step)), w_expand),
            (pl.BlockSpec((1, D), lambda step: (0, step)), b_expand),
            (pl.BlockSpec((D, D), lambda step: (step, 0)), w_reduce),
            (whole((D,)), b_reduce),
        ],
        [
            (whole((DOCS, PAGE, D)), shaped((DOCS, PAGE, D), BF16)),
            (ANY, shaped(less + expand, BF16)),
            (ANY, shaped(half + expand, BF16)),
            (ANY, shaped(less + reduce, BF16)),
            (ANY, shaped(half + reduce, BF16)),
            (whole(full + small), shaped(full + small, BF16)),
            (whole((ROWS, D)), shaped((ROWS, D), F32)),
            (whole((ROWS, D)), shaped((ROWS, D), BF16)),
            (whole((8 * QUADS, ROWS)), shaped((8 * QUADS, ROWS), F32)),
            (whole((ROWS, PAIR)), shaped((ROWS, PAIR), F32)),
            (whole((8, D)), shaped((8, D), F32)),
        ],
        [
            pltpu.VMEM((ROWS, D), BF16),
            pltpu.VMEM((ROWS, D), F32),
            pltpu.VMEM((ROWS, D), BF16),
            pltpu.VMEM((ROWS, D), BF16),
            pltpu.VMEM((ROWS, D), F32),
            pltpu.VMEM((ROWS, D), F32),
            pltpu.VMEM(full + expand, BF16),
            pltpu.VMEM(full + reduce, BF16),
            pltpu.VMEM(part + expand, BF16),
            pltpu.VMEM(part + reduce, BF16),
            pltpu.VMEM(less + expand, BF16),
            pltpu.VMEM(less + reduce, BF16),
            pltpu.SemaphoreType.DMA((2, steps)),
            pltpu.SemaphoreType.DMA((2, steps)),
            pltpu.SemaphoreType.DMA((2, steps // 2)),
            pltpu.SemaphoreType.DMA((2, steps // 2)),
            pltpu.SemaphoreType.DMA((4,)),
        ],
        8 * 10**9,
        25 * 10**6,
        1,
    )


def back(
    cross, own, images, texts, gain, shift, closed, w_pairs, project, w_query, w_gate, w_self,
    hidden, self_out, grad_mixed, grad_logit, joined, last_small, far_sources, jobs, plan, wide, blk,
):
    q_cross, k_cross, v_cross, do_cross, lse_cross, delta_cross = cross
    q_self, k_self, v_self, lse_self = own
    cross_keys, self_keys = k_cross.shape[0], k_self.shape[0]
    names = bit_names(wide, blk)
    groups = group_bits(blk)
    tile = (2,) * len(tile_bits(wide, blk))
    lanes = 2 * D // wide
    stream = shaped((DOCS, PAGE, D), BF16)

    def fixed(array):
        count = len(array.shape)
        spec = pl.BlockSpec(
            array.shape, lambda step: (0,) * count, pipeline_mode=pl.Buffered(buffer_count=1)
        )
        return (spec, array)

    def early(array, rows, offset=0):
        last = QUADS - 1
        return (
            pl.BlockSpec(
                (rows, QUAD), lambda step: (0, offset + step - step // QUADS * (step - last))
            ),
            array,
        )

    def late(array, rows, offset=0):
        return (
            pl.BlockSpec((rows, QUAD), lambda step: (0, offset + step // QUADS * (step - QUADS))),
            array,
        )

    def early_rows(array):
        last = QUADS - 1
        return (
            pl.BlockSpec((8, ROWS), lambda step: (step - step // QUADS * (step - last), 0)), array
        )

    def late_rows(array):
        return (pl.BlockSpec((8, ROWS), lambda step: (step // QUADS * (step - QUADS), 0)), array)

    def tiles(columns_here):
        return pltpu.VMEM(tile + (columns_here // (2 * blk), lanes), BF16)

    def both(job):
        return pltpu.VMEM((2,) * (1 + len(job.after())) + (job.rows, job.lanes), BF16)

    image_rows, text_rows = cross_keys // 2, self_keys // 2
    return call(
        functools.partial(back_kernel, wide, blk, jobs, plan),
        "back",
        2 * QUADS,
        [
            (ANY, images),
            own_pages(images),
            (ANY, texts),
            fixed(gain),
            fixed(shift),
            fixed(closed[0]),
            fixed(closed[1]),
            early(q_cross, ROWS),
            early(k_cross, cross_keys),
            early(v_cross, cross_keys),
            early(do_cross, ROWS),
            early_rows(lse_cross),
            early_rows(delta_cross),
            early(w_pairs, D),
            early(w_pairs, D, QUADS),
            late(q_self, ROWS),
            late(k_self, self_keys),
            late(v_self, self_keys),
            late_rows(lse_self),
            late(project, D),
            late(project, D, QUADS),
            late(project, D, 2 * QUADS),
            fixed(w_query),
            fixed(w_gate),
            (ANY, w_self),
            fixed(hidden),
            fixed(self_out),
            (ANY, grad_mixed),
            fixed(grad_logit),
            fixed(joined),
            fixed(last_small),
        ]
        + [(ANY, source) for source in far_sources],
        [(ANY, stream)] * 3
        + [(whole((SUMS, D)), shaped((SUMS, D), F32)), (whole((8, D)), shaped((8, D), F32))]
        + [(whole(job.result().shape), job.result()) for job in jobs if job.ends],
        [
            pltpu.VMEM((self_keys, D), BF16),
            pltpu.VMEM((self_keys, 2 * QUAD), BF16),
            pltpu.VMEM((self_keys, D), F32),
            pltpu.VMEM((ROWS, D), BF16),
            pltpu.VMEM((PAIR, D), BF16),
            pltpu.VMEM((ROWS, D), F32),
            pltpu.VMEM((ROWS, D), BF16),
            pltpu.VMEM((8 * QUADS, ROWS), F32),
            pltpu.VMEM(texts.shape, BF16),
            pltpu.VMEM((text_rows, D), BF16),
            pltpu.VMEM((text_rows, D), BF16),
            pltpu.VMEM((text_rows, D), BF16),
            pltpu.VMEM((SUMS, D), F32),
            pltpu.SemaphoreType.DMA((4,)),
            tiles(2 * D),
            tiles(D),
            tiles(D),
            tiles(3 * D),
            both(jobs[0]),
            both(jobs[2]),
        ]
        + [kind for job in jobs for kind in job.scratch()]
        + Home.scratch()
        + Rows.scratch(groups, image_rows)
        + Rows.scratch(groups, text_rows)
        + Total.scratch(SUMS)
        + Total.scratch(8),
        23 * 10**9,
        30 * 10**6,
        2,
    )


def finish(pieces, streams, sums, last_sums):
    vmem = pl.BlockSpec(memory_space=pltpu.VMEM)
    operands = [part for parts in pieces for part in parts] + [*streams, sums, last_sums]
    results = []
    for index, parts in enumerate(pieces):
        shape = (parts[0].shape[2], sum(2 * part.shape[1] for part in parts))
        results.append(shaped(shape[::-1] if index + 1 == len(pieces) else shape, F32))
    results += [shaped(stream.shape, BF16) for stream in streams]
    results += [shaped((H, D), F32), shaped((FF,), F32), shaped((D,), F32)]
    results += [shaped((4, D), F32)] * 2
    return pl.pallas_call(
        functools.partial(finish_kernel, tuple(len(parts) for parts in pieces)),
        in_specs=[vmem] * len(operands),
        out_specs=[vmem] * len(results),
        out_shape=results,
        name="finish",
        compiler_params=pltpu.CompilerParams(vmem_limit_bytes=VMEM_LIMIT),
        cost_estimate=pl.CostEstimate(flops=10**6, bytes_accessed=5 * 10**6, transcendentals=0),
    )(*operands)


def body(
    text_blocks,
    image_blocks,
    cotangent,
    text_mask,
    page_regions,
    doc_pages,
    self_project,
    self_output,
    cross_query,
    cross_pairs,
    cross_output,
    gate_weight,
    expand_weight,
    expand_bias,
    reduce_weight,
    reduce_bias,
    norm_gain,
    norm_bias,
):
    wide = lax.axis_size("wide")
    blk = lax.axis_size("blk")
    names = tuple(tile_bits(wide, blk))
    share = 2 * blk
    lanes = 2 * D // wide
    far = 2 * FF // wide
    gate_rows = jnp.transpose(gate_weight)

    (
        self_out, self_lse, self_q, self_k, self_v, text_pages, image_pages, cots, text_closed,
        image_closed,
    ) = self_forward(
        text_blocks, image_blocks, cotangent, text_mask, jnp.transpose(page_regions), doc_pages, norm_gain,
        norm_bias, self_project, wide, blk,
    )
    hidden, gate, raw, cross_lse, cross_q, cross_k, cross_v = cross_forward(
        text_pages, image_pages, self_out, self_output, gate_rows, norm_gain, norm_bias,
        image_closed, cross_query, cross_pairs,
    )
    (
        joined, *partial, d_cross_output, grad_mixed, grad_raw, cross_delta,
        grad_logit, small_last,
    ) = forward_back(
        hidden, raw, gate, cots, cross_output, norm_gain, norm_bias, expand_weight,
        expand_bias.reshape(1, FF), reduce_weight, reduce_bias, wide, blk,
    )

    core, y, x, z, far_z = ("w", 0), ("w", 1), ("b", 0), ("b", 1), ("b", 2)
    ends = {"ends": True, "near": True}
    expand_shape = (0, FF // share, lanes)
    reduce_shape = (0, D // share, far)
    one = (0, D // share, lanes)
    rows = 3 * D // share
    split = 80
    jobs = (
        Job((z, x), (z,), *expand_shape, False, inner=True),
        Job((y, z, x), (y, z), *expand_shape, False, inner=True),
        Job((far_z, z), (z,), *reduce_shape, False, inner=True),
        Job((far_z, z, x), (x, z), *reduce_shape, False, inner=True),
        Job((far_z, x), (far_z, x), *expand_shape, **ends),
        Job((y, far_z), (y, far_z), *reduce_shape, **ends),
        Job(names, (core, x, y, z, far_z), 0, 2 * D // share, lanes, **ends),
        Job(names, (core, y, x, z, far_z), *one, **ends),
        Job(names, (core, y, x, z, far_z), *one, True),
        Job(names, (core, y, x, z, far_z), *one, **ends),
        Job(names, (core, y, x, z, far_z), 0, split, lanes, **ends),
        Job(names, (core, z, y, x, far_z), split, rows - split, lanes, **ends),
    )
    plan = {
        0: (1, 3, 0, 2,),
        4: (1, 3, 0, 2,),
        6: (6, 7, 8, 9,),
        7: (7, 8, 9,),
        8: (1, 3,),
        9: (4, 6, 5,),
        12: (10, 11,),
        13: (10, 11, 7, 8, 9, 5,),
        14: (4, 6,),
        15: (10, 11,),
        16: (7, 8, 9, 6, 10, 11,),
        17: (7, 8, 9, 6, 10, 11,),
    }
    joined_home, text_home, image_home, sums, last_sums, *pieces = back(
        (cross_q, cross_k, cross_v, grad_raw, cross_lse, cross_delta),
        (self_q, self_k, self_v, self_lse),
        image_pages, text_pages, norm_gain, norm_bias, (image_closed, text_closed), cross_pairs,
        self_project, cross_query, gate_rows, self_output, hidden, self_out, grad_mixed,
        grad_logit, joined, small_last, (*partial, d_cross_output), jobs, plan, wide, blk,
    )
    expand_piece, reduce_piece, *cross_pieces = pieces[:6]
    project_pieces = pieces[6:]
    (
        grad_cross_pairs, grad_cross_query, grad_cross_output, grad_self_output,
        grad_expand_weight, grad_self_project, grad_reduce_weight,
        joined_blocks, text_grad, image_grad,
        grad_gate_weight, grad_expand_bias, grad_reduce_bias, gains, shifts,
    ) = finish(
        [[piece] for piece in cross_pieces] + [[expand_piece], project_pieces, [reduce_piece]],
        [joined_home, text_home, image_home], sums, last_sums,
    )
    return (
        joined_blocks,
        text_grad,
        image_grad,
        grad_self_project,
        grad_self_output,
        grad_cross_query,
        grad_cross_pairs,
        grad_cross_output,
        grad_expand_weight,
        jnp.transpose(grad_reduce_weight),
        jnp.transpose(grad_gate_weight),
        grad_expand_bias,
        grad_reduce_bias,
        gains,
        shifts,
    )


def normalize(values, gains, biases):
    scaled, inverse = standardize(values)
    return (scaled * gains + biases, scaled, inverse)


def normalize_back(upstream, scaled, inverse, gains):
    result = norm_back(upstream, scaled, inverse, gains)
    return (result, jnp.sum(upstream * scaled, axis=0), jnp.sum(upstream, axis=0))


def gelu_tanh(values):
    return jax.nn.gelu(values, approximate=True)


def forward_doc(queries, carried, key_pairs, allowed, scaling):
    running_max, summed, accumulated = carried
    key_count = key_pairs.shape[0]
    keys_part = key_pairs[:, :D].reshape(key_count, H, HD)
    values_part = key_pairs[:, D:].reshape(key_count, H, HD)
    open_keys = (allowed > 0)[None, None, :]
    scores = (
        jnp.einsum("qhd,khd->hqk", queries, keys_part, preferred_element_type=F32) * scaling
    )
    scores = jnp.where(open_keys, scores, NEGATIVE)
    new_max = jnp.maximum(running_max, jnp.max(scores, axis=-1))
    fading = jnp.exp(running_max - new_max)
    weights = jnp.where(open_keys, jnp.exp(scores - new_max[..., None]), 0.0)
    summed = summed * fading + jnp.sum(weights, axis=-1)
    accumulated = accumulated * fading[..., None] + jnp.einsum(
        "hqk,khd->hqd",
        weights.astype(BF16),
        values_part,
        preferred_element_type=F32,
    )
    return (new_max, summed, accumulated)


def forward_fold(queries, scaling, carried, pieces):
    key_pairs, allowed = pieces

    def forward_per_doc(doc_items):
        doc_queries, doc_max, doc_sum, doc_acc, doc_pairs, doc_allowed = doc_items
        doc_carry = (doc_max, doc_sum, doc_acc)
        result = forward_doc(doc_queries, doc_carry, doc_pairs, doc_allowed, scaling)
        return result

    return lax.map(
        forward_per_doc, (queries, carried[0], carried[1], carried[2], key_pairs, allowed)
    )


def backward_doc(queries, grad_out, log_sum, row_delta, key_pairs, allowed, scaling):
    key_count = key_pairs.shape[0]
    keys_part = key_pairs[:, :D].reshape(key_count, H, HD)
    values_part = key_pairs[:, D:].reshape(key_count, H, HD)
    open_keys = (allowed > 0)[None, None, :]
    scores = (
        jnp.einsum("qhd,khd->hqk", queries, keys_part, preferred_element_type=F32) * scaling
    )
    probabilities = jnp.where(open_keys, jnp.exp(scores - log_sum[..., None]), 0.0)
    grad_probs = jnp.einsum(
        "qhd,khd->hqk", grad_out, values_part, preferred_element_type=F32
    )
    grad_scores = (probabilities * (grad_probs - row_delta[..., None])).astype(BF16)
    query_grad = (
        jnp.einsum("hqk,khd->qhd", grad_scores, keys_part, preferred_element_type=F32)
        * scaling
    )
    key_grad = (
        jnp.einsum("hqk,qhd->khd", grad_scores, queries, preferred_element_type=F32)
        * scaling
    )
    value_grad = jnp.einsum(
        "hqk,qhd->khd",
        probabilities.astype(BF16),
        grad_out,
        preferred_element_type=F32,
    )
    return (
        query_grad,
        jnp.concatenate(
            [key_grad.reshape(key_count, D), value_grad.reshape(key_count, D)], axis=-1
        ),
    )


def backward_fold(queries, grad_out, log_sum, row_delta, scaling, pieces):
    key_pairs, allowed = pieces

    def backward_per_doc(doc_items):
        doc_queries, doc_grad, doc_log, doc_delta, doc_pairs, doc_allowed = doc_items
        result = backward_doc(
            doc_queries, doc_grad, doc_log, doc_delta, doc_pairs, doc_allowed, scaling
        )
        return result

    query_parts, pair_parts = lax.map(
        backward_per_doc, (queries, grad_out, log_sum, row_delta, key_pairs, allowed)
    )
    return (query_parts, pair_parts)


def start_state():
    return (
        jnp.full((DOCS, H, PAGE), NEGATIVE, F32),
        jnp.zeros((DOCS, H, PAGE), F32),
        jnp.zeros((DOCS, H, PAGE, HD), F32),
    )


def finish_state(state):
    running_max, summed, accumulated = state
    result = jnp.transpose(accumulated / summed[..., None], (0, 2, 1, 3))
    return (result, running_max + jnp.log(summed))


def tile_order(grad, wide_count, blk_count):
    rows, cols = grad.shape
    tiled = grad.reshape(wide_count, rows // wide_count, blk_count, cols // blk_count)
    return jnp.transpose(tiled, (0, 2, 1, 3)).reshape(
        wide_count * blk_count * (rows // wide_count), cols // blk_count
    )


def plain_body(
    text_blocks,
    image_blocks,
    cotangent,
    text_mask,
    page_regions,
    doc_pages,
    self_project,
    self_output,
    cross_query,
    cross_pairs,
    cross_output,
    gate_weight,
    expand_weight,
    expand_bias,
    reduce_weight,
    reduce_bias,
    norm_gain,
    norm_bias,
):
    scaling = HD ** (-0.5)
    block_shape = text_blocks.shape
    offsets = jnp.arange(PAGE, dtype=jnp.int32)
    living = (lax.axis_index("blk") < doc_pages)[:, None]
    text_open = (living & ((text_mask > 0) | (offsets[None, :] == 0))).astype(BF16)
    image_open = (living & (offsets[None, :] < page_regions)).astype(BF16)
    text_rows = text_blocks.reshape(-1, D).astype(F32)
    image_rows = image_blocks.reshape(-1, D).astype(F32)
    normed_text, scaled_first, inverse_first = normalize(text_rows, norm_gain[0], norm_bias[0])
    normed_low = normed_text.astype(BF16)
    triples = product(normed_low, self_project).astype(BF16)
    self_queries = triples[:, :D].reshape(DOCS, PAGE, H, HD)
    self_pairs = triples[:, D:].reshape(DOCS, PAGE, 2 * D)
    self_state = forward_fold(
        self_queries,
        scaling,
        start_state(),
        (
            lax.all_gather(self_pairs, "blk", axis=1, tiled=True),
            lax.all_gather(text_open, "blk", axis=1, tiled=True),
        ),
    )
    self_result, self_logsum = finish_state(self_state)
    self_low = self_result.reshape(-1, D).astype(BF16)
    hidden = text_rows + product(self_low, self_output)
    cross_normed, scaled_cross, inverse_cross = normalize(hidden, norm_gain[1], norm_bias[1])
    cross_low = cross_normed.astype(BF16)
    gate_values = jax.nn.sigmoid(product(cross_low, gate_weight))
    image_normed, scaled_image, inverse_image = normalize(image_rows, norm_gain[2], norm_bias[2])
    image_low = image_normed.astype(BF16)
    image_pairs = product(image_low, cross_pairs).astype(BF16).reshape(DOCS, PAGE, 2 * D)
    cross_queries = product(cross_low, cross_query).astype(BF16).reshape(DOCS, PAGE, H, HD)
    cross_state = forward_fold(
        cross_queries,
        scaling,
        start_state(),
        (
            lax.all_gather(image_pairs, "blk", axis=1, tiled=True),
            lax.all_gather(image_open, "blk", axis=1, tiled=True),
        ),
    )
    cross_result, cross_logsum = finish_state(cross_state)
    gate_heads = gate_values.reshape(DOCS, PAGE, H, 1)
    gated_low = (cross_result * gate_heads).reshape(-1, D).astype(BF16)
    mixed_rows = hidden + product(gated_low, cross_output)
    final_normed, scaled_final, inverse_final = normalize(mixed_rows, norm_gain[3], norm_bias[3])
    final_low = final_normed.astype(BF16)
    inner_rows = product(final_low, expand_weight) + expand_bias
    active_low = gelu_tanh(inner_rows).astype(BF16)
    joined_blocks = (
        (mixed_rows + product(active_low, reduce_weight) + reduce_bias)
        .reshape(block_shape)
        .astype(BF16)
    )
    upstream = cotangent.reshape(-1, D)
    upstream_float = upstream.astype(F32)
    grad_reduce_bias = jnp.sum(upstream_float, axis=0)
    grad_reduce_weight = transposed(active_low, upstream)
    grad_active = against(upstream, reduce_weight).astype(BF16)
    gelu_value, gelu_pull = jax.vjp(gelu_tanh, inner_rows)
    grad_inner = gelu_pull(grad_active.astype(F32))[0].astype(BF16)
    grad_expand_bias = jnp.sum(grad_inner.astype(F32), axis=0)
    grad_expand_weight = transposed(final_low, grad_inner)
    back_final, gain_final, shift_final = normalize_back(
        against(grad_inner, expand_weight), scaled_final, inverse_final, norm_gain[3]
    )
    grad_mixed = upstream_float + back_final
    grad_branch = grad_mixed.astype(BF16)
    grad_cross_output = transposed(gated_low, grad_branch)
    grad_gated = against(grad_branch, cross_output).astype(BF16)
    grad_gated_heads = grad_gated.astype(F32).reshape(DOCS, PAGE, H, HD)
    grad_gate = jnp.sum(grad_gated_heads * cross_result, axis=-1).reshape(-1, H)
    grad_logit = grad_gate * gate_values * (1.0 - gate_values)
    grad_gate_weight = lax.dot_general(
        cross_low.astype(F32), grad_logit, (((0,), (0,)), ((), ())), precision=HIGHEST
    )
    grad_raw = (grad_gated_heads * gate_heads).astype(BF16)
    cross_delta = jnp.transpose(
        jnp.sum(grad_raw.astype(F32) * cross_result, axis=-1), (0, 2, 1)
    )
    cross_carry = backward_fold(
        cross_queries,
        grad_raw,
        cross_logsum,
        cross_delta,
        scaling,
        (
            lax.all_gather(image_pairs, "blk", axis=1, tiled=True),
            lax.all_gather(image_open, "blk", axis=1, tiled=True),
        ),
    )
    cross_home = lax.psum_scatter(
        cross_carry[1].astype(BF16), "blk", scatter_dimension=1, tiled=True
    ).astype(F32)
    cross_query_sum = cross_carry[0]
    cross_query_low = cross_query_sum.reshape(-1, D).astype(BF16)
    cross_pair_low = cross_home.reshape(-1, 2 * D).astype(BF16)
    grad_cross_query = transposed(cross_low, cross_query_low)
    grad_cross_pairs = transposed(image_low, cross_pair_low)
    back_image, gain_image, shift_image = normalize_back(
        against(cross_pair_low, cross_pairs), scaled_image, inverse_image, norm_gain[2]
    )
    image_grad = back_image.reshape(block_shape).astype(BF16)
    grad_cross_in = against(cross_query_low, cross_query) + lax.dot_general(
        grad_logit, gate_weight.astype(F32), (((1,), (1,)), ((), ())), precision=HIGHEST
    )
    back_cross, gain_cross, shift_cross = normalize_back(
        grad_cross_in, scaled_cross, inverse_cross, norm_gain[1]
    )
    grad_hidden = grad_mixed + back_cross
    grad_self_branch = grad_hidden.astype(BF16)
    grad_self_output = transposed(self_low, grad_self_branch)
    grad_self_result = (
        against(grad_self_branch, self_output).astype(BF16).reshape(DOCS, PAGE, H, HD)
    )
    self_delta = jnp.transpose(
        jnp.sum(grad_self_result.astype(F32) * self_result, axis=-1), (0, 2, 1)
    )
    self_carry = backward_fold(
        self_queries,
        grad_self_result,
        self_logsum,
        self_delta,
        scaling,
        (
            lax.all_gather(self_pairs, "blk", axis=1, tiled=True),
            lax.all_gather(text_open, "blk", axis=1, tiled=True),
        ),
    )
    self_home = lax.psum_scatter(
        self_carry[1].astype(BF16), "blk", scatter_dimension=1, tiled=True
    ).astype(F32)
    self_query_sum = self_carry[0]
    grad_triples = jnp.concatenate(
        [self_query_sum.reshape(-1, D), self_home.reshape(-1, 2 * D)], axis=-1
    ).astype(BF16)
    grad_self_project = transposed(normed_low, grad_triples)
    back_first, gain_first, shift_first = normalize_back(
        against(grad_triples, self_project), scaled_first, inverse_first, norm_gain[0]
    )
    text_grad = (grad_hidden + back_first).reshape(block_shape).astype(BF16)
    wide_count = lax.axis_size("wide")
    blk_count = lax.axis_size("blk")
    large_grads = (
        grad_self_project,
        grad_self_output,
        grad_cross_query,
        grad_cross_pairs,
        grad_cross_output,
        grad_expand_weight,
        grad_reduce_weight,
    )
    ordered = tuple((tile_order(grad, wide_count, blk_count) for grad in large_grads))
    summed_grads = lax.psum_scatter(ordered, ("wide", "blk"), scatter_dimension=0, tiled=True)
    small_sums = lax.psum(
        (
            grad_gate_weight,
            grad_expand_bias,
            grad_reduce_bias,
            jnp.stack([gain_first, gain_cross, gain_image, gain_final]),
            jnp.stack([shift_first, shift_cross, shift_image, shift_final]),
        ),
        ("wide", "blk"),
    )
    return (
        joined_blocks,
        text_grad,
        image_grad,
        summed_grads[0],
        summed_grads[1],
        summed_grads[2],
        summed_grads[3],
        summed_grads[4],
        summed_grads[5],
        summed_grads[6],
        small_sums[0],
        small_sums[1],
        small_sums[2],
        small_sums[3],
        small_sums[4],
    )


def solution(mesh):
    rows = P("wide", "blk", None)
    fits = (mesh.shape["wide"], mesh.shape["blk"]) == PLANNED
    return jax.shard_map(
        body if fits else plain_body,
        mesh=mesh,
        in_specs=(rows,) * 3 + (P("wide", "blk"),) * 2 + (P("wide"),) + (P(),) * 12,
        out_specs=(rows,) * 3 + (P("wide", "blk"),) * 7 + (P(),) * 5,
        check_vma=False,
    )
```

```python
import functools
from typing import NamedTuple

import jax
import jax.numpy as jnp
from jax import lax
from jax.experimental import pallas as pl
from jax.experimental.pallas import tpu as pltpu
from jax.sharding import PartitionSpec as P

D = 768
H = 12
HD = 64
FF = 3072
PAGE = 128
DOCS = 2
ROWS = DOCS * PAGE
QUAD = 256
QUADS = D // QUAD
PAIR = 128
IMAGE = 112
EXTRA = 16
SUMS = 24
PLANNED = (4, 8)
EPSILON = 1e-05
NEGATIVE = -1e30
HIGHEST = lax.Precision.HIGHEST
BF16 = jnp.bfloat16
F32 = jnp.float32
VMEM_LIMIT = 62 * 1024 * 1024


def product(left, right):
    return jnp.dot(left, right, preferred_element_type=F32)


def against(left, right, precision=None):
    return lax.dot_general(
        left, right, (((1,), (1,)), ((), ())), preferred_element_type=F32, precision=precision
    )


def transposed(left, right, precision=None):
    return lax.dot_general(
        left, right, (((0,), (0,)), ((), ())), preferred_element_type=F32, precision=precision
    )


def standardize(values):
    centred = values - jnp.mean(values, axis=-1, keepdims=True)
    inverse = lax.rsqrt(jnp.mean(centred * centred, axis=-1, keepdims=True) + EPSILON)
    return centred * inverse, inverse


def norm_back(upstream, scaled, inverse, gains):
    weighted = upstream * gains
    return inverse * (
        weighted
        - jnp.mean(weighted, axis=-1, keepdims=True)
        - scaled * jnp.mean(weighted * scaled, axis=-1, keepdims=True)
    )


def column_sum(values):
    return jnp.sum(values, axis=0, keepdims=True)


def normalize_page(page, index, gain, shift, normed):
    rows = page.shape[0]
    scaled, _ = standardize(page[...].astype(F32))
    normed[index * rows : (index + 1) * rows, :] = (scaled * gain + shift).astype(BF16)


def normalize_pages(pages, gain, shift, normed):
    for index in range(pages.shape[0]):
        normalize_page(pages.at[index], index, gain, shift, normed)


def lane_index(rows):
    return lax.broadcasted_iota(jnp.int32, (rows, PAIR), 1)


def side_masks(rows):
    lanes = lane_index(rows)
    return [(lanes < HD).astype(BF16), (lanes >= HD).astype(BF16)]


def attend_forward(q_ref, k_ref, v_ref, closed_ref, out_ref, lse_ref):
    lanes = lane_index(ROWS)
    masks = side_masks(ROWS)
    first_lane = (lanes == 0).astype(BF16)
    stats = jnp.zeros((ROWS, PAIR), F32)
    for pair in range(QUAD // PAIR):
        cols = slice(pair * PAIR, (pair + 1) * PAIR)
        keys = jnp.concatenate([k_ref[:, cols], closed_ref[...]], axis=1)
        values = v_ref[:, cols]
        queries = q_ref[:, cols]
        results = []
        for side in range(2):
            query = jnp.concatenate([queries * masks[side], first_lane], axis=1)
            scores = against(query, keys)
            top = jnp.max(scores, axis=1, keepdims=True)
            weights = jnp.exp(scores - top)
            total = jnp.sum(weights, axis=1, keepdims=True)
            results.append(product(weights.astype(BF16), values) / total)
            stats = jnp.where(lanes == pair * 2 + side, top + jnp.log(total), stats)
        out_ref[:, cols] = jnp.where(lanes < HD, results[0], results[1])
    lse_ref[...] = jnp.transpose(stats)[:8, :]


def attend_backward(q_ref, k_ref, v_ref, do_ref, lse_ref, delta_ref, closed_ref, dq_ref, dkv_ref, hook):
    lanes = lane_index(ROWS)
    masks = side_masks(ROWS)
    first_lane = (lanes == 0).astype(BF16)
    for pair in range(QUAD // PAIR):
        cols = slice(pair * PAIR, (pair + 1) * PAIR)
        key_part = k_ref[:, cols]
        keys = jnp.concatenate([key_part, closed_ref[...]], axis=1)
        values = v_ref[:, cols]
        dq_parts = []
        dk = None
        dv = None
        for side in range(2):
            row = pair * 2 + side
            query = q_ref[:, cols] * masks[side]
            grad_out = do_ref[:, cols] * masks[side]
            scores = against(keys, jnp.concatenate([query, first_lane], axis=1))
            weights = jnp.exp(scores - lse_ref[row : row + 1, :])
            grad_weights = against(values, grad_out)
            grad_scores = (weights * (grad_weights - delta_ref[row : row + 1, :])).astype(BF16)
            dv_part = product(weights.astype(BF16), grad_out)
            dk_part = product(grad_scores, query)
            dv = dv_part if dv is None else dv + dv_part
            dk = dk_part if dk is None else dk + dk_part
            dq_parts.append(transposed(grad_scores, key_part))
        dq_ref[:, cols] = (jnp.where(lanes < HD, dq_parts[0], dq_parts[1]) * HD ** (-0.5)).astype(
            BF16
        )
        dkv_ref[:, cols] = dk.astype(BF16)
        dkv_ref[:, QUAD + pair * PAIR : QUAD + (pair + 1) * PAIR] = dv.astype(BF16)
        if pair == 0:
            hook()


def head_sums(values):
    sums = []
    lanes = lane_index(values.shape[0])
    for pair in range(H // 2):
        part = values[:, pair * PAIR : (pair + 1) * PAIR]
        sums.append(jnp.sum(jnp.where(lanes < HD, part, 0.0), axis=1, keepdims=True))
        sums.append(jnp.sum(jnp.where(lanes >= HD, part, 0.0), axis=1, keepdims=True))
    return sums


def head_rows(sums):
    lanes = lane_index(ROWS)
    stats = jnp.zeros((ROWS, PAIR), F32)
    for head, value in enumerate(sums):
        stats = jnp.where(lanes == (head // 4) * 8 + head % 4, value, stats)
    return jnp.transpose(stats)[: 8 * QUADS, :]


def spread_heads(gates):
    lanes = lane_index(gates.shape[0])
    parts = []
    for pair in range(H // 2):
        parts.append(
            jnp.where(lanes < HD, gates[:, 2 * pair : 2 * pair + 1], gates[:, 2 * pair + 1 : 2 * pair + 2])
        )
    return jnp.concatenate(parts, axis=1)


def put_rows(out, start, value):
    rows, lanes = out.shape[-2:]
    cuts = (value.shape[1] // lanes).bit_length() - 1
    lead = len(out.shape) - 2
    low = start
    while low < start + value.shape[0]:
        tile = low // rows
        high = min(start + value.shape[0], (tile + 1) * rows)
        for cut in range(1 << cuts):
            piece = value[low - start : high - start, cut * lanes : (cut + 1) * lanes]
            at = bits_of(cut, cuts) + bits_of(tile, lead - cuts)
            out[at + (slice(low - tile * rows, high - tile * rows), slice(None))] = piece
        low = high


class Gather:
    def __init__(self, places, names, packed, landed, waits):
        self.places = places
        self.names = names
        self.packed = packed
        self.landed = landed
        self.sends, self.receives = waits

    @staticmethod
    def waits(names):
        count = DOCS << len(names)
        return [pltpu.SemaphoreType.DMA((count,))] * 2

    def swap(self, turn):
        doc = self.places.turn if turn == 0 else 1 - self.places.turn
        return remote(
            self.packed.at[doc], self.landed.at[turn], self.sends.at[turn], self.receives.at[turn],
            self.places.swap(turn),
        )

    def start(self):
        stays = self.places.swap_stays()
        pl.when(jnp.logical_not(stays))(lambda: self.swap(0).start())
        self.swap(1).start()

        @pl.when(stays)
        def _():
            self.landed[0] = self.packed[self.places.turn]

    def copy(self, block, turn):
        stage = block.bit_length() - 1
        source = (block - (1 << stage)) * DOCS + turn
        at = block * DOCS + turn
        return remote(
            self.landed.at[source], self.landed.at[at], self.sends.at[at], self.receives.at[at],
            self.places.flip(self.names[stage]),
        )

    def arrive(self, block, turn):
        if block > 0:
            self.copy(block, turn).wait_recv()
        elif turn > 0:
            self.swap(turn).wait_recv()
        else:
            stays = self.places.swap_stays()
            pl.when(jnp.logical_not(stays))(lambda: self.swap(0).wait_recv())
        for stage in range(block.bit_length(), len(self.names)):
            self.copy(block + (1 << stage), turn).start()

    def end(self):
        stays = self.places.swap_stays()
        pl.when(jnp.logical_not(stays))(lambda: self.swap(0).wait_send())
        self.swap(1).wait_send()
        for block in range(1, 1 << len(self.names)):
            for turn in range(DOCS):
                self.copy(block, turn).wait_send()


def closed_rows(is_open):
    row = jnp.where(is_open, 0.0, NEGATIVE)
    wide = jnp.concatenate([row, jnp.zeros((1, D - PAGE), F32)], axis=1)
    return jnp.broadcast_to(wide, (EXTRA, D)).astype(BF16)


def closed_column(rows):
    row = rows[0:1, 0:PAGE].astype(F32)
    turned = jnp.transpose(jnp.broadcast_to(row, (PAGE, PAGE)))
    return jnp.where(lane_index(PAGE) == 0, turned, 0.0).astype(BF16)


def self_forward_kernel(
    wide, blk,
    regions, doc_pages, text_in, image_in, cot_in, mask, gain, shift, wq, wk, wv,
    out, lse, q_out, k_out, v_out, text_out, image_out, cot_out, text_closed, image_closed,
    normed, text_packed, image_packed, text_landed, image_landed, cot_landed,
    text_sends, text_receives, image_sends, image_receives, cot_sends, cot_receives, local,
):
    step = pl.program_id(0)
    places = Places(wide, blk)
    groups = group_bits(blk)
    blocks = 1 << len(groups)
    text = Gather(places, groups, text_packed, text_landed, (text_sends, text_receives))
    image = Gather(places, groups, image_packed, image_landed, (image_sends, image_receives))
    cot = Gather(places, [], cot_in, cot_landed, (cot_sends, cot_receives))
    outward = [
        pltpu.make_async_copy(text_landed.at[:, pl.ds(0, PAGE)], text_out, local.at[0]),
        pltpu.make_async_copy(image_landed.at[:, pl.ds(0, IMAGE)], image_out, local.at[1]),
        pltpu.make_async_copy(cot_landed, cot_out, local.at[2]),
    ]

    @pl.when(step == 0)
    def _():
        offsets = lax.broadcasted_iota(jnp.int32, (1, PAGE), 1)
        for doc in range(DOCS):
            text_packed[doc, 0:PAGE, :] = text_in[doc]
            living = places.b < doc_pages[doc]
            is_open = ((mask[doc : doc + 1, :] > 0) | (offsets == 0)) & living
            text_packed[doc, PAGE : PAGE + EXTRA, :] = closed_rows(is_open)
        greet(places, groups, True)
        text.start()
        for doc in range(DOCS):
            image_packed[doc, 0:IMAGE, :] = image_in[doc, 0:IMAGE, :]
            living = places.b < doc_pages[doc]
            is_open = (offsets < regions[0:1, doc : doc + 1]) & living
            image_packed[doc, IMAGE : IMAGE + EXTRA, :] = closed_rows(is_open)
        text.arrive(0, 0)
        text.arrive(0, 1)
        image.start()

        def take(block, turn):
            index = block * DOCS + turn
            page = text_landed.at[index, pl.ds(0, PAGE)]
            normalize_page(page, index, gain[0:1, :], shift[0:1, :], normed)
            text_closed[index * PAGE : (index + 1) * PAGE, :] = closed_column(
                text_landed[index, PAGE : PAGE + EXTRA, :]
            )

        for turn in range(DOCS):
            take(0, turn)
        for block in range(1, blocks):
            for turn in range(DOCS):
                text.arrive(block, turn)
            if block == 1:
                image.arrive(0, 0)
                image.arrive(0, 1)
                cot.start()
            for turn in range(DOCS):
                take(block, turn)

    @pl.when(step == 1)
    def _():
        outward[0].start()
        for block in range(1, blocks // 2):
            for turn in range(DOCS):
                image.arrive(block, turn)

    q_out[...] = (product(normed[0:ROWS, :], wq[...]).astype(BF16) * HD ** (-0.5)).astype(BF16)
    k_out[...] = product(normed[...], wk[...]).astype(BF16)
    v_out[...] = product(normed[...], wv[...]).astype(BF16)
    attend_forward(q_out, k_out, v_out, text_closed, out, lse)

    @pl.when(step == QUADS - 1)
    def _():
        for turn in range(DOCS):
            cot.arrive(0, turn)
        outward[2].start()
        for block in range(max(1, blocks // 2), blocks):
            for turn in range(DOCS):
                image.arrive(block, turn)
        outward[1].start()
        for index in range(blocks * DOCS):
            column = closed_column(image_landed[index, IMAGE : IMAGE + EXTRA, :])
            image_closed[index * IMAGE : (index + 1) * IMAGE, :] = column[0:IMAGE, :]
        for stream in (text, image, cot):
            stream.end()
        for copy in outward:
            copy.wait()


def cross_forward_kernel(
    text, pages, self_out, w_self, w_gate, gain, shift, closed, wq, wk, wv,
    hidden, gate, out, lse, q_out, k_out, v_out,
    normed, cross, gates,
):
    @pl.when(pl.program_id(0) == 0)
    def _():
        normalize_pages(pages, gain[2:3, :], shift[2:3, :], normed)
        branch = product(self_out[...].astype(BF16), w_self[...])
        for index in range(DOCS):
            rows = slice(index * PAGE, (index + 1) * PAGE)
            hidden[rows, :] = text[index].astype(F32) + branch[rows, :]
        scaled, _ = standardize(hidden[...])
        cross[...] = (scaled * gain[1:2, :] + shift[1:2, :]).astype(BF16)
        gates[...] = jnp.zeros_like(gates)
        gates[0:H, :] = w_gate[...]
        gate[...] = jax.nn.sigmoid(against(cross[...], gates[...]))

    q_out[...] = (product(cross[...], wq[...]).astype(BF16) * HD ** (-0.5)).astype(BF16)
    k_out[...] = product(normed[...], wk[...]).astype(BF16)
    v_out[...] = product(normed[...], wv[...]).astype(BF16)
    attend_forward(q_out, k_out, v_out, closed, out, lse)


def expand_part(wide, blk, step):
    few = (slice(None),) * (wide.bit_length() - 2)
    rest = (slice(None),) * (blk.bit_length() - 3)
    return few + (step // 2, step % 2) + rest, (slice(None), slice(None))


def reduce_part(wide, blk, step):
    cuts = wide.bit_length() - 2
    rest = (slice(None),) * (blk.bit_length() - 1)
    if cuts >= 2:
        lead = (step // 2, step % 2) + (slice(None),) * (cuts - 2) + rest
        return lead, (slice(None), slice(None))
    lanes = pl.ds(pl.multiple_of((step % 2) * D, D), D)
    return (step // 2,) + rest, (slice(None), lanes)


def put_expand(out, value, step, wide, blk):
    cuts, bits = wide.bit_length() - 2, blk.bit_length() - 1
    rows, lanes = out.shape[-2:]
    for cut in range(1 << cuts):
        for part in range(D // rows):
            at = bits_of(cut, cuts) + (step // 2, step % 2) + bits_of(part, bits - 1)
            out[at] = value[part * rows : (part + 1) * rows, cut * lanes : (cut + 1) * lanes]


def put_reduce(out, value, step, wide, blk):
    cuts, bits = wide.bit_length() - 2, blk.bit_length() - 1
    rows, lanes = out.shape[-2:]
    for part in range(D // rows):
        place = bits_of(part, bits + 1)
        piece = value[part * rows : (part + 1) * rows, :]
        if cuts >= 2:
            for cut in range(D // lanes):
                at = (step // 2, step % 2) + bits_of(cut, cuts - 2) + place
                out[at] = piece[:, cut * lanes : (cut + 1) * lanes]
        else:
            out[(step // 2,) + place + (slice(None), pl.ds(pl.multiple_of((step % 2) * D, D), D))] = piece


def forward_back_kernel(
    steps, wide, blk,
    hidden, raw, gate, cots, w_out, gain, shift, w_expand, b_expand, w_reduce, b_reduce,
    joined, early_expand, late_expand, early_reduce, late_reduce, d_out, grad_mixed, grad_raw,
    delta, grad_logit, small,
    gated, mixed, final, upstream, joined_sum, back_sum,
    expand_all, reduce_all, expand_got, reduce_got, expand_next, reduce_next,
    sends, receives, next_sends, next_receives, local,
):
    step = pl.program_id(0)
    places = Places(wide, blk)
    core, along, across = ("w", 0), ("w", 1), ("b", 0)
    cuts = wide.bit_length() - 2
    kinds = (
        (expand_part, expand_all, expand_got, expand_next, along),
        (reduce_part, reduce_all, reduce_got, reduce_next, across),
    )

    def copies(at):
        found = []
        for index, (part, grad, got, _, _) in enumerate(kinds):
            lead, tail = part(wide, blk, at)
            found.append(
                remote(
                    grad.at[lead + (1 - places.bit(core),) + tail],
                    got.at[lead + tail],
                    sends.at[index, at],
                    receives.at[index, at],
                    places.flip(core),
                )
            )
        return found

    def add(at):
        for (part, grad, got, _, _), copy in zip(kinds, copies(at)):
            copy.wait_recv()
            lead, tail = part(wide, blk, at)
            add_blocks(got.at[lead + tail], grad.at[lead + (places.bit(core),) + tail])

    def pieces(at):
        (lead, tail), (far_lead, far_tail) = (
            expand_part(wide, blk, at), reduce_part(wide, blk, at)
        )
        bit, far_bit = places.bit(along), places.bit(across)
        head, rest = lead[: cuts - 1], lead[cuts:]
        yield (
            expand_got.at[head + (bit,) + rest + tail],
            expand_got.at[head + (1 - bit,) + rest + tail],
            expand_next.at[head + rest[1:] + tail],
        )
        yield (
            reduce_got.at[far_lead[:-1] + (far_bit,) + far_tail],
            reduce_got.at[far_lead[:-1] + (1 - far_bit,) + far_tail],
            reduce_next.at[far_lead[1:-1] + far_tail],
        )

    def onward(at):
        return [
            remote(
                send, land, next_sends.at[index, at], next_receives.at[index, at],
                places.flip(kinds[index][4]),
            )
            for index, (_, send, land) in enumerate(pieces(at))
        ]

    @pl.when(step == 0)
    def _():
        greet(places, [core, along, across], False)
        upstream[0:PAGE, :] = cots[0]
        upstream[PAGE:ROWS, :] = cots[1]
        small[...] = jnp.zeros_like(small)
        gated[...] = (spread_heads(gate[...]) * raw[...]).astype(BF16)
        rows = hidden[...] + product(gated[...], w_out[...])
        mixed[...] = rows
        scaled, _ = standardize(rows)
        final[...] = (scaled * gain[3:4, :] + shift[3:4, :]).astype(BF16)
        joined_sum[...] = rows + b_reduce[...].reshape(1, D)
        back_sum[...] = jnp.zeros_like(back_sum)

    inner = product(final[...], w_expand[...]) + b_expand[...]
    squared = inner * inner
    root = (2.0 / jnp.pi) ** 0.5
    curve = jnp.tanh(root * inner * (1.0 + 0.044715 * squared))
    half = 0.5 * (1.0 + curve)
    active = (inner * half).astype(BF16)
    slope = half + 0.5 * inner * (1.0 - curve * curve) * (root * (1.0 + 3.0 * 0.044715 * squared))
    joined_sum[...] += product(active, w_reduce[...])
    grad_active = against(upstream[...], w_reduce[...]).astype(BF16)
    grad_inner = (grad_active.astype(F32) * slope).astype(BF16)
    small[pl.ds(4 + step, 1), :] = column_sum(grad_inner.astype(F32))
    back_sum[...] += against(grad_inner, w_expand[...])
    put_expand(expand_all, transposed(grad_inner, final[...]).astype(BF16), step, wide, blk)
    put_reduce(reduce_all, transposed(upstream[...], active).astype(BF16), step, wide, blk)
    for copy in copies(step):
        copy.start()
    for at in range(steps - 1):

        @pl.when(step == at + 1)
        def _():
            add(at)
            if at < steps // 2:
                for copy in onward(at):
                    copy.start()

    @pl.when(step == steps - 1)
    def _():
        total = joined_sum[...].astype(BF16)
        joined[0] = total[:PAGE]
        joined[1] = total[PAGE:]
        scaled, inverse = standardize(mixed[...])
        back = back_sum[...]
        cotangent = upstream[...].astype(F32)
        grad = cotangent + norm_back(back, scaled, inverse, gain[3:4, :])
        grad_mixed[...] = grad
        branch = grad.astype(BF16)
        put_rows(d_out, 0, transposed(branch, gated[...]).astype(BF16))
        grad_gated = against(branch, w_out[...]).astype(BF16).astype(F32)
        gates = gate[...]
        lanes = lane_index(ROWS)
        logit = jnp.zeros((ROWS, PAIR), F32)
        for head, value in enumerate(head_sums(grad_gated * raw[...])):
            logit = jnp.where(lanes == head, value, logit)
        grad_logit[...] = logit * gates * (1.0 - gates)
        rounded = (spread_heads(gates) * grad_gated).astype(BF16)
        grad_raw[...] = rounded
        delta[...] = head_rows(head_sums(rounded.astype(F32) * raw[...]))
        small[0:1, :] = column_sum(cotangent)
        small[1:2, :] = column_sum(back * scaled)
        small[2:3, :] = column_sum(back)
        add(steps - 1)
        half = (slice(None),) * cuts
        moves = [
            pltpu.make_async_copy(expand_got.at[half + (1,)], late_expand, local.at[0]),
            pltpu.make_async_copy(reduce_got.at[1], late_reduce, local.at[1]),
        ]
        for move in moves:
            move.start()
        for at in range(steps // 2):
            for copy, (kept, _, land) in zip(onward(at), pieces(at)):
                copy.wait()
                add_blocks(land, kept)
        moves += [
            pltpu.make_async_copy(expand_next, early_expand, local.at[2]),
            pltpu.make_async_copy(reduce_next, early_reduce, local.at[3]),
        ]
        for move in moves[2:]:
            move.start()
        for at in range(steps):
            for copy in copies(at):
                copy.wait_send()
        for move in moves:
            move.wait()


def spread_back(dkv, wk, wv, dx):
    weights = jnp.concatenate([wk[...], wv[...]], axis=1)

    size = dx.shape[0] // 4

    def chunk(index, carry):
        rows = pl.ds(pl.multiple_of(index * size, 16), size)
        dx[rows, :] += against(dkv[rows, :], weights)
        return carry

    lax.fori_loop(0, 4, chunk, 0)


def round_pages(dx, keep, send):
    half = dx.shape[0] // 2
    for target, start in ((send, half), (keep, 0)):
        size = half // 4
        for part in range(4):
            low = start + part * size
            target[part * size : (part + 1) * size, :] = dx[low : low + size, :].astype(BF16)


def page_sums(pages, dx):
    gain_sum = jnp.zeros((1, D), F32)
    shift_sum = jnp.zeros((1, D), F32)
    count, size, _ = pages.shape
    for index in range(count):
        scaled, _ = standardize(pages[index].astype(F32))
        part = dx[index * size : (index + 1) * size, :]
        gain_sum += column_sum(part * scaled)
        shift_sum += column_sum(part)
    return gain_sum, shift_sum


END = 99


def moves_of(plan, jobs):
    done = [-1] * len(jobs)
    moves = {}
    for point in sorted(plan):
        moves[point] = []
        for index in plan[point]:
            moves[point].append((index, done[index]))
            done[index] += 1
    moves[END] = [
        (index, stage)
        for stage in range(-1, max(len(job.order) for job in jobs))
        for index, job in enumerate(jobs)
        if done[index] <= stage < len(job.order)
    ]
    return moves


def run_moves(moves, point, scatters):
    for index, stage in moves.get(point, ()):
        if stage < 0:
            scatters[index].start()
        else:
            scatters[index].add(stage)


def back_kernel(wide, blk, jobs, plan, *refs):
    refs = iter(refs)
    (
        images, image_own, texts, gain, shift, cross_closed, self_closed,
        q_cross, k_cross, v_cross, do_cross, lse_cross, delta_cross, wk_cross, wv_cross,
        q_self, k_self, v_self, lse_self, wq_self, wk_self, wv_self,
        w_query, w_gate, w_self, hidden, self_out, grad_mixed, grad_logit, joined, last_small,
    ) = (next(refs) for _ in range(31))
    early_expand, late_expand, early_reduce, late_reduce, d_cross_output = (
        next(refs) for _ in range(5)
    )
    joined_out, text_out, image_out, sums_out, last_out = (next(refs) for _ in range(5))
    outs = [next(refs) if job.ends else None for job in jobs]
    normed, dkv, dx, dq, gates, grad_hidden, self_do, self_delta = (next(refs) for _ in range(8))
    pages, keep, send, row_sums, sums_in, local = (next(refs) for _ in range(6))
    d_pairs, d_query, d_self_output, d_project, expand_both, reduce_both = (
        next(refs) for _ in range(6)
    )
    sources = [
        early_expand, late_expand, early_reduce, late_reduce, expand_both, reduce_both,
        d_pairs, d_query, d_cross_output, d_self_output,
    ] + [d_project] * (len(jobs) - 10)
    lands = [expand_both.at[0], expand_both.at[1], reduce_both.at[0], reduce_both.at[1]]
    lands += [None] * (len(jobs) - 4)
    step = pl.program_id(0)
    places = Places(wide, blk)
    names = bit_names(wide, blk)
    groups = group_bits(blk)
    scatters = [
        Scatter(places, job, source, refs, last)
        for job, source, last in zip(jobs, sources, lands)
    ]
    moves = moves_of(plan, jobs)
    home = Home(places, refs)
    image_rows = pl.ds(0, k_cross.shape[0] // 2)
    image = Rows(
        places, groups, keep.at[image_rows], send.at[image_rows], row_sums.at[image_rows], refs
    )
    text = Rows(places, groups, keep, send, row_sums, refs)
    image_pages = pages.at[:, pl.ds(0, IMAGE)]
    fetches = [
        pltpu.make_async_copy(images, image_pages, local.at[0]),
        pltpu.make_async_copy(texts, pages, local.at[1]),
        pltpu.make_async_copy(grad_mixed, grad_hidden, local.at[2]),
        pltpu.make_async_copy(w_self, normed.at[pl.ds(0, D)], local.at[3]),
    ]
    sums = Total(places, refs)
    last_sums = Total(places, refs)

    def pump(point):
        if point in (7, 9, 11):
            sums.add((point - 7) // 2, sums_out)
        if point == 7:
            image.add(0)
        if point == 11:
            for stage in range(1, len(groups)):
                image.add(stage)
            image.norm(image_own, gain[2:3, :], None)
        run_moves(moves, point, scatters)

    def pumps(points):
        for point in points:
            pl.when(step == (point - 1) // 2)(functools.partial(pump, point))

    @pl.when(step == 0)
    def _():
        fetches[0].start()
        fetches[2].start()
        greet(places, names, True, ((("w", 1), ("b", 0)), (("b", 2), ("b", 1))))
        pump(0)
        for turn in range(DOCS):
            home.put(turn, joined[turn])

    @pl.when(step < QUADS)
    def _():
        keys = k_cross.shape[0]
        rows = pl.ds(0, keys)
        my_normed, my_dkv, my_dx = normed.at[rows], dkv.at[rows], dx.at[rows]

        @pl.when(step == 0)
        def _():
            fetches[0].wait()
            normalize_pages(image_pages, gain[2:3, :], shift[2:3, :], my_normed)
            my_dx[...] = jnp.zeros(my_dx.shape, F32)

        cols = pl.ds(pl.multiple_of(step * QUAD, QUAD), QUAD)
        attend_backward(
            q_cross, k_cross, v_cross, do_cross, lse_cross, delta_cross, cross_closed,
            dq.at[:, cols], my_dkv, lambda: pumps((1, 3, 5)),
        )
        spread_back(my_dkv, wk_cross, wv_cross, my_dx)
        for part in range(2):
            value = transposed(my_dkv[:, part * QUAD : (part + 1) * QUAD], my_normed[...])
            value = value.astype(BF16)
            for at in range(QUADS):

                @pl.when(step == at)
                def _():
                    put_rows(d_pairs, part * D + at * QUAD, value)

        pumps((2, 4))

        @pl.when(step == QUADS - 1)
        def _():
            round_pages(my_dx, image.keep, image.send)
            image.start()
            image_gain, image_shift = page_sums(image_pages, my_dx)
            fetches[1].start()
            fetches[3].start()
            scaled, inverse = standardize(hidden[...])
            cross = (scaled * gain[1:2, :] + shift[1:2, :]).astype(BF16)
            grad_query = dq[...]
            put_rows(d_query, 0, transposed(grad_query, cross).astype(BF16))
            d_gate = transposed(grad_logit[...], cross.astype(F32), HIGHEST)[:H, :]
            gates[...] = jnp.zeros_like(gates)
            gates[0:H, :] = w_gate[...]
            upstream = against(grad_query, w_query[...]) + jnp.dot(
                grad_logit[...], gates[...].astype(F32), precision=HIGHEST
            )
            fetches[2].wait()
            grad = grad_hidden[...] + norm_back(upstream, scaled, inverse, gain[1:2, :])
            grad_hidden[...] = grad
            branch = grad.astype(BF16)
            put_rows(
                d_self_output, 0, transposed(branch, self_out[...].astype(BF16)).astype(BF16)
            )
            fetches[3].wait()
            grad_result = against(branch, normed[0:D, :]).astype(BF16)
            self_do[...] = grad_result
            self_delta[...] = head_rows(head_sums(grad_result.astype(F32) * self_out[...]))
            sums_in[0:H, :] = d_gate
            sums_in[H : H + 8, :] = last_small[...]
            sums_in[H + 8 : SUMS, :] = jnp.concatenate(
                [column_sum(upstream * scaled), column_sum(upstream), image_gain, image_shift],
                axis=0,
            )
            sums.start(sums_in[...])
            home.end(joined_out)
            pump(6)
            fetches[1].wait()
            normalize_pages(pages, gain[0:1, :], shift[0:1, :], normed)
            dx[...] = jnp.zeros(dx.shape, F32)

    @pl.when(step >= QUADS)
    def _():
        quad = step - QUADS
        cols = pl.ds(pl.multiple_of(quad * QUAD, QUAD), QUAD)
        my_dq = dq.at[:, cols]
        attend_backward(
            q_self, k_self, v_self, self_do.at[:, cols], lse_self,
            self_delta.at[pl.ds(pl.multiple_of(quad * 8, 8), 8)], self_closed,
            my_dq, dkv, lambda: pumps((7, 9, 11)),
        )
        spread_back(dkv, wk_self, wv_self, dx)
        dx[0:ROWS, :] += against(my_dq[...], wq_self[...])

        @pl.when(quad == QUADS - 1)
        def _():
            round_pages(dx, keep, send)
            text.start()

        for part in range(3):
            if part == 0:
                value = transposed(my_dq[...], normed[0:ROWS, :])
            else:
                value = transposed(dkv[:, (part - 1) * QUAD : part * QUAD], normed[...])
            value = value.astype(BF16)
            for at in range(QUADS):

                @pl.when(quad == at)
                def _():
                    put_rows(d_project, part * D + at * QUAD, value)

        pumps((8, 10))

        @pl.when(quad == QUADS - 1)
        def _():
            run_moves(moves, 12, scatters)
            for stage in range(len(groups) - 1):
                text.add(stage)
            gain_sum, shift_sum = page_sums(pages, dx)
            last_sums.start(jnp.concatenate([gain_sum, shift_sum, jnp.zeros((6, D), F32)], axis=0))
            run_moves(moves, 13, scatters)
            text.add(len(groups) - 1)
            text.norm(pages, gain[0:1, :], grad_hidden)
            last_sums.add(0, last_out)
            run_moves(moves, 14, scatters)
            run_moves(moves, 15, scatters)
            last_sums.add(1, last_out)
            run_moves(moves, 16, scatters)
            last_sums.add(2, last_out)
            run_moves(moves, 17, scatters)
            image.end(image_out)
            text.end(text_out)
            run_moves(moves, END, scatters)
            for scatter, out in zip(scatters, outs):
                scatter.end(out)


class Places:
    def __init__(self, wide, blk):
        self.wide = wide
        self.blk = blk
        self.part = blk // 4
        self.w = lax.axis_index("wide")
        self.b = lax.axis_index("blk")
        self.quarter = self.b // self.part
        self.turn = self.quarter % 2

    def bit(self, name):
        axis, bit = name
        return ((self.w if axis == "w" else self.b) // (1 << bit)) % 2

    def flip(self, name):
        axis, bit = name
        step = (1 << bit) * (1 - 2 * self.bit(name))
        return (self.w + step, self.b) if axis == "w" else (self.w, self.b + step)

    def flips(self, names, which):
        w, b = self.w, self.b
        for name, taken in zip(names, (which // 2, which % 2)):
            if taken:
                there = self.flip(name)
                w, b = w + there[0] - self.w, b + there[1] - self.b
        return w, b

    def index(self, names):
        return 2 * self.bit(names[0]) + self.bit(names[1])

    def swap(self, turn):
        core = self.w % 2
        turned = self.turn if turn == 0 else 1 - self.turn
        return (
            self.w - core + self.quarter // 2,
            (2 * core + turned) * self.part + self.b % self.part,
        )

    def swap_stays(self):
        return self.w % 2 == self.quarter // 2


def bit_names(wide, blk):
    return [("w", bit) for bit in range(wide.bit_length() - 1)] + [
        ("b", bit) for bit in range(blk.bit_length() - 1)
    ]


def group_bits(blk):
    return [("b", bit) for bit in range((blk // 4).bit_length() - 1)] + [("w", 0)]


def tile_bits(wide, blk):
    return (
        [("w", bit) for bit in range(wide.bit_length() - 2, 0, -1)]
        + [("b", bit) for bit in range(blk.bit_length() - 2, -1, -1)]
        + [("w", 0)]
    )


def remote(source, target, send, receive, device):
    return pltpu.make_async_remote_copy(
        src_ref=source,
        dst_ref=target,
        send_sem=send,
        recv_sem=receive,
        device_id=device,
        device_id_type=pl.DeviceIdType.MESH,
    )


def greet(places, names, swaps, pairs=()):
    barrier = pltpu.get_barrier_semaphore()
    devices = [places.flip(name) for name in names] + [places.flips(pair, 3) for pair in pairs]
    for device in devices:
        pl.semaphore_signal(
            barrier, inc=1, device_id=device, device_id_type=pl.DeviceIdType.MESH
        )
    count = len(devices)
    if swaps:
        pl.semaphore_signal(
            barrier, inc=1, device_id=places.swap(1), device_id_type=pl.DeviceIdType.MESH
        )

        @pl.when(jnp.logical_not(places.swap_stays()))
        def _():
            pl.semaphore_signal(
                barrier, inc=1, device_id=places.swap(0), device_id_type=pl.DeviceIdType.MESH
            )

        count = count + 2 - places.swap_stays().astype(jnp.int32)
    pl.semaphore_wait(barrier, count)


class Job(NamedTuple):
    left: tuple
    order: tuple
    start: int
    rows: int
    lanes: int
    ends: bool
    near: bool = False
    inner: bool = False

    def after(self):
        return tuple(name for name in self.left if name not in self.order)

    def scratch(self):
        count = len(self.left)
        kinds = []
        if not self.near:
            kinds.append(pltpu.VMEM((2,) * (count - 1) + (self.rows, self.lanes), BF16))
        for stage in range(len(self.order) - int(self.inner)):
            kinds.append(pltpu.VMEM((2,) * (count - 1 - stage) + (self.rows, self.lanes), BF16))
        if self.ends:
            kinds.append(pltpu.VMEM((2, self.rows, self.lanes // 2), BF16))
        waits = len(self.order) + int(self.ends)
        return kinds + [pltpu.SemaphoreType.DMA((waits,))] * 2 + [pltpu.SemaphoreType.DMA]

    def result(self):
        return shaped((2, self.rows, self.lanes // 2), BF16)


def bits_of(index, count):
    return tuple((index // (1 << (count - 1 - place))) % 2 for place in range(count))


def add_blocks(target, source):
    lead = len(target.shape) - 2
    if lead == 0:
        target[...] = target[...] + source[...]
        return

    def block(index, carry):
        at = bits_of(index, lead)
        target[at] = target[at] + source[at]
        return carry

    lax.fori_loop(0, 1 << lead, block, 0)


class Scatter:
    def __init__(self, places, job, source, scratch, last=None):
        self.places = places
        self.job = job
        self.source = source
        self.own = None if job.near else next(scratch)
        self.got = [next(scratch) for _ in range(len(job.order) - int(job.inner))]
        if job.inner:
            self.got.append(last)
        self.ends = next(scratch) if job.ends else None
        self.sends, self.receives, self.local = next(scratch), next(scratch), next(scratch)
        self.stages = len(job.order)
        self.axes = []
        left = list(job.left)
        for name in job.order:
            self.axes.append(left.index(name))
            left.remove(name)

    def cut(self, ref, stage, index):
        axis = self.axes[stage]
        at = (slice(None),) * axis + (index,)
        if ref.shape[-2] != self.job.rows:
            at += (slice(None),) * (len(ref.shape) - 3 - axis)
            at += (pl.ds(self.job.start, self.job.rows), slice(None))
        return ref.at[at]

    def copy(self, stage):
        if stage == self.stages:
            source, target, name = self.ends.at[0], self.ends.at[1], ("w", 0)
        else:
            name = self.job.order[stage]
            source = self.source if stage == 0 else self.got[stage - 1]
            source = self.cut(source, stage, 1 - self.places.bit(name))
            target = self.got[stage]
        return remote(
            source, target, self.sends.at[stage], self.receives.at[stage], self.places.flip(name)
        )

    def fetch(self):
        kept = self.cut(self.source, 0, self.places.bit(self.job.order[0]))
        return pltpu.make_async_copy(kept, self.own, self.local)

    def start(self):
        self.copy(0).start()
        if not self.job.near:
            self.fetch().start()

    def halve(self):
        lanes = self.job.lanes // 2
        piece = self.got[-1][...]
        second = self.places.bit(("w", 0)) == 1
        self.ends[0] = jnp.where(second, piece[:, :lanes], piece[:, lanes:])

    def add(self, stage):
        self.copy(stage).wait_recv()
        if stage == 0 and not self.job.near:
            self.fetch().wait()
            source = self.own
        else:
            bit = self.places.bit(self.job.order[stage])
            source = self.cut(self.source if stage == 0 else self.got[stage - 1], stage, bit)
        add_blocks(self.got[stage], source)
        if stage + 1 < self.stages:
            self.copy(stage + 1).start()
        elif self.job.ends:
            self.halve()
            self.copy(stage + 1).start()

    def end(self, out):
        for stage in range(self.stages + int(self.job.ends)):
            self.copy(stage).wait_send()
        if not self.job.ends:
            return
        self.copy(self.stages).wait_recv()
        lanes = self.job.lanes // 2
        piece = self.got[-1][...]
        other = self.ends[1]
        second = self.places.bit(("w", 0)) == 1
        mine = jnp.where(second, piece[:, lanes:], piece[:, :lanes])
        out[0] = jnp.where(second, other, mine)
        out[1] = jnp.where(second, mine, other)


class Home:
    def __init__(self, places, scratch):
        self.places = places
        self.home, self.landed, self.sends, self.receives, self.local = (
            next(scratch) for _ in range(5)
        )

    @staticmethod
    def scratch():
        waits = [pltpu.SemaphoreType.DMA((DOCS,))] * 2 + [pltpu.SemaphoreType.DMA]
        return [pltpu.VMEM((DOCS, PAGE, D), BF16)] * 2 + waits

    def copy(self, turn):
        return remote(
            self.home.at[turn], self.landed.at[self.places.turn], self.sends.at[turn],
            self.receives.at[turn], self.places.swap(turn),
        )

    def go(self, turn, begin):
        def carry():
            if begin:
                self.copy(turn).start()
            else:
                self.copy(turn).wait()

        if turn > 0:
            carry()
            return
        stays = self.places.swap_stays()
        pl.when(jnp.logical_not(stays))(carry)
        if begin:

            @pl.when(stays)
            def _():
                self.landed[self.places.turn] = self.home[turn]

    def put(self, turn, page):
        self.home[turn] = page
        self.go(turn, True)

    def end(self, out):
        for turn in range(DOCS):
            self.go(turn, False)
        copy = pltpu.make_async_copy(self.landed, out, self.local)
        copy.start()
        copy.wait()


class Rows:
    def __init__(self, places, names, keep, send, sums, scratch):
        self.places = places
        self.size = keep.shape[0] // (DOCS << (len(names) - 1))
        self.names = list(reversed(names))
        self.keep = keep
        self.send = send
        self.sums = sums
        self.got = [next(scratch) for _ in names]
        self.sends, self.receives = next(scratch), next(scratch)
        self.back = Home(places, scratch)

    @staticmethod
    def scratch(names, rows):
        kinds = [pltpu.VMEM((rows >> stage, D), BF16) for stage in range(len(names))]
        return kinds + [pltpu.SemaphoreType.DMA((len(names),))] * 2 + Home.scratch()

    def copy(self, stage):
        source = self.send if stage == 0 else self.sums
        rows = self.got[stage].shape[0]
        if stage > 0:
            source = source.at[pl.ds(rows, rows)]
        return remote(
            source, self.got[stage], self.sends.at[stage], self.receives.at[stage],
            self.places.flip(self.names[stage]),
        )

    def start(self):
        self.copy(0).start()

    def add(self, stage):
        self.copy(stage).wait()
        source = self.keep if stage == 0 else self.sums
        rows = self.got[stage].shape[0]

        def block(index, carry):
            at = pl.ds(pl.multiple_of(index * self.size, 16), self.size)
            self.sums[at, :] = source[at, :] + self.got[stage][at, :]
            return carry

        lax.fori_loop(0, rows // self.size, block, 0)
        if stage + 1 < len(self.names):
            self.copy(stage + 1).start()

    def norm(self, pages, gain, added):
        for turn in range(DOCS):
            rows = slice(turn * self.size, (turn + 1) * self.size)
            scaled, inverse = standardize(pages[turn].astype(F32))
            grad = norm_back(self.sums[rows, :].astype(F32), scaled, inverse, gain)
            if added is not None:
                grad = grad + added[rows, :]
            if self.size < PAGE:
                rest = jnp.zeros((PAGE - self.size, D), F32)
                grad = jnp.concatenate([grad, rest], axis=0)
            self.back.put(turn, grad.astype(BF16))

    def end(self, out):
        self.back.end(out)


class Total:
    ROUNDS = 3

    def __init__(self, places, scratch):
        self.places = places
        self.chip, self.plane, self.line, self.sends, self.receives = (
            next(scratch) for _ in range(5)
        )

    @staticmethod
    def scratch(rows):
        return [
            pltpu.VMEM((2, rows, D), F32),
            pltpu.VMEM((4, rows, D), F32),
            pltpu.VMEM((4, rows, D), F32),
            pltpu.SemaphoreType.DMA((7,)),
            pltpu.SemaphoreType.DMA((7,)),
        ]

    def copies(self, stage):
        if stage == 0:
            return [
                remote(
                    self.chip.at[0], self.chip.at[1], self.sends.at[0], self.receives.at[0],
                    self.places.flip(("w", 0)),
                )
            ]
        names = (("w", 1), ("b", 0)) if stage == 1 else (("b", 2), ("b", 1))
        slots = self.plane if stage == 1 else self.line
        mine = slots.at[self.places.index(names)]
        found = []
        for which in range(1, 4):
            at = 3 * stage - 3 + which
            found.append(
                remote(
                    mine, mine, self.sends.at[at], self.receives.at[at],
                    self.places.flips(names, which),
                )
            )
        return found

    def start(self, value):
        self.chip[0] = value
        self.copies(0)[0].start()

    def add(self, stage, out):
        for copy in self.copies(stage):
            copy.wait()
        if stage == 0:
            value = self.chip[0] + self.chip[1]
            self.plane[self.places.index((("w", 1), ("b", 0)))] = value
        else:
            slots = self.plane if stage == 1 else self.line
            value = (slots[0] + slots[1]) + (slots[2] + slots[3])
            if stage == 1:
                self.line[self.places.index((("b", 2), ("b", 1)))] = value
        if stage + 1 < self.ROUNDS:
            for copy in self.copies(stage + 1):
                copy.start()
        else:
            out[...] = value


def finish_kernel(layout, *refs):
    refs = iter(refs)
    pieces = [[next(refs) for _ in range(count)] for count in layout]
    streams = [next(refs) for _ in range(3)]
    sums, last_sums = next(refs), next(refs)
    for index, parts in enumerate(pieces):
        out = next(refs)
        halves = [part[half] for half in range(2) for part in parts]
        value = jnp.concatenate(halves, axis=0).astype(F32)
        out[...] = value if index + 1 == len(pieces) else jnp.transpose(value)
    for stream in streams:
        out = next(refs)
        out[...] = stream[...]
    gate, bias, last, gains, shifts = (next(refs) for _ in range(5))
    gate[...] = sums[0:H, :]
    for index in range(FF // D):
        bias[pl.ds(index * D, D)] = sums[H + 4 + index, :]
    last[...] = sums[H, :]
    for out, at in ((gains, 0), (shifts, 1)):
        out[0:1, :] = last_sums[at : at + 1, :]
        for index, row in enumerate((H + 8 + at, H + 10 + at, H + 1 + at)):
            out[index + 1 : index + 2, :] = sums[row : row + 1, :]


def whole(shape):
    return pl.BlockSpec(shape, lambda step: (0,) * len(shape))


def columns(rows, offset=0):
    return pl.BlockSpec((rows, QUAD), lambda step: (0, offset + step))


def stat_rows():
    return pl.BlockSpec((8, ROWS), lambda step: (step, 0))


def shaped(shape, kind):
    return jax.ShapeDtypeStruct(shape, kind)


ANY = pl.BlockSpec(memory_space=pl.ANY)


def call(kernel, name, steps, ins, outs, scratch, flops, byte_count, collective=None):
    in_specs, operands = zip(*ins)
    out_specs, out_shapes = zip(*outs)
    return pl.pallas_call(
        kernel,
        grid=(steps,),
        in_specs=list(in_specs),
        out_specs=list(out_specs),
        out_shape=list(out_shapes),
        scratch_shapes=scratch,
        name=name,
        compiler_params=pltpu.CompilerParams(
            vmem_limit_bytes=VMEM_LIMIT,
            collective_id=collective,
            has_side_effects=collective is not None,
        ),
        cost_estimate=pl.CostEstimate(flops=flops, bytes_accessed=byte_count, transcendentals=0),
    )(*operands)


def own_pages(pages):
    return (whole((DOCS, *pages.shape[1:])), pages)


SMEM = pl.BlockSpec(memory_space=pltpu.SMEM)


def self_forward(texts, images, cots, mask, regions, doc_pages, gain, shift, project, wide, blk):
    groups = group_bits(blk)
    count = DOCS << len(groups)
    keys = count * PAGE
    return call(
        functools.partial(self_forward_kernel, wide, blk),
        "self_forward",
        QUADS,
        [
            (whole(regions.shape), regions),
            (SMEM, doc_pages),
            (whole(texts.shape), texts),
            (whole(images.shape), images),
            (whole(cots.shape), cots),
            (whole(mask.shape), mask),
            (whole(gain.shape), gain),
            (whole(shift.shape), shift),
            (columns(D), project),
            (columns(D, QUADS), project),
            (columns(D, 2 * QUADS), project),
        ],
        [
            (columns(ROWS), shaped((ROWS, D), F32)),
            (stat_rows(), shaped((8 * QUADS, ROWS), F32)),
            (columns(ROWS), shaped((ROWS, D), BF16)),
            (columns(keys), shaped((keys, D), BF16)),
            (columns(keys), shaped((keys, D), BF16)),
            (ANY, shaped((count, PAGE, D), BF16)),
            (ANY, shaped((count, IMAGE, D), BF16)),
            (ANY, shaped((DOCS, PAGE, D), BF16)),
            (whole((keys, PAIR)), shaped((keys, PAIR), BF16)),
            (whole((count * IMAGE, PAIR)), shaped((count * IMAGE, PAIR), BF16)),
        ],
        [
            pltpu.VMEM((keys, D), BF16),
            pltpu.VMEM((DOCS, PAGE + EXTRA, D), BF16),
            pltpu.VMEM((DOCS, IMAGE + EXTRA, D), BF16),
            pltpu.VMEM((count, PAGE + EXTRA, D), BF16),
            pltpu.VMEM((count, IMAGE + EXTRA, D), BF16),
            pltpu.VMEM((DOCS, PAGE, D), BF16),
        ]
        + Gather.waits(groups) * 2
        + Gather.waits([])
        + [pltpu.SemaphoreType.DMA((3,))],
        6 * 10**9,
        12 * 10**6,
        0,
    )


def cross_forward(texts, pages, self_out, w_self, w_gate, gain, shift, closed, w_query, w_pairs):
    keys = closed.shape[0]
    return call(
        cross_forward_kernel,
        "cross_forward",
        QUADS,
        [
            own_pages(texts),
            (whole(pages.shape), pages),
            (whole(self_out.shape), self_out),
            (whole(w_self.shape), w_self),
            (whole(w_gate.shape), w_gate),
            (whole(gain.shape), gain),
            (whole(shift.shape), shift),
            (whole(closed.shape), closed),
            (columns(D), w_query),
            (columns(D), w_pairs),
            (columns(D, QUADS), w_pairs),
        ],
        [
            (whole((ROWS, D)), shaped((ROWS, D), F32)),
            (whole((ROWS, PAIR)), shaped((ROWS, PAIR), F32)),
            (columns(ROWS), shaped((ROWS, D), F32)),
            (stat_rows(), shaped((8 * QUADS, ROWS), F32)),
            (columns(ROWS), shaped((ROWS, D), BF16)),
            (columns(keys), shaped((keys, D), BF16)),
            (columns(keys), shaped((keys, D), BF16)),
        ],
        [
            pltpu.VMEM((keys, D), BF16),
            pltpu.VMEM((ROWS, D), BF16),
            pltpu.VMEM((PAIR, D), BF16),
        ],
        7 * 10**9,
        14 * 10**6,
    )


def forward_back(
    hidden, raw, gate, cots, w_out, gain, shift, w_expand, b_expand, w_reduce, b_reduce, wide, blk
):
    steps = FF // D
    names = tile_bits(wide, blk)
    small = (D // (2 * blk), D // (wide // 2))
    expand = (FF // (2 * blk), D // (wide // 2))
    reduce = (D // (2 * blk), FF // (wide // 2))
    full, part, half, less = ((2,) * (len(names) - gone) for gone in range(4))
    return call(
        functools.partial(forward_back_kernel, steps, wide, blk),
        "forward_back",
        steps,
        [
            (whole((ROWS, D)), hidden),
            (whole((ROWS, D)), raw),
            (whole((ROWS, PAIR)), gate),
            (whole((DOCS, PAGE, D)), cots),
            (whole((D, D)), w_out),
            (whole(gain.shape), gain),
            (whole(shift.shape), shift),
            (pl.BlockSpec((D, D), lambda step: (0, step)), w_expand),
            (pl.BlockSpec((1, D), lambda step: (0, step)), b_expand),
            (pl.BlockSpec((D, D), lambda step: (step, 0)), w_reduce),
            (whole((D,)), b_reduce),
        ],
        [
            (whole((DOCS, PAGE, D)), shaped((DOCS, PAGE, D), BF16)),
            (ANY, shaped(less + expand, BF16)),
            (ANY, shaped(half + expand, BF16)),
            (ANY, shaped(less + reduce, BF16)),
            (ANY, shaped(half + reduce, BF16)),
            (whole(full + small), shaped(full + small, BF16)),
            (whole((ROWS, D)), shaped((ROWS, D), F32)),
            (whole((ROWS, D)), shaped((ROWS, D), BF16)),
            (whole((8 * QUADS, ROWS)), shaped((8 * QUADS, ROWS), F32)),
            (whole((ROWS, PAIR)), shaped((ROWS, PAIR), F32)),
            (whole((8, D)), shaped((8, D), F32)),
        ],
        [
            pltpu.VMEM((ROWS, D), BF16),
            pltpu.VMEM((ROWS, D), F32),
            pltpu.VMEM((ROWS, D), BF16),
            pltpu.VMEM((ROWS, D), BF16),
            pltpu.VMEM((ROWS, D), F32),
            pltpu.VMEM((ROWS, D), F32),
            pltpu.VMEM(full + expand, BF16),
            pltpu.VMEM(full + reduce, BF16),
            pltpu.VMEM(part + expand, BF16),
            pltpu.VMEM(part + reduce, BF16),
            pltpu.VMEM(less + expand, BF16),
            pltpu.VMEM(less + reduce, BF16),
            pltpu.SemaphoreType.DMA((2, steps)),
            pltpu.SemaphoreType.DMA((2, steps)),
            pltpu.SemaphoreType.DMA((2, steps // 2)),
            pltpu.SemaphoreType.DMA((2, steps // 2)),
            pltpu.SemaphoreType.DMA((4,)),
        ],
        8 * 10**9,
        25 * 10**6,
        1,
    )


def back(
    cross, own, images, texts, gain, shift, closed, w_pairs, project, w_query, w_gate, w_self,
    hidden, self_out, grad_mixed, grad_logit, joined, last_small, far_sources, jobs, plan, wide, blk,
):
    q_cross, k_cross, v_cross, do_cross, lse_cross, delta_cross = cross
    q_self, k_self, v_self, lse_self = own
    cross_keys, self_keys = k_cross.shape[0], k_self.shape[0]
    names = bit_names(wide, blk)
    groups = group_bits(blk)
    tile = (2,) * len(tile_bits(wide, blk))
    lanes = 2 * D // wide
    stream = shaped((DOCS, PAGE, D), BF16)

    def fixed(array):
        count = len(array.shape)
        spec = pl.BlockSpec(
            array.shape, lambda step: (0,) * count, pipeline_mode=pl.Buffered(buffer_count=1)
        )
        return (spec, array)

    def early(array, rows, offset=0):
        last = QUADS - 1
        return (
            pl.BlockSpec(
                (rows, QUAD), lambda step: (0, offset + step - step // QUADS * (step - last))
            ),
            array,
        )

    def late(array, rows, offset=0):
        return (
            pl.BlockSpec((rows, QUAD), lambda step: (0, offset + step // QUADS * (step - QUADS))),
            array,
        )

    def early_rows(array):
        last = QUADS - 1
        return (
            pl.BlockSpec((8, ROWS), lambda step: (step - step // QUADS * (step - last), 0)), array
        )

    def late_rows(array):
        return (pl.BlockSpec((8, ROWS), lambda step: (step // QUADS * (step - QUADS), 0)), array)

    def tiles(columns_here):
        return pltpu.VMEM(tile + (columns_here // (2 * blk), lanes), BF16)

    def both(job):
        return pltpu.VMEM((2,) * (1 + len(job.after())) + (job.rows, job.lanes), BF16)

    image_rows, text_rows = cross_keys // 2, self_keys // 2
    return call(
        functools.partial(back_kernel, wide, blk, jobs, plan),
        "back",
        2 * QUADS,
        [
            (ANY, images),
            own_pages(images),
            (ANY, texts),
            fixed(gain),
            fixed(shift),
            fixed(closed[0]),
            fixed(closed[1]),
            early(q_cross, ROWS),
            early(k_cross, cross_keys),
            early(v_cross, cross_keys),
            early(do_cross, ROWS),
            early_rows(lse_cross),
            early_rows(delta_cross),
            early(w_pairs, D),
            early(w_pairs, D, QUADS),
            late(q_self, ROWS),
            late(k_self, self_keys),
            late(v_self, self_keys),
            late_rows(lse_self),
            late(project, D),
            late(project, D, QUADS),
            late(project, D, 2 * QUADS),
            fixed(w_query),
            fixed(w_gate),
            (ANY, w_self),
            fixed(hidden),
            fixed(self_out),
            (ANY, grad_mixed),
            fixed(grad_logit),
            fixed(joined),
            fixed(last_small),
        ]
        + [(ANY, source) for source in far_sources],
        [(ANY, stream)] * 3
        + [(whole((SUMS, D)), shaped((SUMS, D), F32)), (whole((8, D)), shaped((8, D), F32))]
        + [(whole(job.result().shape), job.result()) for job in jobs if job.ends],
        [
            pltpu.VMEM((self_keys, D), BF16),
            pltpu.VMEM((self_keys, 2 * QUAD), BF16),
            pltpu.VMEM((self_keys, D), F32),
            pltpu.VMEM((ROWS, D), BF16),
            pltpu.VMEM((PAIR, D), BF16),
            pltpu.VMEM((ROWS, D), F32),
            pltpu.VMEM((ROWS, D), BF16),
            pltpu.VMEM((8 * QUADS, ROWS), F32),
            pltpu.VMEM(texts.shape, BF16),
            pltpu.VMEM((text_rows, D), BF16),
            pltpu.VMEM((text_rows, D), BF16),
            pltpu.VMEM((text_rows, D), BF16),
            pltpu.VMEM((SUMS, D), F32),
            pltpu.SemaphoreType.DMA((4,)),
            tiles(2 * D),
            tiles(D),
            tiles(D),
            tiles(3 * D),
            both(jobs[0]),
            both(jobs[2]),
        ]
        + [kind for job in jobs for kind in job.scratch()]
        + Home.scratch()
        + Rows.scratch(groups, image_rows)
        + Rows.scratch(groups, text_rows)
        + Total.scratch(SUMS)
        + Total.scratch(8),
        23 * 10**9,
        30 * 10**6,
        2,
    )


def finish(pieces, streams, sums, last_sums):
    vmem = pl.BlockSpec(memory_space=pltpu.VMEM)
    operands = [part for parts in pieces for part in parts] + [*streams, sums, last_sums]
    results = []
    for index, parts in enumerate(pieces):
        shape = (parts[0].shape[2], sum(2 * part.shape[1] for part in parts))
        results.append(shaped(shape[::-1] if index + 1 == len(pieces) else shape, F32))
    results += [shaped(stream.shape, BF16) for stream in streams]
    results += [shaped((H, D), F32), shaped((FF,), F32), shaped((D,), F32)]
    results += [shaped((4, D), F32)] * 2
    return pl.pallas_call(
        functools.partial(finish_kernel, tuple(len(parts) for parts in pieces)),
        in_specs=[vmem] * len(operands),
        out_specs=[vmem] * len(results),
        out_shape=results,
        name="finish",
        compiler_params=pltpu.CompilerParams(vmem_limit_bytes=VMEM_LIMIT),
        cost_estimate=pl.CostEstimate(flops=10**6, bytes_accessed=5 * 10**6, transcendentals=0),
    )(*operands)


def body(
    text_blocks,
    image_blocks,
    cotangent,
    text_mask,
    page_regions,
    doc_pages,
    self_project,
    self_output,
    cross_query,
    cross_pairs,
    cross_output,
    gate_weight,
    expand_weight,
    expand_bias,
    reduce_weight,
    reduce_bias,
    norm_gain,
    norm_bias,
):
    wide = lax.axis_size("wide")
    blk = lax.axis_size("blk")
    names = tuple(tile_bits(wide, blk))
    share = 2 * blk
    lanes = 2 * D // wide
    far = 2 * FF // wide
    gate_rows = jnp.transpose(gate_weight)

    (
        self_out, self_lse, self_q, self_k, self_v, text_pages, image_pages, cots, text_closed,
        image_closed,
    ) = self_forward(
        text_blocks, image_blocks, cotangent, text_mask, jnp.transpose(page_regions), doc_pages, norm_gain,
        norm_bias, self_project, wide, blk,
    )
    hidden, gate, raw, cross_lse, cross_q, cross_k, cross_v = cross_forward(
        text_pages, image_pages, self_out, self_output, gate_rows, norm_gain, norm_bias,
        image_closed, cross_query, cross_pairs,
    )
    (
        joined, *partial, d_cross_output, grad_mixed, grad_raw, cross_delta,
        grad_logit, small_last,
    ) = forward_back(
        hidden, raw, gate, cots, cross_output, norm_gain, norm_bias, expand_weight,
        expand_bias.reshape(1, FF), reduce_weight, reduce_bias, wide, blk,
    )

    core, y, x, z, far_z = ("w", 0), ("w", 1), ("b", 0), ("b", 1), ("b", 2)
    ends = {"ends": True, "near": True}
    expand_shape = (0, FF // share, lanes)
    reduce_shape = (0, D // share, far)
    one = (0, D // share, lanes)
    rows = 3 * D // share
    split = 80
    jobs = (
        Job((z, x), (z,), *expand_shape, False, inner=True),
        Job((y, z, x), (y, z), *expand_shape, False, inner=True),
        Job((far_z, z), (z,), *reduce_shape, False, inner=True),
        Job((far_z, z, x), (x, z), *reduce_shape, False, inner=True),
        Job((far_z, x), (far_z, x), *expand_shape, **ends),
        Job((y, far_z), (y, far_z), *reduce_shape, **ends),
        Job(names, (core, x, y, z, far_z), 0, 2 * D // share, lanes, **ends),
        Job(names, (core, y, x, z, far_z), *one, **ends),
        Job(names, (core, y, x, z, far_z), *one, True),
        Job(names, (core, y, x, z, far_z), *one, **ends),
        Job(names, (core, y, x, z, far_z), 0, split, lanes, **ends),
        Job(names, (core, z, y, x, far_z), split, rows - split, lanes, **ends),
    )
    plan = {
        0: (1, 3, 0, 2,),
        4: (1, 3, 0, 2,),
        6: (6, 7, 8, 9,),
        7: (7, 8, 9,),
        8: (1, 3,),
        9: (6, 5,),
        11: (4,),
        12: (10, 11,),
        13: (10, 11, 7, 8, 9,),
        14: (6, 5,),
        15: (10, 11,),
        16: (7, 8, 9, 6, 10, 11, 4,),
        17: (7, 8, 9, 6, 10, 11,),
    }
    joined_home, text_home, image_home, sums, last_sums, *pieces = back(
        (cross_q, cross_k, cross_v, grad_raw, cross_lse, cross_delta),
        (self_q, self_k, self_v, self_lse),
        image_pages, text_pages, norm_gain, norm_bias, (image_closed, text_closed), cross_pairs,
        self_project, cross_query, gate_rows, self_output, hidden, self_out, grad_mixed,
        grad_logit, joined, small_last, (*partial, d_cross_output), jobs, plan, wide, blk,
    )
    expand_piece, reduce_piece, *cross_pieces = pieces[:6]
    project_pieces = pieces[6:]
    (
        grad_cross_pairs, grad_cross_query, grad_cross_output, grad_self_output,
        grad_expand_weight, grad_self_project, grad_reduce_weight,
        joined_blocks, text_grad, image_grad,
        grad_gate_weight, grad_expand_bias, grad_reduce_bias, gains, shifts,
    ) = finish(
        [[piece] for piece in cross_pieces] + [[expand_piece], project_pieces, [reduce_piece]],
        [joined_home, text_home, image_home], sums, last_sums,
    )
    return (
        joined_blocks,
        text_grad,
        image_grad,
        grad_self_project,
        grad_self_output,
        grad_cross_query,
        grad_cross_pairs,
        grad_cross_output,
        grad_expand_weight,
        jnp.transpose(grad_reduce_weight),
        jnp.transpose(grad_gate_weight),
        grad_expand_bias,
        grad_reduce_bias,
        gains,
        shifts,
    )


def normalize(values, gains, biases):
    scaled, inverse = standardize(values)
    return (scaled * gains + biases, scaled, inverse)


def normalize_back(upstream, scaled, inverse, gains):
    result = norm_back(upstream, scaled, inverse, gains)
    return (result, jnp.sum(upstream * scaled, axis=0), jnp.sum(upstream, axis=0))


def gelu_tanh(values):
    return jax.nn.gelu(values, approximate=True)


def forward_doc(queries, carried, key_pairs, allowed, scaling):
    running_max, summed, accumulated = carried
    key_count = key_pairs.shape[0]
    keys_part = key_pairs[:, :D].reshape(key_count, H, HD)
    values_part = key_pairs[:, D:].reshape(key_count, H, HD)
    open_keys = (allowed > 0)[None, None, :]
    scores = (
        jnp.einsum("qhd,khd->hqk", queries, keys_part, preferred_element_type=F32) * scaling
    )
    scores = jnp.where(open_keys, scores, NEGATIVE)
    new_max = jnp.maximum(running_max, jnp.max(scores, axis=-1))
    fading = jnp.exp(running_max - new_max)
    weights = jnp.where(open_keys, jnp.exp(scores - new_max[..., None]), 0.0)
    summed = summed * fading + jnp.sum(weights, axis=-1)
    accumulated = accumulated * fading[..., None] + jnp.einsum(
        "hqk,khd->hqd",
        weights.astype(BF16),
        values_part,
        preferred_element_type=F32,
    )
    return (new_max, summed, accumulated)


def forward_fold(queries, scaling, carried, pieces):
    key_pairs, allowed = pieces

    def forward_per_doc(doc_items):
        doc_queries, doc_max, doc_sum, doc_acc, doc_pairs, doc_allowed = doc_items
        doc_carry = (doc_max, doc_sum, doc_acc)
        result = forward_doc(doc_queries, doc_carry, doc_pairs, doc_allowed, scaling)
        return result

    return lax.map(
        forward_per_doc, (queries, carried[0], carried[1], carried[2], key_pairs, allowed)
    )


def backward_doc(queries, grad_out, log_sum, row_delta, key_pairs, allowed, scaling):
    key_count = key_pairs.shape[0]
    keys_part = key_pairs[:, :D].reshape(key_count, H, HD)
    values_part = key_pairs[:, D:].reshape(key_count, H, HD)
    open_keys = (allowed > 0)[None, None, :]
    scores = (
        jnp.einsum("qhd,khd->hqk", queries, keys_part, preferred_element_type=F32) * scaling
    )
    probabilities = jnp.where(open_keys, jnp.exp(scores - log_sum[..., None]), 0.0)
    grad_probs = jnp.einsum(
        "qhd,khd->hqk", grad_out, values_part, preferred_element_type=F32
    )
    grad_scores = (probabilities * (grad_probs - row_delta[..., None])).astype(BF16)
    query_grad = (
        jnp.einsum("hqk,khd->qhd", grad_scores, keys_part, preferred_element_type=F32)
        * scaling
    )
    key_grad = (
        jnp.einsum("hqk,qhd->khd", grad_scores, queries, preferred_element_type=F32)
        * scaling
    )
    value_grad = jnp.einsum(
        "hqk,qhd->khd",
        probabilities.astype(BF16),
        grad_out,
        preferred_element_type=F32,
    )
    return (
        query_grad,
        jnp.concatenate(
            [key_grad.reshape(key_count, D), value_grad.reshape(key_count, D)], axis=-1
        ),
    )


def backward_fold(queries, grad_out, log_sum, row_delta, scaling, pieces):
    key_pairs, allowed = pieces

    def backward_per_doc(doc_items):
        doc_queries, doc_grad, doc_log, doc_delta, doc_pairs, doc_allowed = doc_items
        result = backward_doc(
            doc_queries, doc_grad, doc_log, doc_delta, doc_pairs, doc_allowed, scaling
        )
        return result

    query_parts, pair_parts = lax.map(
        backward_per_doc, (queries, grad_out, log_sum, row_delta, key_pairs, allowed)
    )
    return (query_parts, pair_parts)


def start_state():
    return (
        jnp.full((DOCS, H, PAGE), NEGATIVE, F32),
        jnp.zeros((DOCS, H, PAGE), F32),
        jnp.zeros((DOCS, H, PAGE, HD), F32),
    )


def finish_state(state):
    running_max, summed, accumulated = state
    result = jnp.transpose(accumulated / summed[..., None], (0, 2, 1, 3))
    return (result, running_max + jnp.log(summed))


def tile_order(grad, wide_count, blk_count):
    rows, cols = grad.shape
    tiled = grad.reshape(wide_count, rows // wide_count, blk_count, cols // blk_count)
    return jnp.transpose(tiled, (0, 2, 1, 3)).reshape(
        wide_count * blk_count * (rows // wide_count), cols // blk_count
    )


def plain_body(
    text_blocks,
    image_blocks,
    cotangent,
    text_mask,
    page_regions,
    doc_pages,
    self_project,
    self_output,
    cross_query,
    cross_pairs,
    cross_output,
    gate_weight,
    expand_weight,
    expand_bias,
    reduce_weight,
    reduce_bias,
    norm_gain,
    norm_bias,
):
    scaling = HD ** (-0.5)
    block_shape = text_blocks.shape
    offsets = jnp.arange(PAGE, dtype=jnp.int32)
    living = (lax.axis_index("blk") < doc_pages)[:, None]
    text_open = (living & ((text_mask > 0) | (offsets[None, :] == 0))).astype(BF16)
    image_open = (living & (offsets[None, :] < page_regions)).astype(BF16)
    text_rows = text_blocks.reshape(-1, D).astype(F32)
    image_rows = image_blocks.reshape(-1, D).astype(F32)
    normed_text, scaled_first, inverse_first = normalize(text_rows, norm_gain[0], norm_bias[0])
    normed_low = normed_text.astype(BF16)
    triples = product(normed_low, self_project).astype(BF16)
    self_queries = triples[:, :D].reshape(DOCS, PAGE, H, HD)
    self_pairs = triples[:, D:].reshape(DOCS, PAGE, 2 * D)
    self_state = forward_fold(
        self_queries,
        scaling,
        start_state(),
        (
            lax.all_gather(self_pairs, "blk", axis=1, tiled=True),
            lax.all_gather(text_open, "blk", axis=1, tiled=True),
        ),
    )
    self_result, self_logsum = finish_state(self_state)
    self_low = self_result.reshape(-1, D).astype(BF16)
    hidden = text_rows + product(self_low, self_output)
    cross_normed, scaled_cross, inverse_cross = normalize(hidden, norm_gain[1], norm_bias[1])
    cross_low = cross_normed.astype(BF16)
    gate_values = jax.nn.sigmoid(product(cross_low, gate_weight))
    image_normed, scaled_image, inverse_image = normalize(image_rows, norm_gain[2], norm_bias[2])
    image_low = image_normed.astype(BF16)
    image_pairs = product(image_low, cross_pairs).astype(BF16).reshape(DOCS, PAGE, 2 * D)
    cross_queries = product(cross_low, cross_query).astype(BF16).reshape(DOCS, PAGE, H, HD)
    cross_state = forward_fold(
        cross_queries,
        scaling,
        start_state(),
        (
            lax.all_gather(image_pairs, "blk", axis=1, tiled=True),
            lax.all_gather(image_open, "blk", axis=1, tiled=True),
        ),
    )
    cross_result, cross_logsum = finish_state(cross_state)
    gate_heads = gate_values.reshape(DOCS, PAGE, H, 1)
    gated_low = (cross_result * gate_heads).reshape(-1, D).astype(BF16)
    mixed_rows = hidden + product(gated_low, cross_output)
    final_normed, scaled_final, inverse_final = normalize(mixed_rows, norm_gain[3], norm_bias[3])
    final_low = final_normed.astype(BF16)
    inner_rows = product(final_low, expand_weight) + expand_bias
    active_low = gelu_tanh(inner_rows).astype(BF16)
    joined_blocks = (
        (mixed_rows + product(active_low, reduce_weight) + reduce_bias)
        .reshape(block_shape)
        .astype(BF16)
    )
    upstream = cotangent.reshape(-1, D)
    upstream_float = upstream.astype(F32)
    grad_reduce_bias = jnp.sum(upstream_float, axis=0)
    grad_reduce_weight = transposed(active_low, upstream)
    grad_active = against(upstream, reduce_weight).astype(BF16)
    gelu_value, gelu_pull = jax.vjp(gelu_tanh, inner_rows)
    grad_inner = gelu_pull(grad_active.astype(F32))[0].astype(BF16)
    grad_expand_bias = jnp.sum(grad_inner.astype(F32), axis=0)
    grad_expand_weight = transposed(final_low, grad_inner)
    back_final, gain_final, shift_final = normalize_back(
        against(grad_inner, expand_weight), scaled_final, inverse_final, norm_gain[3]
    )
    grad_mixed = upstream_float + back_final
    grad_branch = grad_mixed.astype(BF16)
    grad_cross_output = transposed(gated_low, grad_branch)
    grad_gated = against(grad_branch, cross_output).astype(BF16)
    grad_gated_heads = grad_gated.astype(F32).reshape(DOCS, PAGE, H, HD)
    grad_gate = jnp.sum(grad_gated_heads * cross_result, axis=-1).reshape(-1, H)
    grad_logit = grad_gate * gate_values * (1.0 - gate_values)
    grad_gate_weight = lax.dot_general(
        cross_low.astype(F32), grad_logit, (((0,), (0,)), ((), ())), precision=HIGHEST
    )
    grad_raw = (grad_gated_heads * gate_heads).astype(BF16)
    cross_delta = jnp.transpose(
        jnp.sum(grad_raw.astype(F32) * cross_result, axis=-1), (0, 2, 1)
    )
    cross_carry = backward_fold(
        cross_queries,
        grad_raw,
        cross_logsum,
        cross_delta,
        scaling,
        (
            lax.all_gather(image_pairs, "blk", axis=1, tiled=True),
            lax.all_gather(image_open, "blk", axis=1, tiled=True),
        ),
    )
    cross_home = lax.psum_scatter(
        cross_carry[1].astype(BF16), "blk", scatter_dimension=1, tiled=True
    ).astype(F32)
    cross_query_sum = cross_carry[0]
    cross_query_low = cross_query_sum.reshape(-1, D).astype(BF16)
    cross_pair_low = cross_home.reshape(-1, 2 * D).astype(BF16)
    grad_cross_query = transposed(cross_low, cross_query_low)
    grad_cross_pairs = transposed(image_low, cross_pair_low)
    back_image, gain_image, shift_image = normalize_back(
        against(cross_pair_low, cross_pairs), scaled_image, inverse_image, norm_gain[2]
    )
    image_grad = back_image.reshape(block_shape).astype(BF16)
    grad_cross_in = against(cross_query_low, cross_query) + lax.dot_general(
        grad_logit, gate_weight.astype(F32), (((1,), (1,)), ((), ())), precision=HIGHEST
    )
    back_cross, gain_cross, shift_cross = normalize_back(
        grad_cross_in, scaled_cross, inverse_cross, norm_gain[1]
    )
    grad_hidden = grad_mixed + back_cross
    grad_self_branch = grad_hidden.astype(BF16)
    grad_self_output = transposed(self_low, grad_self_branch)
    grad_self_result = (
        against(grad_self_branch, self_output).astype(BF16).reshape(DOCS, PAGE, H, HD)
    )
    self_delta = jnp.transpose(
        jnp.sum(grad_self_result.astype(F32) * self_result, axis=-1), (0, 2, 1)
    )
    self_carry = backward_fold(
        self_queries,
        grad_self_result,
        self_logsum,
        self_delta,
        scaling,
        (
            lax.all_gather(self_pairs, "blk", axis=1, tiled=True),
            lax.all_gather(text_open, "blk", axis=1, tiled=True),
        ),
    )
    self_home = lax.psum_scatter(
        self_carry[1].astype(BF16), "blk", scatter_dimension=1, tiled=True
    ).astype(F32)
    self_query_sum = self_carry[0]
    grad_triples = jnp.concatenate(
        [self_query_sum.reshape(-1, D), self_home.reshape(-1, 2 * D)], axis=-1
    ).astype(BF16)
    grad_self_project = transposed(normed_low, grad_triples)
    back_first, gain_first, shift_first = normalize_back(
        against(grad_triples, self_project), scaled_first, inverse_first, norm_gain[0]
    )
    text_grad = (grad_hidden + back_first).reshape(block_shape).astype(BF16)
    wide_count = lax.axis_size("wide")
    blk_count = lax.axis_size("blk")
    large_grads = (
        grad_self_project,
        grad_self_output,
        grad_cross_query,
        grad_cross_pairs,
        grad_cross_output,
        grad_expand_weight,
        grad_reduce_weight,
    )
    ordered = tuple((tile_order(grad, wide_count, blk_count) for grad in large_grads))
    summed_grads = lax.psum_scatter(ordered, ("wide", "blk"), scatter_dimension=0, tiled=True)
    small_sums = lax.psum(
        (
            grad_gate_weight,
            grad_expand_bias,
            grad_reduce_bias,
            jnp.stack([gain_first, gain_cross, gain_image, gain_final]),
            jnp.stack([shift_first, shift_cross, shift_image, shift_final]),
        ),
        ("wide", "blk"),
    )
    return (
        joined_blocks,
        text_grad,
        image_grad,
        summed_grads[0],
        summed_grads[1],
        summed_grads[2],
        summed_grads[3],
        summed_grads[4],
        summed_grads[5],
        summed_grads[6],
        small_sums[0],
        small_sums[1],
        small_sums[2],
        small_sums[3],
        small_sums[4],
    )


def solution(mesh):
    rows = P("wide", "blk", None)
    fits = (mesh.shape["wide"], mesh.shape["blk"]) == PLANNED
    return jax.shard_map(
        body if fits else plain_body,
        mesh=mesh,
        in_specs=(rows,) * 3 + (P("wide", "blk"),) * 2 + (P("wide"),) + (P(),) * 12,
        out_specs=(rows,) * 3 + (P("wide", "blk"),) * 7 + (P(),) * 5,
        check_vma=False,
    )
```

```python
import functools
from typing import NamedTuple

import jax
import jax.numpy as jnp
from jax import lax
from jax.experimental import pallas as pl
from jax.experimental.pallas import tpu as pltpu
from jax.sharding import PartitionSpec as P

D = 768
H = 12
HD = 64
FF = 3072
PAGE = 128
DOCS = 2
ROWS = DOCS * PAGE
QUAD = 256
QUADS = D // QUAD
PAIR = 128
IMAGE = 112
EXTRA = 16
SUMS = 24
PLANNED = (4, 8)
EPSILON = 1e-05
NEGATIVE = -1e30
HIGHEST = lax.Precision.HIGHEST
BF16 = jnp.bfloat16
F32 = jnp.float32
VMEM_LIMIT = 62 * 1024 * 1024


def product(left, right):
    return jnp.dot(left, right, preferred_element_type=F32)


def against(left, right, precision=None):
    return lax.dot_general(
        left, right, (((1,), (1,)), ((), ())), preferred_element_type=F32, precision=precision
    )


def transposed(left, right, precision=None):
    return lax.dot_general(
        left, right, (((0,), (0,)), ((), ())), preferred_element_type=F32, precision=precision
    )


def standardize(values):
    centred = values - jnp.mean(values, axis=-1, keepdims=True)
    inverse = lax.rsqrt(jnp.mean(centred * centred, axis=-1, keepdims=True) + EPSILON)
    return centred * inverse, inverse


def norm_back(upstream, scaled, inverse, gains):
    weighted = upstream * gains
    return inverse * (
        weighted
        - jnp.mean(weighted, axis=-1, keepdims=True)
        - scaled * jnp.mean(weighted * scaled, axis=-1, keepdims=True)
    )


def column_sum(values):
    return jnp.sum(values, axis=0, keepdims=True)


def normalize_page(page, index, gain, shift, normed):
    rows = page.shape[0]
    scaled, _ = standardize(page[...].astype(F32))
    normed[index * rows : (index + 1) * rows, :] = (scaled * gain + shift).astype(BF16)


def normalize_pages(pages, gain, shift, normed):
    for index in range(pages.shape[0]):
        normalize_page(pages.at[index], index, gain, shift, normed)


def lane_index(rows):
    return lax.broadcasted_iota(jnp.int32, (rows, PAIR), 1)


def side_masks(rows):
    lanes = lane_index(rows)
    return [(lanes < HD).astype(BF16), (lanes >= HD).astype(BF16)]


def attend_forward(q_ref, k_ref, v_ref, closed_ref, out_ref, lse_ref):
    lanes = lane_index(ROWS)
    masks = side_masks(ROWS)
    first_lane = (lanes == 0).astype(BF16)
    stats = jnp.zeros((ROWS, PAIR), F32)
    for pair in range(QUAD // PAIR):
        cols = slice(pair * PAIR, (pair + 1) * PAIR)
        keys = jnp.concatenate([k_ref[:, cols], closed_ref[...]], axis=1)
        values = v_ref[:, cols]
        queries = q_ref[:, cols]
        results = []
        for side in range(2):
            query = jnp.concatenate([queries * masks[side], first_lane], axis=1)
            scores = against(query, keys)
            top = jnp.max(scores, axis=1, keepdims=True)
            weights = jnp.exp(scores - top)
            total = jnp.sum(weights, axis=1, keepdims=True)
            results.append(product(weights.astype(BF16), values) / total)
            stats = jnp.where(lanes == pair * 2 + side, top + jnp.log(total), stats)
        out_ref[:, cols] = jnp.where(lanes < HD, results[0], results[1])
    lse_ref[...] = jnp.transpose(stats)[:8, :]


def attend_backward(q_ref, k_ref, v_ref, do_ref, lse_ref, delta_ref, closed_ref, dq_ref, dkv_ref, hook):
    lanes = lane_index(ROWS)
    masks = side_masks(ROWS)
    first_lane = (lanes == 0).astype(BF16)
    for pair in range(QUAD // PAIR):
        cols = slice(pair * PAIR, (pair + 1) * PAIR)
        key_part = k_ref[:, cols]
        keys = jnp.concatenate([key_part, closed_ref[...]], axis=1)
        values = v_ref[:, cols]
        dq_parts = []
        dk = None
        dv = None
        for side in range(2):
            row = pair * 2 + side
            query = q_ref[:, cols] * masks[side]
            grad_out = do_ref[:, cols] * masks[side]
            scores = against(keys, jnp.concatenate([query, first_lane], axis=1))
            weights = jnp.exp(scores - lse_ref[row : row + 1, :])
            grad_weights = against(values, grad_out)
            grad_scores = (weights * (grad_weights - delta_ref[row : row + 1, :])).astype(BF16)
            dv_part = product(weights.astype(BF16), grad_out)
            dk_part = product(grad_scores, query)
            dv = dv_part if dv is None else dv + dv_part
            dk = dk_part if dk is None else dk + dk_part
            dq_parts.append(transposed(grad_scores, key_part))
        dq_ref[:, cols] = (jnp.where(lanes < HD, dq_parts[0], dq_parts[1]) * HD ** (-0.5)).astype(
            BF16
        )
        dkv_ref[:, cols] = dk.astype(BF16)
        dkv_ref[:, QUAD + pair * PAIR : QUAD + (pair + 1) * PAIR] = dv.astype(BF16)
        if pair == 0:
            hook()


def head_sums(values):
    sums = []
    lanes = lane_index(values.shape[0])
    for pair in range(H // 2):
        part = values[:, pair * PAIR : (pair + 1) * PAIR]
        sums.append(jnp.sum(jnp.where(lanes < HD, part, 0.0), axis=1, keepdims=True))
        sums.append(jnp.sum(jnp.where(lanes >= HD, part, 0.0), axis=1, keepdims=True))
    return sums


def head_rows(sums):
    lanes = lane_index(ROWS)
    stats = jnp.zeros((ROWS, PAIR), F32)
    for head, value in enumerate(sums):
        stats = jnp.where(lanes == (head // 4) * 8 + head % 4, value, stats)
    return jnp.transpose(stats)[: 8 * QUADS, :]


def spread_heads(gates):
    lanes = lane_index(gates.shape[0])
    parts = []
    for pair in range(H // 2):
        parts.append(
            jnp.where(lanes < HD, gates[:, 2 * pair : 2 * pair + 1], gates[:, 2 * pair + 1 : 2 * pair + 2])
        )
    return jnp.concatenate(parts, axis=1)


def put_rows(out, start, value):
    rows, lanes = out.shape[-2:]
    cuts = (value.shape[1] // lanes).bit_length() - 1
    lead = len(out.shape) - 2
    low = start
    while low < start + value.shape[0]:
        tile = low // rows
        high = min(start + value.shape[0], (tile + 1) * rows)
        for cut in range(1 << cuts):
            piece = value[low - start : high - start, cut * lanes : (cut + 1) * lanes]
            at = bits_of(cut, cuts) + bits_of(tile, lead - cuts)
            out[at + (slice(low - tile * rows, high - tile * rows), slice(None))] = piece
        low = high


class Gather:
    def __init__(self, places, names, packed, landed, waits):
        self.places = places
        self.names = names
        self.packed = packed
        self.landed = landed
        self.sends, self.receives = waits

    @staticmethod
    def waits(names):
        count = DOCS << len(names)
        return [pltpu.SemaphoreType.DMA((count,))] * 2

    def swap(self, turn):
        doc = self.places.turn if turn == 0 else 1 - self.places.turn
        return remote(
            self.packed.at[doc], self.landed.at[turn], self.sends.at[turn], self.receives.at[turn],
            self.places.swap(turn),
        )

    def start(self):
        stays = self.places.swap_stays()
        pl.when(jnp.logical_not(stays))(lambda: self.swap(0).start())
        self.swap(1).start()

        @pl.when(stays)
        def _():
            self.landed[0] = self.packed[self.places.turn]

    def copy(self, block, turn):
        stage = block.bit_length() - 1
        source = (block - (1 << stage)) * DOCS + turn
        at = block * DOCS + turn
        return remote(
            self.landed.at[source], self.landed.at[at], self.sends.at[at], self.receives.at[at],
            self.places.flip(self.names[stage]),
        )

    def arrive(self, block, turn):
        if block > 0:
            self.copy(block, turn).wait_recv()
        elif turn > 0:
            self.swap(turn).wait_recv()
        else:
            stays = self.places.swap_stays()
            pl.when(jnp.logical_not(stays))(lambda: self.swap(0).wait_recv())
        for stage in range(block.bit_length(), len(self.names)):
            self.copy(block + (1 << stage), turn).start()

    def end(self):
        stays = self.places.swap_stays()
        pl.when(jnp.logical_not(stays))(lambda: self.swap(0).wait_send())
        self.swap(1).wait_send()
        for block in range(1, 1 << len(self.names)):
            for turn in range(DOCS):
                self.copy(block, turn).wait_send()


def closed_rows(is_open):
    row = jnp.where(is_open, 0.0, NEGATIVE)
    wide = jnp.concatenate([row, jnp.zeros((1, D - PAGE), F32)], axis=1)
    return jnp.broadcast_to(wide, (EXTRA, D)).astype(BF16)


def closed_column(rows):
    row = rows[0:1, 0:PAGE].astype(F32)
    turned = jnp.transpose(jnp.broadcast_to(row, (PAGE, PAGE)))
    return jnp.where(lane_index(PAGE) == 0, turned, 0.0).astype(BF16)


def self_forward_kernel(
    wide, blk,
    regions, doc_pages, text_in, image_in, cot_in, mask, gain, shift, wq, wk, wv,
    out, lse, q_out, k_out, v_out, text_out, image_out, cot_out, text_closed, image_closed,
    normed, text_packed, image_packed, text_landed, image_landed, cot_landed,
    text_sends, text_receives, image_sends, image_receives, cot_sends, cot_receives, local,
):
    step = pl.program_id(0)
    places = Places(wide, blk)
    groups = group_bits(blk)
    blocks = 1 << len(groups)
    text = Gather(places, groups, text_packed, text_landed, (text_sends, text_receives))
    image = Gather(places, groups, image_packed, image_landed, (image_sends, image_receives))
    cot = Gather(places, [], cot_in, cot_landed, (cot_sends, cot_receives))
    outward = [
        pltpu.make_async_copy(text_landed.at[:, pl.ds(0, PAGE)], text_out, local.at[0]),
        pltpu.make_async_copy(image_landed.at[:, pl.ds(0, IMAGE)], image_out, local.at[1]),
        pltpu.make_async_copy(cot_landed, cot_out, local.at[2]),
    ]

    @pl.when(step == 0)
    def _():
        offsets = lax.broadcasted_iota(jnp.int32, (1, PAGE), 1)
        for doc in range(DOCS):
            text_packed[doc, 0:PAGE, :] = text_in[doc]
            living = places.b < doc_pages[doc]
            is_open = ((mask[doc : doc + 1, :] > 0) | (offsets == 0)) & living
            text_packed[doc, PAGE : PAGE + EXTRA, :] = closed_rows(is_open)
        greet(places, groups, True)
        text.start()
        for doc in range(DOCS):
            image_packed[doc, 0:IMAGE, :] = image_in[doc, 0:IMAGE, :]
            living = places.b < doc_pages[doc]
            is_open = (offsets < regions[0:1, doc : doc + 1]) & living
            image_packed[doc, IMAGE : IMAGE + EXTRA, :] = closed_rows(is_open)
        text.arrive(0, 0)
        text.arrive(0, 1)
        image.start()

        def take(block, turn):
            index = block * DOCS + turn
            page = text_landed.at[index, pl.ds(0, PAGE)]
            normalize_page(page, index, gain[0:1, :], shift[0:1, :], normed)
            text_closed[index * PAGE : (index + 1) * PAGE, :] = closed_column(
                text_landed[index, PAGE : PAGE + EXTRA, :]
            )

        for turn in range(DOCS):
            take(0, turn)
        for block in range(1, blocks):
            for turn in range(DOCS):
                text.arrive(block, turn)
            if block == 1:
                image.arrive(0, 0)
                image.arrive(0, 1)
                cot.start()
            for turn in range(DOCS):
                take(block, turn)

    @pl.when(step == 1)
    def _():
        outward[0].start()
        for block in range(1, blocks // 2):
            for turn in range(DOCS):
                image.arrive(block, turn)

    q_out[...] = (product(normed[0:ROWS, :], wq[...]).astype(BF16) * HD ** (-0.5)).astype(BF16)
    k_out[...] = product(normed[...], wk[...]).astype(BF16)
    v_out[...] = product(normed[...], wv[...]).astype(BF16)
    attend_forward(q_out, k_out, v_out, text_closed, out, lse)

    @pl.when(step == QUADS - 1)
    def _():
        for turn in range(DOCS):
            cot.arrive(0, turn)
        outward[2].start()
        for block in range(max(1, blocks // 2), blocks):
            for turn in range(DOCS):
                image.arrive(block, turn)
        outward[1].start()
        for index in range(blocks * DOCS):
            column = closed_column(image_landed[index, IMAGE : IMAGE + EXTRA, :])
            image_closed[index * IMAGE : (index + 1) * IMAGE, :] = column[0:IMAGE, :]
        for stream in (text, image, cot):
            stream.end()
        for copy in outward:
            copy.wait()


def cross_forward_kernel(
    text, pages, self_out, w_self, w_gate, gain, shift, closed, wq, wk, wv,
    hidden, gate, out, lse, q_out, k_out, v_out,
    normed, cross, gates,
):
    @pl.when(pl.program_id(0) == 0)
    def _():
        normalize_pages(pages, gain[2:3, :], shift[2:3, :], normed)
        branch = product(self_out[...].astype(BF16), w_self[...])
        for index in range(DOCS):
            rows = slice(index * PAGE, (index + 1) * PAGE)
            hidden[rows, :] = text[index].astype(F32) + branch[rows, :]
        scaled, _ = standardize(hidden[...])
        cross[...] = (scaled * gain[1:2, :] + shift[1:2, :]).astype(BF16)
        gates[...] = jnp.zeros_like(gates)
        gates[0:H, :] = w_gate[...]
        gate[...] = jax.nn.sigmoid(against(cross[...], gates[...]))

    q_out[...] = (product(cross[...], wq[...]).astype(BF16) * HD ** (-0.5)).astype(BF16)
    k_out[...] = product(normed[...], wk[...]).astype(BF16)
    v_out[...] = product(normed[...], wv[...]).astype(BF16)
    attend_forward(q_out, k_out, v_out, closed, out, lse)


def expand_part(wide, blk, step):
    few = (slice(None),) * (wide.bit_length() - 2)
    rest = (slice(None),) * (blk.bit_length() - 3)
    return few + (step // 2, step % 2) + rest, (slice(None), slice(None))


def reduce_part(wide, blk, step):
    cuts = wide.bit_length() - 2
    rest = (slice(None),) * (blk.bit_length() - 1)
    if cuts >= 2:
        lead = (step // 2, step % 2) + (slice(None),) * (cuts - 2) + rest
        return lead, (slice(None), slice(None))
    lanes = pl.ds(pl.multiple_of((step % 2) * D, D), D)
    return (step // 2,) + rest, (slice(None), lanes)


def put_expand(out, value, step, wide, blk):
    cuts, bits = wide.bit_length() - 2, blk.bit_length() - 1
    rows, lanes = out.shape[-2:]
    for cut in range(1 << cuts):
        for part in range(D // rows):
            at = bits_of(cut, cuts) + (step // 2, step % 2) + bits_of(part, bits - 1)
            out[at] = value[part * rows : (part + 1) * rows, cut * lanes : (cut + 1) * lanes]


def put_reduce(out, value, step, wide, blk):
    cuts, bits = wide.bit_length() - 2, blk.bit_length() - 1
    rows, lanes = out.shape[-2:]
    for part in range(D // rows):
        place = bits_of(part, bits + 1)
        piece = value[part * rows : (part + 1) * rows, :]
        if cuts >= 2:
            for cut in range(D // lanes):
                at = (step // 2, step % 2) + bits_of(cut, cuts - 2) + place
                out[at] = piece[:, cut * lanes : (cut + 1) * lanes]
        else:
            out[(step // 2,) + place + (slice(None), pl.ds(pl.multiple_of((step % 2) * D, D), D))] = piece


def forward_back_kernel(
    steps, wide, blk,
    hidden, raw, gate, cots, w_out, gain, shift, w_expand, b_expand, w_reduce, b_reduce,
    joined, early_expand, late_expand, early_reduce, late_reduce, d_out, grad_mixed, grad_raw,
    delta, grad_logit, small,
    gated, mixed, final, upstream, joined_sum, back_sum,
    expand_all, reduce_all, expand_got, reduce_got, expand_next, reduce_next,
    sends, receives, next_sends, next_receives, local,
):
    step = pl.program_id(0)
    places = Places(wide, blk)
    core, along, across = ("w", 0), ("w", 1), ("b", 0)
    cuts = wide.bit_length() - 2
    kinds = (
        (expand_part, expand_all, expand_got, expand_next, along),
        (reduce_part, reduce_all, reduce_got, reduce_next, across),
    )

    def copies(at):
        found = []
        for index, (part, grad, got, _, _) in enumerate(kinds):
            lead, tail = part(wide, blk, at)
            found.append(
                remote(
                    grad.at[lead + (1 - places.bit(core),) + tail],
                    got.at[lead + tail],
                    sends.at[index, at],
                    receives.at[index, at],
                    places.flip(core),
                )
            )
        return found

    def add(at):
        for (part, grad, got, _, _), copy in zip(kinds, copies(at)):
            copy.wait_recv()
            lead, tail = part(wide, blk, at)
            add_blocks(got.at[lead + tail], grad.at[lead + (places.bit(core),) + tail])

    def pieces(at):
        (lead, tail), (far_lead, far_tail) = (
            expand_part(wide, blk, at), reduce_part(wide, blk, at)
        )
        bit, far_bit = places.bit(along), places.bit(across)
        head, rest = lead[: cuts - 1], lead[cuts:]
        yield (
            expand_got.at[head + (bit,) + rest + tail],
            expand_got.at[head + (1 - bit,) + rest + tail],
            expand_next.at[head + rest[1:] + tail],
        )
        yield (
            reduce_got.at[far_lead[:-1] + (far_bit,) + far_tail],
            reduce_got.at[far_lead[:-1] + (1 - far_bit,) + far_tail],
            reduce_next.at[far_lead[1:-1] + far_tail],
        )

    def onward(at):
        return [
            remote(
                send, land, next_sends.at[index, at], next_receives.at[index, at],
                places.flip(kinds[index][4]),
            )
            for index, (_, send, land) in enumerate(pieces(at))
        ]

    @pl.when(step == 0)
    def _():
        greet(places, [core, along, across], False)
        upstream[0:PAGE, :] = cots[0]
        upstream[PAGE:ROWS, :] = cots[1]
        small[...] = jnp.zeros_like(small)
        gated[...] = (spread_heads(gate[...]) * raw[...]).astype(BF16)
        rows = hidden[...] + product(gated[...], w_out[...])
        mixed[...] = rows
        scaled, _ = standardize(rows)
        final[...] = (scaled * gain[3:4, :] + shift[3:4, :]).astype(BF16)
        joined_sum[...] = rows + b_reduce[...].reshape(1, D)
        back_sum[...] = jnp.zeros_like(back_sum)

    inner = product(final[...], w_expand[...]) + b_expand[...]
    squared = inner * inner
    root = (2.0 / jnp.pi) ** 0.5
    curve = jnp.tanh(root * inner * (1.0 + 0.044715 * squared))
    half = 0.5 * (1.0 + curve)
    active = (inner * half).astype(BF16)
    slope = half + 0.5 * inner * (1.0 - curve * curve) * (root * (1.0 + 3.0 * 0.044715 * squared))
    joined_sum[...] += product(active, w_reduce[...])
    grad_active = against(upstream[...], w_reduce[...]).astype(BF16)
    grad_inner = (grad_active.astype(F32) * slope).astype(BF16)
    small[pl.ds(4 + step, 1), :] = column_sum(grad_inner.astype(F32))
    back_sum[...] += against(grad_inner, w_expand[...])
    put_expand(expand_all, transposed(grad_inner, final[...]).astype(BF16), step, wide, blk)
    put_reduce(reduce_all, transposed(upstream[...], active).astype(BF16), step, wide, blk)
    for copy in copies(step):
        copy.start()
    for at in range(steps - 1):

        @pl.when(step == at + 1)
        def _():
            add(at)
            if at < steps // 2:
                for copy in onward(at):
                    copy.start()

    @pl.when(step == steps - 1)
    def _():
        total = joined_sum[...].astype(BF16)
        joined[0] = total[:PAGE]
        joined[1] = total[PAGE:]
        scaled, inverse = standardize(mixed[...])
        back = back_sum[...]
        cotangent = upstream[...].astype(F32)
        grad = cotangent + norm_back(back, scaled, inverse, gain[3:4, :])
        grad_mixed[...] = grad
        branch = grad.astype(BF16)
        put_rows(d_out, 0, transposed(branch, gated[...]).astype(BF16))
        grad_gated = against(branch, w_out[...]).astype(BF16).astype(F32)
        gates = gate[...]
        lanes = lane_index(ROWS)
        logit = jnp.zeros((ROWS, PAIR), F32)
        for head, value in enumerate(head_sums(grad_gated * raw[...])):
            logit = jnp.where(lanes == head, value, logit)
        grad_logit[...] = logit * gates * (1.0 - gates)
        rounded = (spread_heads(gates) * grad_gated).astype(BF16)
        grad_raw[...] = rounded
        delta[...] = head_rows(head_sums(rounded.astype(F32) * raw[...]))
        small[0:1, :] = column_sum(cotangent)
        small[1:2, :] = column_sum(back * scaled)
        small[2:3, :] = column_sum(back)
        add(steps - 1)
        half = (slice(None),) * cuts
        moves = [
            pltpu.make_async_copy(expand_got.at[half + (1,)], late_expand, local.at[0]),
            pltpu.make_async_copy(reduce_got.at[1], late_reduce, local.at[1]),
        ]
        for move in moves:
            move.start()
        for at in range(steps // 2):
            for copy, (kept, _, land) in zip(onward(at), pieces(at)):
                copy.wait()
                add_blocks(land, kept)
        moves += [
            pltpu.make_async_copy(expand_next, early_expand, local.at[2]),
            pltpu.make_async_copy(reduce_next, early_reduce, local.at[3]),
        ]
        for move in moves[2:]:
            move.start()
        for at in range(steps):
            for copy in copies(at):
                copy.wait_send()
        for move in moves:
            move.wait()


def spread_back(dkv, wk, wv, dx):
    weights = jnp.concatenate([wk[...], wv[...]], axis=1)

    size = dx.shape[0] // 4

    def chunk(index, carry):
        rows = pl.ds(pl.multiple_of(index * size, 16), size)
        dx[rows, :] += against(dkv[rows, :], weights)
        return carry

    lax.fori_loop(0, 4, chunk, 0)


def round_pages(dx, keep, send):
    half = dx.shape[0] // 2
    for target, start in ((send, half), (keep, 0)):
        size = half // 4
        for part in range(4):
            low = start + part * size
            target[part * size : (part + 1) * size, :] = dx[low : low + size, :].astype(BF16)


def page_sums(pages, dx):
    gain_sum = jnp.zeros((1, D), F32)
    shift_sum = jnp.zeros((1, D), F32)
    count, size, _ = pages.shape
    for index in range(count):
        scaled, _ = standardize(pages[index].astype(F32))
        part = dx[index * size : (index + 1) * size, :]
        gain_sum += column_sum(part * scaled)
        shift_sum += column_sum(part)
    return gain_sum, shift_sum


END = 99


def moves_of(plan, jobs):
    done = [-1] * len(jobs)
    moves = {}
    for point in sorted(plan):
        moves[point] = []
        for index in plan[point]:
            moves[point].append((index, done[index]))
            done[index] += 1
    moves[END] = [
        (index, stage)
        for stage in range(-1, max(len(job.order) for job in jobs))
        for index, job in enumerate(jobs)
        if done[index] <= stage < len(job.order)
    ]
    return moves


def run_moves(moves, point, scatters):
    for index, stage in moves.get(point, ()):
        if stage < 0:
            scatters[index].start()
        else:
            scatters[index].add(stage)


def back_kernel(wide, blk, jobs, plan, *refs):
    refs = iter(refs)
    (
        images, image_own, texts, gain, shift, cross_closed, self_closed,
        q_cross, k_cross, v_cross, do_cross, lse_cross, delta_cross, wk_cross, wv_cross,
        q_self, k_self, v_self, lse_self, wq_self, wk_self, wv_self,
        w_query, w_gate, w_self, hidden, self_out, grad_mixed, grad_logit, joined, last_small,
    ) = (next(refs) for _ in range(31))
    early_expand, late_expand, early_reduce, late_reduce, d_cross_output = (
        next(refs) for _ in range(5)
    )
    joined_out, text_out, image_out, sums_out, last_out = (next(refs) for _ in range(5))
    outs = [next(refs) if job.ends else None for job in jobs]
    normed, dkv, dx, dq, gates, grad_hidden, self_do, self_delta = (next(refs) for _ in range(8))
    pages, keep, send, row_sums, sums_in, local = (next(refs) for _ in range(6))
    d_pairs, d_query, d_self_output, d_project, expand_both, reduce_both = (
        next(refs) for _ in range(6)
    )
    sources = [
        early_expand, late_expand, early_reduce, late_reduce, expand_both, reduce_both,
        d_pairs, d_query, d_cross_output, d_self_output,
    ] + [d_project] * (len(jobs) - 10)
    lands = [expand_both.at[0], expand_both.at[1], reduce_both.at[0], reduce_both.at[1]]
    lands += [None] * (len(jobs) - 4)
    step = pl.program_id(0)
    places = Places(wide, blk)
    names = bit_names(wide, blk)
    groups = group_bits(blk)
    scatters = [
        Scatter(places, job, source, refs, last)
        for job, source, last in zip(jobs, sources, lands)
    ]
    moves = moves_of(plan, jobs)
    home = Home(places, refs)
    image_rows = pl.ds(0, k_cross.shape[0] // 2)
    image = Rows(
        places, groups, keep.at[image_rows], send.at[image_rows], row_sums.at[image_rows], refs
    )
    text = Rows(places, groups, keep, send, row_sums, refs)
    image_pages = pages.at[:, pl.ds(0, IMAGE)]
    fetches = [
        pltpu.make_async_copy(images, image_pages, local.at[0]),
        pltpu.make_async_copy(texts, pages, local.at[1]),
        pltpu.make_async_copy(grad_mixed, grad_hidden, local.at[2]),
        pltpu.make_async_copy(w_self, normed.at[pl.ds(0, D)], local.at[3]),
    ]
    sums = Total(places, refs)
    last_sums = Total(places, refs)

    def pump(point):
        if point in (7, 9, 11):
            sums.add((point - 7) // 2, sums_out)
        if point == 7:
            image.add(0)
        if point == 11:
            for stage in range(1, len(groups)):
                image.add(stage)
            image.norm(image_own, gain[2:3, :], None)
        run_moves(moves, point, scatters)

    def pumps(points):
        for point in points:
            pl.when(step == (point - 1) // 2)(functools.partial(pump, point))

    @pl.when(step == 0)
    def _():
        fetches[0].start()
        fetches[2].start()
        greet(places, names, True, ((("w", 1), ("b", 0)), (("b", 2), ("b", 1))))
        pump(0)
        for turn in range(DOCS):
            home.put(turn, joined[turn])

    @pl.when(step < QUADS)
    def _():
        keys = k_cross.shape[0]
        rows = pl.ds(0, keys)
        my_normed, my_dkv, my_dx = normed.at[rows], dkv.at[rows], dx.at[rows]

        @pl.when(step == 0)
        def _():
            fetches[0].wait()
            normalize_pages(image_pages, gain[2:3, :], shift[2:3, :], my_normed)
            my_dx[...] = jnp.zeros(my_dx.shape, F32)

        cols = pl.ds(pl.multiple_of(step * QUAD, QUAD), QUAD)
        attend_backward(
            q_cross, k_cross, v_cross, do_cross, lse_cross, delta_cross, cross_closed,
            dq.at[:, cols], my_dkv, lambda: pumps((1, 3, 5)),
        )
        spread_back(my_dkv, wk_cross, wv_cross, my_dx)
        for part in range(2):
            value = transposed(my_dkv[:, part * QUAD : (part + 1) * QUAD], my_normed[...])
            value = value.astype(BF16)
            for at in range(QUADS):

                @pl.when(step == at)
                def _():
                    put_rows(d_pairs, part * D + at * QUAD, value)

        pumps((2, 4))

        @pl.when(step == QUADS - 1)
        def _():
            round_pages(my_dx, image.keep, image.send)
            image.start()
            image_gain, image_shift = page_sums(image_pages, my_dx)
            fetches[1].start()
            fetches[3].start()
            scaled, inverse = standardize(hidden[...])
            cross = (scaled * gain[1:2, :] + shift[1:2, :]).astype(BF16)
            grad_query = dq[...]
            put_rows(d_query, 0, transposed(grad_query, cross).astype(BF16))
            d_gate = transposed(grad_logit[...], cross.astype(F32), HIGHEST)[:H, :]
            gates[...] = jnp.zeros_like(gates)
            gates[0:H, :] = w_gate[...]
            upstream = against(grad_query, w_query[...]) + jnp.dot(
                grad_logit[...], gates[...].astype(F32), precision=HIGHEST
            )
            fetches[2].wait()
            grad = grad_hidden[...] + norm_back(upstream, scaled, inverse, gain[1:2, :])
            grad_hidden[...] = grad
            branch = grad.astype(BF16)
            put_rows(
                d_self_output, 0, transposed(branch, self_out[...].astype(BF16)).astype(BF16)
            )
            fetches[3].wait()
            grad_result = against(branch, normed[0:D, :]).astype(BF16)
            self_do[...] = grad_result
            self_delta[...] = head_rows(head_sums(grad_result.astype(F32) * self_out[...]))
            sums_in[0:H, :] = d_gate
            sums_in[H : H + 8, :] = last_small[...]
            sums_in[H + 8 : SUMS, :] = jnp.concatenate(
                [column_sum(upstream * scaled), column_sum(upstream), image_gain, image_shift],
                axis=0,
            )
            sums.start(sums_in[...])
            home.end(joined_out)
            pump(6)
            fetches[1].wait()
            normalize_pages(pages, gain[0:1, :], shift[0:1, :], normed)
            dx[...] = jnp.zeros(dx.shape, F32)

    @pl.when(step >= QUADS)
    def _():
        quad = step - QUADS
        cols = pl.ds(pl.multiple_of(quad * QUAD, QUAD), QUAD)
        my_dq = dq.at[:, cols]
        attend_backward(
            q_self, k_self, v_self, self_do.at[:, cols], lse_self,
            self_delta.at[pl.ds(pl.multiple_of(quad * 8, 8), 8)], self_closed,
            my_dq, dkv, lambda: pumps((7, 9, 11)),
        )
        spread_back(dkv, wk_self, wv_self, dx)
        dx[0:ROWS, :] += against(my_dq[...], wq_self[...])

        @pl.when(quad == QUADS - 1)
        def _():
            round_pages(dx, keep, send)
            text.start()

        for part in range(3):
            if part == 0:
                value = transposed(my_dq[...], normed[0:ROWS, :])
            else:
                value = transposed(dkv[:, (part - 1) * QUAD : part * QUAD], normed[...])
            value = value.astype(BF16)
            for at in range(QUADS):

                @pl.when(quad == at)
                def _():
                    put_rows(d_project, part * D + at * QUAD, value)

        pumps((8, 10))

        @pl.when(quad == QUADS - 1)
        def _():
            run_moves(moves, 12, scatters)
            for stage in range(len(groups) - 1):
                text.add(stage)
            gain_sum, shift_sum = page_sums(pages, dx)
            last_sums.start(jnp.concatenate([gain_sum, shift_sum, jnp.zeros((6, D), F32)], axis=0))
            run_moves(moves, 13, scatters)
            text.add(len(groups) - 1)
            text.norm(pages, gain[0:1, :], grad_hidden)
            last_sums.add(0, last_out)
            run_moves(moves, 14, scatters)
            run_moves(moves, 15, scatters)
            last_sums.add(1, last_out)
            run_moves(moves, 16, scatters)
            last_sums.add(2, last_out)
            run_moves(moves, 17, scatters)
            image.end(image_out)
            text.end(text_out)
            run_moves(moves, END, scatters)
            for scatter, out in zip(scatters, outs):
                scatter.end(out)


class Places:
    def __init__(self, wide, blk):
        self.wide = wide
        self.blk = blk
        self.part = blk // 4
        self.w = lax.axis_index("wide")
        self.b = lax.axis_index("blk")
        self.quarter = self.b // self.part
        self.turn = self.quarter % 2

    def bit(self, name):
        axis, bit = name
        return ((self.w if axis == "w" else self.b) // (1 << bit)) % 2

    def flip(self, name):
        axis, bit = name
        step = (1 << bit) * (1 - 2 * self.bit(name))
        return (self.w + step, self.b) if axis == "w" else (self.w, self.b + step)

    def flips(self, names, which):
        w, b = self.w, self.b
        for name, taken in zip(names, (which // 2, which % 2)):
            if taken:
                there = self.flip(name)
                w, b = w + there[0] - self.w, b + there[1] - self.b
        return w, b

    def index(self, names):
        return 2 * self.bit(names[0]) + self.bit(names[1])

    def swap(self, turn):
        core = self.w % 2
        turned = self.turn if turn == 0 else 1 - self.turn
        return (
            self.w - core + self.quarter // 2,
            (2 * core + turned) * self.part + self.b % self.part,
        )

    def swap_stays(self):
        return self.w % 2 == self.quarter // 2


def bit_names(wide, blk):
    return [("w", bit) for bit in range(wide.bit_length() - 1)] + [
        ("b", bit) for bit in range(blk.bit_length() - 1)
    ]


def group_bits(blk):
    return [("b", bit) for bit in range((blk // 4).bit_length() - 1)] + [("w", 0)]


def tile_bits(wide, blk):
    return (
        [("w", bit) for bit in range(wide.bit_length() - 2, 0, -1)]
        + [("b", bit) for bit in range(blk.bit_length() - 2, -1, -1)]
        + [("w", 0)]
    )


def remote(source, target, send, receive, device):
    return pltpu.make_async_remote_copy(
        src_ref=source,
        dst_ref=target,
        send_sem=send,
        recv_sem=receive,
        device_id=device,
        device_id_type=pl.DeviceIdType.MESH,
    )


def greet(places, names, swaps, pairs=()):
    barrier = pltpu.get_barrier_semaphore()
    devices = [places.flip(name) for name in names] + [places.flips(pair, 3) for pair in pairs]
    for device in devices:
        pl.semaphore_signal(
            barrier, inc=1, device_id=device, device_id_type=pl.DeviceIdType.MESH
        )
    count = len(devices)
    if swaps:
        pl.semaphore_signal(
            barrier, inc=1, device_id=places.swap(1), device_id_type=pl.DeviceIdType.MESH
        )

        @pl.when(jnp.logical_not(places.swap_stays()))
        def _():
            pl.semaphore_signal(
                barrier, inc=1, device_id=places.swap(0), device_id_type=pl.DeviceIdType.MESH
            )

        count = count + 2 - places.swap_stays().astype(jnp.int32)
    pl.semaphore_wait(barrier, count)


class Job(NamedTuple):
    left: tuple
    order: tuple
    start: int
    rows: int
    lanes: int
    ends: bool
    near: bool = False
    inner: bool = False

    def after(self):
        return tuple(name for name in self.left if name not in self.order)

    def scratch(self):
        count = len(self.left)
        kinds = []
        if not self.near:
            kinds.append(pltpu.VMEM((2,) * (count - 1) + (self.rows, self.lanes), BF16))
        for stage in range(len(self.order) - int(self.inner)):
            kinds.append(pltpu.VMEM((2,) * (count - 1 - stage) + (self.rows, self.lanes), BF16))
        if self.ends:
            kinds.append(pltpu.VMEM((2, self.rows, self.lanes // 2), BF16))
        waits = len(self.order) + int(self.ends)
        return kinds + [pltpu.SemaphoreType.DMA((waits,))] * 2 + [pltpu.SemaphoreType.DMA]

    def result(self):
        return shaped((2, self.rows, self.lanes // 2), BF16)


def bits_of(index, count):
    return tuple((index // (1 << (count - 1 - place))) % 2 for place in range(count))


def add_blocks(target, source):
    lead = len(target.shape) - 2
    if lead == 0:
        target[...] = target[...] + source[...]
        return

    def block(index, carry):
        at = bits_of(index, lead)
        target[at] = target[at] + source[at]
        return carry

    lax.fori_loop(0, 1 << lead, block, 0)


class Scatter:
    def __init__(self, places, job, source, scratch, last=None):
        self.places = places
        self.job = job
        self.source = source
        self.own = None if job.near else next(scratch)
        self.got = [next(scratch) for _ in range(len(job.order) - int(job.inner))]
        if job.inner:
            self.got.append(last)
        self.ends = next(scratch) if job.ends else None
        self.sends, self.receives, self.local = next(scratch), next(scratch), next(scratch)
        self.stages = len(job.order)
        self.axes = []
        left = list(job.left)
        for name in job.order:
            self.axes.append(left.index(name))
            left.remove(name)

    def cut(self, ref, stage, index):
        axis = self.axes[stage]
        at = (slice(None),) * axis + (index,)
        if ref.shape[-2] != self.job.rows:
            at += (slice(None),) * (len(ref.shape) - 3 - axis)
            at += (pl.ds(self.job.start, self.job.rows), slice(None))
        return ref.at[at]

    def copy(self, stage):
        if stage == self.stages:
            source, target, name = self.ends.at[0], self.ends.at[1], ("w", 0)
        else:
            name = self.job.order[stage]
            source = self.source if stage == 0 else self.got[stage - 1]
            source = self.cut(source, stage, 1 - self.places.bit(name))
            target = self.got[stage]
        return remote(
            source, target, self.sends.at[stage], self.receives.at[stage], self.places.flip(name)
        )

    def fetch(self):
        kept = self.cut(self.source, 0, self.places.bit(self.job.order[0]))
        return pltpu.make_async_copy(kept, self.own, self.local)

    def start(self):
        self.copy(0).start()
        if not self.job.near:
            self.fetch().start()

    def halve(self):
        lanes = self.job.lanes // 2
        piece = self.got[-1][...]
        second = self.places.bit(("w", 0)) == 1
        self.ends[0] = jnp.where(second, piece[:, :lanes], piece[:, lanes:])

    def add(self, stage):
        self.copy(stage).wait_recv()
        if stage == 0 and not self.job.near:
            self.fetch().wait()
            source = self.own
        else:
            bit = self.places.bit(self.job.order[stage])
            source = self.cut(self.source if stage == 0 else self.got[stage - 1], stage, bit)
        add_blocks(self.got[stage], source)
        if stage + 1 < self.stages:
            self.copy(stage + 1).start()
        elif self.job.ends:
            self.halve()
            self.copy(stage + 1).start()

    def end(self, out):
        for stage in range(self.stages + int(self.job.ends)):
            self.copy(stage).wait_send()
        if not self.job.ends:
            return
        self.copy(self.stages).wait_recv()
        lanes = self.job.lanes // 2
        piece = self.got[-1][...]
        other = self.ends[1]
        second = self.places.bit(("w", 0)) == 1
        mine = jnp.where(second, piece[:, lanes:], piece[:, :lanes])
        out[0] = jnp.where(second, other, mine)
        out[1] = jnp.where(second, mine, other)


class Home:
    def __init__(self, places, scratch):
        self.places = places
        self.home, self.landed, self.sends, self.receives, self.local = (
            next(scratch) for _ in range(5)
        )

    @staticmethod
    def scratch():
        waits = [pltpu.SemaphoreType.DMA((DOCS,))] * 2 + [pltpu.SemaphoreType.DMA]
        return [pltpu.VMEM((DOCS, PAGE, D), BF16)] * 2 + waits

    def copy(self, turn):
        return remote(
            self.home.at[turn], self.landed.at[self.places.turn], self.sends.at[turn],
            self.receives.at[turn], self.places.swap(turn),
        )

    def go(self, turn, begin):
        def carry():
            if begin:
                self.copy(turn).start()
            else:
                self.copy(turn).wait()

        if turn > 0:
            carry()
            return
        stays = self.places.swap_stays()
        pl.when(jnp.logical_not(stays))(carry)
        if begin:

            @pl.when(stays)
            def _():
                self.landed[self.places.turn] = self.home[turn]

    def put(self, turn, page):
        self.home[turn] = page
        self.go(turn, True)

    def end(self, out):
        for turn in range(DOCS):
            self.go(turn, False)
        copy = pltpu.make_async_copy(self.landed, out, self.local)
        copy.start()
        copy.wait()


class Rows:
    def __init__(self, places, names, keep, send, sums, scratch):
        self.places = places
        self.size = keep.shape[0] // (DOCS << (len(names) - 1))
        self.names = list(reversed(names))
        self.keep = keep
        self.send = send
        self.sums = sums
        self.got = [next(scratch) for _ in names]
        self.sends, self.receives = next(scratch), next(scratch)
        self.back = Home(places, scratch)

    @staticmethod
    def scratch(names, rows):
        kinds = [pltpu.VMEM((rows >> stage, D), BF16) for stage in range(len(names))]
        return kinds + [pltpu.SemaphoreType.DMA((len(names),))] * 2 + Home.scratch()

    def copy(self, stage):
        source = self.send if stage == 0 else self.sums
        rows = self.got[stage].shape[0]
        if stage > 0:
            source = source.at[pl.ds(rows, rows)]
        return remote(
            source, self.got[stage], self.sends.at[stage], self.receives.at[stage],
            self.places.flip(self.names[stage]),
        )

    def start(self):
        self.copy(0).start()

    def add(self, stage):
        self.copy(stage).wait()
        source = self.keep if stage == 0 else self.sums
        rows = self.got[stage].shape[0]

        def block(index, carry):
            at = pl.ds(pl.multiple_of(index * self.size, 16), self.size)
            self.sums[at, :] = source[at, :] + self.got[stage][at, :]
            return carry

        lax.fori_loop(0, rows // self.size, block, 0)
        if stage + 1 < len(self.names):
            self.copy(stage + 1).start()

    def norm(self, pages, gain, added):
        for turn in range(DOCS):
            rows = slice(turn * self.size, (turn + 1) * self.size)
            scaled, inverse = standardize(pages[turn].astype(F32))
            grad = norm_back(self.sums[rows, :].astype(F32), scaled, inverse, gain)
            if added is not None:
                grad = grad + added[rows, :]
            if self.size < PAGE:
                rest = jnp.zeros((PAGE - self.size, D), F32)
                grad = jnp.concatenate([grad, rest], axis=0)
            self.back.put(turn, grad.astype(BF16))

    def end(self, out):
        self.back.end(out)


class Total:
    ROUNDS = 3

    def __init__(self, places, scratch):
        self.places = places
        self.chip, self.plane, self.line, self.sends, self.receives = (
            next(scratch) for _ in range(5)
        )

    @staticmethod
    def scratch(rows):
        return [
            pltpu.VMEM((2, rows, D), F32),
            pltpu.VMEM((4, rows, D), F32),
            pltpu.VMEM((4, rows, D), F32),
            pltpu.SemaphoreType.DMA((7,)),
            pltpu.SemaphoreType.DMA((7,)),
        ]

    def copies(self, stage):
        if stage == 0:
            return [
                remote(
                    self.chip.at[0], self.chip.at[1], self.sends.at[0], self.receives.at[0],
                    self.places.flip(("w", 0)),
                )
            ]
        names = (("w", 1), ("b", 0)) if stage == 1 else (("b", 2), ("b", 1))
        slots = self.plane if stage == 1 else self.line
        mine = slots.at[self.places.index(names)]
        found = []
        for which in range(1, 4):
            at = 3 * stage - 3 + which
            found.append(
                remote(
                    mine, mine, self.sends.at[at], self.receives.at[at],
                    self.places.flips(names, which),
                )
            )
        return found

    def start(self, value):
        self.chip[0] = value
        self.copies(0)[0].start()

    def add(self, stage, out):
        for copy in self.copies(stage):
            copy.wait()
        if stage == 0:
            value = self.chip[0] + self.chip[1]
            self.plane[self.places.index((("w", 1), ("b", 0)))] = value
        else:
            slots = self.plane if stage == 1 else self.line
            value = (slots[0] + slots[1]) + (slots[2] + slots[3])
            if stage == 1:
                self.line[self.places.index((("b", 2), ("b", 1)))] = value
        if stage + 1 < self.ROUNDS:
            for copy in self.copies(stage + 1):
                copy.start()
        else:
            out[...] = value


def finish_kernel(layout, *refs):
    refs = iter(refs)
    pieces = [[next(refs) for _ in range(count)] for count in layout]
    streams = [next(refs) for _ in range(3)]
    sums, last_sums = next(refs), next(refs)
    for index, parts in enumerate(pieces):
        out = next(refs)
        halves = [part[half] for half in range(2) for part in parts]
        value = jnp.concatenate(halves, axis=0).astype(F32)
        out[...] = value if index + 1 == len(pieces) else jnp.transpose(value)
    for stream in streams:
        out = next(refs)
        out[...] = stream[...]
    gate, bias, last, gains, shifts = (next(refs) for _ in range(5))
    gate[...] = sums[0:H, :]
    for index in range(FF // D):
        bias[pl.ds(index * D, D)] = sums[H + 4 + index, :]
    last[...] = sums[H, :]
    for out, at in ((gains, 0), (shifts, 1)):
        out[0:1, :] = last_sums[at : at + 1, :]
        for index, row in enumerate((H + 8 + at, H + 10 + at, H + 1 + at)):
            out[index + 1 : index + 2, :] = sums[row : row + 1, :]


def whole(shape):
    return pl.BlockSpec(shape, lambda step: (0,) * len(shape))


def columns(rows, offset=0):
    return pl.BlockSpec((rows, QUAD), lambda step: (0, offset + step))


def stat_rows():
    return pl.BlockSpec((8, ROWS), lambda step: (step, 0))


def shaped(shape, kind):
    return jax.ShapeDtypeStruct(shape, kind)


ANY = pl.BlockSpec(memory_space=pl.ANY)


def call(kernel, name, steps, ins, outs, scratch, flops, byte_count, collective=None):
    in_specs, operands = zip(*ins)
    out_specs, out_shapes = zip(*outs)
    return pl.pallas_call(
        kernel,
        grid=(steps,),
        in_specs=list(in_specs),
        out_specs=list(out_specs),
        out_shape=list(out_shapes),
        scratch_shapes=scratch,
        name=name,
        compiler_params=pltpu.CompilerParams(
            vmem_limit_bytes=VMEM_LIMIT,
            collective_id=collective,
            has_side_effects=collective is not None,
        ),
        cost_estimate=pl.CostEstimate(flops=flops, bytes_accessed=byte_count, transcendentals=0),
    )(*operands)


def own_pages(pages):
    return (whole((DOCS, *pages.shape[1:])), pages)


SMEM = pl.BlockSpec(memory_space=pltpu.SMEM)


def self_forward(texts, images, cots, mask, regions, doc_pages, gain, shift, project, wide, blk):
    groups = group_bits(blk)
    count = DOCS << len(groups)
    keys = count * PAGE
    return call(
        functools.partial(self_forward_kernel, wide, blk),
        "self_forward",
        QUADS,
        [
            (whole(regions.shape), regions),
            (SMEM, doc_pages),
            (whole(texts.shape), texts),
            (whole(images.shape), images),
            (whole(cots.shape), cots),
            (whole(mask.shape), mask),
            (whole(gain.shape), gain),
            (whole(shift.shape), shift),
            (columns(D), project),
            (columns(D, QUADS), project),
            (columns(D, 2 * QUADS), project),
        ],
        [
            (columns(ROWS), shaped((ROWS, D), F32)),
            (stat_rows(), shaped((8 * QUADS, ROWS), F32)),
            (columns(ROWS), shaped((ROWS, D), BF16)),
            (columns(keys), shaped((keys, D), BF16)),
            (columns(keys), shaped((keys, D), BF16)),
            (ANY, shaped((count, PAGE, D), BF16)),
            (ANY, shaped((count, IMAGE, D), BF16)),
            (ANY, shaped((DOCS, PAGE, D), BF16)),
            (whole((keys, PAIR)), shaped((keys, PAIR), BF16)),
            (whole((count * IMAGE, PAIR)), shaped((count * IMAGE, PAIR), BF16)),
        ],
        [
            pltpu.VMEM((keys, D), BF16),
            pltpu.VMEM((DOCS, PAGE + EXTRA, D), BF16),
            pltpu.VMEM((DOCS, IMAGE + EXTRA, D), BF16),
            pltpu.VMEM((count, PAGE + EXTRA, D), BF16),
            pltpu.VMEM((count, IMAGE + EXTRA, D), BF16),
            pltpu.VMEM((DOCS, PAGE, D), BF16),
        ]
        + Gather.waits(groups) * 2
        + Gather.waits([])
        + [pltpu.SemaphoreType.DMA((3,))],
        6 * 10**9,
        12 * 10**6,
        0,
    )


def cross_forward(texts, pages, self_out, w_self, w_gate, gain, shift, closed, w_query, w_pairs):
    keys = closed.shape[0]
    return call(
        cross_forward_kernel,
        "cross_forward",
        QUADS,
        [
            own_pages(texts),
            (whole(pages.shape), pages),
            (whole(self_out.shape), self_out),
            (whole(w_self.shape), w_self),
            (whole(w_gate.shape), w_gate),
            (whole(gain.shape), gain),
            (whole(shift.shape), shift),
            (whole(closed.shape), closed),
            (columns(D), w_query),
            (columns(D), w_pairs),
            (columns(D, QUADS), w_pairs),
        ],
        [
            (whole((ROWS, D)), shaped((ROWS, D), F32)),
            (whole((ROWS, PAIR)), shaped((ROWS, PAIR), F32)),
            (columns(ROWS), shaped((ROWS, D), F32)),
            (stat_rows(), shaped((8 * QUADS, ROWS), F32)),
            (columns(ROWS), shaped((ROWS, D), BF16)),
            (columns(keys), shaped((keys, D), BF16)),
            (columns(keys), shaped((keys, D), BF16)),
        ],
        [
            pltpu.VMEM((keys, D), BF16),
            pltpu.VMEM((ROWS, D), BF16),
            pltpu.VMEM((PAIR, D), BF16),
        ],
        7 * 10**9,
        14 * 10**6,
    )


def forward_back(
    hidden, raw, gate, cots, w_out, gain, shift, w_expand, b_expand, w_reduce, b_reduce, wide, blk
):
    steps = FF // D
    names = tile_bits(wide, blk)
    small = (D // (2 * blk), D // (wide // 2))
    expand = (FF // (2 * blk), D // (wide // 2))
    reduce = (D // (2 * blk), FF // (wide // 2))
    full, part, half, less = ((2,) * (len(names) - gone) for gone in range(4))
    return call(
        functools.partial(forward_back_kernel, steps, wide, blk),
        "forward_back",
        steps,
        [
            (whole((ROWS, D)), hidden),
            (whole((ROWS, D)), raw),
            (whole((ROWS, PAIR)), gate),
            (whole((DOCS, PAGE, D)), cots),
            (whole((D, D)), w_out),
            (whole(gain.shape), gain),
            (whole(shift.shape), shift),
            (pl.BlockSpec((D, D), lambda step: (0, step)), w_expand),
            (pl.BlockSpec((1, D), lambda step: (0, step)), b_expand),
            (pl.BlockSpec((D, D), lambda step: (step, 0)), w_reduce),
            (whole((D,)), b_reduce),
        ],
        [
            (whole((DOCS, PAGE, D)), shaped((DOCS, PAGE, D), BF16)),
            (ANY, shaped(less + expand, BF16)),
            (ANY, shaped(half + expand, BF16)),
            (ANY, shaped(less + reduce, BF16)),
            (ANY, shaped(half + reduce, BF16)),
            (whole(full + small), shaped(full + small, BF16)),
            (whole((ROWS, D)), shaped((ROWS, D), F32)),
            (whole((ROWS, D)), shaped((ROWS, D), BF16)),
            (whole((8 * QUADS, ROWS)), shaped((8 * QUADS, ROWS), F32)),
            (whole((ROWS, PAIR)), shaped((ROWS, PAIR), F32)),
            (whole((8, D)), shaped((8, D), F32)),
        ],
        [
            pltpu.VMEM((ROWS, D), BF16),
            pltpu.VMEM((ROWS, D), F32),
            pltpu.VMEM((ROWS, D), BF16),
            pltpu.VMEM((ROWS, D), BF16),
            pltpu.VMEM((ROWS, D), F32),
            pltpu.VMEM((ROWS, D), F32),
            pltpu.VMEM(full + expand, BF16),
            pltpu.VMEM(full + reduce, BF16),
            pltpu.VMEM(part + expand, BF16),
            pltpu.VMEM(part + reduce, BF16),
            pltpu.VMEM(less + expand, BF16),
            pltpu.VMEM(less + reduce, BF16),
            pltpu.SemaphoreType.DMA((2, steps)),
            pltpu.SemaphoreType.DMA((2, steps)),
            pltpu.SemaphoreType.DMA((2, steps // 2)),
            pltpu.SemaphoreType.DMA((2, steps // 2)),
            pltpu.SemaphoreType.DMA((4,)),
        ],
        8 * 10**9,
        25 * 10**6,
        1,
    )


def back(
    cross, own, images, texts, gain, shift, closed, w_pairs, project, w_query, w_gate, w_self,
    hidden, self_out, grad_mixed, grad_logit, joined, last_small, far_sources, jobs, plan, wide, blk,
):
    q_cross, k_cross, v_cross, do_cross, lse_cross, delta_cross = cross
    q_self, k_self, v_self, lse_self = own
    cross_keys, self_keys = k_cross.shape[0], k_self.shape[0]
    names = bit_names(wide, blk)
    groups = group_bits(blk)
    tile = (2,) * len(tile_bits(wide, blk))
    lanes = 2 * D // wide
    stream = shaped((DOCS, PAGE, D), BF16)

    def fixed(array):
        count = len(array.shape)
        spec = pl.BlockSpec(
            array.shape, lambda step: (0,) * count, pipeline_mode=pl.Buffered(buffer_count=1)
        )
        return (spec, array)

    def early(array, rows, offset=0):
        last = QUADS - 1
        return (
            pl.BlockSpec(
                (rows, QUAD), lambda step: (0, offset + step - step // QUADS * (step - last))
            ),
            array,
        )

    def late(array, rows, offset=0):
        return (
            pl.BlockSpec((rows, QUAD), lambda step: (0, offset + step // QUADS * (step - QUADS))),
            array,
        )

    def early_rows(array):
        last = QUADS - 1
        return (
            pl.BlockSpec((8, ROWS), lambda step: (step - step // QUADS * (step - last), 0)), array
        )

    def late_rows(array):
        return (pl.BlockSpec((8, ROWS), lambda step: (step // QUADS * (step - QUADS), 0)), array)

    def tiles(columns_here):
        return pltpu.VMEM(tile + (columns_here // (2 * blk), lanes), BF16)

    def both(job):
        return pltpu.VMEM((2,) * (1 + len(job.after())) + (job.rows, job.lanes), BF16)

    image_rows, text_rows = cross_keys // 2, self_keys // 2
    return call(
        functools.partial(back_kernel, wide, blk, jobs, plan),
        "back",
        2 * QUADS,
        [
            (ANY, images),
            own_pages(images),
            (ANY, texts),
            fixed(gain),
            fixed(shift),
            fixed(closed[0]),
            fixed(closed[1]),
            early(q_cross, ROWS),
            early(k_cross, cross_keys),
            early(v_cross, cross_keys),
            early(do_cross, ROWS),
            early_rows(lse_cross),
            early_rows(delta_cross),
            early(w_pairs, D),
            early(w_pairs, D, QUADS),
            late(q_self, ROWS),
            late(k_self, self_keys),
            late(v_self, self_keys),
            late_rows(lse_self),
            late(project, D),
            late(project, D, QUADS),
            late(project, D, 2 * QUADS),
            fixed(w_query),
            fixed(w_gate),
            (ANY, w_self),
            fixed(hidden),
            fixed(self_out),
            (ANY, grad_mixed),
            fixed(grad_logit),
            fixed(joined),
            fixed(last_small),
        ]
        + [(ANY, source) for source in far_sources],
        [(ANY, stream)] * 3
        + [(whole((SUMS, D)), shaped((SUMS, D), F32)), (whole((8, D)), shaped((8, D), F32))]
        + [(whole(job.result().shape), job.result()) for job in jobs if job.ends],
        [
            pltpu.VMEM((self_keys, D), BF16),
            pltpu.VMEM((self_keys, 2 * QUAD), BF16),
            pltpu.VMEM((self_keys, D), F32),
            pltpu.VMEM((ROWS, D), BF16),
            pltpu.VMEM((PAIR, D), BF16),
            pltpu.VMEM((ROWS, D), F32),
            pltpu.VMEM((ROWS, D), BF16),
            pltpu.VMEM((8 * QUADS, ROWS), F32),
            pltpu.VMEM(texts.shape, BF16),
            pltpu.VMEM((text_rows, D), BF16),
            pltpu.VMEM((text_rows, D), BF16),
            pltpu.VMEM((text_rows, D), BF16),
            pltpu.VMEM((SUMS, D), F32),
            pltpu.SemaphoreType.DMA((4,)),
            tiles(2 * D),
            tiles(D),
            tiles(D),
            tiles(3 * D),
            both(jobs[0]),
            both(jobs[2]),
        ]
        + [kind for job in jobs for kind in job.scratch()]
        + Home.scratch()
        + Rows.scratch(groups, image_rows)
        + Rows.scratch(groups, text_rows)
        + Total.scratch(SUMS)
        + Total.scratch(8),
        23 * 10**9,
        30 * 10**6,
        2,
    )


def finish(pieces, streams, sums, last_sums):
    vmem = pl.BlockSpec(memory_space=pltpu.VMEM)
    operands = [part for parts in pieces for part in parts] + [*streams, sums, last_sums]
    results = []
    for index, parts in enumerate(pieces):
        shape = (parts[0].shape[2], sum(2 * part.shape[1] for part in parts))
        results.append(shaped(shape[::-1] if index + 1 == len(pieces) else shape, F32))
    results += [shaped(stream.shape, BF16) for stream in streams]
    results += [shaped((H, D), F32), shaped((FF,), F32), shaped((D,), F32)]
    results += [shaped((4, D), F32)] * 2
    return pl.pallas_call(
        functools.partial(finish_kernel, tuple(len(parts) for parts in pieces)),
        in_specs=[vmem] * len(operands),
        out_specs=[vmem] * len(results),
        out_shape=results,
        name="finish",
        compiler_params=pltpu.CompilerParams(vmem_limit_bytes=VMEM_LIMIT),
        cost_estimate=pl.CostEstimate(flops=10**6, bytes_accessed=5 * 10**6, transcendentals=0),
    )(*operands)


def body(
    text_blocks,
    image_blocks,
    cotangent,
    text_mask,
    page_regions,
    doc_pages,
    self_project,
    self_output,
    cross_query,
    cross_pairs,
    cross_output,
    gate_weight,
    expand_weight,
    expand_bias,
    reduce_weight,
    reduce_bias,
    norm_gain,
    norm_bias,
):
    wide = lax.axis_size("wide")
    blk = lax.axis_size("blk")
    names = tuple(tile_bits(wide, blk))
    share = 2 * blk
    lanes = 2 * D // wide
    far = 2 * FF // wide
    gate_rows = jnp.transpose(gate_weight)

    (
        self_out, self_lse, self_q, self_k, self_v, text_pages, image_pages, cots, text_closed,
        image_closed,
    ) = self_forward(
        text_blocks, image_blocks, cotangent, text_mask, jnp.transpose(page_regions), doc_pages, norm_gain,
        norm_bias, self_project, wide, blk,
    )
    hidden, gate, raw, cross_lse, cross_q, cross_k, cross_v = cross_forward(
        text_pages, image_pages, self_out, self_output, gate_rows, norm_gain, norm_bias,
        image_closed, cross_query, cross_pairs,
    )
    (
        joined, *partial, d_cross_output, grad_mixed, grad_raw, cross_delta,
        grad_logit, small_last,
    ) = forward_back(
        hidden, raw, gate, cots, cross_output, norm_gain, norm_bias, expand_weight,
        expand_bias.reshape(1, FF), reduce_weight, reduce_bias, wide, blk,
    )

    core, y, x, z, far_z = ("w", 0), ("w", 1), ("b", 0), ("b", 1), ("b", 2)
    ends = {"ends": True, "near": True}
    expand_shape = (0, FF // share, lanes)
    reduce_shape = (0, D // share, far)
    one = (0, D // share, lanes)
    rows = 3 * D // share
    split = 80
    jobs = (
        Job((z, x), (z,), *expand_shape, False, inner=True),
        Job((y, z, x), (y, z), *expand_shape, False, inner=True),
        Job((far_z, z), (z,), *reduce_shape, False, inner=True),
        Job((far_z, z, x), (x, z), *reduce_shape, False, inner=True),
        Job((far_z, x), (far_z, x), *expand_shape, **ends),
        Job((y, far_z), (y, far_z), *reduce_shape, **ends),
        Job(names, (core, x, y, z, far_z), 0, 2 * D // share, lanes, **ends),
        Job(names, (core, y, x, z, far_z), *one, **ends),
        Job(names, (core, y, x, z, far_z), *one, True),
        Job(names, (core, y, x, z, far_z), *one, **ends),
        Job(names, (core, y, x, z, far_z), 0, split, lanes, **ends),
        Job(names, (core, z, y, x, far_z), split, rows - split, lanes, **ends),
    )
    plan = {
        0: (1, 3, 0, 2,),
        4: (1, 3, 0, 2,),
        6: (6, 7, 8, 9,),
        7: (7, 8, 9,),
        8: (1, 3, 6,),
        9: (5,),
        11: (4,),
        12: (10, 11,),
        13: (10, 11, 7, 8, 9,),
        14: (6, 5,),
        15: (10, 11,),
        16: (7, 8, 9, 6, 10, 11, 4,),
        17: (7, 8, 9, 6, 10, 11,),
    }
    joined_home, text_home, image_home, sums, last_sums, *pieces = back(
        (cross_q, cross_k, cross_v, grad_raw, cross_lse, cross_delta),
        (self_q, self_k, self_v, self_lse),
        image_pages, text_pages, norm_gain, norm_bias, (image_closed, text_closed), cross_pairs,
        self_project, cross_query, gate_rows, self_output, hidden, self_out, grad_mixed,
        grad_logit, joined, small_last, (*partial, d_cross_output), jobs, plan, wide, blk,
    )
    expand_piece, reduce_piece, *cross_pieces = pieces[:6]
    project_pieces = pieces[6:]
    (
        grad_cross_pairs, grad_cross_query, grad_cross_output, grad_self_output,
        grad_expand_weight, grad_self_project, grad_reduce_weight,
        joined_blocks, text_grad, image_grad,
        grad_gate_weight, grad_expand_bias, grad_reduce_bias, gains, shifts,
    ) = finish(
        [[piece] for piece in cross_pieces] + [[expand_piece], project_pieces, [reduce_piece]],
        [joined_home, text_home, image_home], sums, last_sums,
    )
    return (
        joined_blocks,
        text_grad,
        image_grad,
        grad_self_project,
        grad_self_output,
        grad_cross_query,
        grad_cross_pairs,
        grad_cross_output,
        grad_expand_weight,
        jnp.transpose(grad_reduce_weight),
        jnp.transpose(grad_gate_weight),
        grad_expand_bias,
        grad_reduce_bias,
        gains,
        shifts,
    )


def normalize(values, gains, biases):
    scaled, inverse = standardize(values)
    return (scaled * gains + biases, scaled, inverse)


def normalize_back(upstream, scaled, inverse, gains):
    result = norm_back(upstream, scaled, inverse, gains)
    return (result, jnp.sum(upstream * scaled, axis=0), jnp.sum(upstream, axis=0))


def gelu_tanh(values):
    return jax.nn.gelu(values, approximate=True)


def forward_doc(queries, carried, key_pairs, allowed, scaling):
    running_max, summed, accumulated = carried
    key_count = key_pairs.shape[0]
    keys_part = key_pairs[:, :D].reshape(key_count, H, HD)
    values_part = key_pairs[:, D:].reshape(key_count, H, HD)
    open_keys = (allowed > 0)[None, None, :]
    scores = (
        jnp.einsum("qhd,khd->hqk", queries, keys_part, preferred_element_type=F32) * scaling
    )
    scores = jnp.where(open_keys, scores, NEGATIVE)
    new_max = jnp.maximum(running_max, jnp.max(scores, axis=-1))
    fading = jnp.exp(running_max - new_max)
    weights = jnp.where(open_keys, jnp.exp(scores - new_max[..., None]), 0.0)
    summed = summed * fading + jnp.sum(weights, axis=-1)
    accumulated = accumulated * fading[..., None] + jnp.einsum(
        "hqk,khd->hqd",
        weights.astype(BF16),
        values_part,
        preferred_element_type=F32,
    )
    return (new_max, summed, accumulated)


def forward_fold(queries, scaling, carried, pieces):
    key_pairs, allowed = pieces

    def forward_per_doc(doc_items):
        doc_queries, doc_max, doc_sum, doc_acc, doc_pairs, doc_allowed = doc_items
        doc_carry = (doc_max, doc_sum, doc_acc)
        result = forward_doc(doc_queries, doc_carry, doc_pairs, doc_allowed, scaling)
        return result

    return lax.map(
        forward_per_doc, (queries, carried[0], carried[1], carried[2], key_pairs, allowed)
    )


def backward_doc(queries, grad_out, log_sum, row_delta, key_pairs, allowed, scaling):
    key_count = key_pairs.shape[0]
    keys_part = key_pairs[:, :D].reshape(key_count, H, HD)
    values_part = key_pairs[:, D:].reshape(key_count, H, HD)
    open_keys = (allowed > 0)[None, None, :]
    scores = (
        jnp.einsum("qhd,khd->hqk", queries, keys_part, preferred_element_type=F32) * scaling
    )
    probabilities = jnp.where(open_keys, jnp.exp(scores - log_sum[..., None]), 0.0)
    grad_probs = jnp.einsum(
        "qhd,khd->hqk", grad_out, values_part, preferred_element_type=F32
    )
    grad_scores = (probabilities * (grad_probs - row_delta[..., None])).astype(BF16)
    query_grad = (
        jnp.einsum("hqk,khd->qhd", grad_scores, keys_part, preferred_element_type=F32)
        * scaling
    )
    key_grad = (
        jnp.einsum("hqk,qhd->khd", grad_scores, queries, preferred_element_type=F32)
        * scaling
    )
    value_grad = jnp.einsum(
        "hqk,qhd->khd",
        probabilities.astype(BF16),
        grad_out,
        preferred_element_type=F32,
    )
    return (
        query_grad,
        jnp.concatenate(
            [key_grad.reshape(key_count, D), value_grad.reshape(key_count, D)], axis=-1
        ),
    )


def backward_fold(queries, grad_out, log_sum, row_delta, scaling, pieces):
    key_pairs, allowed = pieces

    def backward_per_doc(doc_items):
        doc_queries, doc_grad, doc_log, doc_delta, doc_pairs, doc_allowed = doc_items
        result = backward_doc(
            doc_queries, doc_grad, doc_log, doc_delta, doc_pairs, doc_allowed, scaling
        )
        return result

    query_parts, pair_parts = lax.map(
        backward_per_doc, (queries, grad_out, log_sum, row_delta, key_pairs, allowed)
    )
    return (query_parts, pair_parts)


def start_state():
    return (
        jnp.full((DOCS, H, PAGE), NEGATIVE, F32),
        jnp.zeros((DOCS, H, PAGE), F32),
        jnp.zeros((DOCS, H, PAGE, HD), F32),
    )


def finish_state(state):
    running_max, summed, accumulated = state
    result = jnp.transpose(accumulated / summed[..., None], (0, 2, 1, 3))
    return (result, running_max + jnp.log(summed))


def tile_order(grad, wide_count, blk_count):
    rows, cols = grad.shape
    tiled = grad.reshape(wide_count, rows // wide_count, blk_count, cols // blk_count)
    return jnp.transpose(tiled, (0, 2, 1, 3)).reshape(
        wide_count * blk_count * (rows // wide_count), cols // blk_count
    )


def plain_body(
    text_blocks,
    image_blocks,
    cotangent,
    text_mask,
    page_regions,
    doc_pages,
    self_project,
    self_output,
    cross_query,
    cross_pairs,
    cross_output,
    gate_weight,
    expand_weight,
    expand_bias,
    reduce_weight,
    reduce_bias,
    norm_gain,
    norm_bias,
):
    scaling = HD ** (-0.5)
    block_shape = text_blocks.shape
    offsets = jnp.arange(PAGE, dtype=jnp.int32)
    living = (lax.axis_index("blk") < doc_pages)[:, None]
    text_open = (living & ((text_mask > 0) | (offsets[None, :] == 0))).astype(BF16)
    image_open = (living & (offsets[None, :] < page_regions)).astype(BF16)
    text_rows = text_blocks.reshape(-1, D).astype(F32)
    image_rows = image_blocks.reshape(-1, D).astype(F32)
    normed_text, scaled_first, inverse_first = normalize(text_rows, norm_gain[0], norm_bias[0])
    normed_low = normed_text.astype(BF16)
    triples = product(normed_low, self_project).astype(BF16)
    self_queries = triples[:, :D].reshape(DOCS, PAGE, H, HD)
    self_pairs = triples[:, D:].reshape(DOCS, PAGE, 2 * D)
    self_state = forward_fold(
        self_queries,
        scaling,
        start_state(),
        (
            lax.all_gather(self_pairs, "blk", axis=1, tiled=True),
            lax.all_gather(text_open, "blk", axis=1, tiled=True),
        ),
    )
    self_result, self_logsum = finish_state(self_state)
    self_low = self_result.reshape(-1, D).astype(BF16)
    hidden = text_rows + product(self_low, self_output)
    cross_normed, scaled_cross, inverse_cross = normalize(hidden, norm_gain[1], norm_bias[1])
    cross_low = cross_normed.astype(BF16)
    gate_values = jax.nn.sigmoid(product(cross_low, gate_weight))
    image_normed, scaled_image, inverse_image = normalize(image_rows, norm_gain[2], norm_bias[2])
    image_low = image_normed.astype(BF16)
    image_pairs = product(image_low, cross_pairs).astype(BF16).reshape(DOCS, PAGE, 2 * D)
    cross_queries = product(cross_low, cross_query).astype(BF16).reshape(DOCS, PAGE, H, HD)
    cross_state = forward_fold(
        cross_queries,
        scaling,
        start_state(),
        (
            lax.all_gather(image_pairs, "blk", axis=1, tiled=True),
            lax.all_gather(image_open, "blk", axis=1, tiled=True),
        ),
    )
    cross_result, cross_logsum = finish_state(cross_state)
    gate_heads = gate_values.reshape(DOCS, PAGE, H, 1)
    gated_low = (cross_result * gate_heads).reshape(-1, D).astype(BF16)
    mixed_rows = hidden + product(gated_low, cross_output)
    final_normed, scaled_final, inverse_final = normalize(mixed_rows, norm_gain[3], norm_bias[3])
    final_low = final_normed.astype(BF16)
    inner_rows = product(final_low, expand_weight) + expand_bias
    active_low = gelu_tanh(inner_rows).astype(BF16)
    joined_blocks = (
        (mixed_rows + product(active_low, reduce_weight) + reduce_bias)
        .reshape(block_shape)
        .astype(BF16)
    )
    upstream = cotangent.reshape(-1, D)
    upstream_float = upstream.astype(F32)
    grad_reduce_bias = jnp.sum(upstream_float, axis=0)
    grad_reduce_weight = transposed(active_low, upstream)
    grad_active = against(upstream, reduce_weight).astype(BF16)
    gelu_value, gelu_pull = jax.vjp(gelu_tanh, inner_rows)
    grad_inner = gelu_pull(grad_active.astype(F32))[0].astype(BF16)
    grad_expand_bias = jnp.sum(grad_inner.astype(F32), axis=0)
    grad_expand_weight = transposed(final_low, grad_inner)
    back_final, gain_final, shift_final = normalize_back(
        against(grad_inner, expand_weight), scaled_final, inverse_final, norm_gain[3]
    )
    grad_mixed = upstream_float + back_final
    grad_branch = grad_mixed.astype(BF16)
    grad_cross_output = transposed(gated_low, grad_branch)
    grad_gated = against(grad_branch, cross_output).astype(BF16)
    grad_gated_heads = grad_gated.astype(F32).reshape(DOCS, PAGE, H, HD)
    grad_gate = jnp.sum(grad_gated_heads * cross_result, axis=-1).reshape(-1, H)
    grad_logit = grad_gate * gate_values * (1.0 - gate_values)
    grad_gate_weight = lax.dot_general(
        cross_low.astype(F32), grad_logit, (((0,), (0,)), ((), ())), precision=HIGHEST
    )
    grad_raw = (grad_gated_heads * gate_heads).astype(BF16)
    cross_delta = jnp.transpose(
        jnp.sum(grad_raw.astype(F32) * cross_result, axis=-1), (0, 2, 1)
    )
    cross_carry = backward_fold(
        cross_queries,
        grad_raw,
        cross_logsum,
        cross_delta,
        scaling,
        (
            lax.all_gather(image_pairs, "blk", axis=1, tiled=True),
            lax.all_gather(image_open, "blk", axis=1, tiled=True),
        ),
    )
    cross_home = lax.psum_scatter(
        cross_carry[1].astype(BF16), "blk", scatter_dimension=1, tiled=True
    ).astype(F32)
    cross_query_sum = cross_carry[0]
    cross_query_low = cross_query_sum.reshape(-1, D).astype(BF16)
    cross_pair_low = cross_home.reshape(-1, 2 * D).astype(BF16)
    grad_cross_query = transposed(cross_low, cross_query_low)
    grad_cross_pairs = transposed(image_low, cross_pair_low)
    back_image, gain_image, shift_image = normalize_back(
        against(cross_pair_low, cross_pairs), scaled_image, inverse_image, norm_gain[2]
    )
    image_grad = back_image.reshape(block_shape).astype(BF16)
    grad_cross_in = against(cross_query_low, cross_query) + lax.dot_general(
        grad_logit, gate_weight.astype(F32), (((1,), (1,)), ((), ())), precision=HIGHEST
    )
    back_cross, gain_cross, shift_cross = normalize_back(
        grad_cross_in, scaled_cross, inverse_cross, norm_gain[1]
    )
    grad_hidden = grad_mixed + back_cross
    grad_self_branch = grad_hidden.astype(BF16)
    grad_self_output = transposed(self_low, grad_self_branch)
    grad_self_result = (
        against(grad_self_branch, self_output).astype(BF16).reshape(DOCS, PAGE, H, HD)
    )
    self_delta = jnp.transpose(
        jnp.sum(grad_self_result.astype(F32) * self_result, axis=-1), (0, 2, 1)
    )
    self_carry = backward_fold(
        self_queries,
        grad_self_result,
        self_logsum,
        self_delta,
        scaling,
        (
            lax.all_gather(self_pairs, "blk", axis=1, tiled=True),
            lax.all_gather(text_open, "blk", axis=1, tiled=True),
        ),
    )
    self_home = lax.psum_scatter(
        self_carry[1].astype(BF16), "blk", scatter_dimension=1, tiled=True
    ).astype(F32)
    self_query_sum = self_carry[0]
    grad_triples = jnp.concatenate(
        [self_query_sum.reshape(-1, D), self_home.reshape(-1, 2 * D)], axis=-1
    ).astype(BF16)
    grad_self_project = transposed(normed_low, grad_triples)
    back_first, gain_first, shift_first = normalize_back(
        against(grad_triples, self_project), scaled_first, inverse_first, norm_gain[0]
    )
    text_grad = (grad_hidden + back_first).reshape(block_shape).astype(BF16)
    wide_count = lax.axis_size("wide")
    blk_count = lax.axis_size("blk")
    large_grads = (
        grad_self_project,
        grad_self_output,
        grad_cross_query,
        grad_cross_pairs,
        grad_cross_output,
        grad_expand_weight,
        grad_reduce_weight,
    )
    ordered = tuple((tile_order(grad, wide_count, blk_count) for grad in large_grads))
    summed_grads = lax.psum_scatter(ordered, ("wide", "blk"), scatter_dimension=0, tiled=True)
    small_sums = lax.psum(
        (
            grad_gate_weight,
            grad_expand_bias,
            grad_reduce_bias,
            jnp.stack([gain_first, gain_cross, gain_image, gain_final]),
            jnp.stack([shift_first, shift_cross, shift_image, shift_final]),
        ),
        ("wide", "blk"),
    )
    return (
        joined_blocks,
        text_grad,
        image_grad,
        summed_grads[0],
        summed_grads[1],
        summed_grads[2],
        summed_grads[3],
        summed_grads[4],
        summed_grads[5],
        summed_grads[6],
        small_sums[0],
        small_sums[1],
        small_sums[2],
        small_sums[3],
        small_sums[4],
    )


def solution(mesh):
    rows = P("wide", "blk", None)
    fits = (mesh.shape["wide"], mesh.shape["blk"]) == PLANNED
    return jax.shard_map(
        body if fits else plain_body,
        mesh=mesh,
        in_specs=(rows,) * 3 + (P("wide", "blk"),) * 2 + (P("wide"),) + (P(),) * 12,
        out_specs=(rows,) * 3 + (P("wide", "blk"),) * 7 + (P(),) * 5,
        check_vma=False,
    )
```
